256 devices in a mesh: gx: 64 (over y_lo, z, x), gy: 4 (over y_hi, core).
Axes of the slice: x: 4, y: 4 (y_hi: 2, y_lo: 2; y = y_hi * 2 + y_lo), z: 8, core: 2. Of those that a mesh axis runs over, the one named last changes fastest.
Arguments:
- populations: float32 [19, 128, 128, 128], P(None, 'gx', 'gy'), may hold values from 0 to 1, as said below
- fluid: int32 [128, 128, 128], P('gx', 'gy'), may hold values 0 or 1
- label: int32 [128, 128, 128], P('gx', 'gy'), may hold values from 0 to 16383, as said below
- wall_wetting: float32 [16384], P('gx'), may hold values from 0.3 to 1
- target: float32 [128, 128, 128], P('gx', 'gy'), may hold values from 0.8 to 1.6
Outputs:
- population_grad: float32 [19, 128, 128, 128], P(None, 'gx', 'gy')
- wetting_grad: float32 [16384], P('gx')
The draws below stay inside these ranges and needn't reach their ends.
Inputs may be any that keep to these rules, and one draw needn't show every extreme that they name: Cells of x slab j (x from j * 2 to j * 2 + 1) carry labels from j * 256 to j * 256 + 255 only; labels are constant on aligned blocks of 2 x 2 x 4 cells, and every label marks exactly 8 such blocks. `populations`: every entry is positive; the 19 entries of a cell sum to between 0.5 and 2.1.
All inputs are finite; a program needn't handle non-finite values. No bound on the sum of `fluid` on one device may be relied on, other than what follows from the above.
Results may differ from the reference program's by a relative error of at most 0.0003.
Values sent between devices are 32-bit elements; how exact they have to be, the bound alone decides.
No kernel may reach another device: no remote copies, remote signals or barrier semaphores. Data moves between devices by JAX's collectives and lax.ppermute only.
A program may use at most 64 MiB of HBM per device.

```python
import jax
import jax.numpy as jnp
from jax import lax

CX = 2
NZ = 128
STEPS = 2
LPD = 256
NX = 128
NY = 128
NLAB = 16384


def draw_populations(key, part):
    key = jax.random.fold_in(key, 5)
    first_key, second = jax.random.split(key)
    weights = jnp.array([1.0 / 3.0] + [1.0 / 18.0] * 6 + [1.0 / 36.0] * 12, jnp.float32).reshape(19, 1, 1, 1)
    density = jax.random.uniform(first_key, (NX, NY, NZ), jnp.float32, 0.8, 1.6)
    jitter = jax.random.uniform(second, (19, NX, NY, NZ), jnp.float32, -0.3, 0.3)
    return weights * density * (1.0 + jitter)


def draw_label(key, part):
    key = jax.random.fold_in(key, 7)
    slab_count = NX // CX
    patches = CX // 2 * (NY // 2) * (NZ // 4)
    slab_keys = jax.random.split(key, slab_count)
    shuffled = jax.vmap(lambda one_key: jax.random.permutation(one_key, patches))(slab_keys)
    local_ids = shuffled % LPD
    global_ids = local_ids + (jnp.arange(slab_count, dtype=jnp.int32) * LPD)[:, None]
    label_grid = global_ids.reshape(NX // 2, NY // 2, NZ // 4)
    label_grid = jnp.repeat(jnp.repeat(jnp.repeat(label_grid, 2, axis=0), 2, axis=1), 4, axis=2)
    return label_grid.astype(jnp.int32)


def set_ends(values, rng, smallest, high):
    spot = [jax.random.randint(jax.random.fold_in(rng, axis), (), 0, length) for axis, length in enumerate(values.shape)]
    main_axis = values.shape.index(max(values.shape))
    beside = spot[:main_axis] + [(spot[main_axis] + 1) % values.shape[main_axis]] + spot[main_axis + 1:]
    return values.at[tuple(spot)].set(smallest).at[tuple(beside)].set(high)


def shard_levels(key, dims, shards, least, high):
    def one(axis_at, shards_of):
        heights = jax.random.uniform(jax.random.fold_in(jax.random.fold_in(key, 6), axis_at), (shards_of,), jnp.float32, least / len(shards), high / len(shards))
        return jnp.repeat(jnp.exp(heights), dims[axis_at] // shards_of).reshape((-1,) + (1,) * (len(dims) - axis_at - 1))

    level = one(*shards[0])
    for cut in shards[1:]:
        level = level * one(*cut)
    return level


def setup_inputs(seed: int = 0) -> dict:
    key_of = jax.random.split(jax.random.key(seed), 6)
    return {
        "populations": draw_populations(jax.random.fold_in(key_of[5], 71), 0),
        "fluid": set_ends((jax.random.randint(key_of[1], (NX, NY, NZ), 0, 10) < 7).astype(jnp.int32), jax.random.fold_in(key_of[1], 1), 0, 1),
        "label": draw_label(jax.random.fold_in(key_of[5], 71), 0),
        "wall_wetting": jnp.clip(0.3 + 0.7 * jax.random.uniform(key_of[3], (NLAB,), jnp.float32) ** shard_levels(key_of[3], (NLAB,), ((0, 64),), -0.2, 0.2), 0.3, 1.0),
        "target": jnp.clip(0.8 + 0.8 * jax.random.uniform(key_of[4], (NX, NY, NZ), jnp.float32) ** shard_levels(key_of[4], (NX, NY, NZ), ((0, 64), (1, 4)), -0.2, 0.2), 0.8, 1.6),
    }


lattice_vectors = ((0, 0, 0), (1, 0, 0), (-1, 0, 0), (0, 1, 0), (0, -1, 0), (0, 0, 1), (0, 0, -1), (1, 1, 0), (-1, -1, 0), (1, -1, 0), (-1, 1, 0), (1, 0, 1), (-1, 0, -1), (1, 0, -1), (-1, 0, 1), (0, 1, 1), (0, -1, -1), (0, 1, -1), (0, -1, 1))
opposite_index = (0, 2, 1, 4, 3, 6, 5, 8, 7, 10, 9, 12, 11, 14, 13, 16, 15, 18, 17)
lattice_weights = (1.0 / 3.0,) + (1.0 / 18.0,) * 6 + (1.0 / 36.0,) * 12
coupling_strength = 5.0
shear_rate = 1.2

def moment_row(along_x, along_y, along_z):
    return [1, along_x, along_y, along_z, along_x * along_x + along_y * along_y + along_z * along_z, along_x * along_x - along_y * along_y, along_y * along_y - along_z * along_z, along_x * along_y, along_y * along_z, along_x * along_z, along_x * along_y * along_y, along_x * along_z * along_z, along_y * along_x * along_x, along_y * along_z * along_z, along_z * along_x * along_x, along_z * along_y * along_y, along_x * along_x * along_y * along_y, along_y * along_y * along_z * along_z, along_x * along_x * along_z * along_z]

def invert_rows(matrix_rows):
    order = len(matrix_rows)
    working = [[float(entry) for entry in matrix_rows[row_index]] + [1.0 if row_index == other_index else 0.0 for other_index in range(order)] for row_index in range(order)]
    for column in range(order):
        pivot_row = max(range(column, order), key=lambda row_index: abs(working[row_index][column]))
        working[column], working[pivot_row] = (working[pivot_row], working[column])
        leading = working[column][column]
        working[column] = [entry / leading for entry in working[column]]
        for row_index in range(order):
            if row_index != column:
                factor = working[row_index][column]
                if factor != 0.0:
                    working[row_index] = [first - factor * second for first, second in zip(working[row_index], working[column])]
    return [row_values[order:] for row_values in working]

def collision_table():
    columns = [moment_row(v[0], v[1], v[2]) for v in lattice_vectors]
    moments = [[float(columns[point][moment]) for point in range(19)] for moment in range(19)]
    rates = [0.0, shear_rate, shear_rate, shear_rate, 1.19] + [shear_rate] * 5 + [1.5] * 6 + [1.4] * 3
    inverse_rows = invert_rows(moments)
    table = []
    for outer in range(19):
        scaled = [inverse_rows[outer][moment] * rates[moment] for moment in range(19)]
        table.append([sum((scaled[moment] * moments[moment][inner] for moment in range(19))) for inner in range(19)])
    return table

def collide(populations, force, fluid_share):
    table = jnp.asarray(collision_table(), jnp.float32)
    vectors = jnp.asarray([[float(v[axis_id]) for v in lattice_vectors] for axis_id in range(3)], jnp.float32)
    weights = jnp.asarray(list(lattice_weights), jnp.float32).reshape((19,) + (1,) * (populations.ndim - 1))
    density = lax.optimization_barrier(jnp.sum(populations, axis=0))
    momentum = jnp.einsum('aq,q...->a...', vectors, populations, precision=lax.Precision.HIGHEST)
    velocity = (momentum + force / shear_rate) / density
    projected = jnp.einsum('aq,a...->q...', vectors, velocity, precision=lax.Precision.HIGHEST)
    speed = lax.optimization_barrier(jnp.sum(velocity * velocity, axis=0))
    balance = weights * density * (1.0 + 3.0 * projected + 4.5 * projected * projected - 1.5 * speed)
    change = jnp.einsum('pq,q...->p...', table, populations - balance, precision=lax.Precision.HIGHEST)
    return populations - fluid_share * change

def shifted(field, along_x, along_y, along_z):
    return jnp.roll(field, (along_x, along_y, along_z), axis=(0, 1, 2))

def advance(populations, fluid_share, wall_pseudo):
    density = lax.optimization_barrier(jnp.sum(populations, axis=0))
    pseudo = 1.0 - jnp.exp(-density)
    effective = fluid_share * pseudo + (1.0 - fluid_share) * wall_pseudo
    parts = [jnp.zeros_like(density), jnp.zeros_like(density), jnp.zeros_like(density)]
    for index in range(1, 19):
        vector = lattice_vectors[index]
        beside = shifted(effective, -vector[0], -vector[1], -vector[2])
        for axis_id in range(3):
            if vector[axis_id] != 0:
                parts[axis_id] = parts[axis_id] + lattice_weights[index] * vector[axis_id] * beside
    pull_sum = jnp.stack(parts)
    force = coupling_strength * pseudo * pull_sum
    relaxed = collide(populations, force, fluid_share)
    moved = []
    for index in range(19):
        vector = lattice_vectors[index]
        source = shifted(relaxed[index], vector[0], vector[1], vector[2])
        share = shifted(fluid_share, vector[0], vector[1], vector[2])
        moved.append(share * source + (1.0 - share) * relaxed[opposite_index[index]])
    return jnp.stack(moved)

def reference(populations, fluid, label, wall_wetting, target):
    fluid_share = fluid.astype(jnp.float32)

    def misfit_of(start, wetting):
        wall_pseudo = jnp.take(wetting, label, axis=0)
        state = start
        for step in range(STEPS):
            state = advance(state, fluid_share, wall_pseudo)
        density = lax.optimization_barrier(jnp.sum(state, axis=0))
        return 0.5 * jnp.sum(fluid_share * (density - target) ** 2)
    _, pullback = jax.vjp(misfit_of, populations, wall_wetting)
    population_grad, wetting_grad = pullback(jnp.ones((), jnp.float32))
    return (population_grad, wetting_grad)
```

```python
import functools

import jax
import jax.numpy as jnp
from jax import lax
from jax.experimental import pallas as pl
from jax.experimental.pallas import tpu as pltpu
from jax.sharding import PartitionSpec as P

HALO = 8
PAD = 8
OWN = 32
ROWS = OWN + 2 * HALO
TALL = ROWS + 2 * PAD
DEPTH = 128
CHUNKS = ROWS // 8
LABELS = 256

VECTORS = (
    (0, 0, 0), (1, 0, 0), (-1, 0, 0), (0, 1, 0), (0, -1, 0), (0, 0, 1), (0, 0, -1),
    (1, 1, 0), (-1, -1, 0), (1, -1, 0), (-1, 1, 0), (1, 0, 1), (-1, 0, -1), (1, 0, -1), (-1, 0, 1),
    (0, 1, 1), (0, -1, -1), (0, 1, -1), (0, -1, 1),
)
OPPOSITE = (0, 2, 1, 4, 3, 6, 5, 8, 7, 10, 9, 12, 11, 14, 13, 16, 15, 18, 17)
INDEX = {v: i for i, v in enumerate(VECTORS)}
RIGHTWARD = tuple(i for i in range(19) if VECTORS[i][0] == 1)
LEFTWARD = tuple(i for i in range(19) if VECTORS[i][0] == -1)
TURNED = tuple(i for i in range(19) if VECTORS[i][2] != 0)
PLANES = ((0, 1), (1, 2), (0, 2))
COUPLING = 5.0
SHEAR = 1.2
BULK = 1.19
THIRD = 1.5
FOURTH = 1.4
TRACE = (BULK - SHEAR) / 3.0
PULL = COUPLING / 36.0


def axis_index_of(axis, sign):
    v = [0, 0, 0]
    v[axis] = sign
    return INDEX[tuple(v)]


def edge_index_of(a, b, sa, sb):
    v = [0, 0, 0]
    v[a], v[b] = sa, sb
    return INDEX[tuple(v)]


def add(*terms):
    total = None
    for term in terms:
        if term is not None:
            total = term if total is None else total + term
    return total


def sub(a, b):
    if b is None:
        return a
    return -b if a is None else a - b


def scale(c, a):
    return None if a is None else c * a


def mul(a, b):
    return None if a is None or b is None else a * b


def moments(f):
    fourth, mixed, third = {}, {}, {}
    for a, b in PLANES:
        pp, mm = f[edge_index_of(a, b, 1, 1)], f[edge_index_of(a, b, -1, -1)]
        pm, mp = f[edge_index_of(a, b, 1, -1)], f[edge_index_of(a, b, -1, 1)]
        even, odd, cross, skew = pp + mm, pp - mm, pm + mp, pm - mp
        fourth[a, b] = even + cross
        mixed[a, b] = even - cross
        third[a, b] = odd + skew
        third[b, a] = odd - skew
    first, diagonal, total = [], [], f[0]
    for a in range(3):
        b, c = [k for k in range(3) if k != a]
        plus, minus = f[axis_index_of(a, 1)], f[axis_index_of(a, -1)]
        both = plus + minus
        total = total + both
        diagonal.append(both + fourth[tuple(sorted((a, b)))] + fourth[tuple(sorted((a, c)))])
        first.append((plus - minus) + third[a, b] + third[a, c])
    total = total + fourth[0, 1] + fourth[1, 2] + fourth[0, 2]
    return total, first, diagonal, mixed, third, fourth


def from_moments(first, diagonal, mixed, third, fourth, which):
    out = {}
    for i in which:
        v = VECTORS[i]
        axes = [a for a in range(3) if v[a] != 0]
        if not axes:
            out[i] = (fourth[0, 1] + fourth[1, 2] + fourth[0, 2]) - (diagonal[0] + diagonal[1] + diagonal[2])
        elif len(axes) == 1:
            a = axes[0]
            b, c = [k for k in range(3) if k != a]
            even = diagonal[a] - fourth[tuple(sorted((a, b)))] - fourth[tuple(sorted((a, c)))]
            odd = first[a] - third[a, b] - third[a, c]
            out[i] = 0.5 * (even + odd if v[a] > 0 else even - odd)
        else:
            a, b = axes
            value = fourth[a, b] + mixed[a, b] if v[a] * v[b] > 0 else fourth[a, b] - mixed[a, b]
            value = value + third[a, b] if v[a] > 0 else value - third[a, b]
            value = value + third[b, a] if v[b] > 0 else value - third[b, a]
            out[i] = 0.25 * value
    return out


def rated(first, diagonal, mixed, third, fourth):
    trace = TRACE * (diagonal[0] + diagonal[1] + diagonal[2])
    return (
        [SHEAR * m for m in first],
        [SHEAR * m + trace for m in diagonal],
        {k: SHEAR * m for k, m in mixed.items()},
        {k: THIRD * m for k, m in third.items()},
        {k: FOURTH * m for k, m in fourth.items()},
    )


def linear_part(f, share, which):
    total, first, diagonal, mixed, third, fourth = moments(f)
    change = from_moments(*rated(first, diagonal, mixed, third, fourth), which)
    return total, first, {i: f[i] - share * change[i] for i in which}


def balance_part(density, flow, velocity, share, which):
    d = density * share
    m = [flow[a] * share for a in range(3)]
    square = [m[a] * velocity[a] for a in range(3)]
    diagonal = [d * (1.0 / 3.0) + square[a] for a in range(3)]
    mixed = {(a, b): m[a] * velocity[b] for a, b in PLANES}
    third = {}
    fourth = {}
    for a, b in PLANES:
        c = 3 - a - b
        third[a, b] = m[a] * (1.0 / 3.0)
        third[b, a] = m[b] * (1.0 / 3.0)
        fourth[a, b] = d * (1.0 / 9.0) + (square[a] + square[b]) * (1.0 / 3.0) - square[c] * (1.0 / 6.0)
    return from_moments(*rated(m, diagonal, mixed, third, fourth), which)


def dual(r):
    get = lambda i: r.get(i)
    first, diagonal = [], []
    plus_of, minus_of = [], []
    for a in range(3):
        p, m = get(axis_index_of(a, 1)), get(axis_index_of(a, -1))
        even = scale(0.5, add(p, m))
        odd = scale(0.5, sub(p, m))
        plus_of.append(even)
        minus_of.append(odd)
        first.append(odd)
        diagonal.append(sub(even, get(0)))
    mixed, third, fourth = {}, {}, {}
    for a, b in PLANES:
        pp, mm = get(edge_index_of(a, b, 1, 1)), get(edge_index_of(a, b, -1, -1))
        pm, mp = get(edge_index_of(a, b, 1, -1)), get(edge_index_of(a, b, -1, 1))
        even, odd, cross, skew = add(pp, mm), sub(pp, mm), add(pm, mp), sub(pm, mp)
        fourth[a, b] = add(sub(sub(scale(0.25, add(even, cross)), plus_of[a]), plus_of[b]), get(0))
        mixed[a, b] = scale(0.25, sub(even, cross))
        third[a, b] = sub(scale(0.25, add(odd, skew)), minus_of[a])
        third[b, a] = sub(scale(0.25, sub(odd, skew)), minus_of[b])
    trace = scale(TRACE, add(*diagonal))
    return (
        [scale(SHEAR, m) for m in first],
        [add(scale(SHEAR, m), trace) for m in diagonal],
        {k: scale(SHEAR, m) for k, m in mixed.items()},
        {k: scale(THIRD, m) for k, m in third.items()},
        {k: scale(FOURTH, m) for k, m in fourth.items()},
    )


def flow_adjoint(first, diagonal, mixed, third, fourth, u):
    q = []
    for a in range(3):
        b, c = [k for k in range(3) if k != a]
        ab, ac, bc = tuple(sorted((a, b))), tuple(sorted((a, c))), tuple(sorted((b, c)))
        along = add(
            scale(2.0, diagonal[a]),
            scale(2.0 / 3.0, add(fourth[ab], fourth[ac])),
            scale(-1.0 / 3.0, fourth[bc]),
        )
        q.append(
            add(
                first[a],
                scale(1.0 / 3.0, add(third[a, b], third[a, c])),
                mul(u[a], along),
                mul(u[b], mixed[ab]),
                mul(u[c], mixed[ac]),
            )
        )
    return q


def collide_adjoint(r, u):
    t = dual(r)
    first, diagonal, mixed, third, fourth = t
    q = flow_adjoint(*t, u)
    square = [u[a] * u[a] for a in range(3)]
    by_density = None
    for a in range(3):
        b, c = [k for k in range(3) if k != a]
        by_density = add(
            by_density,
            u[a] * (first[a] + (1.0 / 3.0) * (third[a, b] + third[a, c]) - q[a]),
            diagonal[a] * (1.0 / 3.0 + square[a]),
        )
    for a, b in PLANES:
        c = 3 - a - b
        by_density = by_density + mixed[a, b] * (u[a] * u[b])
        by_density = by_density + fourth[a, b] * (
            1.0 / 9.0 + (square[a] + square[b]) * (1.0 / 3.0) - square[c] * (1.0 / 6.0)
        )
    drift = [q[a] - first[a] for a in range(3)]
    base = {0: r[0]}
    for a in range(3):
        base[axis_index_of(a, 1)] = r[axis_index_of(a, 1)] + (drift[a] - diagonal[a])
        base[axis_index_of(a, -1)] = r[axis_index_of(a, -1)] - (drift[a] + diagonal[a])
    for a, b in PLANES:
        along = drift[a] - third[a, b]
        across = drift[b] - third[b, a]
        even = diagonal[a] + diagonal[b] + fourth[a, b]
        same, cross = even + mixed[a, b], even - mixed[a, b]
        both, gap = along + across, along - across
        base[edge_index_of(a, b, 1, 1)] = r[edge_index_of(a, b, 1, 1)] + (both - same)
        base[edge_index_of(a, b, -1, -1)] = r[edge_index_of(a, b, -1, -1)] - (both + same)
        base[edge_index_of(a, b, 1, -1)] = r[edge_index_of(a, b, 1, -1)] + (gap - cross)
        base[edge_index_of(a, b, -1, 1)] = r[edge_index_of(a, b, -1, 1)] - (gap + cross)
    return base, by_density, q


def rolled(x, step):
    return x if step == 0 else pltpu.roll(x, step % DEPTH, 1)


def rows_at(t, shift, offset):
    if shift == 0:
        return pl.ds(pl.multiple_of(t * 8 + offset, 8), 8)
    return pl.ds(t * 8 + (offset + shift), 8)


def flat(t):
    return rows_at(t, 0, 0)


def tall(t, shift=0):
    return rows_at(t, shift, PAD)


def each_chunk(body, first=0, last=CHUNKS):
    def step(t, carry):
        body(t)
        return carry

    lax.fori_loop(first, last, step, 0)


def gradient_of(field, doubled, p, t):
    at = lambda dp, dy: field[p + dp, tall(t, dy), :]
    rp, rm, lp, lm = at(1, 1), at(1, -1), at(-1, 1), at(-1, -1)
    along_x = doubled[p + 1, tall(t), :] - doubled[p - 1, tall(t), :] + (rp + rm) - (lp + lm)
    along_y = doubled[p, tall(t, 1), :] - doubled[p, tall(t, -1), :] + (rp + lp) - (rm + lm)
    star = 2.0 * at(0, 0) + at(1, 0) + at(-1, 0) + at(0, 1) + at(0, -1)
    return [along_x, along_y, rolled(star, -1) - rolled(star, 1)]


def with_sides(x):
    return 2.0 * x + rolled(x, 1) + rolled(x, -1)


def edges_kernel(pops, fluid, label, target, low, high):
    low[0:19] = pops[:, :, 0:HALO, :]
    high[0:19] = pops[:, :, OWN - HALO : OWN, :]
    low[19] = fluid[:, 0:HALO, :].astype(jnp.float32)
    high[19] = fluid[:, OWN - HALO : OWN, :].astype(jnp.float32)
    low[20] = label[:, 0:HALO, :].astype(jnp.float32)
    high[20] = label[:, OWN - HALO : OWN, :].astype(jnp.float32)
    low[21] = target[:, 0:HALO, :]
    high[21] = target[:, OWN - HALO : OWN, :]


def put_sends(send_left, send_right, t, lin, first, chosen, effective):
    for k, i in enumerate(LEFTWARD):
        send_left[k, flat(t), :] = lin[0][i]
    for k, i in enumerate(RIGHTWARD):
        send_right[k, flat(t), :] = lin[1][i]
    for a in range(3):
        send_left[5 + a, flat(t), :] = first[0][a]
        send_right[5 + a, flat(t), :] = first[1][a]
    send_left[8, flat(t), :] = chosen[0]
    send_right[8, flat(t), :] = chosen[1]
    send_left[9, flat(t), :] = effective[1]
    send_right[9, flat(t), :] = effective[0]


def start_kernel(
    pops, fluid, label, target, wetting, below, above,
    lin_out, flow_out, density_out, effective_out, share_out, target_out, send_left, send_right,
    wide, label_wide,
):
    wide[:, :, HALO : HALO + OWN, :] = pops[...]
    wide[:, :, 0:HALO, :] = below[0:19]
    wide[:, :, HALO + OWN : ROWS, :] = above[0:19]
    share_out[:, HALO : HALO + OWN, :] = fluid[...].astype(jnp.float32)
    share_out[:, 0:HALO, :] = below[19]
    share_out[:, HALO + OWN : ROWS, :] = above[19]
    label_wide[:, HALO : HALO + OWN, :] = label[...]
    label_wide[:, 0:HALO, :] = below[20].astype(jnp.int32)
    label_wide[:, HALO + OWN : ROWS, :] = above[20].astype(jnp.int32)
    target_out[:, HALO : HALO + OWN, :] = target[...]
    target_out[:, 0:HALO, :] = below[21]
    target_out[:, HALO + OWN : ROWS, :] = above[21]
    half_low = jnp.broadcast_to(wetting[0:1, :], (8, DEPTH))
    half_high = jnp.broadcast_to(wetting[1:2, :], (8, DEPTH))

    def body(t):
        lin, first, chosen, effective = [], [], [], []
        for x in range(2):
            f = {i: wide[i, x, flat(t), :] for i in range(19)}
            share = share_out[x, flat(t), :]
            marks = label_wide[x, flat(t), :]
            spot = jnp.bitwise_and(marks, DEPTH - 1)
            wall = jnp.where(
                jnp.bitwise_and(marks, DEPTH) == 0,
                jnp.take_along_axis(half_low, spot, axis=1),
                jnp.take_along_axis(half_high, spot, axis=1),
            )
            total, momentum, linear = linear_part(f, share, range(19))
            eff = jnp.where(share > 0, 1.0 - jnp.exp(-total), wall)
            for i in range(19):
                lin_out[i, x, flat(t), :] = linear[i]
            for a in range(3):
                flow_out[a, x, flat(t), :] = momentum[a]
            density_out[x, flat(t), :] = total
            effective_out[x, flat(t), :] = eff
            lin.append(linear)
            first.append(momentum)
            chosen.append(jnp.where(share > 0, total, wall))
            effective.append(eff)
        put_sends(send_left, send_right, t, lin, first, chosen, effective)
        send_left[10, flat(t), :] = share_out[0, flat(t), :]
        send_left[11, flat(t), :] = share_out[1, flat(t), :]
        send_right[10, flat(t), :] = share_out[1, flat(t), :]
        send_right[11, flat(t), :] = share_out[0, flat(t), :]

    each_chunk(body)


def step_kernel(is_first, *refs):
    if is_first:
        (lin, flow, density, effective, share, from_left, from_right,
         masks, field, speed, pull_out, lin_out, flow_out, density_out, effective_out, send_left, send_right,
         doubled, relaxed, turned) = refs
    else:
        (lin, flow, density, effective, share, target, masks, from_left, from_right,
         field, speed, pull_out, misfit_out,
         doubled, relaxed, turned) = refs
    sides = ((1, from_left, 0), (4, from_right, 5))

    def place(t):
        def put(p, x, s):
            field[p, tall(t), :] = x
            doubled[p, tall(t), :] = with_sides(x)
            if is_first:
                masks[0, p, tall(t), :] = s
                masks[1, p, tall(t), :] = rolled(s, 1)
                masks[2, p, tall(t), :] = rolled(s, -1)

        for x in range(2):
            put(2 + x, effective[x, flat(t), :], share[x, flat(t), :])
        for near, come, far in sides:
            if is_first:
                s_near, s_far = come[10, flat(t), :], come[11, flat(t), :]
            else:
                s_near, s_far = masks[0, near, tall(t), :], None
            chosen = come[8, flat(t), :]
            put(near, jnp.where(s_near > 0, 1.0 - jnp.exp(-chosen), chosen), s_near)
            put(far, come[9, flat(t), :], s_far)

    each_chunk(place)

    def collide(t):
        for p in range(1, 5):
            own = p in (2, 3)
            pull = gradient_of(field, doubled, p, t)
            psi = field[p, tall(t), :]
            s = masks[0, p, tall(t), :]
            if own:
                rho = density[p - 2, flat(t), :]
                mom = [flow[a, p - 2, flat(t), :] for a in range(3)]
                which = range(19)
                lin_at = {i: lin[i, p - 2, flat(t), :] for i in which}
                for a in range(3):
                    pull_out[a, p - 2, flat(t), :] = pull[a]
            else:
                come = from_left if p == 1 else from_right
                rho = come[8, flat(t), :]
                mom = [come[5 + a, flat(t), :] for a in range(3)]
                which = RIGHTWARD if p == 1 else LEFTWARD
                lin_at = {i: come[k, flat(t), :] for k, i in enumerate(which)}
            push = psi * (PULL / SHEAR)
            full = [mom[a] + push * pull[a] for a in range(3)]
            inverse = 1.0 / rho
            u = [full[a] * inverse for a in range(3)]
            for a in range(3):
                speed[a, p - 1, flat(t), :] = u[a]
            part = balance_part(rho, full, u, s, which)
            for i in which:
                value = lin_at[i] + part[i]
                relaxed[i, p - 1, tall(t), :] = value
                if i in TURNED:
                    turned[TURNED.index(i), p - 1, tall(t), :] = rolled(value, VECTORS[i][2])

    each_chunk(collide)

    def stream(t):
        lin_sent, first_sent, chosen_sent, effective_sent = [], [], [], []
        for x in range(2):
            f = {}
            for i in range(19):
                cx, cy, cz = VECTORS[i]
                if i == 0:
                    f[i] = relaxed[0, 1 + x, tall(t), :]
                    continue
                if cz:
                    source = turned[TURNED.index(i), 1 + x - cx, tall(t, -cy), :]
                else:
                    source = relaxed[i, 1 + x - cx, tall(t, -cy), :]
                open_ = masks[cz % 3, 2 + x - cx, tall(t, -cy), :] > 0
                f[i] = jnp.where(open_, source, relaxed[OPPOSITE[i], 1 + x, tall(t), :])
            s = share[x, flat(t), :]
            if is_first:
                total, momentum, linear = linear_part(f, s, range(19))
                held = effective[x, flat(t), :]
                eff = jnp.where(s > 0, 1.0 - jnp.exp(-total), held)
                for i in range(19):
                    lin_out[i, x, flat(t), :] = linear[i]
                for a in range(3):
                    flow_out[a, x, flat(t), :] = momentum[a]
                density_out[x, flat(t), :] = total
                effective_out[x, flat(t), :] = eff
                lin_sent.append(linear)
                first_sent.append(momentum)
                chosen_sent.append(jnp.where(s > 0, total, held))
                effective_sent.append(eff)
            else:
                total = add(*[f[i] for i in range(19)])
                misfit_out[x, flat(t), :] = s * (total - target[x, flat(t), :])
        if is_first:
            put_sends(send_left, send_right, t, lin_sent, first_sent, chosen_sent, effective_sent)

    each_chunk(stream)


def spread_of(pulled, pulled_doubled, p, t):
    at = lambda a, dp, dy: pulled[a, p + dp, tall(t, dy), :]
    two = lambda a, dp, dy: pulled_doubled[a, p + dp, tall(t, dy), :]
    along_x = two(0, 1, 0) - two(0, -1, 0) + (at(0, 1, 1) + at(0, 1, -1)) - (at(0, -1, 1) + at(0, -1, -1))
    along_y = two(1, 0, 1) - two(1, 0, -1) + (at(1, 1, 1) + at(1, -1, 1)) - (at(1, 1, -1) + at(1, -1, -1))
    star = 2.0 * at(2, 0, 0) + at(2, 1, 0) + at(2, -1, 0) + at(2, 0, 1) + at(2, 0, -1)
    along_z = rolled(star, -1) - rolled(star, 1)
    return (along_x + along_y + along_z) * (-1.0 / 36.0)


def put_pulled(pulled, pulled_doubled, p, t, psi, q):
    for a in range(3):
        s = (COUPLING / SHEAR) * psi * q[a]
        pulled[a, p, tall(t), :] = s
        if a < 2:
            pulled_doubled[a, p, tall(t), :] = with_sides(s)


def mask_ahead(masks, i, p, t):
    cx, cy, cz = VECTORS[i]
    return masks[(-cz) % 3, p + cx, tall(t, cy), :] > 0


def last_reverse_kernel(
    misfit, from_left, from_right, masks, field, speed, pull, early_speed,
    adjoint, turned, wall_out, send_left, send_right,
    ahead, pulled, pulled_doubled, base,
):
    def place(t):
        for p in range(6):
            if p < 2:
                d = from_left[p, flat(t), :]
            elif p < 4:
                d = misfit[p - 2, flat(t), :]
            else:
                d = from_right[p - 4, flat(t), :]
            ahead[0, p, tall(t), :] = d
            ahead[1, p, tall(t), :] = rolled(d, 1)
            ahead[2, p, tall(t), :] = rolled(d, -1)

    each_chunk(place)

    def collide(t):
        for p in range(1, 5):
            s = masks[0, p, tall(t), :]
            here = ahead[0, p, tall(t), :]
            r = {0: here}
            for i in range(1, 19):
                cx, cy, cz = VECTORS[i]
                there = ahead[(-cz) % 3, p + cx, tall(t, cy), :]
                r[i] = s * jnp.where(mask_ahead(masks, i, p, t), there, here)
            psi = field[p, tall(t), :]
            u = [speed[a, p - 1, flat(t), :] for a in range(3)]
            if p in (2, 3):
                rest, by_density, q = collide_adjoint(r, u)
                along = add(*[q[a] * pull[a, p - 2, flat(t), :] for a in range(3)])
                const = by_density + along * ((PULL / SHEAR) * (1.0 - psi))
                for i in range(19):
                    base[i, p - 2, flat(t), :] = rest[i] + const
            else:
                q = flow_adjoint(*dual(r), u)
            put_pulled(pulled, pulled_doubled, p - 1, t, psi, q)

    each_chunk(collide)

    def finish(t):
        for x in range(2):
            s = masks[0, 2 + x, tall(t), :]
            spread = spread_of(pulled, pulled_doubled, 1 + x, t)
            wall_out[x, flat(t), :] = (1.0 - s) * spread
            more = s * spread * (1.0 - field[2 + x, tall(t), :])
            for i in range(19):
                value = base[i, x, flat(t), :] + more
                adjoint[i, x, tall(t), :] = value
                if i in TURNED:
                    turned[TURNED.index(i), x, tall(t), :] = rolled(value, -VECTORS[i][2])

    each_chunk(finish)

    def part(t):
        for x, send, sent, skipped in ((0, send_left, RIGHTWARD, -1), (1, send_right, LEFTWARD, 1)):
            p = 2 + x
            s = masks[0, p, tall(t), :]
            r = {}
            for i in range(19):
                cx, cy, cz = VECTORS[i]
                if cx == skipped:
                    continue
                r[i] = adjoint_ahead(adjoint, turned, masks, i, x, t)
            u = [early_speed[a, p - 1, flat(t), :] for a in range(3)]
            q = flow_adjoint(*dual(r), u)
            for a in range(3):
                send[5 + a, flat(t), :] = s * q[a]
            for k, i in enumerate(sent):
                send[k, flat(t), :] = adjoint[i, x, tall(t), :]

    each_chunk(part)


def adjoint_ahead(adjoint, turned, masks, i, x, t):
    cx, cy, cz = VECTORS[i]
    if i == 0:
        return adjoint[0, x, tall(t), :]
    if cz:
        there = turned[TURNED.index(i), x + cx, tall(t, cy), :]
    else:
        there = adjoint[i, x + cx, tall(t, cy), :]
    return jnp.where(mask_ahead(masks, i, 2 + x, t), there, adjoint[OPPOSITE[i], x, tall(t), :])


def first_reverse_kernel(
    adjoint, turned, wall, from_left, from_right, masks, field, speed, pull, chooser,
    grad, label_part,
    come, pulled, pulled_doubled, base,
):
    sides = ((0, from_left, LEFTWARD), (1, from_right, RIGHTWARD))

    def place(t):
        for side, source, which in sides:
            for k, i in enumerate(which):
                come[side, k, tall(t), :] = rolled(source[k, flat(t), :], -VECTORS[i][2])

    each_chunk(place)

    def collide(t):
        for x in range(2):
            p = 2 + x
            s = masks[0, p, tall(t), :]
            r = {}
            for i in range(19):
                cx, cy, cz = VECTORS[i]
                if (x, cx) in ((0, -1), (1, 1)):
                    side = x
                    there = come[side, sides[side][2].index(i), tall(t, cy), :]
                    value = jnp.where(
                        mask_ahead(masks, i, p, t), there, adjoint[OPPOSITE[i], x, tall(t), :]
                    )
                else:
                    value = adjoint_ahead(adjoint, turned, masks, i, x, t)
                r[i] = s * value
            psi = field[p, tall(t), :]
            u = [speed[a, p - 1, flat(t), :] for a in range(3)]
            rest, by_density, q = collide_adjoint(r, u)
            along = add(*[q[a] * pull[a, x, flat(t), :] for a in range(3)])
            const = by_density + along * ((PULL / SHEAR) * (1.0 - psi))
            for i in range(19):
                base[i, x, flat(t), :] = rest[i] + const
            put_pulled(pulled, pulled_doubled, p - 1, t, psi, q)
        for side, source, which in sides:
            p = 1 if side == 0 else 4
            x = 0 if side == 0 else 1
            s = masks[0, p, tall(t), :]
            r = {}
            for i in [OPPOSITE[j] for j in which]:
                cx, cy, cz = VECTORS[i]
                if cz:
                    there = turned[TURNED.index(i), x, tall(t, cy), :]
                else:
                    there = adjoint[i, x, tall(t, cy), :]
                here = source[which.index(OPPOSITE[i]), flat(t), :]
                r[i] = jnp.where(mask_ahead(masks, i, p, t), there, here)
            u = [speed[a, p - 1, flat(t), :] for a in range(3)]
            more = flow_adjoint(*dual(r), u)
            q = [source[5 + a, flat(t), :] + s * more[a] for a in range(3)]
            put_pulled(pulled, pulled_doubled, p - 1, t, field[p, tall(t), :], q)

    each_chunk(collide)

    def finish(t):
        total = None
        for x in range(2):
            s = masks[0, 2 + x, tall(t), :]
            spread = spread_of(pulled, pulled_doubled, 1 + x, t)
            total = add(total, (1.0 - s) * spread + wall[x, flat(t), :])
            more = s * spread * (1.0 - field[2 + x, tall(t), :])
            for i in range(19):
                grad[i, x, rows_at(t, 0, -HALO), :] = base[i, x, flat(t), :] + more
        base[0, 0, flat(t), :] = total

    each_chunk(finish, HALO // 8, (HALO + OWN) // 8)

    totals = base[0, 0, HALO : HALO + OWN, :]
    blocks = (OWN // 2) * (DEPTH // 4)
    column = lax.broadcasted_iota(jnp.int32, (DEPTH, blocks), 1)
    quad = lax.broadcasted_iota(jnp.int32, (DEPTH, blocks), 0) // 4
    gather = (jnp.bitwise_and(column, DEPTH // 4 - 1) == quad).astype(jnp.bfloat16)
    by_block = exact_dot(totals, gather)
    pair = lax.broadcasted_iota(jnp.int32, (OWN, blocks), 0) // 2
    wanted = lax.broadcasted_iota(jnp.int32, (OWN, blocks), 1) // (DEPTH // 4)
    by_block = jnp.where(pair == wanted, by_block, 0.0)
    by_label = exact_dot(by_block, chooser[...])
    label_part[...] = jnp.sum(by_label, axis=0, keepdims=True)


def exact_dot(values, zero_one):
    high = values.astype(jnp.bfloat16)
    left = values - high.astype(jnp.float32)
    middle = left.astype(jnp.bfloat16)
    low = (left - middle.astype(jnp.float32)).astype(jnp.bfloat16)
    dot = lambda part: jnp.dot(part, zero_one, preferred_element_type=jnp.float32)
    return dot(high) + (dot(middle) + dot(low))


def call(kernel, args, outs, scratch):
    whole = pl.BlockSpec(memory_space=pltpu.VMEM)
    return pl.pallas_call(
        kernel,
        out_shape=[jax.ShapeDtypeStruct(s, jnp.float32) for s in outs],
        in_specs=[whole] * len(args),
        out_specs=[whole] * len(outs),
        scratch_shapes=[pltpu.VMEM(s, d) for s, d in scratch],
        compiler_params=pltpu.CompilerParams(vmem_limit_bytes=40 * 1024 * 1024),
    )(*args)


def ring(axis):
    count = lax.axis_size(axis)
    up = [(i, (i + 1) % count) for i in range(count)]
    return up, [(j, i) for i, j in up]


def both_ways(to_lower, to_upper, axis):
    up, down = ring(axis)
    from_lower = lax.ppermute(to_upper, axis, up)
    from_upper = lax.ppermute(to_lower, axis, down)
    return from_lower, from_upper


def per_device(populations, fluid, label, wall_wetting, target):
    f32 = jnp.float32
    plane = (ROWS, DEPTH)
    two = (2, *plane)
    edge = (22, 2, HALO, DEPTH)
    low, high = call(edges_kernel, (populations, fluid, label, target), (edge, edge), ())
    below, above = both_ways(low, high, "gy")
    marks = jnp.bitwise_and(label[0, ::2, ::4], LABELS - 1).reshape(-1)
    chooser = (marks[:, None] == jnp.arange(LABELS, dtype=jnp.int32)[None, :]).astype(jnp.bfloat16)
    lin, flow, density, effective, share, target_wide, to_left, to_right = call(
        start_kernel,
        (populations, fluid, label, target, wall_wetting.reshape(2, DEPTH), below, above),
        ((19, *two), (3, *two), two, two, two, two, (12, *plane), (12, *plane)),
        (((19, *two), f32), (two, jnp.int32)),
    )
    from_left, from_right = both_ways(to_left, to_right, "gx")
    wide6 = (6, TALL, DEPTH)
    work = ((wide6, f32), ((19, 4, TALL, DEPTH), f32), ((10, 4, TALL, DEPTH), f32))
    masks, field0, speed0, pull0, lin, flow, density, effective, to_left, to_right = call(
        functools.partial(step_kernel, True),
        (lin, flow, density, effective, share, from_left, from_right),
        (
            (3, *wide6), wide6, (3, 4, *plane), (3, *two),
            (19, *two), (3, *two), two, two, (10, *plane), (10, *plane),
        ),
        work,
    )
    from_left, from_right = both_ways(to_left, to_right, "gx")
    field1, speed1, pull1, misfit = call(
        functools.partial(step_kernel, False),
        (lin, flow, density, effective, share, target_wide, masks, from_left, from_right),
        (wide6, (3, 4, *plane), (3, *two), two),
        work,
    )
    from_left, from_right = both_ways(misfit, misfit, "gx")
    pulled = (((3, 4, TALL, DEPTH), f32), ((2, 4, TALL, DEPTH), f32), ((19, *two), f32))
    adjoint, turned, wall, to_left, to_right = call(
        last_reverse_kernel,
        (misfit, from_left, from_right, masks, field1, speed1, pull1, speed0),
        ((19, 2, TALL, DEPTH), (10, 2, TALL, DEPTH), two, (8, *plane), (8, *plane)),
        (((3, *wide6), f32), *pulled),
    )
    from_left, from_right = both_ways(to_left, to_right, "gx")
    grad, label_part = call(
        first_reverse_kernel,
        (adjoint, turned, wall, from_left, from_right, masks, field0, speed0, pull0, chooser),
        (populations.shape, (1, LABELS)),
        (((2, 5, TALL, DEPTH), f32), *pulled),
    )
    count = lax.axis_size("gy")
    wetting_grad = label_part
    for step in range(1, count):
        wetting_grad = wetting_grad + lax.ppermute(
            label_part, "gy", [(i, (i + step) % count) for i in range(count)]
        )
    return (grad, wetting_grad.reshape(-1))


def solution(mesh):
    return jax.shard_map(
        per_device,
        mesh=mesh,
        in_specs=(
            P(None, "gx", "gy", None),
            P("gx", "gy", None),
            P("gx", "gy", None),
            P("gx"),
            P("gx", "gy", None),
        ),
        out_specs=(P(None, "gx", "gy", None), P("gx")),
        check_vma=False,
    )
```

```python
import functools

import jax
import jax.numpy as jnp
import numpy as np
from jax import lax
from jax.experimental import pallas as pl
from jax.experimental.pallas import tpu as pltpu
from jax.sharding import PartitionSpec as P

HALO = 8
PAD = 8
OWN = 32
ROWS = OWN + 2 * HALO
TALL = ROWS + 2 * PAD
DEPTH = 128
CHUNKS = ROWS // 8
LABELS = 256

VECTORS = (
    (0, 0, 0), (1, 0, 0), (-1, 0, 0), (0, 1, 0), (0, -1, 0), (0, 0, 1), (0, 0, -1),
    (1, 1, 0), (-1, -1, 0), (1, -1, 0), (-1, 1, 0), (1, 0, 1), (-1, 0, -1), (1, 0, -1), (-1, 0, 1),
    (0, 1, 1), (0, -1, -1), (0, 1, -1), (0, -1, 1),
)
OPPOSITE = (0, 2, 1, 4, 3, 6, 5, 8, 7, 10, 9, 12, 11, 14, 13, 16, 15, 18, 17)
INDEX = {v: i for i, v in enumerate(VECTORS)}
RIGHTWARD = tuple(i for i in range(19) if VECTORS[i][0] == 1)
LEFTWARD = tuple(i for i in range(19) if VECTORS[i][0] == -1)
TURNED = tuple(i for i in range(19) if VECTORS[i][2] != 0)
PLANES = ((0, 1), (1, 2), (0, 2))
COUPLING = 5.0
SHEAR = 1.2
BULK = 1.19
THIRD = 1.5
FOURTH = 1.4
TRACE = (BULK - SHEAR) / 3.0
PULL = COUPLING / 36.0


def axis_index_of(axis, sign):
    v = [0, 0, 0]
    v[axis] = sign
    return INDEX[tuple(v)]


def edge_index_of(a, b, sa, sb):
    v = [0, 0, 0]
    v[a], v[b] = sa, sb
    return INDEX[tuple(v)]


def add(*terms):
    total = None
    for term in terms:
        if term is not None:
            total = term if total is None else total + term
    return total


def sub(a, b):
    if b is None:
        return a
    return -b if a is None else a - b


def scale(c, a):
    return None if a is None else c * a


def mul(a, b):
    return None if a is None or b is None else a * b


def moments(f):
    fourth, mixed, third = {}, {}, {}
    for a, b in PLANES:
        pp, mm = f[edge_index_of(a, b, 1, 1)], f[edge_index_of(a, b, -1, -1)]
        pm, mp = f[edge_index_of(a, b, 1, -1)], f[edge_index_of(a, b, -1, 1)]
        even, odd, cross, skew = pp + mm, pp - mm, pm + mp, pm - mp
        fourth[a, b] = even + cross
        mixed[a, b] = even - cross
        third[a, b] = odd + skew
        third[b, a] = odd - skew
    first, diagonal, total = [], [], f[0]
    for a in range(3):
        b, c = [k for k in range(3) if k != a]
        plus, minus = f[axis_index_of(a, 1)], f[axis_index_of(a, -1)]
        both = plus + minus
        total = total + both
        diagonal.append(both + fourth[tuple(sorted((a, b)))] + fourth[tuple(sorted((a, c)))])
        first.append((plus - minus) + third[a, b] + third[a, c])
    total = total + fourth[0, 1] + fourth[1, 2] + fourth[0, 2]
    return total, first, diagonal, mixed, third, fourth


def from_moments(first, diagonal, mixed, third, fourth, which):
    out = {}
    for i in which:
        v = VECTORS[i]
        axes = [a for a in range(3) if v[a] != 0]
        if not axes:
            out[i] = (fourth[0, 1] + fourth[1, 2] + fourth[0, 2]) - (diagonal[0] + diagonal[1] + diagonal[2])
        elif len(axes) == 1:
            a = axes[0]
            b, c = [k for k in range(3) if k != a]
            even = diagonal[a] - fourth[tuple(sorted((a, b)))] - fourth[tuple(sorted((a, c)))]
            odd = first[a] - third[a, b] - third[a, c]
            out[i] = 0.5 * (even + odd if v[a] > 0 else even - odd)
        else:
            a, b = axes
            value = fourth[a, b] + mixed[a, b] if v[a] * v[b] > 0 else fourth[a, b] - mixed[a, b]
            value = value + third[a, b] if v[a] > 0 else value - third[a, b]
            value = value + third[b, a] if v[b] > 0 else value - third[b, a]
            out[i] = 0.25 * value
    return out


def rated(first, diagonal, mixed, third, fourth):
    trace = TRACE * (diagonal[0] + diagonal[1] + diagonal[2])
    return (
        [SHEAR * m for m in first],
        [SHEAR * m + trace for m in diagonal],
        {k: SHEAR * m for k, m in mixed.items()},
        {k: THIRD * m for k, m in third.items()},
        {k: FOURTH * m for k, m in fourth.items()},
    )


def linear_part(f, share, which):
    total, first, diagonal, mixed, third, fourth = moments(f)
    change = from_moments(*rated(first, diagonal, mixed, third, fourth), which)
    return total, first, {i: f[i] - share * change[i] for i in which}


def balance_part(density, flow, velocity, share, which):
    d = density * share
    m = [flow[a] * share for a in range(3)]
    square = [m[a] * velocity[a] for a in range(3)]
    diagonal = [d * (1.0 / 3.0) + square[a] for a in range(3)]
    mixed = {(a, b): m[a] * velocity[b] for a, b in PLANES}
    third = {}
    fourth = {}
    for a, b in PLANES:
        c = 3 - a - b
        third[a, b] = m[a] * (1.0 / 3.0)
        third[b, a] = m[b] * (1.0 / 3.0)
        fourth[a, b] = d * (1.0 / 9.0) + (square[a] + square[b]) * (1.0 / 3.0) - square[c] * (1.0 / 6.0)
    return from_moments(*rated(m, diagonal, mixed, third, fourth), which)


def dual(r):
    get = lambda i: r.get(i)
    first, diagonal = [], []
    plus_of, minus_of = [], []
    for a in range(3):
        p, m = get(axis_index_of(a, 1)), get(axis_index_of(a, -1))
        even = scale(0.5, add(p, m))
        odd = scale(0.5, sub(p, m))
        plus_of.append(even)
        minus_of.append(odd)
        first.append(odd)
        diagonal.append(sub(even, get(0)))
    mixed, third, fourth = {}, {}, {}
    for a, b in PLANES:
        pp, mm = get(edge_index_of(a, b, 1, 1)), get(edge_index_of(a, b, -1, -1))
        pm, mp = get(edge_index_of(a, b, 1, -1)), get(edge_index_of(a, b, -1, 1))
        even, odd, cross, skew = add(pp, mm), sub(pp, mm), add(pm, mp), sub(pm, mp)
        fourth[a, b] = add(sub(sub(scale(0.25, add(even, cross)), plus_of[a]), plus_of[b]), get(0))
        mixed[a, b] = scale(0.25, sub(even, cross))
        third[a, b] = sub(scale(0.25, add(odd, skew)), minus_of[a])
        third[b, a] = sub(scale(0.25, sub(odd, skew)), minus_of[b])
    trace = scale(TRACE, add(*diagonal))
    return (
        [scale(SHEAR, m) for m in first],
        [add(scale(SHEAR, m), trace) for m in diagonal],
        {k: scale(SHEAR, m) for k, m in mixed.items()},
        {k: scale(THIRD, m) for k, m in third.items()},
        {k: scale(FOURTH, m) for k, m in fourth.items()},
    )


def flow_adjoint(first, diagonal, mixed, third, fourth, u):
    q = []
    for a in range(3):
        b, c = [k for k in range(3) if k != a]
        ab, ac, bc = tuple(sorted((a, b))), tuple(sorted((a, c))), tuple(sorted((b, c)))
        along = add(
            scale(2.0, diagonal[a]),
            scale(2.0 / 3.0, add(fourth[ab], fourth[ac])),
            scale(-1.0 / 3.0, fourth[bc]),
        )
        q.append(
            add(
                first[a],
                scale(1.0 / 3.0, add(third[a, b], third[a, c])),
                mul(u[a], along),
                mul(u[b], mixed[ab]),
                mul(u[c], mixed[ac]),
            )
        )
    return q


def collide_adjoint(r, u):
    t = dual(r)
    first, diagonal, mixed, third, fourth = t
    q = flow_adjoint(*t, u)
    square = [u[a] * u[a] for a in range(3)]
    by_density = None
    for a in range(3):
        b, c = [k for k in range(3) if k != a]
        by_density = add(
            by_density,
            u[a] * (first[a] + (1.0 / 3.0) * (third[a, b] + third[a, c]) - q[a]),
            diagonal[a] * (1.0 / 3.0 + square[a]),
        )
    for a, b in PLANES:
        c = 3 - a - b
        by_density = by_density + mixed[a, b] * (u[a] * u[b])
        by_density = by_density + fourth[a, b] * (
            1.0 / 9.0 + (square[a] + square[b]) * (1.0 / 3.0) - square[c] * (1.0 / 6.0)
        )
    drift = [q[a] - first[a] for a in range(3)]
    base = {0: r[0]}
    for a in range(3):
        base[axis_index_of(a, 1)] = r[axis_index_of(a, 1)] + (drift[a] - diagonal[a])
        base[axis_index_of(a, -1)] = r[axis_index_of(a, -1)] - (drift[a] + diagonal[a])
    for a, b in PLANES:
        along = drift[a] - third[a, b]
        across = drift[b] - third[b, a]
        even = diagonal[a] + diagonal[b] + fourth[a, b]
        same, cross = even + mixed[a, b], even - mixed[a, b]
        both, gap = along + across, along - across
        base[edge_index_of(a, b, 1, 1)] = r[edge_index_of(a, b, 1, 1)] + (both - same)
        base[edge_index_of(a, b, -1, -1)] = r[edge_index_of(a, b, -1, -1)] - (both + same)
        base[edge_index_of(a, b, 1, -1)] = r[edge_index_of(a, b, 1, -1)] + (gap - cross)
        base[edge_index_of(a, b, -1, 1)] = r[edge_index_of(a, b, -1, 1)] - (gap + cross)
    return base, by_density, q


def rolled(x, step):
    return x if step == 0 else pltpu.roll(x, step % DEPTH, 1)


def rows_at(t, shift, offset):
    if isinstance(t, int):
        return pl.ds(t * 8 + offset + shift, 8)
    if shift == 0:
        return pl.ds(pl.multiple_of(t * 8 + offset, 8), 8)
    return pl.ds(t * 8 + (offset + shift), 8)


def flat(t):
    return rows_at(t, 0, 0)


def tall(t, shift=0):
    return rows_at(t, shift, PAD)


def each_chunk(body, first=0, last=CHUNKS):
    def step(t, carry):
        body(t)
        return carry

    lax.fori_loop(first, last, step, 0)


def gradient_of(field, doubled, p, t):
    at = lambda dp, dy: field[p + dp, tall(t, dy), :]
    rp, rm, lp, lm = at(1, 1), at(1, -1), at(-1, 1), at(-1, -1)
    along_x = doubled[p + 1, tall(t), :] - doubled[p - 1, tall(t), :] + (rp + rm) - (lp + lm)
    along_y = doubled[p, tall(t, 1), :] - doubled[p, tall(t, -1), :] + (rp + lp) - (rm + lm)
    star = 2.0 * at(0, 0) + at(1, 0) + at(-1, 0) + at(0, 1) + at(0, -1)
    return [along_x, along_y, rolled(star, -1) - rolled(star, 1)]


def with_sides(x):
    return 2.0 * x + rolled(x, 1) + rolled(x, -1)


def edges_kernel(pops, fluid, label, target, low, high, whole, sems):
    copies = []

    def copy(source, goal):
        one = pltpu.make_async_copy(source, goal, sems.at[len(copies)])
        one.start()
        copies.append(one)

    for side, goal in ((0, low), (1, high)):
        rows = pl.ds(0, HALO) if side == 0 else pl.ds(OWN - HALO, HALO)
        copy(fluid.at[:, rows, :], whole.at[side, 0])
        copy(label.at[:, rows, :], whole.at[side, 1])
        copy(target.at[:, rows, :], goal.at[21])
        copy(pops.at[:, :, rows, :], goal.at[pl.ds(0, 19)])
    for one in copies:
        one.wait()
    for side, goal in ((0, low), (1, high)):
        goal[19] = whole[side, 0].astype(jnp.float32)
        goal[20] = whole[side, 1].astype(jnp.float32)


def put_sends(send_left, send_right, t, lin, first, chosen, effective):
    for k, i in enumerate(LEFTWARD):
        send_left[k, flat(t), :] = lin[0][i]
    for k, i in enumerate(RIGHTWARD):
        send_right[k, flat(t), :] = lin[1][i]
    for a in range(3):
        send_left[5 + a, flat(t), :] = first[0][a]
        send_right[5 + a, flat(t), :] = first[1][a]
    send_left[8, flat(t), :] = chosen[0]
    send_right[8, flat(t), :] = chosen[1]
    send_left[9, flat(t), :] = effective[1]
    send_right[9, flat(t), :] = effective[0]


def start_rows(t, populations, shares, marks, table, outs):
    lin_out, flow_out, density_out, effective_out, share_out, _, send_left, send_right = outs
    half_low = jnp.broadcast_to(table[0:1, :], (8, DEPTH))
    half_high = jnp.broadcast_to(table[1:2, :], (8, DEPTH))
    lin, first, chosen, effective = [], [], [], []
    for x in range(2):
        share = shares[x]
        spot = jnp.bitwise_and(marks[x], DEPTH - 1)
        wall = jnp.where(
            jnp.bitwise_and(marks[x], DEPTH) == 0,
            jnp.take_along_axis(half_low, spot, axis=1),
            jnp.take_along_axis(half_high, spot, axis=1),
        )
        total, momentum, linear = linear_part(populations[x], share, range(19))
        eff = jnp.where(share > 0, 1.0 - jnp.exp(-total), wall)
        for i in range(19):
            lin_out[i, x, flat(t), :] = linear[i]
        for a in range(3):
            flow_out[a, x, flat(t), :] = momentum[a]
        density_out[x, flat(t), :] = total
        effective_out[x, flat(t), :] = eff
        share_out[x, flat(t), :] = share
        lin.append(linear)
        first.append(momentum)
        chosen.append(jnp.where(share > 0, total, wall))
        effective.append(eff)
    put_sends(send_left, send_right, t, lin, first, chosen, effective)
    send_left[10, flat(t), :] = shares[0]
    send_left[11, flat(t), :] = shares[1]
    send_right[10, flat(t), :] = shares[1]
    send_right[11, flat(t), :] = shares[0]


def own_kernel(pops, fluid, label, target, table, *outs):
    outs[5][:, HALO : HALO + OWN, :] = target[...]

    def body(t):
        rows = rows_at(t, 0, -HALO)
        start_rows(
            t,
            [{i: pops[i, x, rows, :] for i in range(19)} for x in range(2)],
            [fluid[x, rows, :].astype(jnp.float32) for x in range(2)],
            [label[x, rows, :] for x in range(2)],
            table,
            outs,
        )

    each_chunk(body, HALO // 8, (HALO + OWN) // 8)


def halo_kernel(table, below, above, *refs):
    outs = refs[len(refs) // 2 :]
    for t, edge in ((0, below), (CHUNKS - 1, above)):
        outs[5][:, 8 * t : 8 * t + 8, :] = edge[21]
        start_rows(
            t,
            [{i: edge[i, x] for i in range(19)} for x in range(2)],
            [edge[19, x] for x in range(2)],
            [edge[20, x].astype(jnp.int32) for x in range(2)],
            table,
            outs,
        )


def step_kernel(is_first, *refs):
    if is_first:
        (lin, flow, density, effective, share, from_left, from_right,
         masks, field, speed, pull_out, lin_out, flow_out, density_out, effective_out, send_left, send_right,
         doubled, relaxed, turned) = refs
    else:
        (lin, flow, density, effective, share, target, masks, from_left, from_right,
         field, speed, pull_out, misfit_out,
         doubled, relaxed, turned) = refs
    sides = ((1, from_left, 0), (4, from_right, 5))

    def place(t):
        def put(p, x, s):
            field[p, tall(t), :] = x
            doubled[p, tall(t), :] = with_sides(x)
            if is_first:
                masks[0, p, tall(t), :] = s
                masks[1, p, tall(t), :] = rolled(s, 1)
                masks[2, p, tall(t), :] = rolled(s, -1)

        for x in range(2):
            put(2 + x, effective[x, flat(t), :], share[x, flat(t), :])
        for near, come, far in sides:
            if is_first:
                s_near, s_far = come[10, flat(t), :], come[11, flat(t), :]
            else:
                s_near, s_far = masks[0, near, tall(t), :], None
            chosen = come[8, flat(t), :]
            put(near, jnp.where(s_near > 0, 1.0 - jnp.exp(-chosen), chosen), s_near)
            put(far, come[9, flat(t), :], s_far)

    each_chunk(place)

    def collide(t):
        for p in range(1, 5):
            own = p in (2, 3)
            pull = gradient_of(field, doubled, p, t)
            psi = field[p, tall(t), :]
            s = masks[0, p, tall(t), :]
            if own:
                rho = density[p - 2, flat(t), :]
                mom = [flow[a, p - 2, flat(t), :] for a in range(3)]
                which = range(19)
                lin_at = {i: lin[i, p - 2, flat(t), :] for i in which}
                for a in range(3):
                    pull_out[a, p - 2, flat(t), :] = pull[a]
            else:
                come = from_left if p == 1 else from_right
                rho = come[8, flat(t), :]
                mom = [come[5 + a, flat(t), :] for a in range(3)]
                which = RIGHTWARD if p == 1 else LEFTWARD
                lin_at = {i: come[k, flat(t), :] for k, i in enumerate(which)}
            push = psi * (PULL / SHEAR)
            full = [mom[a] + push * pull[a] for a in range(3)]
            inverse = 1.0 / rho
            u = [full[a] * inverse for a in range(3)]
            for a in range(3):
                speed[a, p - 1, flat(t), :] = u[a]
            part = balance_part(rho, full, u, s, which)
            for i in which:
                value = lin_at[i] + part[i]
                relaxed[i, p - 1, tall(t), :] = value
                if i in TURNED:
                    turned[TURNED.index(i), p - 1, tall(t), :] = rolled(value, VECTORS[i][2])

    each_chunk(collide)

    def stream(t):
        lin_sent, first_sent, chosen_sent, effective_sent = [], [], [], []
        for x in range(2):
            f = {}
            for i in range(19):
                cx, cy, cz = VECTORS[i]
                if i == 0:
                    f[i] = relaxed[0, 1 + x, tall(t), :]
                    continue
                if cz:
                    source = turned[TURNED.index(i), 1 + x - cx, tall(t, -cy), :]
                else:
                    source = relaxed[i, 1 + x - cx, tall(t, -cy), :]
                open_ = masks[cz % 3, 2 + x - cx, tall(t, -cy), :] > 0
                f[i] = jnp.where(open_, source, relaxed[OPPOSITE[i], 1 + x, tall(t), :])
            s = share[x, flat(t), :]
            if is_first:
                total, momentum, linear = linear_part(f, s, range(19))
                held = effective[x, flat(t), :]
                eff = jnp.where(s > 0, 1.0 - jnp.exp(-total), held)
                for i in range(19):
                    lin_out[i, x, flat(t), :] = linear[i]
                for a in range(3):
                    flow_out[a, x, flat(t), :] = momentum[a]
                density_out[x, flat(t), :] = total
                effective_out[x, flat(t), :] = eff
                lin_sent.append(linear)
                first_sent.append(momentum)
                chosen_sent.append(jnp.where(s > 0, total, held))
                effective_sent.append(eff)
            else:
                total = add(*[f[i] for i in range(19)])
                misfit_out[x, flat(t), :] = s * (total - target[x, flat(t), :])
        if is_first:
            put_sends(send_left, send_right, t, lin_sent, first_sent, chosen_sent, effective_sent)

    each_chunk(stream)


def spread_of(pulled, pulled_doubled, p, t):
    at = lambda a, dp, dy: pulled[a, p + dp, tall(t, dy), :]
    two = lambda a, dp, dy: pulled_doubled[a, p + dp, tall(t, dy), :]
    along_x = two(0, 1, 0) - two(0, -1, 0) + (at(0, 1, 1) + at(0, 1, -1)) - (at(0, -1, 1) + at(0, -1, -1))
    along_y = two(1, 0, 1) - two(1, 0, -1) + (at(1, 1, 1) + at(1, -1, 1)) - (at(1, 1, -1) + at(1, -1, -1))
    star = 2.0 * at(2, 0, 0) + at(2, 1, 0) + at(2, -1, 0) + at(2, 0, 1) + at(2, 0, -1)
    along_z = rolled(star, -1) - rolled(star, 1)
    return (along_x + along_y + along_z) * (-1.0 / 36.0)


def put_pulled(pulled, pulled_doubled, p, t, psi, q):
    for a in range(3):
        s = (COUPLING / SHEAR) * psi * q[a]
        pulled[a, p, tall(t), :] = s
        if a < 2:
            pulled_doubled[a, p, tall(t), :] = with_sides(s)


def mask_ahead(masks, i, p, t):
    cx, cy, cz = VECTORS[i]
    return masks[(-cz) % 3, p + cx, tall(t, cy), :] > 0


def last_reverse_kernel(
    misfit, from_left, from_right, masks, field, speed, pull, early_speed,
    adjoint, turned, wall_out, send_left, send_right,
    ahead, pulled, pulled_doubled, base,
):
    def place(t):
        for p in range(6):
            if p < 2:
                d = from_left[p, flat(t), :]
            elif p < 4:
                d = misfit[p - 2, flat(t), :]
            else:
                d = from_right[p - 4, flat(t), :]
            ahead[0, p, tall(t), :] = d
            ahead[1, p, tall(t), :] = rolled(d, 1)
            ahead[2, p, tall(t), :] = rolled(d, -1)

    each_chunk(place)

    def collide(t):
        for p in range(1, 5):
            s = masks[0, p, tall(t), :]
            here = ahead[0, p, tall(t), :]
            r = {0: here}
            for i in range(1, 19):
                cx, cy, cz = VECTORS[i]
                there = ahead[(-cz) % 3, p + cx, tall(t, cy), :]
                r[i] = s * jnp.where(mask_ahead(masks, i, p, t), there, here)
            psi = field[p, tall(t), :]
            u = [speed[a, p - 1, flat(t), :] for a in range(3)]
            if p in (2, 3):
                rest, by_density, q = collide_adjoint(r, u)
                along = add(*[q[a] * pull[a, p - 2, flat(t), :] for a in range(3)])
                const = by_density + along * ((PULL / SHEAR) * (1.0 - psi))
                for i in range(19):
                    base[i, p - 2, flat(t), :] = rest[i] + const
            else:
                q = flow_adjoint(*dual(r), u)
            put_pulled(pulled, pulled_doubled, p - 1, t, psi, q)

    each_chunk(collide)

    def finish(t):
        for x in range(2):
            s = masks[0, 2 + x, tall(t), :]
            spread = spread_of(pulled, pulled_doubled, 1 + x, t)
            wall_out[x, flat(t), :] = (1.0 - s) * spread
            more = s * spread * (1.0 - field[2 + x, tall(t), :])
            for i in range(19):
                value = base[i, x, flat(t), :] + more
                adjoint[i, x, tall(t), :] = value
                if i in TURNED:
                    turned[TURNED.index(i), x, tall(t), :] = rolled(value, -VECTORS[i][2])

    each_chunk(finish)

    def part(t):
        for x, send, sent, skipped in ((0, send_left, RIGHTWARD, -1), (1, send_right, LEFTWARD, 1)):
            p = 2 + x
            s = masks[0, p, tall(t), :]
            r = {}
            for i in range(19):
                cx, cy, cz = VECTORS[i]
                if cx == skipped:
                    continue
                r[i] = adjoint_ahead(adjoint, turned, masks, i, x, t)
            u = [early_speed[a, p - 1, flat(t), :] for a in range(3)]
            q = flow_adjoint(*dual(r), u)
            for a in range(3):
                send[5 + a, flat(t), :] = s * q[a]
            for k, i in enumerate(sent):
                send[k, flat(t), :] = adjoint[i, x, tall(t), :]

    each_chunk(part)


def adjoint_ahead(adjoint, turned, masks, i, x, t):
    cx, cy, cz = VECTORS[i]
    if i == 0:
        return adjoint[0, x, tall(t), :]
    if cz:
        there = turned[TURNED.index(i), x + cx, tall(t, cy), :]
    else:
        there = adjoint[i, x + cx, tall(t, cy), :]
    return jnp.where(mask_ahead(masks, i, 2 + x, t), there, adjoint[OPPOSITE[i], x, tall(t), :])


def place_sides(come, from_left, from_right, t):
    for side, source, which in ((0, from_left, LEFTWARD), (1, from_right, RIGHTWARD)):
        for k, i in enumerate(which):
            come[side, k, tall(t), :] = rolled(source[k, flat(t), :], -VECTORS[i][2])


def arrived(come, adjoint, masks, i, x, t):
    which = LEFTWARD if x == 0 else RIGHTWARD
    there = come[x, which.index(i), tall(t, VECTORS[i][1]), :]
    return jnp.where(mask_ahead(masks, i, 2 + x, t), there, adjoint[OPPOSITE[i], x, tall(t), :])


def wall_kernel(
    adjoint, turned, wall, part_left, part_right, from_left, from_right, masks, field, speed, chooser,
    more_out, label_part,
    come, pulled, pulled_doubled, totals,
):
    each_chunk(functools.partial(place_sides, come, from_left, from_right))

    def collide(t):
        for x, part, which in ((0, part_left, LEFTWARD), (1, part_right, RIGHTWARD)):
            p = 2 + x
            s = masks[0, p, tall(t), :]
            r = {i: arrived(come, adjoint, masks, i, x, t) for i in which}
            u = [speed[a, p - 1, flat(t), :] for a in range(3)]
            rest = flow_adjoint(*dual(r), u)
            q = [part[5 + a, flat(t), :] + s * rest[a] for a in range(3)]
            put_pulled(pulled, pulled_doubled, p - 1, t, field[p, tall(t), :], q)
        for x, source, which in ((0, from_left, LEFTWARD), (1, from_right, RIGHTWARD)):
            p = 1 if x == 0 else 4
            s = masks[0, p, tall(t), :]
            r = {}
            for i in [OPPOSITE[j] for j in which]:
                cx, cy, cz = VECTORS[i]
                if cz:
                    there = turned[TURNED.index(i), x, tall(t, cy), :]
                else:
                    there = adjoint[i, x, tall(t, cy), :]
                here = source[which.index(OPPOSITE[i]), flat(t), :]
                r[i] = jnp.where(mask_ahead(masks, i, p, t), there, here)
            u = [speed[a, p - 1, flat(t), :] for a in range(3)]
            rest = flow_adjoint(*dual(r), u)
            q = [source[5 + a, flat(t), :] + s * rest[a] for a in range(3)]
            put_pulled(pulled, pulled_doubled, p - 1, t, field[p, tall(t), :], q)

    each_chunk(collide)

    def finish(t):
        total = None
        for x in range(2):
            s = masks[0, 2 + x, tall(t), :]
            spread = spread_of(pulled, pulled_doubled, 1 + x, t)
            total = add(total, (1.0 - s) * spread + wall[x, flat(t), :])
            more_out[x, rows_at(t, 0, -HALO), :] = s * spread * (1.0 - field[2 + x, tall(t), :])
        totals[rows_at(t, 0, -HALO), :] = total

    each_chunk(finish, HALO // 8, (HALO + OWN) // 8)

    blocks = (OWN // 2) * (DEPTH // 4)
    column = lax.broadcasted_iota(jnp.int32, (DEPTH, blocks), 1)
    quad = lax.broadcasted_iota(jnp.int32, (DEPTH, blocks), 0) // 4
    gather = (jnp.bitwise_and(column, DEPTH // 4 - 1) == quad).astype(jnp.bfloat16)
    by_block = exact_dot(totals[...], gather)
    pair = lax.broadcasted_iota(jnp.int32, (OWN, blocks), 0) // 2
    wanted = lax.broadcasted_iota(jnp.int32, (OWN, blocks), 1) // (DEPTH // 4)
    by_block = jnp.where(pair == wanted, by_block, 0.0)
    by_label = exact_dot(by_block, chooser[...])
    label_part[...] = jnp.sum(by_label, axis=0, keepdims=True)


def grad_kernel(
    adjoint, turned, more, from_left, from_right, masks, field, speed, pull,
    grad,
    come,
):
    each_chunk(functools.partial(place_sides, come, from_left, from_right))

    def collide(t):
        for x in range(2):
            p = 2 + x
            s = masks[0, p, tall(t), :]
            r = {}
            for i in range(19):
                if VECTORS[i][0] == 2 * x - 1:
                    r[i] = s * arrived(come, adjoint, masks, i, x, t)
                else:
                    r[i] = s * adjoint_ahead(adjoint, turned, masks, i, x, t)
            u = [speed[a, p - 1, flat(t), :] for a in range(3)]
            rest, by_density, q = collide_adjoint(r, u)
            along = add(*[q[a] * pull[a, x, flat(t), :] for a in range(3)])
            const = by_density + along * ((PULL / SHEAR) * (1.0 - field[p, tall(t), :]))
            const = const + more[x, rows_at(t, 0, -HALO), :]
            for i in range(19):
                grad[i, x, rows_at(t, 0, -HALO), :] = rest[i] + const

    each_chunk(collide, HALO // 8, (HALO + OWN) // 8)


def exact_dot(values, zero_one):
    high = values.astype(jnp.bfloat16)
    left = values - high.astype(jnp.float32)
    middle = left.astype(jnp.bfloat16)
    low = (left - middle.astype(jnp.float32)).astype(jnp.bfloat16)
    dot = lambda part: jnp.dot(part, zero_one, preferred_element_type=jnp.float32)
    return dot(high) + (dot(middle) + dot(low))


def call(kernel, args, outs, scratch, anywhere=0, grant=12, filled=0):
    whole = pl.BlockSpec(memory_space=pltpu.VMEM)
    there = pl.BlockSpec(memory_space=pl.ANY)
    size = 4 * sum(int(np.prod(s)) for s in outs) + sum(a.size * a.dtype.itemsize for a in args)
    return pl.pallas_call(
        kernel,
        out_shape=[jax.ShapeDtypeStruct(s, jnp.float32) for s in outs],
        in_specs=[there] * anywhere + [whole] * (len(args) - anywhere),
        out_specs=[whole] * len(outs),
        scratch_shapes=scratch,
        input_output_aliases={len(args) - filled + k: k for k in range(filled)},
        compiler_params=pltpu.CompilerParams(vmem_limit_bytes=grant * 1024 * 1024),
        cost_estimate=pl.CostEstimate(flops=0, bytes_accessed=size, transcendentals=0),
    )(*args)


def ring(axis):
    count = lax.axis_size(axis)
    up = [(i, (i + 1) % count) for i in range(count)]
    return up, [(j, i) for i, j in up]


def both_ways(to_lower, to_upper, axis):
    up, down = ring(axis)
    from_lower = lax.ppermute(to_upper, axis, up)
    from_upper = lax.ppermute(to_lower, axis, down)
    return from_lower, from_upper


def per_device(populations, fluid, label, wall_wetting, target):
    vmem = lambda *shape: pltpu.VMEM(shape, jnp.float32)
    plane = (ROWS, DEPTH)
    two = (2, *plane)
    edge = (22, 2, HALO, DEPTH)
    low, high = call(
        edges_kernel,
        (populations, fluid, label, target),
        (edge, edge),
        (pltpu.VMEM((2, 2, 2, HALO, DEPTH), jnp.int32), pltpu.SemaphoreType.DMA((8,))),
        anywhere=4,
        grant=56,
    )
    below, above = both_ways(low, high, "gy")
    marks = jnp.bitwise_and(label[0, ::2, ::4], LABELS - 1).reshape(-1)
    chooser = (marks[:, None] == jnp.arange(LABELS, dtype=jnp.int32)[None, :]).astype(jnp.bfloat16)
    table = wall_wetting.reshape(2, DEPTH)
    started = ((19, *two), (3, *two), two, two, two, two, (12, *plane), (12, *plane))
    own = call(own_kernel, (populations, fluid, label, target, table), started, ())
    lin, flow, density, effective, share, target_wide, to_left, to_right = call(
        halo_kernel, (table, below, above, *own), started, (), filled=len(started)
    )
    from_left, from_right = both_ways(to_left, to_right, "gx")
    wide6 = (6, TALL, DEPTH)
    work = (vmem(*wide6), vmem(19, 4, TALL, DEPTH), vmem(10, 4, TALL, DEPTH))
    masks, field0, speed0, pull0, lin, flow, density, effective, to_left, to_right = call(
        functools.partial(step_kernel, True),
        (lin, flow, density, effective, share, from_left, from_right),
        (
            (3, *wide6), wide6, (3, 4, *plane), (3, *two),
            (19, *two), (3, *two), two, two, (10, *plane), (10, *plane),
        ),
        work,
    )
    from_left, from_right = both_ways(to_left, to_right, "gx")
    field1, speed1, pull1, misfit = call(
        functools.partial(step_kernel, False),
        (lin, flow, density, effective, share, target_wide, masks, from_left, from_right),
        (wide6, (3, 4, *plane), (3, *two), two),
        work,
    )
    from_left, from_right = both_ways(misfit, misfit, "gx")
    pulled = (vmem(3, 4, TALL, DEPTH), vmem(2, 4, TALL, DEPTH))
    adjoint, turned, wall, to_left, to_right = call(
        last_reverse_kernel,
        (misfit, from_left, from_right, masks, field1, speed1, pull1, speed0),
        ((19, 2, TALL, DEPTH), (10, 2, TALL, DEPTH), two, (8, *plane), (8, *plane)),
        (vmem(3, *wide6), *pulled, vmem(19, *two)),
    )
    from_left, from_right = both_ways(to_left, to_right, "gx")
    come = vmem(2, 5, TALL, DEPTH)
    more, label_part = call(
        wall_kernel,
        (adjoint, turned, wall, to_left, to_right, from_left, from_right, masks, field0, speed0, chooser),
        ((2, OWN, DEPTH), (1, LABELS)),
        (come, *pulled, vmem(OWN, DEPTH)),
    )
    count = lax.axis_size("gy")
    wetting_grad = label_part
    for step in range(1, count):
        wetting_grad = wetting_grad + lax.ppermute(
            label_part, "gy", [(i, (i + step) % count) for i in range(count)]
        )
    (grad,) = call(
        grad_kernel,
        (adjoint, turned, more, from_left, from_right, masks, field0, speed0, pull0),
        (populations.shape,),
        (come,),
    )
    return (grad, wetting_grad.reshape(-1))


def solution(mesh):
    return jax.shard_map(
        per_device,
        mesh=mesh,
        in_specs=(
            P(None, "gx", "gy", None),
            P("gx", "gy", None),
            P("gx", "gy", None),
            P("gx"),
            P("gx", "gy", None),
        ),
        out_specs=(P(None, "gx", "gy", None), P("gx")),
        check_vma=False,
    )
```

```python
import functools

import jax
import jax.numpy as jnp
from jax import lax
from jax.experimental import pallas as pl
from jax.experimental.pallas import tpu as pltpu
from jax.sharding import PartitionSpec as P

HALO = 8
PAD = 8
OWN = 32
ROWS = OWN + 2 * HALO
TALL = ROWS + 2 * PAD
MID = OWN + HALO
DEPTH = 128
CHUNKS = ROWS // 8
LABELS = 256

VECTORS = (
    (0, 0, 0), (1, 0, 0), (-1, 0, 0), (0, 1, 0), (0, -1, 0), (0, 0, 1), (0, 0, -1),
    (1, 1, 0), (-1, -1, 0), (1, -1, 0), (-1, 1, 0), (1, 0, 1), (-1, 0, -1), (1, 0, -1), (-1, 0, 1),
    (0, 1, 1), (0, -1, -1), (0, 1, -1), (0, -1, 1),
)
OPPOSITE = (0, 2, 1, 4, 3, 6, 5, 8, 7, 10, 9, 12, 11, 14, 13, 16, 15, 18, 17)
INDEX = {v: i for i, v in enumerate(VECTORS)}
RIGHTWARD = tuple(i for i in range(19) if VECTORS[i][0] == 1)
LEFTWARD = tuple(i for i in range(19) if VECTORS[i][0] == -1)
TURNED = tuple(i for i in range(19) if VECTORS[i][2] != 0)
PLANES = ((0, 1), (1, 2), (0, 2))
COUPLING = 5.0
SHEAR = 1.2
BULK = 1.19
THIRD = 1.5
FOURTH = 1.4
TRACE = (BULK - SHEAR) / 3.0
PULL = COUPLING / 36.0


def axis_index_of(axis, sign):
    v = [0, 0, 0]
    v[axis] = sign
    return INDEX[tuple(v)]


def edge_index_of(a, b, sa, sb):
    v = [0, 0, 0]
    v[a], v[b] = sa, sb
    return INDEX[tuple(v)]


def add(*terms):
    total = None
    for term in terms:
        if term is not None:
            total = term if total is None else total + term
    return total


def sub(a, b):
    if b is None:
        return a
    return -b if a is None else a - b


def scale(c, a):
    return None if a is None else c * a


def mul(a, b):
    return None if a is None or b is None else a * b


def moments(f):
    fourth, mixed, third = {}, {}, {}
    for a, b in PLANES:
        pp, mm = f[edge_index_of(a, b, 1, 1)], f[edge_index_of(a, b, -1, -1)]
        pm, mp = f[edge_index_of(a, b, 1, -1)], f[edge_index_of(a, b, -1, 1)]
        even, odd, cross, skew = pp + mm, pp - mm, pm + mp, pm - mp
        fourth[a, b] = even + cross
        mixed[a, b] = even - cross
        third[a, b] = odd + skew
        third[b, a] = odd - skew
    first, diagonal, total = [], [], f[0]
    for a in range(3):
        b, c = [k for k in range(3) if k != a]
        plus, minus = f[axis_index_of(a, 1)], f[axis_index_of(a, -1)]
        both = plus + minus
        total = total + both
        diagonal.append(both + fourth[tuple(sorted((a, b)))] + fourth[tuple(sorted((a, c)))])
        first.append((plus - minus) + third[a, b] + third[a, c])
    total = total + fourth[0, 1] + fourth[1, 2] + fourth[0, 2]
    return total, first, diagonal, mixed, third, fourth


def from_moments(first, diagonal, mixed, third, fourth, which):
    out = {}
    for a, b in PLANES:
        even, cross = fourth[a, b] + mixed[a, b], fourth[a, b] - mixed[a, b]
        odd, skew = third[a, b] + third[b, a], third[a, b] - third[b, a]
        out[edge_index_of(a, b, 1, 1)] = even + odd
        out[edge_index_of(a, b, -1, -1)] = even - odd
        out[edge_index_of(a, b, 1, -1)] = cross + skew
        out[edge_index_of(a, b, -1, 1)] = cross - skew
    for a in range(3):
        b, c = [k for k in range(3) if k != a]
        even = diagonal[a] - 2.0 * (fourth[tuple(sorted((a, b)))] + fourth[tuple(sorted((a, c)))])
        odd = first[a] - 2.0 * (third[a, b] + third[a, c])
        out[axis_index_of(a, 1)] = even + odd
        out[axis_index_of(a, -1)] = even - odd
    out[0] = 4.0 * (fourth[0, 1] + fourth[1, 2] + fourth[0, 2]) - 2.0 * (diagonal[0] + diagonal[1] + diagonal[2])
    return {i: out[i] for i in which}


def linear_part(f, share, which):
    total, first, diagonal, mixed, third, fourth = moments(f)
    half, quarter = (0.5 * SHEAR) * share, (0.25 * SHEAR) * share
    trace = (0.5 * TRACE) * share * (diagonal[0] + diagonal[1] + diagonal[2])
    by_third, by_fourth = (0.25 * THIRD) * share, (0.25 * FOURTH) * share
    change = from_moments(
        [half * m for m in first],
        [half * m + trace for m in diagonal],
        {k: quarter * m for k, m in mixed.items()},
        {k: by_third * m for k, m in third.items()},
        {k: by_fourth * m for k, m in fourth.items()},
        which,
    )
    return total, first, {i: f[i] - change[i] for i in which}


def balance_part(density, flow, velocity, share, which):
    d = density * share
    m = [flow[a] * share for a in range(3)]
    square = [m[a] * velocity[a] for a in range(3)]
    whole = square[0] + square[1] + square[2]
    level = d * (SHEAR / 6.0 + 0.5 * TRACE) + whole * (0.5 * TRACE)
    diagonal = [(0.5 * SHEAR) * square[a] + level for a in range(3)]
    scaled = [(0.25 * SHEAR) * velocity[a] for a in range(3)]
    mixed = {(a, b): m[a] * scaled[b] for a, b in PLANES}
    part = [(THIRD / 12.0) * m[a] for a in range(3)]
    third = {}
    fourth = {}
    level = d * (FOURTH / 36.0) + whole * (FOURTH / 12.0)
    for a, b in PLANES:
        third[a, b], third[b, a] = part[a], part[b]
        fourth[a, b] = level - (FOURTH / 8.0) * square[3 - a - b]
    return from_moments([(0.5 * SHEAR) * m[a] for a in range(3)], diagonal, mixed, third, fourth, which)


def dual(r):
    get = lambda i: r.get(i)
    first, diagonal = [], []
    plus_of, minus_of = [], []
    for a in range(3):
        p, m = get(axis_index_of(a, 1)), get(axis_index_of(a, -1))
        even = scale(0.5, add(p, m))
        odd = scale(0.5, sub(p, m))
        plus_of.append(even)
        minus_of.append(odd)
        first.append(odd)
        diagonal.append(sub(even, get(0)))
    mixed, third, fourth = {}, {}, {}
    for a, b in PLANES:
        pp, mm = get(edge_index_of(a, b, 1, 1)), get(edge_index_of(a, b, -1, -1))
        pm, mp = get(edge_index_of(a, b, 1, -1)), get(edge_index_of(a, b, -1, 1))
        even, odd, cross, skew = add(pp, mm), sub(pp, mm), add(pm, mp), sub(pm, mp)
        fourth[a, b] = add(sub(sub(scale(0.25, add(even, cross)), plus_of[a]), plus_of[b]), get(0))
        mixed[a, b] = scale(0.25, sub(even, cross))
        third[a, b] = sub(scale(0.25, add(odd, skew)), minus_of[a])
        third[b, a] = sub(scale(0.25, sub(odd, skew)), minus_of[b])
    trace = scale(TRACE, add(*diagonal))
    return (
        [scale(SHEAR, m) for m in first],
        [add(scale(SHEAR, m), trace) for m in diagonal],
        {k: scale(SHEAR, m) for k, m in mixed.items()},
        {k: scale(THIRD, m) for k, m in third.items()},
        {k: scale(FOURTH, m) for k, m in fourth.items()},
    )


def flow_adjoint(first, diagonal, mixed, third, fourth, u):
    q = []
    for a in range(3):
        b, c = [k for k in range(3) if k != a]
        ab, ac, bc = tuple(sorted((a, b))), tuple(sorted((a, c))), tuple(sorted((b, c)))
        along = add(
            scale(2.0, diagonal[a]),
            scale(2.0 / 3.0, add(fourth[ab], fourth[ac])),
            scale(-1.0 / 3.0, fourth[bc]),
        )
        q.append(
            add(
                first[a],
                scale(1.0 / 3.0, add(third[a, b], third[a, c])),
                mul(u[a], along),
                mul(u[b], mixed[ab]),
                mul(u[c], mixed[ac]),
            )
        )
    return q


def collide_adjoint(r, u):
    t = dual(r)
    first, diagonal, mixed, third, fourth = t
    q = flow_adjoint(*t, u)
    square = [u[a] * u[a] for a in range(3)]
    by_density = None
    for a in range(3):
        b, c = [k for k in range(3) if k != a]
        by_density = add(
            by_density,
            u[a] * (first[a] + (1.0 / 3.0) * (third[a, b] + third[a, c]) - q[a]),
            diagonal[a] * (1.0 / 3.0 + square[a]),
        )
    for a, b in PLANES:
        c = 3 - a - b
        by_density = by_density + mixed[a, b] * (u[a] * u[b])
        by_density = by_density + fourth[a, b] * (
            1.0 / 9.0 + (square[a] + square[b]) * (1.0 / 3.0) - square[c] * (1.0 / 6.0)
        )
    drift = [q[a] - first[a] for a in range(3)]
    base = {0: r[0]}
    for a in range(3):
        base[axis_index_of(a, 1)] = r[axis_index_of(a, 1)] + (drift[a] - diagonal[a])
        base[axis_index_of(a, -1)] = r[axis_index_of(a, -1)] - (drift[a] + diagonal[a])
    for a, b in PLANES:
        along = drift[a] - third[a, b]
        across = drift[b] - third[b, a]
        even = diagonal[a] + diagonal[b] + fourth[a, b]
        same, cross = even + mixed[a, b], even - mixed[a, b]
        both, gap = along + across, along - across
        base[edge_index_of(a, b, 1, 1)] = r[edge_index_of(a, b, 1, 1)] + (both - same)
        base[edge_index_of(a, b, -1, -1)] = r[edge_index_of(a, b, -1, -1)] - (both + same)
        base[edge_index_of(a, b, 1, -1)] = r[edge_index_of(a, b, 1, -1)] + (gap - cross)
        base[edge_index_of(a, b, -1, 1)] = r[edge_index_of(a, b, -1, 1)] - (gap + cross)
    return base, by_density, q


def rolled(x, step):
    return x if step == 0 else pltpu.roll(x, step % DEPTH, 1)


def rows_at(t, shift, offset):
    if isinstance(t, int):
        return pl.ds(t * 8 + offset + shift, 8)
    if shift == 0:
        return pl.ds(pl.multiple_of(t * 8 + offset, 8), 8)
    return pl.ds(t * 8 + (offset + shift), 8)


def flat(t):
    return rows_at(t, 0, 0)


def tall(t, shift=0):
    return rows_at(t, shift, PAD)


def mid(t):
    return pl.ds(t * 8 + (ROWS - MID) // 2, 8)


def mid_tall(t, shift=0):
    return pl.ds(t * 8 + ((ROWS - MID) // 2 + PAD + shift), 8)


def each_chunk(body, first=0, last=CHUNKS):
    def step(t, carry):
        body(t)
        return carry

    lax.fori_loop(first, last, step, 0)


def gradient_of(field, doubled, p, t):
    at = lambda dp, dy: field[p + dp, tall(t, dy), :]
    rp, rm, lp, lm = at(1, 1), at(1, -1), at(-1, 1), at(-1, -1)
    along_x = doubled[p + 1, tall(t), :] - doubled[p - 1, tall(t), :] + (rp + rm) - (lp + lm)
    along_y = doubled[p, tall(t, 1), :] - doubled[p, tall(t, -1), :] + (rp + lp) - (rm + lm)
    star = 2.0 * at(0, 0) + at(1, 0) + at(-1, 0) + at(0, 1) + at(0, -1)
    return [along_x, along_y, rolled(star, -1) - rolled(star, 1)]


def with_sides(x):
    return 2.0 * x + rolled(x, 1) + rolled(x, -1)


def inner_gradient(field, doubled, here, inner, t):
    at = lambda x, dy: field[x, tall(t, dy), :]
    up, down = at(inner, 1), at(inner, -1)
    along_x = doubled[inner, tall(t), :] + (up + down)
    along_y = doubled[here, tall(t, 1), :] - doubled[here, tall(t, -1), :] + (up - down)
    star = 2.0 * at(here, 0) + at(inner, 0) + at(here, 1) + at(here, -1)
    return [along_x if inner > here else -along_x, along_y, rolled(star, -1) - rolled(star, 1)]


def outer_gradient(field, doubled, p, inner, t):
    at = lambda dy: field[inner, tall(t, dy), :]
    up, down, here = at(1), at(-1), at(0)
    along_x = doubled[inner, tall(t), :] + (up + down)
    return [along_x if inner > p else -along_x, up - down, rolled(here, -1) - rolled(here, 1)]


def send_flow(send_left, send_right, flow, field, doubled, t):
    for send, here, inner in ((send_left, 0, 1), (send_right, 1, 0)):
        push = field[here, tall(t), :] * (PULL / SHEAR)
        pull = inner_gradient(field, doubled, here, inner, t)
        for a in range(3):
            send[5 + a, flat(t), :] = flow[a, here, flat(t), :] + push * pull[a]


def edges_kernel(pops, fluid, label, target, table, low, high, small, whole, values, sems):
    copies = []

    def copy(source, goal):
        one = pltpu.make_async_copy(source, goal, sems.at[len(copies)])
        one.start()
        copies.append(one)

    copy(fluid, whole.at[0])
    copy(label, whole.at[1])
    copy(target, small.at[2])
    copy(table, values)
    copy(pops.at[:, :, pl.ds(0, HALO), :], low.at[pl.ds(0, 19)])
    copy(pops.at[:, :, pl.ds(OWN - HALO, HALO), :], high.at[pl.ds(0, 19)])
    for one in copies:
        one.wait()
    small[0] = whole[0].astype(jnp.float32)
    small[1] = whole[1].astype(jnp.float32)
    small[3, 0, 0:2, :] = values[...]
    low[19:22] = small[0:3, :, 0:HALO, :]
    high[19:22] = small[0:3, :, OWN - HALO : OWN, :]


def put_sends(send_left, send_right, t, lin, chosen):
    for k, i in enumerate(LEFTWARD):
        send_left[k, flat(t), :] = lin[0][i]
    for k, i in enumerate(RIGHTWARD):
        send_right[k, flat(t), :] = lin[1][i]
    send_left[8, flat(t), :] = chosen[0]
    send_right[8, flat(t), :] = chosen[1]


def start_rows(t, populations, shares, marks, table, outs):
    lin_out, flow_out, density_out, effective_out, share_out, _, send_left, send_right = outs
    half_low = jnp.broadcast_to(table[0:1, :], (8, DEPTH))
    half_high = jnp.broadcast_to(table[1:2, :], (8, DEPTH))
    lin, chosen = [], []
    for x in range(2):
        share = shares[x]
        spot = jnp.bitwise_and(marks[x], DEPTH - 1)
        wall = jnp.where(
            jnp.bitwise_and(marks[x], DEPTH) == 0,
            jnp.take_along_axis(half_low, spot, axis=1),
            jnp.take_along_axis(half_high, spot, axis=1),
        )
        total, momentum, linear = linear_part(populations[x], share, range(19))
        for i in range(19):
            lin_out[i, x, flat(t), :] = linear[i]
        for a in range(3):
            flow_out[a, x, flat(t), :] = momentum[a]
        density_out[x, flat(t), :] = total
        effective_out[x, flat(t), :] = jnp.where(share > 0, 1.0 - jnp.exp(-total), wall)
        share_out[x, flat(t), :] = share
        lin.append(linear)
        chosen.append(jnp.where(share > 0, total, wall))
    put_sends(send_left, send_right, t, lin, chosen)
    send_left[9, flat(t), :] = shares[0]
    send_right[9, flat(t), :] = shares[1]


def own_kernel(pops, small, *refs):
    outs, chooser, turned_label = refs[:8], refs[8], refs[9]
    outs[5][:, HALO : HALO + OWN, :] = small[2]

    def body(t):
        rows = rows_at(t, 0, -HALO)
        start_rows(
            t,
            [{i: pops[i, x, rows, :] for i in range(19)} for x in range(2)],
            [small[0, x, rows, :] for x in range(2)],
            [small[1, x, rows, :].astype(jnp.int32) for x in range(2)],
            small[3, 0, 0:2, :],
            outs,
        )

    each_chunk(body, HALO // 8, (HALO + OWN) // 8)

    marks = jnp.bitwise_and(small[1, 0].astype(jnp.int32), LABELS - 1).astype(jnp.float32)
    turned_label[...] = jnp.transpose(marks)
    quads = DEPTH // 4
    by_quad = turned_label[pl.ds(0, quads, stride=4), :]
    names = lax.broadcasted_iota(jnp.int32, (quads, LABELS), 1).astype(jnp.float32)
    for k in range(OWN // 2):
        column = jnp.broadcast_to(by_quad[:, 2 * k : 2 * k + 1], (quads, LABELS))
        chooser[quads * k : quads * (k + 1), :] = (column == names).astype(jnp.bfloat16)


def halo_kernel(small, below, above, *refs):
    outs, field, doubled = refs[8:16], refs[16], refs[17]
    for t, edge in ((0, below), (CHUNKS - 1, above)):
        outs[5][:, 8 * t : 8 * t + 8, :] = edge[21]
        start_rows(
            t,
            [{i: edge[i, x] for i in range(19)} for x in range(2)],
            [edge[19, x] for x in range(2)],
            [edge[20, x].astype(jnp.int32) for x in range(2)],
            small[3, 0, 0:2, :],
            outs,
        )
    flow, effective, send_left, send_right = outs[1], outs[3], outs[6], outs[7]

    def place(t):
        for x in range(2):
            value = effective[x, flat(t), :]
            field[x, tall(t), :] = value
            doubled[x, tall(t), :] = with_sides(value)

    each_chunk(place)
    each_chunk(functools.partial(send_flow, send_left, send_right, flow, field, doubled))


def step_kernel(is_first, *refs):
    if is_first:
        (lin, flow, density, effective, share, from_left, from_right,
         masks, field, speed, pull_out, lin_out, flow_out, density_out, effective_out, send_left, send_right,
         doubled, relaxed, turned, next_field, next_doubled) = refs
    else:
        (lin, flow, density, effective, share, target, masks, from_left, from_right,
         field, speed, pull_out, misfit_out, send_left, send_right,
         doubled, relaxed, turned) = refs

    def place(t):
        def put(p, x, s):
            field[p, tall(t), :] = x
            doubled[p, tall(t), :] = with_sides(x)
            if is_first:
                masks[0, p, tall(t), :] = s
                masks[1, p, tall(t), :] = rolled(s, 1)
                masks[2, p, tall(t), :] = rolled(s, -1)

        for x in range(2):
            put(2 + x, effective[x, flat(t), :], share[x, flat(t), :])
        for near, come in ((1, from_left), (4, from_right)):
            s = come[9, flat(t), :] if is_first else masks[0, near, tall(t), :]
            chosen = come[8, flat(t), :]
            put(near, jnp.where(s > 0, 1.0 - jnp.exp(-chosen), chosen), s)

    each_chunk(place)

    def collide(t):
        for p in range(1, 5):
            psi = field[p, tall(t), :]
            s = masks[0, p, tall(t), :]
            if p in (2, 3):
                pull = gradient_of(field, doubled, p, t)
                rho = density[p - 2, flat(t), :]
                mom = [flow[a, p - 2, flat(t), :] for a in range(3)]
                which = range(19)
                lin_at = {i: lin[i, p - 2, flat(t), :] for i in which}
                for a in range(3):
                    pull_out[a, p - 2, flat(t), :] = pull[a]
            else:
                pull = outer_gradient(field, doubled, p, 2 if p == 1 else 3, t)
                come = from_left if p == 1 else from_right
                rho = come[8, flat(t), :]
                mom = [come[5 + a, flat(t), :] for a in range(3)]
                which = RIGHTWARD if p == 1 else LEFTWARD
                lin_at = {i: come[k, flat(t), :] for k, i in enumerate(which)}
            push = psi * (PULL / SHEAR)
            full = [mom[a] + push * pull[a] for a in range(3)]
            inverse = 1.0 / rho
            u = [full[a] * inverse for a in range(3)]
            for a in range(3):
                speed[a, p - 1, flat(t), :] = u[a]
            part = balance_part(rho, full, u, s, which)
            for i in which:
                value = lin_at[i] + part[i]
                relaxed[i, p - 1, tall(t), :] = value
                if i in TURNED:
                    turned[TURNED.index(i), p - 1, tall(t), :] = rolled(value, VECTORS[i][2])

    each_chunk(collide)

    def streamed(x, rows):
        f = {0: relaxed[0, 1 + x, rows(0), :]}
        for i in range(1, 19):
            cx, cy, cz = VECTORS[i]
            if cz:
                source = turned[TURNED.index(i), 1 + x - cx, rows(-cy), :]
            else:
                source = relaxed[i, 1 + x - cx, rows(-cy), :]
            open_ = masks[cz % 3, 2 + x - cx, rows(-cy), :] > 0
            f[i] = jnp.where(open_, source, relaxed[OPPOSITE[i], 1 + x, rows(0), :])
        return f

    def stream(t):
        lin_sent, chosen_sent = [], []
        for x in range(2):
            s = share[x, flat(t), :]
            total, momentum, linear = linear_part(streamed(x, lambda dy: tall(t, dy)), s, range(19))
            held = effective[x, flat(t), :]
            eff = jnp.where(s > 0, 1.0 - jnp.exp(-total), held)
            for i in range(19):
                lin_out[i, x, flat(t), :] = linear[i]
            for a in range(3):
                flow_out[a, x, flat(t), :] = momentum[a]
            density_out[x, flat(t), :] = total
            effective_out[x, flat(t), :] = eff
            next_field[x, tall(t), :] = eff
            next_doubled[x, tall(t), :] = with_sides(eff)
            lin_sent.append(linear)
            chosen_sent.append(jnp.where(s > 0, total, held))
        put_sends(send_left, send_right, t, lin_sent, chosen_sent)

    def compare(t):
        for x, near, far in ((0, send_left, send_right), (1, send_right, send_left)):
            f = streamed(x, lambda dy: mid_tall(t, dy))
            s = share[x, mid(t), :]
            misfit = s * (add(*[f[i] for i in range(19)]) - target[x, mid(t), :])
            misfit_out[x, flat(t), :] = misfit
            near[0, flat(t), :] = misfit
            far[1, flat(t), :] = misfit
            far[2, flat(t), :] = s

    if is_first:
        each_chunk(stream)
        each_chunk(functools.partial(send_flow, send_left, send_right, flow_out, next_field, next_doubled))
    else:
        each_chunk(compare, 0, MID // 8)


def spread_of(pulled, pulled_doubled, p, rows):
    at = lambda a, dp, dy: pulled[a, p + dp, rows(dy), :]
    two = lambda a, dp, dy: pulled_doubled[a, p + dp, rows(dy), :]
    along_x = two(0, 1, 0) - two(0, -1, 0) + (at(0, 1, 1) + at(0, 1, -1)) - (at(0, -1, 1) + at(0, -1, -1))
    along_y = two(1, 0, 1) - two(1, 0, -1) + (at(1, 1, 1) + at(1, -1, 1)) - (at(1, 1, -1) + at(1, -1, -1))
    star = 2.0 * at(2, 0, 0) + at(2, 1, 0) + at(2, -1, 0) + at(2, 0, 1) + at(2, 0, -1)
    along_z = rolled(star, -1) - rolled(star, 1)
    return (along_x + along_y + along_z) * (-1.0 / 36.0)


def put_pulled(pulled, pulled_doubled, p, rows, psi, q):
    for a in range(3):
        s = (COUPLING / SHEAR) * psi * q[a]
        pulled[a, p, rows(0), :] = s
        if a < 2:
            pulled_doubled[a, p, rows(0), :] = with_sides(s)


def mask_ahead(masks, i, p, rows):
    cx, cy, cz = VECTORS[i]
    return masks[(-cz) % 3, p + cx, rows(cy), :] > 0


def middle(t):
    return lambda dy: mid_tall(t, dy)


def last_reverse_kernel(
    misfit, from_left, from_right, masks, field, speed, pull, early_speed,
    adjoint, turned, wall_out, send_left, send_right,
    ahead, far_masks, pulled, pulled_doubled, base,
):
    def place(t):
        rows = middle(t)
        for p in range(6):
            if p < 2:
                d = from_left[1 - p, flat(t), :]
            elif p < 4:
                d = misfit[p - 2, flat(t), :]
            else:
                d = from_right[p - 4, flat(t), :]
            ahead[0, p, rows(0), :] = d
            ahead[1, p, rows(0), :] = rolled(d, 1)
            ahead[2, p, rows(0), :] = rolled(d, -1)
        for k, source in enumerate((from_left, from_right)):
            s = source[2, flat(t), :]
            far_masks[0, k, rows(0), :] = s
            far_masks[1, k, rows(0), :] = rolled(s, 1)
            far_masks[2, k, rows(0), :] = rolled(s, -1)

    each_chunk(place, 0, MID // 8)

    def collide(t):
        rows = middle(t)
        for p in range(1, 5):
            s = masks[0, p, rows(0), :]
            here = ahead[0, p, rows(0), :]
            r = {0: here}
            for i in range(1, 19):
                cx, cy, cz = VECTORS[i]
                there = ahead[(-cz) % 3, p + cx, rows(cy), :]
                if p + cx in (0, 5):
                    open_ = far_masks[(-cz) % 3, (p + cx) // 5, rows(cy), :] > 0
                else:
                    open_ = mask_ahead(masks, i, p, rows)
                r[i] = s * jnp.where(open_, there, here)
            psi = field[p, rows(0), :]
            u = [speed[a, p - 1, mid(t), :] for a in range(3)]
            if p in (2, 3):
                rest, by_density, q = collide_adjoint(r, u)
                along = add(*[q[a] * pull[a, p - 2, mid(t), :] for a in range(3)])
                const = by_density + along * ((PULL / SHEAR) * (1.0 - psi))
                for i in range(19):
                    base[i, p - 2, flat(t), :] = rest[i] + const
            else:
                q = flow_adjoint(*dual(r), u)
            put_pulled(pulled, pulled_doubled, p - 1, rows, psi, q)

    each_chunk(collide, 0, MID // 8)

    def finish(t):
        rows = middle(t)
        for x in range(2):
            s = masks[0, 2 + x, rows(0), :]
            spread = spread_of(pulled, pulled_doubled, 1 + x, rows)
            wall_out[x, flat(t), :] = (1.0 - s) * spread
            more = s * spread * (1.0 - field[2 + x, rows(0), :])
            for i in range(19):
                value = base[i, x, flat(t), :] + more
                adjoint[i, x, rows(0), :] = value
                if i in TURNED:
                    turned[TURNED.index(i), x, rows(0), :] = rolled(value, -VECTORS[i][2])

    each_chunk(finish, 0, MID // 8)

    def part(t):
        rows = middle(t)
        for x, send, sent, skipped in ((0, send_left, RIGHTWARD, -1), (1, send_right, LEFTWARD, 1)):
            p = 2 + x
            s = masks[0, p, rows(0), :]
            r = {}
            for i in range(19):
                if VECTORS[i][0] != skipped:
                    r[i] = adjoint_ahead(adjoint, turned, masks, i, x, rows)
            u = [early_speed[a, p - 1, mid(t), :] for a in range(3)]
            q = flow_adjoint(*dual(r), u)
            for a in range(3):
                send[5 + a, flat(t), :] = s * q[a]
            for k, i in enumerate(sent):
                send[k, flat(t), :] = adjoint[i, x, rows(0), :]

    each_chunk(part, 0, MID // 8)


def adjoint_ahead(adjoint, turned, masks, i, x, rows):
    cx, cy, cz = VECTORS[i]
    if i == 0:
        return adjoint[0, x, rows(0), :]
    if cz:
        there = turned[TURNED.index(i), x + cx, rows(cy), :]
    else:
        there = adjoint[i, x + cx, rows(cy), :]
    return jnp.where(mask_ahead(masks, i, 2 + x, rows), there, adjoint[OPPOSITE[i], x, rows(0), :])


def place_sides(come, from_left, from_right, t):
    for side, source, which in ((0, from_left, LEFTWARD), (1, from_right, RIGHTWARD)):
        for k, i in enumerate(which):
            come[side, k, mid_tall(t), :] = rolled(source[k, flat(t), :], -VECTORS[i][2])


def arrived(come, adjoint, masks, i, x, rows):
    which = LEFTWARD if x == 0 else RIGHTWARD
    there = come[x, which.index(i), rows(VECTORS[i][1]), :]
    return jnp.where(mask_ahead(masks, i, 2 + x, rows), there, adjoint[OPPOSITE[i], x, rows(0), :])


def wall_kernel(
    adjoint, turned, wall, part_left, part_right, from_left, from_right, masks, field, speed, chooser,
    more_out, label_part,
    come, pulled, pulled_doubled, totals,
):
    each_chunk(functools.partial(place_sides, come, from_left, from_right), 0, MID // 8)

    def collide(t):
        rows = middle(t)
        for x, part, which in ((0, part_left, LEFTWARD), (1, part_right, RIGHTWARD)):
            p = 2 + x
            s = masks[0, p, rows(0), :]
            r = {i: arrived(come, adjoint, masks, i, x, rows) for i in which}
            u = [speed[a, p - 1, mid(t), :] for a in range(3)]
            rest = flow_adjoint(*dual(r), u)
            q = [part[5 + a, flat(t), :] + s * rest[a] for a in range(3)]
            put_pulled(pulled, pulled_doubled, p - 1, rows, field[p, rows(0), :], q)
        for x, source, which in ((0, from_left, LEFTWARD), (1, from_right, RIGHTWARD)):
            p = 1 if x == 0 else 4
            s = masks[0, p, rows(0), :]
            r = {}
            for i in [OPPOSITE[j] for j in which]:
                cx, cy, cz = VECTORS[i]
                if cz:
                    there = turned[TURNED.index(i), x, rows(cy), :]
                else:
                    there = adjoint[i, x, rows(cy), :]
                here = source[which.index(OPPOSITE[i]), flat(t), :]
                r[i] = jnp.where(mask_ahead(masks, i, p, rows), there, here)
            u = [speed[a, p - 1, mid(t), :] for a in range(3)]
            rest = flow_adjoint(*dual(r), u)
            q = [source[5 + a, flat(t), :] + s * rest[a] for a in range(3)]
            put_pulled(pulled, pulled_doubled, p - 1, rows, field[p, rows(0), :], q)

    each_chunk(collide, 0, MID // 8)

    def finish(t):
        total = None
        for x in range(2):
            s = masks[0, 2 + x, tall(t), :]
            spread = spread_of(pulled, pulled_doubled, 1 + x, lambda dy: tall(t, dy))
            step_wall = wall[x, pl.ds(t * 8 - (ROWS - MID) // 2, 8), :]
            total = add(total, (1.0 - s) * spread + step_wall)
            more_out[x, rows_at(t, 0, -HALO), :] = s * spread * (1.0 - field[2 + x, tall(t), :])
        totals[rows_at(t, 0, -HALO), :] = total

    each_chunk(finish, HALO // 8, (HALO + OWN) // 8)

    blocks = (OWN // 2) * (DEPTH // 4)
    column = lax.broadcasted_iota(jnp.int32, (DEPTH, blocks), 1)
    quad = lax.broadcasted_iota(jnp.int32, (DEPTH, blocks), 0) // 4
    gather = (jnp.bitwise_and(column, DEPTH // 4 - 1) == quad).astype(jnp.bfloat16)
    by_block = exact_dot(totals[...], gather)
    pair = lax.broadcasted_iota(jnp.int32, (OWN, blocks), 0) // 2
    wanted = lax.broadcasted_iota(jnp.int32, (OWN, blocks), 1) // (DEPTH // 4)
    by_block = jnp.where(pair == wanted, by_block, 0.0)
    by_label = exact_dot(by_block, chooser[...])
    label_part[...] = jnp.sum(by_label, axis=0, keepdims=True)


def grad_kernel(
    adjoint, turned, more, from_left, from_right, masks, field, speed, pull,
    grad,
    come,
):
    each_chunk(functools.partial(place_sides, come, from_left, from_right), 0, MID // 8)

    def collide(t):
        rows = lambda dy: tall(t, dy)
        for x in range(2):
            p = 2 + x
            s = masks[0, p, tall(t), :]
            r = {}
            for i in range(19):
                if VECTORS[i][0] == 2 * x - 1:
                    r[i] = s * arrived(come, adjoint, masks, i, x, rows)
                else:
                    r[i] = s * adjoint_ahead(adjoint, turned, masks, i, x, rows)
            u = [speed[a, p - 1, flat(t), :] for a in range(3)]
            rest, by_density, q = collide_adjoint(r, u)
            along = add(*[q[a] * pull[a, x, flat(t), :] for a in range(3)])
            const = by_density + along * ((PULL / SHEAR) * (1.0 - field[p, tall(t), :]))
            const = const + more[x, rows_at(t, 0, -HALO), :]
            for i in range(19):
                grad[i, x, rows_at(t, 0, -HALO), :] = rest[i] + const

    each_chunk(collide, HALO // 8, (HALO + OWN) // 8)


def exact_dot(values, zero_one):
    high = values.astype(jnp.bfloat16)
    left = values - high.astype(jnp.float32)
    middle = left.astype(jnp.bfloat16)
    low = (left - middle.astype(jnp.float32)).astype(jnp.bfloat16)
    dot = lambda part: jnp.dot(part, zero_one, preferred_element_type=jnp.float32)
    return dot(high) + (dot(middle) + dot(low))


def call(kernel, args, outs, scratch, anywhere=0, grant=12, filled=0):
    whole = pl.BlockSpec(memory_space=pltpu.VMEM)
    there = pl.BlockSpec(memory_space=pl.ANY)
    size = sum(a.size * a.dtype.itemsize for a in args)
    return pl.pallas_call(
        kernel,
        out_shape=[s if hasattr(s, "dtype") else jax.ShapeDtypeStruct(s, jnp.float32) for s in outs],
        in_specs=[there] * anywhere + [whole] * (len(args) - anywhere),
        out_specs=[whole] * len(outs),
        scratch_shapes=scratch,
        input_output_aliases={len(args) - filled + k: k for k in range(filled)},
        compiler_params=pltpu.CompilerParams(vmem_limit_bytes=grant * 1024 * 1024),
        cost_estimate=pl.CostEstimate(flops=0, bytes_accessed=size, transcendentals=0),
    )(*args)


def ring(axis):
    count = lax.axis_size(axis)
    up = [(i, (i + 1) % count) for i in range(count)]
    return up, [(j, i) for i, j in up]


def both_ways(to_lower, to_upper, axis):
    up, down = ring(axis)
    from_lower = lax.ppermute(to_upper, axis, up)
    from_upper = lax.ppermute(to_lower, axis, down)
    return from_lower, from_upper


def per_device(populations, fluid, label, wall_wetting, target):
    vmem = lambda *shape: pltpu.VMEM(shape, jnp.float32)
    plane = (ROWS, DEPTH)
    two = (2, *plane)
    edge = (22, 2, HALO, DEPTH)
    low, high, small = call(
        edges_kernel,
        (populations, fluid, label, target, wall_wetting.reshape(2, DEPTH)),
        (edge, edge, (4, 2, OWN, DEPTH)),
        (
            pltpu.VMEM((2, 2, OWN, DEPTH), jnp.int32),
            vmem(2, DEPTH),
            pltpu.SemaphoreType.DMA((6,)),
        ),
        anywhere=5,
        grant=56,
    )
    below, above = both_ways(low, high, "gy")
    blocks = (OWN // 2) * (DEPTH // 4)
    started = ((19, *two), (3, *two), two, two, two, two, (10, *plane), (10, *plane))
    *own, chooser = call(
        own_kernel,
        (populations, small),
        (*started, jax.ShapeDtypeStruct((blocks, LABELS), jnp.bfloat16)),
        (vmem(DEPTH, OWN),),
    )
    beside = (vmem(2, TALL, DEPTH), vmem(2, TALL, DEPTH))
    lin, flow, density, effective, share, target_wide, to_left, to_right = call(
        halo_kernel, (small, below, above, *own), started, beside, filled=len(started)
    )
    from_left, from_right = both_ways(to_left, to_right, "gx")
    wide6 = (6, TALL, DEPTH)
    work = (vmem(*wide6), vmem(19, 4, TALL, DEPTH), vmem(10, 4, TALL, DEPTH))
    masks, field0, speed0, pull0, lin, flow, density, effective, to_left, to_right = call(
        functools.partial(step_kernel, True),
        (lin, flow, density, effective, share, from_left, from_right),
        (
            (3, *wide6), wide6, (3, 4, *plane), (3, *two),
            (19, *two), (3, *two), two, two, (9, *plane), (9, *plane),
        ),
        (*work, *beside),
    )
    from_left, from_right = both_ways(to_left, to_right, "gx")
    less = (MID, DEPTH)
    field1, speed1, pull1, misfit, to_left, to_right = call(
        functools.partial(step_kernel, False),
        (lin, flow, density, effective, share, target_wide, masks, from_left, from_right),
        (wide6, (3, 4, *plane), (3, *two), (2, *less), (3, *less), (3, *less)),
        work,
    )
    from_left, from_right = both_ways(to_left, to_right, "gx")
    pulled = (vmem(3, 4, TALL, DEPTH), vmem(2, 4, TALL, DEPTH))
    adjoint, turned, wall, to_left, to_right = call(
        last_reverse_kernel,
        (misfit, from_left, from_right, masks, field1, speed1, pull1, speed0),
        ((19, 2, TALL, DEPTH), (10, 2, TALL, DEPTH), (2, *less), (8, *less), (8, *less)),
        (vmem(3, *wide6), vmem(3, 2, TALL, DEPTH), *pulled, vmem(19, 2, *less)),
    )
    from_left, from_right = both_ways(to_left, to_right, "gx")
    come = vmem(2, 5, TALL, DEPTH)
    more, label_part = call(
        wall_kernel,
        (adjoint, turned, wall, to_left, to_right, from_left, from_right, masks, field0, speed0, chooser),
        ((2, OWN, DEPTH), (1, LABELS)),
        (come, *pulled, vmem(OWN, DEPTH)),
    )
    count = lax.axis_size("gy")
    wetting_grad = label_part
    for step in range(1, count):
        wetting_grad = wetting_grad + lax.ppermute(
            label_part, "gy", [(i, (i + step) % count) for i in range(count)]
        )
    (grad,) = call(
        grad_kernel,
        (adjoint, turned, more, from_left, from_right, masks, field0, speed0, pull0),
        (populations.shape,),
        (come,),
    )
    return (grad, wetting_grad.reshape(-1))


def solution(mesh):
    return jax.shard_map(
        per_device,
        mesh=mesh,
        in_specs=(
            P(None, "gx", "gy", None),
            P("gx", "gy", None),
            P("gx", "gy", None),
            P("gx"),
            P("gx", "gy", None),
        ),
        out_specs=(P(None, "gx", "gy", None), P("gx")),
        check_vma=False,
    )
```

```python
import functools

import jax
import jax.numpy as jnp
from jax import lax
from jax.experimental import pallas as pl
from jax.experimental.pallas import tpu as pltpu
from jax.sharding import PartitionSpec as P

HALO = 8
PAD = 8
OWN = 32
ROWS = OWN + 2 * HALO
TALL = ROWS + 2 * PAD
MID = OWN + HALO
DEPTH = 128
CHUNKS = ROWS // 8
LABELS = 256

VECTORS = (
    (0, 0, 0), (1, 0, 0), (-1, 0, 0), (0, 1, 0), (0, -1, 0), (0, 0, 1), (0, 0, -1),
    (1, 1, 0), (-1, -1, 0), (1, -1, 0), (-1, 1, 0), (1, 0, 1), (-1, 0, -1), (1, 0, -1), (-1, 0, 1),
    (0, 1, 1), (0, -1, -1), (0, 1, -1), (0, -1, 1),
)
OPPOSITE = (0, 2, 1, 4, 3, 6, 5, 8, 7, 10, 9, 12, 11, 14, 13, 16, 15, 18, 17)
INDEX = {v: i for i, v in enumerate(VECTORS)}
RIGHTWARD = tuple(i for i in range(19) if VECTORS[i][0] == 1)
LEFTWARD = tuple(i for i in range(19) if VECTORS[i][0] == -1)
TURNED = tuple(i for i in range(19) if VECTORS[i][2] != 0)
PLANES = ((0, 1), (1, 2), (0, 2))
COUPLING = 5.0
SHEAR = 1.2
BULK = 1.19
THIRD = 1.5
FOURTH = 1.4
TRACE = (BULK - SHEAR) / 3.0
PULL = COUPLING / 36.0


def axis_index_of(axis, sign):
    v = [0, 0, 0]
    v[axis] = sign
    return INDEX[tuple(v)]


def edge_index_of(a, b, sa, sb):
    v = [0, 0, 0]
    v[a], v[b] = sa, sb
    return INDEX[tuple(v)]


def add(*terms):
    total = None
    for term in terms:
        if term is not None:
            total = term if total is None else total + term
    return total


def sub(a, b):
    if b is None:
        return a
    return -b if a is None else a - b


def scale(c, a):
    return None if a is None else c * a


def mul(a, b):
    return None if a is None or b is None else a * b


def moments(f):
    fourth, mixed, third = {}, {}, {}
    for a, b in PLANES:
        pp, mm = f[edge_index_of(a, b, 1, 1)], f[edge_index_of(a, b, -1, -1)]
        pm, mp = f[edge_index_of(a, b, 1, -1)], f[edge_index_of(a, b, -1, 1)]
        even, odd, cross, skew = pp + mm, pp - mm, pm + mp, pm - mp
        fourth[a, b] = even + cross
        mixed[a, b] = even - cross
        third[a, b] = odd + skew
        third[b, a] = odd - skew
    first, diagonal, total = [], [], f[0]
    for a in range(3):
        b, c = [k for k in range(3) if k != a]
        plus, minus = f[axis_index_of(a, 1)], f[axis_index_of(a, -1)]
        both = plus + minus
        total = total + both
        diagonal.append(both + fourth[tuple(sorted((a, b)))] + fourth[tuple(sorted((a, c)))])
        first.append((plus - minus) + third[a, b] + third[a, c])
    total = total + fourth[0, 1] + fourth[1, 2] + fourth[0, 2]
    return total, first, diagonal, mixed, third, fourth


def from_moments(first, diagonal, mixed, third, fourth, which):
    out = {}
    for a, b in PLANES:
        even, cross = fourth[a, b] + mixed[a, b], fourth[a, b] - mixed[a, b]
        odd, skew = third[a, b] + third[b, a], third[a, b] - third[b, a]
        out[edge_index_of(a, b, 1, 1)] = even + odd
        out[edge_index_of(a, b, -1, -1)] = even - odd
        out[edge_index_of(a, b, 1, -1)] = cross + skew
        out[edge_index_of(a, b, -1, 1)] = cross - skew
    for a in range(3):
        b, c = [k for k in range(3) if k != a]
        even = diagonal[a] - 2.0 * (fourth[tuple(sorted((a, b)))] + fourth[tuple(sorted((a, c)))])
        odd = first[a] - 2.0 * (third[a, b] + third[a, c])
        out[axis_index_of(a, 1)] = even + odd
        out[axis_index_of(a, -1)] = even - odd
    out[0] = 4.0 * (fourth[0, 1] + fourth[1, 2] + fourth[0, 2]) - 2.0 * (diagonal[0] + diagonal[1] + diagonal[2])
    return {i: out[i] for i in which}


def linear_part(f, share, which):
    total, first, diagonal, mixed, third, fourth = moments(f)
    half, quarter = (0.5 * SHEAR) * share, (0.25 * SHEAR) * share
    trace = (0.5 * TRACE) * share * (diagonal[0] + diagonal[1] + diagonal[2])
    by_third, by_fourth = (0.25 * THIRD) * share, (0.25 * FOURTH) * share
    change = from_moments(
        [half * m for m in first],
        [half * m + trace for m in diagonal],
        {k: quarter * m for k, m in mixed.items()},
        {k: by_third * m for k, m in third.items()},
        {k: by_fourth * m for k, m in fourth.items()},
        which,
    )
    return total, first, {i: f[i] - change[i] for i in which}


def balance_part(density, flow, velocity, share, which):
    d = density * share
    m = [flow[a] * share for a in range(3)]
    square = [m[a] * velocity[a] for a in range(3)]
    whole = square[0] + square[1] + square[2]
    level = d * (SHEAR / 6.0 + 0.5 * TRACE) + whole * (0.5 * TRACE)
    diagonal = [(0.5 * SHEAR) * square[a] + level for a in range(3)]
    scaled = [(0.25 * SHEAR) * velocity[a] for a in range(3)]
    mixed = {(a, b): m[a] * scaled[b] for a, b in PLANES}
    part = [(THIRD / 12.0) * m[a] for a in range(3)]
    third = {}
    fourth = {}
    level = d * (FOURTH / 36.0) + whole * (FOURTH / 12.0)
    for a, b in PLANES:
        third[a, b], third[b, a] = part[a], part[b]
        fourth[a, b] = level - (FOURTH / 8.0) * square[3 - a - b]
    return from_moments([(0.5 * SHEAR) * m[a] for a in range(3)], diagonal, mixed, third, fourth, which)


def dual(r):
    get = lambda i: r.get(i)
    first, diagonal = [], []
    plus_of, minus_of = [], []
    for a in range(3):
        p, m = get(axis_index_of(a, 1)), get(axis_index_of(a, -1))
        even = scale(0.5, add(p, m))
        odd = scale(0.5, sub(p, m))
        plus_of.append(even)
        minus_of.append(odd)
        first.append(odd)
        diagonal.append(sub(even, get(0)))
    mixed, third, fourth = {}, {}, {}
    for a, b in PLANES:
        pp, mm = get(edge_index_of(a, b, 1, 1)), get(edge_index_of(a, b, -1, -1))
        pm, mp = get(edge_index_of(a, b, 1, -1)), get(edge_index_of(a, b, -1, 1))
        even, odd, cross, skew = add(pp, mm), sub(pp, mm), add(pm, mp), sub(pm, mp)
        fourth[a, b] = add(sub(sub(scale(0.25, add(even, cross)), plus_of[a]), plus_of[b]), get(0))
        mixed[a, b] = scale(0.25, sub(even, cross))
        third[a, b] = sub(scale(0.25, add(odd, skew)), minus_of[a])
        third[b, a] = sub(scale(0.25, sub(odd, skew)), minus_of[b])
    trace = scale(TRACE, add(*diagonal))
    return (
        [scale(SHEAR, m) for m in first],
        [add(scale(SHEAR, m), trace) for m in diagonal],
        {k: scale(SHEAR, m) for k, m in mixed.items()},
        {k: scale(THIRD, m) for k, m in third.items()},
        {k: scale(FOURTH, m) for k, m in fourth.items()},
    )


def flow_adjoint(first, diagonal, mixed, third, fourth, u):
    q = []
    for a in range(3):
        b, c = [k for k in range(3) if k != a]
        ab, ac, bc = tuple(sorted((a, b))), tuple(sorted((a, c))), tuple(sorted((b, c)))
        along = add(
            scale(2.0, diagonal[a]),
            scale(2.0 / 3.0, add(fourth[ab], fourth[ac])),
            scale(-1.0 / 3.0, fourth[bc]),
        )
        q.append(
            add(
                first[a],
                scale(1.0 / 3.0, add(third[a, b], third[a, c])),
                mul(u[a], along),
                mul(u[b], mixed[ab]),
                mul(u[c], mixed[ac]),
            )
        )
    return q


def collide_adjoint(r, u):
    t = dual(r)
    first, diagonal, mixed, third, fourth = t
    q = flow_adjoint(*t, u)
    square = [u[a] * u[a] for a in range(3)]
    by_density = None
    for a in range(3):
        b, c = [k for k in range(3) if k != a]
        by_density = add(
            by_density,
            u[a] * (first[a] + (1.0 / 3.0) * (third[a, b] + third[a, c]) - q[a]),
            diagonal[a] * (1.0 / 3.0 + square[a]),
        )
    for a, b in PLANES:
        c = 3 - a - b
        by_density = by_density + mixed[a, b] * (u[a] * u[b])
        by_density = by_density + fourth[a, b] * (
            1.0 / 9.0 + (square[a] + square[b]) * (1.0 / 3.0) - square[c] * (1.0 / 6.0)
        )
    drift = [q[a] - first[a] for a in range(3)]
    base = {0: r[0]}
    for a in range(3):
        base[axis_index_of(a, 1)] = r[axis_index_of(a, 1)] + (drift[a] - diagonal[a])
        base[axis_index_of(a, -1)] = r[axis_index_of(a, -1)] - (drift[a] + diagonal[a])
    for a, b in PLANES:
        along = drift[a] - third[a, b]
        across = drift[b] - third[b, a]
        even = diagonal[a] + diagonal[b] + fourth[a, b]
        same, cross = even + mixed[a, b], even - mixed[a, b]
        both, gap = along + across, along - across
        base[edge_index_of(a, b, 1, 1)] = r[edge_index_of(a, b, 1, 1)] + (both - same)
        base[edge_index_of(a, b, -1, -1)] = r[edge_index_of(a, b, -1, -1)] - (both + same)
        base[edge_index_of(a, b, 1, -1)] = r[edge_index_of(a, b, 1, -1)] + (gap - cross)
        base[edge_index_of(a, b, -1, 1)] = r[edge_index_of(a, b, -1, 1)] - (gap + cross)
    return base, by_density, q


def rolled(x, step):
    return x if step == 0 else pltpu.roll(x, step % DEPTH, 1)


def rows_at(t, shift, offset):
    if isinstance(t, int):
        return pl.ds(t * 8 + offset + shift, 8)
    if shift == 0:
        return pl.ds(pl.multiple_of(t * 8 + offset, 8), 8)
    return pl.ds(t * 8 + (offset + shift), 8)


def flat(t):
    return rows_at(t, 0, 0)


def tall(t, shift=0):
    return rows_at(t, shift, PAD)


def mid(t):
    return pl.ds(t * 8 + (ROWS - MID) // 2, 8)


def mid_tall(t, shift=0):
    return pl.ds(t * 8 + ((ROWS - MID) // 2 + PAD + shift), 8)


def each_chunk(body, first=0, last=CHUNKS):
    for t in range(first, last):
        body(t)


def gradient_of(field, doubled, p, t):
    at = lambda dp, dy: field[p + dp, tall(t, dy), :]
    rp, rm, lp, lm = at(1, 1), at(1, -1), at(-1, 1), at(-1, -1)
    along_x = doubled[p + 1, tall(t), :] - doubled[p - 1, tall(t), :] + (rp + rm) - (lp + lm)
    along_y = doubled[p, tall(t, 1), :] - doubled[p, tall(t, -1), :] + (rp + lp) - (rm + lm)
    star = 2.0 * at(0, 0) + at(1, 0) + at(-1, 0) + at(0, 1) + at(0, -1)
    return [along_x, along_y, rolled(star, -1) - rolled(star, 1)]


def with_sides(x):
    return 2.0 * x + rolled(x, 1) + rolled(x, -1)


def inner_gradient(field, doubled, here, inner, t):
    at = lambda x, dy: field[x, tall(t, dy), :]
    up, down = at(inner, 1), at(inner, -1)
    along_x = doubled[inner, tall(t), :] + (up + down)
    along_y = doubled[here, tall(t, 1), :] - doubled[here, tall(t, -1), :] + (up - down)
    star = 2.0 * at(here, 0) + at(inner, 0) + at(here, 1) + at(here, -1)
    return [along_x if inner > here else -along_x, along_y, rolled(star, -1) - rolled(star, 1)]


def outer_gradient(field, doubled, p, inner, t):
    at = lambda dy: field[inner, tall(t, dy), :]
    up, down, here = at(1), at(-1), at(0)
    along_x = doubled[inner, tall(t), :] + (up + down)
    return [along_x if inner > p else -along_x, up - down, rolled(here, -1) - rolled(here, 1)]


def send_flow(send_left, send_right, flow, field, doubled, t):
    for send, here, inner in ((send_left, 0, 1), (send_right, 1, 0)):
        push = field[here, tall(t), :] * (PULL / SHEAR)
        pull = inner_gradient(field, doubled, here, inner, t)
        for a in range(3):
            send[5 + a, flat(t), :] = flow[a, here, flat(t), :] + push * pull[a]


def edges_kernel(pops, fluid, label, target, table, low, high, small, whole, values, sems):
    copies = []

    def copy(source, goal):
        one = pltpu.make_async_copy(source, goal, sems.at[len(copies)])
        one.start()
        copies.append(one)

    copy(fluid, whole.at[0])
    copy(label, whole.at[1])
    copy(target, small.at[2])
    copy(table, values)
    copy(pops.at[:, :, pl.ds(0, HALO), :], low.at[pl.ds(0, 19)])
    copy(pops.at[:, :, pl.ds(OWN - HALO, HALO), :], high.at[pl.ds(0, 19)])
    for one in copies:
        one.wait()
    small[0] = whole[0].astype(jnp.float32)
    small[1] = whole[1].astype(jnp.float32)
    small[3, 0, 0:2, :] = values[...]
    low[19:22] = small[0:3, :, 0:HALO, :]
    high[19:22] = small[0:3, :, OWN - HALO : OWN, :]


def put_sends(send_left, send_right, t, lin, chosen):
    for k, i in enumerate(LEFTWARD):
        send_left[k, flat(t), :] = lin[0][i]
    for k, i in enumerate(RIGHTWARD):
        send_right[k, flat(t), :] = lin[1][i]
    send_left[8, flat(t), :] = chosen[0]
    send_right[8, flat(t), :] = chosen[1]


def start_rows(t, populations, shares, marks, table, outs):
    lin_out, flow_out, density_out, effective_out, share_out, _, send_left, send_right = outs
    half_low = jnp.broadcast_to(table[0:1, :], (8, DEPTH))
    half_high = jnp.broadcast_to(table[1:2, :], (8, DEPTH))
    lin, chosen = [], []
    for x in range(2):
        share = shares[x]
        spot = jnp.bitwise_and(marks[x], DEPTH - 1)
        wall = jnp.where(
            jnp.bitwise_and(marks[x], DEPTH) == 0,
            jnp.take_along_axis(half_low, spot, axis=1),
            jnp.take_along_axis(half_high, spot, axis=1),
        )
        total, momentum, linear = linear_part(populations[x], share, range(19))
        for i in range(19):
            lin_out[i, x, flat(t), :] = linear[i]
        for a in range(3):
            flow_out[a, x, flat(t), :] = momentum[a]
        density_out[x, flat(t), :] = total
        effective_out[x, flat(t), :] = jnp.where(share > 0, 1.0 - jnp.exp(-total), wall)
        share_out[x, flat(t), :] = share
        lin.append(linear)
        chosen.append(jnp.where(share > 0, total, wall))
    put_sends(send_left, send_right, t, lin, chosen)
    send_left[9, flat(t), :] = shares[0]
    send_right[9, flat(t), :] = shares[1]


def own_kernel(pops, small, *refs):
    outs, chooser, turned_label = refs[:8], refs[8], refs[9]
    outs[5][:, HALO : HALO + OWN, :] = small[2]

    def body(t):
        rows = rows_at(t, 0, -HALO)
        start_rows(
            t,
            [{i: pops[i, x, rows, :] for i in range(19)} for x in range(2)],
            [small[0, x, rows, :] for x in range(2)],
            [small[1, x, rows, :].astype(jnp.int32) for x in range(2)],
            small[3, 0, 0:2, :],
            outs,
        )

    each_chunk(body, HALO // 8, (HALO + OWN) // 8)

    marks = jnp.bitwise_and(small[1, 0].astype(jnp.int32), LABELS - 1).astype(jnp.float32)
    turned_label[...] = jnp.transpose(marks)
    quads = DEPTH // 4
    by_quad = turned_label[pl.ds(0, quads, stride=4), :]
    names = lax.broadcasted_iota(jnp.int32, (quads, LABELS), 1).astype(jnp.float32)
    for k in range(OWN // 2):
        column = jnp.broadcast_to(by_quad[:, 2 * k : 2 * k + 1], (quads, LABELS))
        chooser[quads * k : quads * (k + 1), :] = (column == names).astype(jnp.bfloat16)


def halo_kernel(small, below, above, *refs):
    outs, field, doubled = refs[8:16], refs[16], refs[17]
    for t, edge in ((0, below), (CHUNKS - 1, above)):
        outs[5][:, 8 * t : 8 * t + 8, :] = edge[21]
        start_rows(
            t,
            [{i: edge[i, x] for i in range(19)} for x in range(2)],
            [edge[19, x] for x in range(2)],
            [edge[20, x].astype(jnp.int32) for x in range(2)],
            small[3, 0, 0:2, :],
            outs,
        )
    flow, effective, send_left, send_right = outs[1], outs[3], outs[6], outs[7]

    def place(t):
        for x in range(2):
            value = effective[x, flat(t), :]
            field[x, tall(t), :] = value
            doubled[x, tall(t), :] = with_sides(value)

    each_chunk(place)
    each_chunk(functools.partial(send_flow, send_left, send_right, flow, field, doubled))


def step_kernel(is_first, *refs):
    if is_first:
        (lin, flow, density, effective, share, from_left, from_right,
         masks, field, speed, pull_out, lin_out, flow_out, density_out, effective_out, send_left, send_right,
         doubled, relaxed, turned, next_field, next_doubled) = refs
    else:
        (lin, flow, density, effective, share, target, masks, from_left, from_right,
         field, speed, pull_out, misfit_out, send_left, send_right,
         doubled, relaxed, turned) = refs

    def place(t):
        def put(p, x, s):
            field[p, tall(t), :] = x
            doubled[p, tall(t), :] = with_sides(x)
            if is_first:
                masks[0, p, tall(t), :] = s
                masks[1, p, tall(t), :] = rolled(s, 1)
                masks[2, p, tall(t), :] = rolled(s, -1)

        for x in range(2):
            put(2 + x, effective[x, flat(t), :], share[x, flat(t), :])
        for near, come in ((1, from_left), (4, from_right)):
            s = come[9, flat(t), :] if is_first else masks[0, near, tall(t), :]
            chosen = come[8, flat(t), :]
            put(near, jnp.where(s > 0, 1.0 - jnp.exp(-chosen), chosen), s)

    each_chunk(place)

    def collide(t):
        for p in range(1, 5):
            psi = field[p, tall(t), :]
            s = masks[0, p, tall(t), :]
            if p in (2, 3):
                pull = gradient_of(field, doubled, p, t)
                rho = density[p - 2, flat(t), :]
                mom = [flow[a, p - 2, flat(t), :] for a in range(3)]
                which = range(19)
                lin_at = {i: lin[i, p - 2, flat(t), :] for i in which}
                for a in range(3):
                    pull_out[a, p - 2, flat(t), :] = pull[a]
            else:
                pull = outer_gradient(field, doubled, p, 2 if p == 1 else 3, t)
                come = from_left if p == 1 else from_right
                rho = come[8, flat(t), :]
                mom = [come[5 + a, flat(t), :] for a in range(3)]
                which = RIGHTWARD if p == 1 else LEFTWARD
                lin_at = {i: come[k, flat(t), :] for k, i in enumerate(which)}
            push = psi * (PULL / SHEAR)
            full = [mom[a] + push * pull[a] for a in range(3)]
            inverse = 1.0 / rho
            u = [full[a] * inverse for a in range(3)]
            for a in range(3):
                speed[a, p - 1, flat(t), :] = u[a]
            part = balance_part(rho, full, u, s, which)
            for i in which:
                value = lin_at[i] + part[i]
                relaxed[i, p - 1, tall(t), :] = value
                if i in TURNED:
                    turned[TURNED.index(i), p - 1, tall(t), :] = rolled(value, VECTORS[i][2])

    each_chunk(collide)

    def streamed(x, rows):
        f = {0: relaxed[0, 1 + x, rows(0), :]}
        for i in range(1, 19):
            cx, cy, cz = VECTORS[i]
            if cz:
                source = turned[TURNED.index(i), 1 + x - cx, rows(-cy), :]
            else:
                source = relaxed[i, 1 + x - cx, rows(-cy), :]
            open_ = masks[cz % 3, 2 + x - cx, rows(-cy), :] > 0
            f[i] = jnp.where(open_, source, relaxed[OPPOSITE[i], 1 + x, rows(0), :])
        return f

    def stream(t):
        lin_sent, chosen_sent = [], []
        for x in range(2):
            s = share[x, flat(t), :]
            total, momentum, linear = linear_part(streamed(x, lambda dy: tall(t, dy)), s, range(19))
            held = effective[x, flat(t), :]
            eff = jnp.where(s > 0, 1.0 - jnp.exp(-total), held)
            for i in range(19):
                lin_out[i, x, flat(t), :] = linear[i]
            for a in range(3):
                flow_out[a, x, flat(t), :] = momentum[a]
            density_out[x, flat(t), :] = total
            effective_out[x, flat(t), :] = eff
            next_field[x, tall(t), :] = eff
            next_doubled[x, tall(t), :] = with_sides(eff)
            lin_sent.append(linear)
            chosen_sent.append(jnp.where(s > 0, total, held))
        put_sends(send_left, send_right, t, lin_sent, chosen_sent)

    def compare(t):
        for x, near, far in ((0, send_left, send_right), (1, send_right, send_left)):
            f = streamed(x, lambda dy: mid_tall(t, dy))
            s = share[x, mid(t), :]
            misfit = s * (add(*[f[i] for i in range(19)]) - target[x, mid(t), :])
            misfit_out[x, flat(t), :] = misfit
            near[0, flat(t), :] = misfit
            far[1, flat(t), :] = misfit
            far[2, flat(t), :] = s

    if is_first:
        each_chunk(stream)
        each_chunk(functools.partial(send_flow, send_left, send_right, flow_out, next_field, next_doubled))
    else:
        each_chunk(compare, 0, MID // 8)


def spread_of(pulled, pulled_doubled, p, rows):
    at = lambda a, dp, dy: pulled[a, p + dp, rows(dy), :]
    two = lambda a, dp, dy: pulled_doubled[a, p + dp, rows(dy), :]
    along_x = two(0, 1, 0) - two(0, -1, 0) + (at(0, 1, 1) + at(0, 1, -1)) - (at(0, -1, 1) + at(0, -1, -1))
    along_y = two(1, 0, 1) - two(1, 0, -1) + (at(1, 1, 1) + at(1, -1, 1)) - (at(1, 1, -1) + at(1, -1, -1))
    star = 2.0 * at(2, 0, 0) + at(2, 1, 0) + at(2, -1, 0) + at(2, 0, 1) + at(2, 0, -1)
    along_z = rolled(star, -1) - rolled(star, 1)
    return (along_x + along_y + along_z) * (-1.0 / 36.0)


def put_pulled(pulled, pulled_doubled, p, rows, psi, q):
    for a in range(3):
        s = (COUPLING / SHEAR) * psi * q[a]
        pulled[a, p, rows(0), :] = s
        if a < 2:
            pulled_doubled[a, p, rows(0), :] = with_sides(s)


def mask_ahead(masks, i, p, rows):
    cx, cy, cz = VECTORS[i]
    return masks[(-cz) % 3, p + cx, rows(cy), :] > 0


def middle(t):
    return lambda dy: mid_tall(t, dy)


def last_reverse_kernel(
    misfit, from_left, from_right, masks, field, speed, pull, early_speed,
    adjoint, turned, wall_out, send_left, send_right, part_left, part_right,
    ahead, far_masks, pulled, pulled_doubled, base,
):
    def place(t):
        rows = middle(t)
        for p in range(6):
            if p < 2:
                d = from_left[1 - p, flat(t), :]
            elif p < 4:
                d = misfit[p - 2, flat(t), :]
            else:
                d = from_right[p - 4, flat(t), :]
            ahead[0, p, rows(0), :] = d
            ahead[1, p, rows(0), :] = rolled(d, 1)
            ahead[2, p, rows(0), :] = rolled(d, -1)
        for k, source in enumerate((from_left, from_right)):
            s = source[2, flat(t), :]
            far_masks[0, k, rows(0), :] = s
            far_masks[1, k, rows(0), :] = rolled(s, 1)
            far_masks[2, k, rows(0), :] = rolled(s, -1)

    each_chunk(place, 0, MID // 8)

    def collide(t):
        rows = middle(t)
        for p in range(1, 5):
            s = masks[0, p, rows(0), :]
            here = ahead[0, p, rows(0), :]
            r = {0: here}
            for i in range(1, 19):
                cx, cy, cz = VECTORS[i]
                there = ahead[(-cz) % 3, p + cx, rows(cy), :]
                if p + cx in (0, 5):
                    open_ = far_masks[(-cz) % 3, (p + cx) // 5, rows(cy), :] > 0
                else:
                    open_ = mask_ahead(masks, i, p, rows)
                r[i] = s * jnp.where(open_, there, here)
            psi = field[p, rows(0), :]
            u = [speed[a, p - 1, mid(t), :] for a in range(3)]
            if p in (2, 3):
                rest, by_density, q = collide_adjoint(r, u)
                along = add(*[q[a] * pull[a, p - 2, mid(t), :] for a in range(3)])
                const = by_density + along * ((PULL / SHEAR) * (1.0 - psi))
                for i in range(19):
                    base[i, p - 2, flat(t), :] = rest[i] + const
            else:
                q = flow_adjoint(*dual(r), u)
            put_pulled(pulled, pulled_doubled, p - 1, rows, psi, q)

    each_chunk(collide, 0, MID // 8)

    def finish(t):
        rows = middle(t)
        for x in range(2):
            s = masks[0, 2 + x, rows(0), :]
            spread = spread_of(pulled, pulled_doubled, 1 + x, rows)
            wall_out[x, flat(t), :] = (1.0 - s) * spread
            more = s * spread * (1.0 - field[2 + x, rows(0), :])
            for i in range(19):
                value = base[i, x, flat(t), :] + more
                adjoint[i, x, rows(0), :] = value
                if i in TURNED:
                    turned[TURNED.index(i), x, rows(0), :] = rolled(value, -VECTORS[i][2])

    each_chunk(finish, 0, MID // 8)

    def part(t):
        rows = middle(t)
        for x, send, kept, sent, skipped in ((0, send_left, part_left, RIGHTWARD, -1), (1, send_right, part_right, LEFTWARD, 1)):
            p = 2 + x
            s = masks[0, p, rows(0), :]
            r = {}
            for i in range(19):
                if VECTORS[i][0] != skipped:
                    r[i] = adjoint_ahead(adjoint, turned, masks, i, x, rows)
            u = [early_speed[a, p - 1, mid(t), :] for a in range(3)]
            q = flow_adjoint(*dual(r), u)
            for a in range(3):
                send[5 + a, flat(t), :] = s * q[a]
                kept[a, flat(t), :] = s * q[a]
            for k, i in enumerate(sent):
                send[k, flat(t), :] = adjoint[i, x, rows(0), :]

    each_chunk(part, 0, MID // 8)


def adjoint_ahead(adjoint, turned, masks, i, x, rows):
    cx, cy, cz = VECTORS[i]
    if i == 0:
        return adjoint[0, x, rows(0), :]
    if cz:
        there = turned[TURNED.index(i), x + cx, rows(cy), :]
    else:
        there = adjoint[i, x + cx, rows(cy), :]
    return jnp.where(mask_ahead(masks, i, 2 + x, rows), there, adjoint[OPPOSITE[i], x, rows(0), :])


def place_sides(come, from_left, from_right, t):
    for side, source, which in ((0, from_left, LEFTWARD), (1, from_right, RIGHTWARD)):
        for k, i in enumerate(which):
            come[side, k, mid_tall(t), :] = rolled(source[k, flat(t), :], -VECTORS[i][2])


def arrived(come, adjoint, masks, i, x, rows):
    which = LEFTWARD if x == 0 else RIGHTWARD
    there = come[x, which.index(i), rows(VECTORS[i][1]), :]
    return jnp.where(mask_ahead(masks, i, 2 + x, rows), there, adjoint[OPPOSITE[i], x, rows(0), :])


def wall_kernel(
    adjoint, turned, wall, part_left, part_right, from_left, from_right, masks, field, speed, chooser,
    more_out, label_part,
    come, pulled, pulled_doubled, totals,
):
    each_chunk(functools.partial(place_sides, come, from_left, from_right), 0, MID // 8)

    def collide(t):
        rows = middle(t)
        for x, part, which in ((0, part_left, LEFTWARD), (1, part_right, RIGHTWARD)):
            p = 2 + x
            s = masks[0, p, rows(0), :]
            r = {i: arrived(come, adjoint, masks, i, x, rows) for i in which}
            u = [speed[a, p - 1, mid(t), :] for a in range(3)]
            rest = flow_adjoint(*dual(r), u)
            q = [part[a, flat(t), :] + s * rest[a] for a in range(3)]
            put_pulled(pulled, pulled_doubled, p - 1, rows, field[p, rows(0), :], q)
        for x, source, which in ((0, from_left, LEFTWARD), (1, from_right, RIGHTWARD)):
            p = 1 if x == 0 else 4
            s = masks[0, p, rows(0), :]
            r = {}
            for i in [OPPOSITE[j] for j in which]:
                cx, cy, cz = VECTORS[i]
                if cz:
                    there = turned[TURNED.index(i), x, rows(cy), :]
                else:
                    there = adjoint[i, x, rows(cy), :]
                here = source[which.index(OPPOSITE[i]), flat(t), :]
                r[i] = jnp.where(mask_ahead(masks, i, p, rows), there, here)
            u = [speed[a, p - 1, mid(t), :] for a in range(3)]
            rest = flow_adjoint(*dual(r), u)
            q = [source[5 + a, flat(t), :] + s * rest[a] for a in range(3)]
            put_pulled(pulled, pulled_doubled, p - 1, rows, field[p, rows(0), :], q)

    each_chunk(collide, 0, MID // 8)

    def finish(t):
        total = None
        for x in range(2):
            s = masks[0, 2 + x, tall(t), :]
            spread = spread_of(pulled, pulled_doubled, 1 + x, lambda dy: tall(t, dy))
            step_wall = wall[x, pl.ds(t * 8 - (ROWS - MID) // 2, 8), :]
            total = add(total, (1.0 - s) * spread + step_wall)
            more_out[x, rows_at(t, 0, -HALO), :] = s * spread * (1.0 - field[2 + x, tall(t), :])
        totals[rows_at(t, 0, -HALO), :] = total

    each_chunk(finish, HALO // 8, (HALO + OWN) // 8)

    blocks = (OWN // 2) * (DEPTH // 4)
    column = lax.broadcasted_iota(jnp.int32, (DEPTH, blocks), 1)
    quad = lax.broadcasted_iota(jnp.int32, (DEPTH, blocks), 0) // 4
    gather = (jnp.bitwise_and(column, DEPTH // 4 - 1) == quad).astype(jnp.bfloat16)
    by_block = exact_dot(totals[...], gather)
    pair = lax.broadcasted_iota(jnp.int32, (OWN, blocks), 0) // 2
    wanted = lax.broadcasted_iota(jnp.int32, (OWN, blocks), 1) // (DEPTH // 4)
    by_block = jnp.where(pair == wanted, by_block, 0.0)
    by_label = exact_dot(by_block, chooser[...])
    label_part[...] = jnp.sum(by_label, axis=0, keepdims=True)


def grad_kernel(
    adjoint, turned, more, from_left, from_right, masks, field, speed, pull,
    grad,
    come,
):
    each_chunk(functools.partial(place_sides, come, from_left, from_right), 0, MID // 8)

    def collide(t):
        rows = lambda dy: tall(t, dy)
        for x in range(2):
            p = 2 + x
            s = masks[0, p, tall(t), :]
            r = {}
            for i in range(19):
                if VECTORS[i][0] == 2 * x - 1:
                    r[i] = s * arrived(come, adjoint, masks, i, x, rows)
                else:
                    r[i] = s * adjoint_ahead(adjoint, turned, masks, i, x, rows)
            u = [speed[a, p - 1, flat(t), :] for a in range(3)]
            rest, by_density, q = collide_adjoint(r, u)
            along = add(*[q[a] * pull[a, x, flat(t), :] for a in range(3)])
            const = by_density + along * ((PULL / SHEAR) * (1.0 - field[p, tall(t), :]))
            const = const + more[x, rows_at(t, 0, -HALO), :]
            for i in range(19):
                grad[i, x, rows_at(t, 0, -HALO), :] = rest[i] + const

    each_chunk(collide, HALO // 8, (HALO + OWN) // 8)


def exact_dot(values, zero_one):
    high = values.astype(jnp.bfloat16)
    left = values - high.astype(jnp.float32)
    middle = left.astype(jnp.bfloat16)
    low = (left - middle.astype(jnp.float32)).astype(jnp.bfloat16)
    dot = lambda part: jnp.dot(part, zero_one, preferred_element_type=jnp.float32)
    return dot(high) + (dot(middle) + dot(low))


def call(kernel, args, outs, scratch, anywhere=0, grant=12, filled=0):
    whole = pl.BlockSpec(memory_space=pltpu.VMEM)
    there = pl.BlockSpec(memory_space=pl.ANY)
    size = sum(a.size * a.dtype.itemsize for a in args)
    return pl.pallas_call(
        kernel,
        out_shape=[s if hasattr(s, "dtype") else jax.ShapeDtypeStruct(s, jnp.float32) for s in outs],
        in_specs=[there] * anywhere + [whole] * (len(args) - anywhere),
        out_specs=[whole] * len(outs),
        scratch_shapes=scratch,
        input_output_aliases={len(args) - filled + k: k for k in range(filled)},
        compiler_params=pltpu.CompilerParams(vmem_limit_bytes=grant * 1024 * 1024),
        cost_estimate=pl.CostEstimate(flops=0, bytes_accessed=size, transcendentals=0),
    )(*args)


def ring(axis):
    count = lax.axis_size(axis)
    up = [(i, (i + 1) % count) for i in range(count)]
    return up, [(j, i) for i, j in up]


def both_ways(to_lower, to_upper, axis):
    up, down = ring(axis)
    from_lower = lax.ppermute(to_upper, axis, up)
    from_upper = lax.ppermute(to_lower, axis, down)
    return from_lower, from_upper


def per_device(populations, fluid, label, wall_wetting, target):
    vmem = lambda *shape: pltpu.VMEM(shape, jnp.float32)
    plane = (ROWS, DEPTH)
    two = (2, *plane)
    edge = (22, 2, HALO, DEPTH)
    low, high, small = call(
        edges_kernel,
        (populations, fluid, label, target, wall_wetting.reshape(2, DEPTH)),
        (edge, edge, (4, 2, OWN, DEPTH)),
        (
            pltpu.VMEM((2, 2, OWN, DEPTH), jnp.int32),
            vmem(2, DEPTH),
            pltpu.SemaphoreType.DMA((6,)),
        ),
        anywhere=5,
        grant=56,
    )
    below, above = both_ways(low, high, "gy")
    blocks = (OWN // 2) * (DEPTH // 4)
    started = ((19, *two), (3, *two), two, two, two, two, (10, *plane), (10, *plane))
    *own, chooser = call(
        own_kernel,
        (populations, small),
        (*started, jax.ShapeDtypeStruct((blocks, LABELS), jnp.bfloat16)),
        (vmem(DEPTH, OWN),),
    )
    beside = (vmem(2, TALL, DEPTH), vmem(2, TALL, DEPTH))
    lin, flow, density, effective, share, target_wide, to_left, to_right = call(
        halo_kernel, (small, below, above, *own), started, beside, filled=len(started)
    )
    from_left, from_right = both_ways(to_left, to_right, "gx")
    wide6 = (6, TALL, DEPTH)
    work = (vmem(*wide6), vmem(19, 4, TALL, DEPTH), vmem(10, 4, TALL, DEPTH))
    masks, field0, speed0, pull0, lin, flow, density, effective, to_left, to_right = call(
        functools.partial(step_kernel, True),
        (lin, flow, density, effective, share, from_left, from_right),
        (
            (3, *wide6), wide6, (3, 4, *plane), (3, *two),
            (19, *two), (3, *two), two, two, (9, *plane), (9, *plane),
        ),
        (*work, *beside),
    )
    from_left, from_right = both_ways(to_left, to_right, "gx")
    less = (MID, DEPTH)
    field1, speed1, pull1, misfit, to_left, to_right = call(
        functools.partial(step_kernel, False),
        (lin, flow, density, effective, share, target_wide, masks, from_left, from_right),
        (wide6, (3, 4, *plane), (3, *two), (2, *less), (3, *less), (3, *less)),
        work,
    )
    from_left, from_right = both_ways(to_left, to_right, "gx")
    pulled = (vmem(3, 4, TALL, DEPTH), vmem(2, 4, TALL, DEPTH))
    adjoint, turned, wall, to_left, to_right, part_left, part_right = call(
        last_reverse_kernel,
        (misfit, from_left, from_right, masks, field1, speed1, pull1, speed0),
        ((19, 2, TALL, DEPTH), (10, 2, TALL, DEPTH), (2, *less), (8, *less), (8, *less), (3, *less), (3, *less)),
        (vmem(3, *wide6), vmem(3, 2, TALL, DEPTH), *pulled, vmem(19, 2, *less)),
    )
    from_left, from_right = both_ways(to_left, to_right, "gx")
    come = vmem(2, 5, TALL, DEPTH)
    more, label_part = call(
        wall_kernel,
        (adjoint, turned, wall, part_left, part_right, from_left, from_right, masks, field0, speed0, chooser),
        ((2, OWN, DEPTH), (1, LABELS)),
        (come, *pulled, vmem(OWN, DEPTH)),
    )
    count = lax.axis_size("gy")
    wetting_grad = label_part
    for step in range(1, count):
        wetting_grad = wetting_grad + lax.ppermute(
            label_part, "gy", [(i, (i + step) % count) for i in range(count)]
        )
    (grad,) = call(
        grad_kernel,
        (adjoint, turned, more, from_left, from_right, masks, field0, speed0, pull0),
        (populations.shape,),
        (come,),
    )
    return (grad, wetting_grad.reshape(-1))


def solution(mesh):
    return jax.shard_map(
        per_device,
        mesh=mesh,
        in_specs=(
            P(None, "gx", "gy", None),
            P("gx", "gy", None),
            P("gx", "gy", None),
            P("gx"),
            P("gx", "gy", None),
        ),
        out_specs=(P(None, "gx", "gy", None), P("gx")),
        check_vma=False,
    )
```

```python
import functools

import jax
import jax.numpy as jnp
from jax import lax
from jax.experimental import pallas as pl
from jax.experimental.pallas import tpu as pltpu
from jax.sharding import PartitionSpec as P

HALO = 8
PAD = 8
OWN = 32
ROWS = OWN + 2 * HALO
TALL = ROWS + 2 * PAD
MID = OWN + HALO
DEPTH = 128
CHUNKS = ROWS // 8
LABELS = 256

VECTORS = (
    (0, 0, 0), (1, 0, 0), (-1, 0, 0), (0, 1, 0), (0, -1, 0), (0, 0, 1), (0, 0, -1),
    (1, 1, 0), (-1, -1, 0), (1, -1, 0), (-1, 1, 0), (1, 0, 1), (-1, 0, -1), (1, 0, -1), (-1, 0, 1),
    (0, 1, 1), (0, -1, -1), (0, 1, -1), (0, -1, 1),
)
OPPOSITE = (0, 2, 1, 4, 3, 6, 5, 8, 7, 10, 9, 12, 11, 14, 13, 16, 15, 18, 17)
INDEX = {v: i for i, v in enumerate(VECTORS)}
RIGHTWARD = tuple(i for i in range(19) if VECTORS[i][0] == 1)
LEFTWARD = tuple(i for i in range(19) if VECTORS[i][0] == -1)
TURNED = tuple(i for i in range(19) if VECTORS[i][2] != 0)
PLANES = ((0, 1), (1, 2), (0, 2))
COUPLING = 5.0
SHEAR = 1.2
BULK = 1.19
THIRD = 1.5
FOURTH = 1.4
TRACE = (BULK - SHEAR) / 3.0
PULL = COUPLING / 36.0


def axis_index_of(axis, sign):
    v = [0, 0, 0]
    v[axis] = sign
    return INDEX[tuple(v)]


def edge_index_of(a, b, sa, sb):
    v = [0, 0, 0]
    v[a], v[b] = sa, sb
    return INDEX[tuple(v)]


def add(*terms):
    total = None
    for term in terms:
        if term is not None:
            total = term if total is None else total + term
    return total


def sub(a, b):
    if b is None:
        return a
    return -b if a is None else a - b


def scale(c, a):
    return None if a is None else c * a


def mul(a, b):
    return None if a is None or b is None else a * b


def moments(f):
    fourth, mixed, third = {}, {}, {}
    for a, b in PLANES:
        pp, mm = f[edge_index_of(a, b, 1, 1)], f[edge_index_of(a, b, -1, -1)]
        pm, mp = f[edge_index_of(a, b, 1, -1)], f[edge_index_of(a, b, -1, 1)]
        even, odd, cross, skew = pp + mm, pp - mm, pm + mp, pm - mp
        fourth[a, b] = even + cross
        mixed[a, b] = even - cross
        third[a, b] = odd + skew
        third[b, a] = odd - skew
    first, diagonal, total = [], [], f[0]
    for a in range(3):
        b, c = [k for k in range(3) if k != a]
        plus, minus = f[axis_index_of(a, 1)], f[axis_index_of(a, -1)]
        both = plus + minus
        total = total + both
        diagonal.append(both + fourth[tuple(sorted((a, b)))] + fourth[tuple(sorted((a, c)))])
        first.append((plus - minus) + third[a, b] + third[a, c])
    total = total + fourth[0, 1] + fourth[1, 2] + fourth[0, 2]
    return total, first, diagonal, mixed, third, fourth


def from_moments(first, diagonal, mixed, third, fourth, which):
    out = {}
    for a, b in PLANES:
        even, cross = fourth[a, b] + mixed[a, b], fourth[a, b] - mixed[a, b]
        odd, skew = third[a, b] + third[b, a], third[a, b] - third[b, a]
        out[edge_index_of(a, b, 1, 1)] = even + odd
        out[edge_index_of(a, b, -1, -1)] = even - odd
        out[edge_index_of(a, b, 1, -1)] = cross + skew
        out[edge_index_of(a, b, -1, 1)] = cross - skew
    for a in range(3):
        b, c = [k for k in range(3) if k != a]
        even = diagonal[a] - 2.0 * (fourth[tuple(sorted((a, b)))] + fourth[tuple(sorted((a, c)))])
        odd = first[a] - 2.0 * (third[a, b] + third[a, c])
        out[axis_index_of(a, 1)] = even + odd
        out[axis_index_of(a, -1)] = even - odd
    out[0] = 4.0 * (fourth[0, 1] + fourth[1, 2] + fourth[0, 2]) - 2.0 * (diagonal[0] + diagonal[1] + diagonal[2])
    return {i: out[i] for i in which}


def linear_part(f, share, which):
    total, first, diagonal, mixed, third, fourth = moments(f)
    half, quarter = (0.5 * SHEAR) * share, (0.25 * SHEAR) * share
    trace = (0.5 * TRACE) * share * (diagonal[0] + diagonal[1] + diagonal[2])
    by_third, by_fourth = (0.25 * THIRD) * share, (0.25 * FOURTH) * share
    change = from_moments(
        [half * m for m in first],
        [half * m + trace for m in diagonal],
        {k: quarter * m for k, m in mixed.items()},
        {k: by_third * m for k, m in third.items()},
        {k: by_fourth * m for k, m in fourth.items()},
        which,
    )
    return total, first, {i: f[i] - change[i] for i in which}


def balance_part(density, flow, velocity, share, which):
    d = density * share
    m = [flow[a] * share for a in range(3)]
    square = [m[a] * velocity[a] for a in range(3)]
    whole = square[0] + square[1] + square[2]
    level = d * (SHEAR / 6.0 + 0.5 * TRACE) + whole * (0.5 * TRACE)
    diagonal = [(0.5 * SHEAR) * square[a] + level for a in range(3)]
    scaled = [(0.25 * SHEAR) * velocity[a] for a in range(3)]
    mixed = {(a, b): m[a] * scaled[b] for a, b in PLANES}
    part = [(THIRD / 12.0) * m[a] for a in range(3)]
    third = {}
    fourth = {}
    level = d * (FOURTH / 36.0) + whole * (FOURTH / 12.0)
    for a, b in PLANES:
        third[a, b], third[b, a] = part[a], part[b]
        fourth[a, b] = level - (FOURTH / 8.0) * square[3 - a - b]
    return from_moments([(0.5 * SHEAR) * m[a] for a in range(3)], diagonal, mixed, third, fourth, which)


def dual(r):
    get = lambda i: r.get(i)
    first, diagonal = [], []
    plus_of, minus_of = [], []
    for a in range(3):
        p, m = get(axis_index_of(a, 1)), get(axis_index_of(a, -1))
        even = scale(0.5, add(p, m))
        odd = scale(0.5, sub(p, m))
        plus_of.append(even)
        minus_of.append(odd)
        first.append(odd)
        diagonal.append(sub(even, get(0)))
    mixed, third, fourth = {}, {}, {}
    for a, b in PLANES:
        pp, mm = get(edge_index_of(a, b, 1, 1)), get(edge_index_of(a, b, -1, -1))
        pm, mp = get(edge_index_of(a, b, 1, -1)), get(edge_index_of(a, b, -1, 1))
        even, odd, cross, skew = add(pp, mm), sub(pp, mm), add(pm, mp), sub(pm, mp)
        fourth[a, b] = add(sub(sub(scale(0.25, add(even, cross)), plus_of[a]), plus_of[b]), get(0))
        mixed[a, b] = scale(0.25, sub(even, cross))
        third[a, b] = sub(scale(0.25, add(odd, skew)), minus_of[a])
        third[b, a] = sub(scale(0.25, sub(odd, skew)), minus_of[b])
    trace = scale(TRACE, add(*diagonal))
    return (
        [scale(SHEAR, m) for m in first],
        [add(scale(SHEAR, m), trace) for m in diagonal],
        {k: scale(SHEAR, m) for k, m in mixed.items()},
        {k: scale(THIRD, m) for k, m in third.items()},
        {k: scale(FOURTH, m) for k, m in fourth.items()},
    )


def flow_adjoint(first, diagonal, mixed, third, fourth, u):
    q = []
    for a in range(3):
        b, c = [k for k in range(3) if k != a]
        ab, ac, bc = tuple(sorted((a, b))), tuple(sorted((a, c))), tuple(sorted((b, c)))
        along = add(
            scale(2.0, diagonal[a]),
            scale(2.0 / 3.0, add(fourth[ab], fourth[ac])),
            scale(-1.0 / 3.0, fourth[bc]),
        )
        q.append(
            add(
                first[a],
                scale(1.0 / 3.0, add(third[a, b], third[a, c])),
                mul(u[a], along),
                mul(u[b], mixed[ab]),
                mul(u[c], mixed[ac]),
            )
        )
    return q


def collide_adjoint(r, u):
    t = dual(r)
    first, diagonal, mixed, third, fourth = t
    q = flow_adjoint(*t, u)
    square = [u[a] * u[a] for a in range(3)]
    by_density = None
    for a in range(3):
        b, c = [k for k in range(3) if k != a]
        by_density = add(
            by_density,
            u[a] * (first[a] + (1.0 / 3.0) * (third[a, b] + third[a, c]) - q[a]),
            diagonal[a] * (1.0 / 3.0 + square[a]),
        )
    for a, b in PLANES:
        c = 3 - a - b
        by_density = by_density + mixed[a, b] * (u[a] * u[b])
        by_density = by_density + fourth[a, b] * (
            1.0 / 9.0 + (square[a] + square[b]) * (1.0 / 3.0) - square[c] * (1.0 / 6.0)
        )
    drift = [q[a] - first[a] for a in range(3)]
    base = {0: r[0]}
    for a in range(3):
        base[axis_index_of(a, 1)] = r[axis_index_of(a, 1)] + (drift[a] - diagonal[a])
        base[axis_index_of(a, -1)] = r[axis_index_of(a, -1)] - (drift[a] + diagonal[a])
    for a, b in PLANES:
        along = drift[a] - third[a, b]
        across = drift[b] - third[b, a]
        even = diagonal[a] + diagonal[b] + fourth[a, b]
        same, cross = even + mixed[a, b], even - mixed[a, b]
        both, gap = along + across, along - across
        base[edge_index_of(a, b, 1, 1)] = r[edge_index_of(a, b, 1, 1)] + (both - same)
        base[edge_index_of(a, b, -1, -1)] = r[edge_index_of(a, b, -1, -1)] - (both + same)
        base[edge_index_of(a, b, 1, -1)] = r[edge_index_of(a, b, 1, -1)] + (gap - cross)
        base[edge_index_of(a, b, -1, 1)] = r[edge_index_of(a, b, -1, 1)] - (gap + cross)
    return base, by_density, q


def rolled(x, step):
    return x if step == 0 else pltpu.roll(x, step % DEPTH, 1)


def rows_at(t, shift, offset):
    if isinstance(t, int):
        return pl.ds(t * 8 + offset + shift, 8)
    if shift == 0:
        return pl.ds(pl.multiple_of(t * 8 + offset, 8), 8)
    return pl.ds(t * 8 + (offset + shift), 8)


def flat(t):
    return rows_at(t, 0, 0)


def tall(t, shift=0):
    return rows_at(t, shift, PAD)


def mid(t):
    return pl.ds(t * 8 + (ROWS - MID) // 2, 8)


def mid_tall(t, shift=0):
    return pl.ds(t * 8 + ((ROWS - MID) // 2 + PAD + shift), 8)


class Packed:
    def __init__(self, spans, limit):
        self.spans, self.shift, at = spans, [], spans[0][0]
        for low, high in spans:
            self.shift.append(at - low)
            at += high - low
        self.shape = (-(-(max(self.shift) + limit) // 8) * 8, DEPTH)

    def put(self, ref, k, t, value):
        low, high = max(8 * t, self.spans[k][0]), min(8 * t + 8, self.spans[k][1])
        if low < high:
            ref[self.shift[k] + low : self.shift[k] + high, :] = value[low - 8 * t : high - 8 * t, :]

    def get(self, ref, k, t):
        return ref[pl.ds(8 * t + self.shift[k], 8), :]


def step_spans(first, last, which, more):
    return [(first - VECTORS[i][1], last - VECTORS[i][1]) for i in which] + [(first - 1, last + 1)] * 3 + more


def adjoint_spans(which):
    first, last = (MID - OWN) // 2 - 1, (MID + OWN) // 2 + 1
    rows = [(first + min(VECTORS[i][1], 0), last + max(VECTORS[i][1], 0)) for i in which]
    return rows + [(first, last)] * 3


START = {
    which: Packed(step_spans(2, ROWS - 2, which, [(0, ROWS)] * 2), ROWS) for which in (LEFTWARD, RIGHTWARD)
}
SECOND = {
    which: Packed(step_spans(4, ROWS - 4, which, [(2, ROWS - 2)]), ROWS) for which in (LEFTWARD, RIGHTWARD)
}
BACK = {which: Packed(adjoint_spans(which), MID) for which in (LEFTWARD, RIGHTWARD)}


def each_chunk(body, first=0, last=CHUNKS, unroll=0):
    if unroll == 0:
        for t in range(first, last):
            body(t)
        return

    def step(t, carry):
        body(t)
        return carry

    lax.fori_loop(first, last, step, 0, unroll=unroll)


def gradient_of(field, doubled, p, t):
    at = lambda dp, dy: field[p + dp, tall(t, dy), :]
    rp, rm, lp, lm = at(1, 1), at(1, -1), at(-1, 1), at(-1, -1)
    along_x = doubled[p + 1, tall(t), :] - doubled[p - 1, tall(t), :] + (rp + rm) - (lp + lm)
    along_y = doubled[p, tall(t, 1), :] - doubled[p, tall(t, -1), :] + (rp + lp) - (rm + lm)
    star = 2.0 * at(0, 0) + at(1, 0) + at(-1, 0) + at(0, 1) + at(0, -1)
    return [along_x, along_y, rolled(star, -1) - rolled(star, 1)]


def with_sides(x):
    return 2.0 * x + rolled(x, 1) + rolled(x, -1)


def inner_gradient(field, doubled, here, inner, t):
    at = lambda x, dy: field[x, tall(t, dy), :]
    up, down = at(inner, 1), at(inner, -1)
    along_x = doubled[inner, tall(t), :] + (up + down)
    along_y = doubled[here, tall(t, 1), :] - doubled[here, tall(t, -1), :] + (up - down)
    star = 2.0 * at(here, 0) + at(inner, 0) + at(here, 1) + at(here, -1)
    return [along_x if inner > here else -along_x, along_y, rolled(star, -1) - rolled(star, 1)]


def outer_gradient(field, doubled, p, inner, t):
    at = lambda dy: field[inner, tall(t, dy), :]
    up, down, here = at(1), at(-1), at(0)
    along_x = doubled[inner, tall(t), :] + (up + down)
    return [along_x if inner > p else -along_x, up - down, rolled(here, -1) - rolled(here, 1)]


def send_flow(packed, send_left, send_right, flow, field, doubled, t):
    for send, which, here, inner in ((send_left, LEFTWARD, 0, 1), (send_right, RIGHTWARD, 1, 0)):
        push = field[here, tall(t), :] * (PULL / SHEAR)
        pull = inner_gradient(field, doubled, here, inner, t)
        for a in range(3):
            packed[which].put(send, 5 + a, t, flow[a, here, flat(t), :] + push * pull[a])


def edges_kernel(pops, fluid, label, target, table, low, high, small, whole, values, sems):
    copies = []

    def copy(source, goal):
        one = pltpu.make_async_copy(source, goal, sems.at[len(copies)])
        one.start()
        copies.append(one)

    copy(fluid, whole.at[0])
    copy(label, whole.at[1])
    copy(target, small.at[2])
    copy(table, values)
    copy(pops.at[:, :, pl.ds(0, HALO), :], low.at[pl.ds(0, 19)])
    copy(pops.at[:, :, pl.ds(OWN - HALO, HALO), :], high.at[pl.ds(0, 19)])
    for one in copies:
        one.wait()
    small[0] = whole[0].astype(jnp.float32)
    small[1] = whole[1].astype(jnp.float32)
    small[3, 0, 0:2, :] = values[...]
    low[19:22] = small[0:3, :, 0:HALO, :]
    high[19:22] = small[0:3, :, OWN - HALO : OWN, :]


def put_sends(packed, send_left, send_right, t, lin, chosen):
    for x, send, which in ((0, send_left, LEFTWARD), (1, send_right, RIGHTWARD)):
        for k, i in enumerate(which):
            packed[which].put(send, k, t, lin[x][i])
        packed[which].put(send, 8, t, chosen[x])


def start_rows(t, populations, shares, marks, table, outs):
    lin_out, flow_out, density_out, effective_out, share_out, _, send_left, send_right = outs
    half_low = jnp.broadcast_to(table[0:1, :], (8, DEPTH))
    half_high = jnp.broadcast_to(table[1:2, :], (8, DEPTH))
    lin, chosen = [], []
    for x in range(2):
        share = shares[x]
        spot = jnp.bitwise_and(marks[x], DEPTH - 1)
        wall = jnp.where(
            jnp.bitwise_and(marks[x], DEPTH) == 0,
            jnp.take_along_axis(half_low, spot, axis=1),
            jnp.take_along_axis(half_high, spot, axis=1),
        )
        total, momentum, linear = linear_part(populations[x], share, range(19))
        for i in range(19):
            lin_out[i, x, flat(t), :] = linear[i]
        for a in range(3):
            flow_out[a, x, flat(t), :] = momentum[a]
        density_out[x, flat(t), :] = total
        effective_out[x, flat(t), :] = jnp.where(share > 0, 1.0 - jnp.exp(-total), wall)
        share_out[x, flat(t), :] = share
        lin.append(linear)
        chosen.append(jnp.where(share > 0, total, wall))
    put_sends(START, send_left, send_right, t, lin, chosen)
    START[LEFTWARD].put(send_left, 9, t, shares[0])
    START[RIGHTWARD].put(send_right, 9, t, shares[1])


def own_kernel(pops, small, *refs):
    outs, chooser, turned_label = refs[:8], refs[8], refs[9]
    outs[5][:, HALO : HALO + OWN, :] = small[2]

    def body(t):
        rows = rows_at(t, 0, -HALO)
        start_rows(
            t,
            [{i: pops[i, x, rows, :] for i in range(19)} for x in range(2)],
            [small[0, x, rows, :] for x in range(2)],
            [small[1, x, rows, :].astype(jnp.int32) for x in range(2)],
            small[3, 0, 0:2, :],
            outs,
        )

    each_chunk(body, HALO // 8, (HALO + OWN) // 8)

    marks = jnp.bitwise_and(small[1, 0].astype(jnp.int32), LABELS - 1).astype(jnp.float32)
    turned_label[...] = jnp.transpose(marks)
    quads = DEPTH // 4
    by_quad = turned_label[pl.ds(0, quads, stride=4), :]
    names = lax.broadcasted_iota(jnp.int32, (quads, LABELS), 1).astype(jnp.float32)
    for k in range(OWN // 2):
        column = jnp.broadcast_to(by_quad[:, 2 * k : 2 * k + 1], (quads, LABELS))
        chooser[quads * k : quads * (k + 1), :] = (column == names).astype(jnp.bfloat16)


def halo_kernel(small, below, above, *refs):
    outs, field, doubled = refs[8:16], refs[16], refs[17]
    for t, edge in ((0, below), (CHUNKS - 1, above)):
        outs[5][:, 8 * t : 8 * t + 8, :] = edge[21]
        start_rows(
            t,
            [{i: edge[i, x] for i in range(19)} for x in range(2)],
            [edge[19, x] for x in range(2)],
            [edge[20, x].astype(jnp.int32) for x in range(2)],
            small[3, 0, 0:2, :],
            outs,
        )
    flow, effective, send_left, send_right = outs[1], outs[3], outs[6], outs[7]

    def place(t):
        for x in range(2):
            value = effective[x, flat(t), :]
            field[x, tall(t), :] = value
            doubled[x, tall(t), :] = with_sides(value)

    each_chunk(place)
    each_chunk(functools.partial(send_flow, START, send_left, send_right, flow, field, doubled))


def step_kernel(is_first, *refs):
    if is_first:
        (lin, flow, density, effective, share, from_left, from_right,
         masks, field, speed, pull_out, lin_out, flow_out, density_out, effective_out, send_left, send_right,
         doubled, relaxed, turned, next_field, next_doubled) = refs
    else:
        (lin, flow, density, effective, share, target, masks, from_left, from_right,
         field, speed, pull_out, misfit_out, send_left, send_right,
         doubled, relaxed, turned) = refs

    packed = START if is_first else SECOND

    def place(t):
        def put(p, x, s):
            field[p, tall(t), :] = x
            doubled[p, tall(t), :] = with_sides(x)
            if is_first:
                masks[0, p, tall(t), :] = s
                masks[1, p, tall(t), :] = rolled(s, 1)
                masks[2, p, tall(t), :] = rolled(s, -1)

        for x in range(2):
            put(2 + x, effective[x, flat(t), :], share[x, flat(t), :])
        for near, come, which in ((1, from_left, RIGHTWARD), (4, from_right, LEFTWARD)):
            s = packed[which].get(come, 9, t) if is_first else masks[0, near, tall(t), :]
            chosen = packed[which].get(come, 8, t)
            put(near, jnp.where(s > 0, 1.0 - jnp.exp(-chosen), chosen), s)

    each_chunk(place)

    def collide(t):
        for p in range(1, 5):
            psi = field[p, tall(t), :]
            s = masks[0, p, tall(t), :]
            if p in (2, 3):
                pull = gradient_of(field, doubled, p, t)
                rho = density[p - 2, flat(t), :]
                mom = [flow[a, p - 2, flat(t), :] for a in range(3)]
                which = range(19)
                lin_at = {i: lin[i, p - 2, flat(t), :] for i in which}
                for a in range(3):
                    pull_out[a, p - 2, flat(t), :] = pull[a]
            else:
                pull = outer_gradient(field, doubled, p, 2 if p == 1 else 3, t)
                come = from_left if p == 1 else from_right
                which = RIGHTWARD if p == 1 else LEFTWARD
                rho = packed[which].get(come, 8, t)
                mom = [packed[which].get(come, 5 + a, t) for a in range(3)]
                lin_at = {i: packed[which].get(come, k, t) for k, i in enumerate(which)}
            push = psi * (PULL / SHEAR)
            full = [mom[a] + push * pull[a] for a in range(3)]
            inverse = 1.0 / rho
            u = [full[a] * inverse for a in range(3)]
            for a in range(3):
                speed[a, p - 1, flat(t), :] = u[a]
            part = balance_part(rho, full, u, s, which)
            for i in which:
                value = lin_at[i] + part[i]
                relaxed[i, p - 1, tall(t), :] = value
                if i in TURNED:
                    turned[TURNED.index(i), p - 1, tall(t), :] = rolled(value, VECTORS[i][2])

    each_chunk(collide, unroll=3)

    def streamed(x, rows):
        f = {0: relaxed[0, 1 + x, rows(0), :]}
        for i in range(1, 19):
            cx, cy, cz = VECTORS[i]
            if cz:
                source = turned[TURNED.index(i), 1 + x - cx, rows(-cy), :]
            else:
                source = relaxed[i, 1 + x - cx, rows(-cy), :]
            open_ = masks[cz % 3, 2 + x - cx, rows(-cy), :] > 0
            f[i] = jnp.where(open_, source, relaxed[OPPOSITE[i], 1 + x, rows(0), :])
        return f

    def stream(t):
        lin_sent, chosen_sent = [], []
        for x in range(2):
            s = share[x, flat(t), :]
            total, momentum, linear = linear_part(streamed(x, lambda dy: tall(t, dy)), s, range(19))
            held = effective[x, flat(t), :]
            eff = jnp.where(s > 0, 1.0 - jnp.exp(-total), held)
            for i in range(19):
                lin_out[i, x, flat(t), :] = linear[i]
            for a in range(3):
                flow_out[a, x, flat(t), :] = momentum[a]
            density_out[x, flat(t), :] = total
            effective_out[x, flat(t), :] = eff
            next_field[x, tall(t), :] = eff
            next_doubled[x, tall(t), :] = with_sides(eff)
            lin_sent.append(linear)
            chosen_sent.append(jnp.where(s > 0, total, held))
        put_sends(SECOND, send_left, send_right, t, lin_sent, chosen_sent)

    def compare(t):
        for x, near, far in ((0, send_left, send_right), (1, send_right, send_left)):
            f = streamed(x, lambda dy: mid_tall(t, dy))
            s = share[x, mid(t), :]
            misfit = s * (add(*[f[i] for i in range(19)]) - target[x, mid(t), :])
            misfit_out[x, flat(t), :] = misfit
            near[0, flat(t), :] = misfit
            far[1, flat(t), :] = misfit
            far[2, flat(t), :] = s

    if is_first:
        each_chunk(stream)
        each_chunk(functools.partial(send_flow, SECOND, send_left, send_right, flow_out, next_field, next_doubled))
    else:
        each_chunk(compare, 0, MID // 8)


def spread_of(pulled, pulled_doubled, p, rows):
    at = lambda a, dp, dy: pulled[a, p + dp, rows(dy), :]
    two = lambda a, dp, dy: pulled_doubled[a, p + dp, rows(dy), :]
    along_x = two(0, 1, 0) - two(0, -1, 0) + (at(0, 1, 1) + at(0, 1, -1)) - (at(0, -1, 1) + at(0, -1, -1))
    along_y = two(1, 0, 1) - two(1, 0, -1) + (at(1, 1, 1) + at(1, -1, 1)) - (at(1, 1, -1) + at(1, -1, -1))
    star = 2.0 * at(2, 0, 0) + at(2, 1, 0) + at(2, -1, 0) + at(2, 0, 1) + at(2, 0, -1)
    along_z = rolled(star, -1) - rolled(star, 1)
    return (along_x + along_y + along_z) * (-1.0 / 36.0)


def put_pulled(pulled, pulled_doubled, p, rows, psi, q):
    for a in range(3):
        s = (COUPLING / SHEAR) * psi * q[a]
        pulled[a, p, rows(0), :] = s
        if a < 2:
            pulled_doubled[a, p, rows(0), :] = with_sides(s)


def mask_ahead(masks, i, p, rows):
    cx, cy, cz = VECTORS[i]
    return masks[(-cz) % 3, p + cx, rows(cy), :] > 0


def middle(t):
    return lambda dy: mid_tall(t, dy)


def last_reverse_kernel(
    misfit, from_left, from_right, masks, field, speed, pull, early_speed,
    adjoint, turned, wall_out, send_left, send_right, part_left, part_right,
    ahead, far_masks, pulled, pulled_doubled, base,
):
    def place(t):
        rows = middle(t)
        for p in range(6):
            if p < 2:
                d = from_left[1 - p, flat(t), :]
            elif p < 4:
                d = misfit[p - 2, flat(t), :]
            else:
                d = from_right[p - 4, flat(t), :]
            ahead[0, p, rows(0), :] = d
            ahead[1, p, rows(0), :] = rolled(d, 1)
            ahead[2, p, rows(0), :] = rolled(d, -1)
        for k, source in enumerate((from_left, from_right)):
            s = source[2, flat(t), :]
            far_masks[0, k, rows(0), :] = s
            far_masks[1, k, rows(0), :] = rolled(s, 1)
            far_masks[2, k, rows(0), :] = rolled(s, -1)

    each_chunk(place, 0, MID // 8)

    def collide(t):
        rows = middle(t)
        for p in range(1, 5):
            s = masks[0, p, rows(0), :]
            here = ahead[0, p, rows(0), :]
            r = {0: here}
            for i in range(1, 19):
                cx, cy, cz = VECTORS[i]
                there = ahead[(-cz) % 3, p + cx, rows(cy), :]
                if p + cx in (0, 5):
                    open_ = far_masks[(-cz) % 3, (p + cx) // 5, rows(cy), :] > 0
                else:
                    open_ = mask_ahead(masks, i, p, rows)
                r[i] = s * jnp.where(open_, there, here)
            psi = field[p, rows(0), :]
            u = [speed[a, p - 1, mid(t), :] for a in range(3)]
            if p in (2, 3):
                rest, by_density, q = collide_adjoint(r, u)
                along = add(*[q[a] * pull[a, p - 2, mid(t), :] for a in range(3)])
                const = by_density + along * ((PULL / SHEAR) * (1.0 - psi))
                for i in range(19):
                    base[i, p - 2, flat(t), :] = rest[i] + const
            else:
                q = flow_adjoint(*dual(r), u)
            put_pulled(pulled, pulled_doubled, p - 1, rows, psi, q)

    each_chunk(collide, 0, MID // 8)

    def finish(t):
        rows = middle(t)
        for x in range(2):
            s = masks[0, 2 + x, rows(0), :]
            spread = spread_of(pulled, pulled_doubled, 1 + x, rows)
            wall_out[x, flat(t), :] = (1.0 - s) * spread
            more = s * spread * (1.0 - field[2 + x, rows(0), :])
            for i in range(19):
                value = base[i, x, flat(t), :] + more
                adjoint[i, x, rows(0), :] = value
                if i in TURNED:
                    turned[TURNED.index(i), x, rows(0), :] = rolled(value, -VECTORS[i][2])

    each_chunk(finish, 0, MID // 8)

    def part(t):
        rows = middle(t)
        for x, send, kept, sent, skipped in ((0, send_left, part_left, RIGHTWARD, -1), (1, send_right, part_right, LEFTWARD, 1)):
            p = 2 + x
            s = masks[0, p, rows(0), :]
            r = {}
            for i in range(19):
                if VECTORS[i][0] != skipped:
                    r[i] = adjoint_ahead(adjoint, turned, masks, i, x, rows)
            u = [early_speed[a, p - 1, mid(t), :] for a in range(3)]
            q = flow_adjoint(*dual(r), u)
            for a in range(3):
                BACK[sent].put(send, 5 + a, t, s * q[a])
                kept[a, flat(t), :] = s * q[a]
            for k, i in enumerate(sent):
                BACK[sent].put(send, k, t, adjoint[i, x, rows(0), :])

    each_chunk(part, 0, MID // 8)


def adjoint_ahead(adjoint, turned, masks, i, x, rows):
    cx, cy, cz = VECTORS[i]
    if i == 0:
        return adjoint[0, x, rows(0), :]
    if cz:
        there = turned[TURNED.index(i), x + cx, rows(cy), :]
    else:
        there = adjoint[i, x + cx, rows(cy), :]
    return jnp.where(mask_ahead(masks, i, 2 + x, rows), there, adjoint[OPPOSITE[i], x, rows(0), :])


def place_sides(come, from_left, from_right, t):
    for side, source, which in ((0, from_left, LEFTWARD), (1, from_right, RIGHTWARD)):
        for k, i in enumerate(which):
            come[side, k, mid_tall(t), :] = rolled(BACK[which].get(source, k, t), -VECTORS[i][2])


def arrived(come, adjoint, masks, i, x, rows):
    which = LEFTWARD if x == 0 else RIGHTWARD
    there = come[x, which.index(i), rows(VECTORS[i][1]), :]
    return jnp.where(mask_ahead(masks, i, 2 + x, rows), there, adjoint[OPPOSITE[i], x, rows(0), :])


def wall_kernel(
    adjoint, turned, wall, part_left, part_right, from_left, from_right, masks, field, speed, chooser,
    more_out, label_part,
    come, pulled, pulled_doubled, totals,
):
    each_chunk(functools.partial(place_sides, come, from_left, from_right), 0, MID // 8)

    def collide(t):
        rows = middle(t)
        for x, part, which in ((0, part_left, LEFTWARD), (1, part_right, RIGHTWARD)):
            p = 2 + x
            s = masks[0, p, rows(0), :]
            r = {i: arrived(come, adjoint, masks, i, x, rows) for i in which}
            u = [speed[a, p - 1, mid(t), :] for a in range(3)]
            rest = flow_adjoint(*dual(r), u)
            q = [part[a, flat(t), :] + s * rest[a] for a in range(3)]
            put_pulled(pulled, pulled_doubled, p - 1, rows, field[p, rows(0), :], q)
        for x, source, which in ((0, from_left, LEFTWARD), (1, from_right, RIGHTWARD)):
            p = 1 if x == 0 else 4
            s = masks[0, p, rows(0), :]
            r = {}
            for i in [OPPOSITE[j] for j in which]:
                cx, cy, cz = VECTORS[i]
                if cz:
                    there = turned[TURNED.index(i), x, rows(cy), :]
                else:
                    there = adjoint[i, x, rows(cy), :]
                here = BACK[which].get(source, which.index(OPPOSITE[i]), t)
                r[i] = jnp.where(mask_ahead(masks, i, p, rows), there, here)
            u = [speed[a, p - 1, mid(t), :] for a in range(3)]
            rest = flow_adjoint(*dual(r), u)
            q = [BACK[which].get(source, 5 + a, t) + s * rest[a] for a in range(3)]
            put_pulled(pulled, pulled_doubled, p - 1, rows, field[p, rows(0), :], q)

    each_chunk(collide, 0, MID // 8)

    def finish(t):
        total = None
        for x in range(2):
            s = masks[0, 2 + x, tall(t), :]
            spread = spread_of(pulled, pulled_doubled, 1 + x, lambda dy: tall(t, dy))
            step_wall = wall[x, pl.ds(t * 8 - (ROWS - MID) // 2, 8), :]
            total = add(total, (1.0 - s) * spread + step_wall)
            more_out[x, rows_at(t, 0, -HALO), :] = s * spread * (1.0 - field[2 + x, tall(t), :])
        totals[rows_at(t, 0, -HALO), :] = total

    each_chunk(finish, HALO // 8, (HALO + OWN) // 8)

    blocks = (OWN // 2) * (DEPTH // 4)
    column = lax.broadcasted_iota(jnp.int32, (DEPTH, blocks), 1)
    quad = lax.broadcasted_iota(jnp.int32, (DEPTH, blocks), 0) // 4
    gather = (jnp.bitwise_and(column, DEPTH // 4 - 1) == quad).astype(jnp.bfloat16)
    by_block = exact_dot(totals[...], gather)
    pair = lax.broadcasted_iota(jnp.int32, (OWN, blocks), 0) // 2
    wanted = lax.broadcasted_iota(jnp.int32, (OWN, blocks), 1) // (DEPTH // 4)
    by_block = jnp.where(pair == wanted, by_block, 0.0)
    by_label = exact_dot(by_block, chooser[...])
    label_part[...] = jnp.sum(by_label, axis=0, keepdims=True)


def grad_kernel(
    adjoint, turned, more, from_left, from_right, masks, field, speed, pull,
    grad,
    come,
):
    each_chunk(functools.partial(place_sides, come, from_left, from_right), 0, MID // 8)

    def collide(t):
        rows = lambda dy: tall(t, dy)
        for x in range(2):
            p = 2 + x
            s = masks[0, p, tall(t), :]
            r = {}
            for i in range(19):
                if VECTORS[i][0] == 2 * x - 1:
                    r[i] = s * arrived(come, adjoint, masks, i, x, rows)
                else:
                    r[i] = s * adjoint_ahead(adjoint, turned, masks, i, x, rows)
            u = [speed[a, p - 1, flat(t), :] for a in range(3)]
            rest, by_density, q = collide_adjoint(r, u)
            along = add(*[q[a] * pull[a, x, flat(t), :] for a in range(3)])
            const = by_density + along * ((PULL / SHEAR) * (1.0 - field[p, tall(t), :]))
            const = const + more[x, rows_at(t, 0, -HALO), :]
            for i in range(19):
                grad[i, x, rows_at(t, 0, -HALO), :] = rest[i] + const

    each_chunk(collide, HALO // 8, (HALO + OWN) // 8)


def exact_dot(values, zero_one):
    high = values.astype(jnp.bfloat16)
    left = values - high.astype(jnp.float32)
    middle = left.astype(jnp.bfloat16)
    low = (left - middle.astype(jnp.float32)).astype(jnp.bfloat16)
    dot = lambda part: jnp.dot(part, zero_one, preferred_element_type=jnp.float32)
    return dot(high) + (dot(middle) + dot(low))


def call(kernel, args, outs, scratch, anywhere=0, grant=12, filled=0):
    whole = pl.BlockSpec(memory_space=pltpu.VMEM)
    there = pl.BlockSpec(memory_space=pl.ANY)
    size = sum(a.size * a.dtype.itemsize for a in args)
    return pl.pallas_call(
        kernel,
        out_shape=[s if hasattr(s, "dtype") else jax.ShapeDtypeStruct(s, jnp.float32) for s in outs],
        in_specs=[there] * anywhere + [whole] * (len(args) - anywhere),
        out_specs=[whole] * len(outs),
        scratch_shapes=scratch,
        input_output_aliases={len(args) - filled + k: k for k in range(filled)},
        compiler_params=pltpu.CompilerParams(vmem_limit_bytes=grant * 1024 * 1024),
        cost_estimate=pl.CostEstimate(flops=0, bytes_accessed=size, transcendentals=0),
    )(*args)


def ring(axis):
    count = lax.axis_size(axis)
    up = [(i, (i + 1) % count) for i in range(count)]
    return up, [(j, i) for i, j in up]


def both_ways(to_lower, to_upper, axis):
    up, down = ring(axis)
    from_lower = lax.ppermute(to_upper, axis, up)
    from_upper = lax.ppermute(to_lower, axis, down)
    return from_lower, from_upper


def per_device(populations, fluid, label, wall_wetting, target):
    vmem = lambda *shape: pltpu.VMEM(shape, jnp.float32)
    plane = (ROWS, DEPTH)
    two = (2, *plane)
    edge = (22, 2, HALO, DEPTH)
    low, high, small = call(
        edges_kernel,
        (populations, fluid, label, target, wall_wetting.reshape(2, DEPTH)),
        (edge, edge, (4, 2, OWN, DEPTH)),
        (
            pltpu.VMEM((2, 2, OWN, DEPTH), jnp.int32),
            vmem(2, DEPTH),
            pltpu.SemaphoreType.DMA((6,)),
        ),
        anywhere=5,
        grant=56,
    )
    below, above = both_ways(low, high, "gy")
    blocks = (OWN // 2) * (DEPTH // 4)
    started = ((19, *two), (3, *two), two, two, two, two, START[LEFTWARD].shape, START[RIGHTWARD].shape)
    *own, chooser = call(
        own_kernel,
        (populations, small),
        (*started, jax.ShapeDtypeStruct((blocks, LABELS), jnp.bfloat16)),
        (vmem(DEPTH, OWN),),
    )
    beside = (vmem(2, TALL, DEPTH), vmem(2, TALL, DEPTH))
    lin, flow, density, effective, share, target_wide, to_left, to_right = call(
        halo_kernel, (small, below, above, *own), started, beside, filled=len(started)
    )
    from_left, from_right = both_ways(to_left, to_right, "gx")
    wide6 = (6, TALL, DEPTH)
    work = (vmem(*wide6), vmem(19, 4, TALL, DEPTH), vmem(10, 4, TALL, DEPTH))
    masks, field0, speed0, pull0, lin, flow, density, effective, to_left, to_right = call(
        functools.partial(step_kernel, True),
        (lin, flow, density, effective, share, from_left, from_right),
        (
            (3, *wide6), wide6, (3, 4, *plane), (3, *two),
            (19, *two), (3, *two), two, two, SECOND[LEFTWARD].shape, SECOND[RIGHTWARD].shape,
        ),
        (*work, *beside),
    )
    from_left, from_right = both_ways(to_left, to_right, "gx")
    less = (MID, DEPTH)
    field1, speed1, pull1, misfit, to_left, to_right = call(
        functools.partial(step_kernel, False),
        (lin, flow, density, effective, share, target_wide, masks, from_left, from_right),
        (wide6, (3, 4, *plane), (3, *two), (2, *less), (3, *less), (3, *less)),
        work,
    )
    from_left, from_right = both_ways(to_left, to_right, "gx")
    pulled = (vmem(3, 4, TALL, DEPTH), vmem(2, 4, TALL, DEPTH))
    adjoint, turned, wall, to_left, to_right, part_left, part_right = call(
        last_reverse_kernel,
        (misfit, from_left, from_right, masks, field1, speed1, pull1, speed0),
        ((19, 2, TALL, DEPTH), (10, 2, TALL, DEPTH), (2, *less), BACK[RIGHTWARD].shape, BACK[LEFTWARD].shape, (3, *less), (3, *less)),
        (vmem(3, *wide6), vmem(3, 2, TALL, DEPTH), *pulled, vmem(19, 2, *less)),
    )
    from_left, from_right = both_ways(to_left, to_right, "gx")
    come = vmem(2, 5, TALL, DEPTH)
    more, label_part = call(
        wall_kernel,
        (adjoint, turned, wall, part_left, part_right, from_left, from_right, masks, field0, speed0, chooser),
        ((2, OWN, DEPTH), (1, LABELS)),
        (come, *pulled, vmem(OWN, DEPTH)),
    )
    count = lax.axis_size("gy")
    wetting_grad = label_part
    for step in range(1, count):
        wetting_grad = wetting_grad + lax.ppermute(
            label_part, "gy", [(i, (i + step) % count) for i in range(count)]
        )
    (grad,) = call(
        grad_kernel,
        (adjoint, turned, more, from_left, from_right, masks, field0, speed0, pull0),
        (populations.shape,),
        (come,),
    )
    return (grad, wetting_grad.reshape(-1))


def solution(mesh):
    return jax.shard_map(
        per_device,
        mesh=mesh,
        in_specs=(
            P(None, "gx", "gy", None),
            P("gx", "gy", None),
            P("gx", "gy", None),
            P("gx"),
            P("gx", "gy", None),
        ),
        out_specs=(P(None, "gx", "gy", None), P("gx")),
        check_vma=False,
    )
```

```python
import functools

import jax
import jax.numpy as jnp
from jax import lax
from jax.experimental import pallas as pl
from jax.experimental.pallas import tpu as pltpu
from jax.sharding import PartitionSpec as P

HALO = 8
PAD = 8
OWN = 32
ROWS = OWN + 2 * HALO
TALL = ROWS + 2 * PAD
MID = OWN + HALO
DEPTH = 128
CHUNKS = ROWS // 8
LABELS = 256

VECTORS = (
    (0, 0, 0), (1, 0, 0), (-1, 0, 0), (0, 1, 0), (0, -1, 0), (0, 0, 1), (0, 0, -1),
    (1, 1, 0), (-1, -1, 0), (1, -1, 0), (-1, 1, 0), (1, 0, 1), (-1, 0, -1), (1, 0, -1), (-1, 0, 1),
    (0, 1, 1), (0, -1, -1), (0, 1, -1), (0, -1, 1),
)
OPPOSITE = (0, 2, 1, 4, 3, 6, 5, 8, 7, 10, 9, 12, 11, 14, 13, 16, 15, 18, 17)
INDEX = {v: i for i, v in enumerate(VECTORS)}
RIGHTWARD = tuple(i for i in range(19) if VECTORS[i][0] == 1)
LEFTWARD = tuple(i for i in range(19) if VECTORS[i][0] == -1)
TURNED = tuple(i for i in range(19) if VECTORS[i][2] != 0)
PLANES = ((0, 1), (1, 2), (0, 2))
COUPLING = 5.0
SHEAR = 1.2
BULK = 1.19
THIRD = 1.5
FOURTH = 1.4
TRACE = (BULK - SHEAR) / 3.0
PULL = COUPLING / 36.0


def axis_index_of(axis, sign):
    v = [0, 0, 0]
    v[axis] = sign
    return INDEX[tuple(v)]


def edge_index_of(a, b, sa, sb):
    v = [0, 0, 0]
    v[a], v[b] = sa, sb
    return INDEX[tuple(v)]


def add(*terms):
    total = None
    for term in terms:
        if term is not None:
            total = term if total is None else total + term
    return total


def sub(a, b):
    if b is None:
        return a
    return -b if a is None else a - b


def scale(c, a):
    return None if a is None else c * a


def mul(a, b):
    return None if a is None or b is None else a * b


def moments(f):
    fourth, mixed, third = {}, {}, {}
    for a, b in PLANES:
        pp, mm = f[edge_index_of(a, b, 1, 1)], f[edge_index_of(a, b, -1, -1)]
        pm, mp = f[edge_index_of(a, b, 1, -1)], f[edge_index_of(a, b, -1, 1)]
        even, odd, cross, skew = pp + mm, pp - mm, pm + mp, pm - mp
        fourth[a, b] = even + cross
        mixed[a, b] = even - cross
        third[a, b] = odd + skew
        third[b, a] = odd - skew
    first, diagonal, total = [], [], f[0]
    for a in range(3):
        b, c = [k for k in range(3) if k != a]
        plus, minus = f[axis_index_of(a, 1)], f[axis_index_of(a, -1)]
        both = plus + minus
        total = total + both
        diagonal.append(both + fourth[tuple(sorted((a, b)))] + fourth[tuple(sorted((a, c)))])
        first.append((plus - minus) + third[a, b] + third[a, c])
    total = total + fourth[0, 1] + fourth[1, 2] + fourth[0, 2]
    return total, first, diagonal, mixed, third, fourth


def from_moments(first, diagonal, mixed, third, fourth, which):
    out = {}
    for a, b in PLANES:
        even, cross = fourth[a, b] + mixed[a, b], fourth[a, b] - mixed[a, b]
        odd, skew = third[a, b] + third[b, a], third[a, b] - third[b, a]
        out[edge_index_of(a, b, 1, 1)] = even + odd
        out[edge_index_of(a, b, -1, -1)] = even - odd
        out[edge_index_of(a, b, 1, -1)] = cross + skew
        out[edge_index_of(a, b, -1, 1)] = cross - skew
    for a in range(3):
        b, c = [k for k in range(3) if k != a]
        even = diagonal[a] - 2.0 * (fourth[tuple(sorted((a, b)))] + fourth[tuple(sorted((a, c)))])
        odd = first[a] - 2.0 * (third[a, b] + third[a, c])
        out[axis_index_of(a, 1)] = even + odd
        out[axis_index_of(a, -1)] = even - odd
    out[0] = 4.0 * (fourth[0, 1] + fourth[1, 2] + fourth[0, 2]) - 2.0 * (diagonal[0] + diagonal[1] + diagonal[2])
    return {i: out[i] for i in which}


def linear_part(f, share, which):
    total, first, diagonal, mixed, third, fourth = moments(f)
    half, quarter = (0.5 * SHEAR) * share, (0.25 * SHEAR) * share
    trace = (0.5 * TRACE) * share * (diagonal[0] + diagonal[1] + diagonal[2])
    by_third, by_fourth = (0.25 * THIRD) * share, (0.25 * FOURTH) * share
    change = from_moments(
        [half * m for m in first],
        [half * m + trace for m in diagonal],
        {k: quarter * m for k, m in mixed.items()},
        {k: by_third * m for k, m in third.items()},
        {k: by_fourth * m for k, m in fourth.items()},
        which,
    )
    return total, first, {i: f[i] - change[i] for i in which}


def balance_part(density, flow, velocity, share, which):
    d = density * share
    m = [flow[a] * share for a in range(3)]
    square = [m[a] * velocity[a] for a in range(3)]
    whole = square[0] + square[1] + square[2]
    level = d * (SHEAR / 6.0 + 0.5 * TRACE) + whole * (0.5 * TRACE)
    diagonal = [(0.5 * SHEAR) * square[a] + level for a in range(3)]
    scaled = [(0.25 * SHEAR) * velocity[a] for a in range(3)]
    mixed = {(a, b): m[a] * scaled[b] for a, b in PLANES}
    part = [(THIRD / 12.0) * m[a] for a in range(3)]
    third = {}
    fourth = {}
    level = d * (FOURTH / 36.0) + whole * (FOURTH / 12.0)
    for a, b in PLANES:
        third[a, b], third[b, a] = part[a], part[b]
        fourth[a, b] = level - (FOURTH / 8.0) * square[3 - a - b]
    return from_moments([(0.5 * SHEAR) * m[a] for a in range(3)], diagonal, mixed, third, fourth, which)


def dual(r):
    get = lambda i: r.get(i)
    first, diagonal = [], []
    plus_of, minus_of = [], []
    for a in range(3):
        p, m = get(axis_index_of(a, 1)), get(axis_index_of(a, -1))
        even = scale(0.5, add(p, m))
        odd = scale(0.5, sub(p, m))
        plus_of.append(even)
        minus_of.append(odd)
        first.append(odd)
        diagonal.append(sub(even, get(0)))
    mixed, third, fourth = {}, {}, {}
    for a, b in PLANES:
        pp, mm = get(edge_index_of(a, b, 1, 1)), get(edge_index_of(a, b, -1, -1))
        pm, mp = get(edge_index_of(a, b, 1, -1)), get(edge_index_of(a, b, -1, 1))
        even, odd, cross, skew = add(pp, mm), sub(pp, mm), add(pm, mp), sub(pm, mp)
        fourth[a, b] = add(sub(sub(scale(0.25, add(even, cross)), plus_of[a]), plus_of[b]), get(0))
        mixed[a, b] = scale(0.25, sub(even, cross))
        third[a, b] = sub(scale(0.25, add(odd, skew)), minus_of[a])
        third[b, a] = sub(scale(0.25, sub(odd, skew)), minus_of[b])
    trace = scale(TRACE, add(*diagonal))
    return (
        [scale(SHEAR, m) for m in first],
        [add(scale(SHEAR, m), trace) for m in diagonal],
        {k: scale(SHEAR, m) for k, m in mixed.items()},
        {k: scale(THIRD, m) for k, m in third.items()},
        {k: scale(FOURTH, m) for k, m in fourth.items()},
    )


def flow_adjoint(first, diagonal, mixed, third, fourth, u):
    q = []
    for a in range(3):
        b, c = [k for k in range(3) if k != a]
        ab, ac, bc = tuple(sorted((a, b))), tuple(sorted((a, c))), tuple(sorted((b, c)))
        along = add(
            scale(2.0, diagonal[a]),
            scale(2.0 / 3.0, add(fourth[ab], fourth[ac])),
            scale(-1.0 / 3.0, fourth[bc]),
        )
        q.append(
            add(
                first[a],
                scale(1.0 / 3.0, add(third[a, b], third[a, c])),
                mul(u[a], along),
                mul(u[b], mixed[ab]),
                mul(u[c], mixed[ac]),
            )
        )
    return q


def collide_adjoint(r, u):
    t = dual(r)
    first, diagonal, mixed, third, fourth = t
    q = flow_adjoint(*t, u)
    square = [u[a] * u[a] for a in range(3)]
    by_density = None
    for a in range(3):
        b, c = [k for k in range(3) if k != a]
        by_density = add(
            by_density,
            u[a] * (first[a] + (1.0 / 3.0) * (third[a, b] + third[a, c]) - q[a]),
            diagonal[a] * (1.0 / 3.0 + square[a]),
        )
    for a, b in PLANES:
        c = 3 - a - b
        by_density = by_density + mixed[a, b] * (u[a] * u[b])
        by_density = by_density + fourth[a, b] * (
            1.0 / 9.0 + (square[a] + square[b]) * (1.0 / 3.0) - square[c] * (1.0 / 6.0)
        )
    drift = [q[a] - first[a] for a in range(3)]
    base = {0: r[0]}
    for a in range(3):
        base[axis_index_of(a, 1)] = r[axis_index_of(a, 1)] + (drift[a] - diagonal[a])
        base[axis_index_of(a, -1)] = r[axis_index_of(a, -1)] - (drift[a] + diagonal[a])
    for a, b in PLANES:
        along = drift[a] - third[a, b]
        across = drift[b] - third[b, a]
        even = diagonal[a] + diagonal[b] + fourth[a, b]
        same, cross = even + mixed[a, b], even - mixed[a, b]
        both, gap = along + across, along - across
        base[edge_index_of(a, b, 1, 1)] = r[edge_index_of(a, b, 1, 1)] + (both - same)
        base[edge_index_of(a, b, -1, -1)] = r[edge_index_of(a, b, -1, -1)] - (both + same)
        base[edge_index_of(a, b, 1, -1)] = r[edge_index_of(a, b, 1, -1)] + (gap - cross)
        base[edge_index_of(a, b, -1, 1)] = r[edge_index_of(a, b, -1, 1)] - (gap + cross)
    return base, by_density, q


def rolled(x, step):
    return x if step == 0 else pltpu.roll(x, step % DEPTH, 1)


def rows_at(t, shift, offset):
    if isinstance(t, int):
        return pl.ds(t * 8 + offset + shift, 8)
    if shift == 0:
        return pl.ds(pl.multiple_of(t * 8 + offset, 8), 8)
    return pl.ds(t * 8 + (offset + shift), 8)


def flat(t):
    return rows_at(t, 0, 0)


def tall(t, shift=0):
    return rows_at(t, shift, PAD)


def mid(t):
    return pl.ds(t * 8 + (ROWS - MID) // 2, 8)


def mid_tall(t, shift=0):
    return pl.ds(t * 8 + ((ROWS - MID) // 2 + PAD + shift), 8)


class Packed:
    def __init__(self, spans, limit):
        self.spans, self.shift, at = spans, [], spans[0][0]
        for low, high in spans:
            self.shift.append(at - low)
            at += high - low
        self.shape = (-(-(max(self.shift) + limit) // 8) * 8, DEPTH)

    def put(self, ref, k, t, value):
        low, high = max(8 * t, self.spans[k][0]), min(8 * t + 8, self.spans[k][1])
        if low < high:
            ref[self.shift[k] + low : self.shift[k] + high, :] = value[low - 8 * t : high - 8 * t, :]

    def get(self, ref, k, t):
        return ref[pl.ds(8 * t + self.shift[k], 8), :]


def step_spans(first, last, which, more):
    return [(first - VECTORS[i][1], last - VECTORS[i][1]) for i in which] + [(first - 1, last + 1)] * 3 + more


def adjoint_spans(which):
    first, last = (MID - OWN) // 2 - 1, (MID + OWN) // 2 + 1
    rows = [(first + min(VECTORS[i][1], 0), last + max(VECTORS[i][1], 0)) for i in which]
    return rows + [(first, last)] * 3


START = {
    which: Packed(step_spans(2, ROWS - 2, which, [(0, ROWS)] * 2), ROWS) for which in (LEFTWARD, RIGHTWARD)
}
SECOND = {
    which: Packed(step_spans(4, ROWS - 4, which, [(2, ROWS - 2)]), ROWS) for which in (LEFTWARD, RIGHTWARD)
}
BACK = {which: Packed(adjoint_spans(which), MID) for which in (LEFTWARD, RIGHTWARD)}


def each_chunk(body, first=0, last=CHUNKS, unroll=0):
    if unroll == 0:
        for t in range(first, last):
            body(t)
        return

    def step(t, carry):
        body(t)
        return carry

    lax.fori_loop(first, last, step, 0, unroll=unroll)


def gradient_of(field, doubled, p, t):
    at = lambda dp, dy: field[p + dp, tall(t, dy), :]
    rp, rm, lp, lm = at(1, 1), at(1, -1), at(-1, 1), at(-1, -1)
    along_x = doubled[p + 1, tall(t), :] - doubled[p - 1, tall(t), :] + (rp + rm) - (lp + lm)
    along_y = doubled[p, tall(t, 1), :] - doubled[p, tall(t, -1), :] + (rp + lp) - (rm + lm)
    star = 2.0 * at(0, 0) + at(1, 0) + at(-1, 0) + at(0, 1) + at(0, -1)
    return [along_x, along_y, rolled(star, -1) - rolled(star, 1)]


def with_sides(x):
    return 2.0 * x + rolled(x, 1) + rolled(x, -1)


def inner_gradient(field, doubled, here, inner, t):
    at = lambda x, dy: field[x, tall(t, dy), :]
    up, down = at(inner, 1), at(inner, -1)
    along_x = doubled[inner, tall(t), :] + (up + down)
    along_y = doubled[here, tall(t, 1), :] - doubled[here, tall(t, -1), :] + (up - down)
    star = 2.0 * at(here, 0) + at(inner, 0) + at(here, 1) + at(here, -1)
    return [along_x if inner > here else -along_x, along_y, rolled(star, -1) - rolled(star, 1)]


def outer_gradient(field, doubled, p, inner, t):
    at = lambda dy: field[inner, tall(t, dy), :]
    up, down, here = at(1), at(-1), at(0)
    along_x = doubled[inner, tall(t), :] + (up + down)
    return [along_x if inner > p else -along_x, up - down, rolled(here, -1) - rolled(here, 1)]


def send_flow(packed, send_left, send_right, flow, field, doubled, t):
    for send, which, here, inner in ((send_left, LEFTWARD, 0, 1), (send_right, RIGHTWARD, 1, 0)):
        push = field[here, tall(t), :] * (PULL / SHEAR)
        pull = inner_gradient(field, doubled, here, inner, t)
        for a in range(3):
            packed[which].put(send, 5 + a, t, flow[a, here, flat(t), :] + push * pull[a])


def edges_kernel(pops, fluid, label, target, table, low, high, small, whole, values, sems):
    copies = []

    def copy(source, goal):
        one = pltpu.make_async_copy(source, goal, sems.at[len(copies)])
        one.start()
        copies.append(one)

    copy(fluid, whole.at[0])
    copy(label, whole.at[1])
    copy(target, small.at[2])
    copy(table, values)
    copy(pops.at[:, :, pl.ds(0, HALO), :], low.at[pl.ds(0, 19)])
    copy(pops.at[:, :, pl.ds(OWN - HALO, HALO), :], high.at[pl.ds(0, 19)])
    for one in copies:
        one.wait()
    small[0] = whole[0].astype(jnp.float32)
    small[1] = whole[1].astype(jnp.float32)
    small[3, 0, 0:2, :] = values[...]
    low[19:22] = small[0:3, :, 0:HALO, :]
    high[19:22] = small[0:3, :, OWN - HALO : OWN, :]


def put_sends(packed, send_left, send_right, t, lin, chosen):
    for x, send, which in ((0, send_left, LEFTWARD), (1, send_right, RIGHTWARD)):
        for k, i in enumerate(which):
            packed[which].put(send, k, t, lin[x][i])
        packed[which].put(send, 8, t, chosen[x])


def start_rows(t, populations, shares, marks, table, outs):
    lin_out, flow_out, density_out, effective_out, share_out, _, send_left, send_right = outs
    half_low = jnp.broadcast_to(table[0:1, :], (8, DEPTH))
    half_high = jnp.broadcast_to(table[1:2, :], (8, DEPTH))
    lin, chosen = [], []
    for x in range(2):
        share = shares[x]
        spot = jnp.bitwise_and(marks[x], DEPTH - 1)
        wall = jnp.where(
            jnp.bitwise_and(marks[x], DEPTH) == 0,
            jnp.take_along_axis(half_low, spot, axis=1),
            jnp.take_along_axis(half_high, spot, axis=1),
        )
        total, momentum, linear = linear_part(populations[x], share, range(19))
        for i in range(19):
            lin_out[i, x, flat(t), :] = linear[i]
        for a in range(3):
            flow_out[a, x, flat(t), :] = momentum[a]
        density_out[x, flat(t), :] = total
        effective_out[x, flat(t), :] = jnp.where(share > 0, 1.0 - jnp.exp(-total), wall)
        share_out[x, flat(t), :] = share
        lin.append(linear)
        chosen.append(jnp.where(share > 0, total, wall))
    put_sends(START, send_left, send_right, t, lin, chosen)
    START[LEFTWARD].put(send_left, 9, t, shares[0])
    START[RIGHTWARD].put(send_right, 9, t, shares[1])


def own_kernel(pops, small, *refs):
    outs, chooser, turned_label = refs[:8], refs[8], refs[9]
    outs[5][:, HALO : HALO + OWN, :] = small[2]

    def body(t):
        rows = rows_at(t, 0, -HALO)
        start_rows(
            t,
            [{i: pops[i, x, rows, :] for i in range(19)} for x in range(2)],
            [small[0, x, rows, :] for x in range(2)],
            [small[1, x, rows, :].astype(jnp.int32) for x in range(2)],
            small[3, 0, 0:2, :],
            outs,
        )

    each_chunk(body, HALO // 8, (HALO + OWN) // 8)

    marks = jnp.bitwise_and(small[1, 0].astype(jnp.int32), LABELS - 1).astype(jnp.float32)
    turned_label[...] = jnp.transpose(marks)
    quads = DEPTH // 4
    by_quad = turned_label[pl.ds(0, quads, stride=4), :]
    names = lax.broadcasted_iota(jnp.int32, (quads, LABELS), 1).astype(jnp.float32)
    for k in range(OWN // 2):
        column = jnp.broadcast_to(by_quad[:, 2 * k : 2 * k + 1], (quads, LABELS))
        chooser[quads * k : quads * (k + 1), :] = (column == names).astype(jnp.bfloat16)


def halo_kernel(small, below, above, *refs):
    outs, field, doubled = refs[8:16], refs[16], refs[17]
    for t, edge in ((0, below), (CHUNKS - 1, above)):
        outs[5][:, 8 * t : 8 * t + 8, :] = edge[21]
        start_rows(
            t,
            [{i: edge[i, x] for i in range(19)} for x in range(2)],
            [edge[19, x] for x in range(2)],
            [edge[20, x].astype(jnp.int32) for x in range(2)],
            small[3, 0, 0:2, :],
            outs,
        )
    flow, effective, send_left, send_right = outs[1], outs[3], outs[6], outs[7]

    def place(t):
        for x in range(2):
            value = effective[x, flat(t), :]
            field[x, tall(t), :] = value
            doubled[x, tall(t), :] = with_sides(value)

    each_chunk(place)
    each_chunk(functools.partial(send_flow, START, send_left, send_right, flow, field, doubled))


def put_field(field, doubled, p, t, value):
    field[p, tall(t), :] = value
    doubled[p, tall(t), :] = with_sides(value)


def put_masks(masks, p, t, share):
    masks[0, p, tall(t), :] = share
    masks[1, p, tall(t), :] = rolled(share, 1)
    masks[2, p, tall(t), :] = rolled(share, -1)


def first_flight_kernel(effective, share, masks, field, doubled):
    def body(t):
        for x in range(2):
            put_field(field, doubled, 2 + x, t, effective[x, flat(t), :])
            put_masks(masks, 2 + x, t, share[x, flat(t), :])

    each_chunk(body)


def second_flight_kernel(state, effective, share, field, doubled, lin):
    def body(t):
        for x in range(2):
            put_field(field, doubled, 2 + x, t, effective[x, flat(t), :])
            f = {i: state[i, x, flat(t), :] for i in range(19)}
            linear = linear_part(f, share[x, flat(t), :], range(19))[2]
            for i in range(19):
                lin[i, x, flat(t), :] = linear[i]

    each_chunk(body)


def step_kernel(is_first, *refs):
    if is_first:
        (lin, flow, density, effective, share, from_left, from_right, _, _, _,
         masks, field, doubled, speed, pull_out, state_out, flow_out, density_out, effective_out,
         send_left, send_right,
         relaxed, turned, next_field, next_doubled) = refs
    else:
        (lin, flow, density, share, target, masks, from_left, from_right, _, _,
         field, doubled, speed, pull_out, misfit_out, send_left, send_right,
         relaxed, turned) = refs

    packed = START if is_first else SECOND

    def place(t):
        for near, come, which in ((1, from_left, RIGHTWARD), (4, from_right, LEFTWARD)):
            s = packed[which].get(come, 9, t) if is_first else masks[0, near, tall(t), :]
            chosen = packed[which].get(come, 8, t)
            put_field(field, doubled, near, t, jnp.where(s > 0, 1.0 - jnp.exp(-chosen), chosen))
            if is_first:
                put_masks(masks, near, t, s)

    each_chunk(place)

    def collide(t):
        for p in range(1, 5):
            psi = field[p, tall(t), :]
            s = masks[0, p, tall(t), :]
            if p in (2, 3):
                pull = gradient_of(field, doubled, p, t)
                rho = density[p - 2, flat(t), :]
                mom = [flow[a, p - 2, flat(t), :] for a in range(3)]
                which = range(19)
                lin_at = {i: lin[i, p - 2, flat(t), :] for i in which}
                for a in range(3):
                    pull_out[a, p - 2, flat(t), :] = pull[a]
            else:
                pull = outer_gradient(field, doubled, p, 2 if p == 1 else 3, t)
                come = from_left if p == 1 else from_right
                which = RIGHTWARD if p == 1 else LEFTWARD
                rho = packed[which].get(come, 8, t)
                mom = [packed[which].get(come, 5 + a, t) for a in range(3)]
                lin_at = {i: packed[which].get(come, k, t) for k, i in enumerate(which)}
            push = psi * (PULL / SHEAR)
            full = [mom[a] + push * pull[a] for a in range(3)]
            inverse = 1.0 / rho
            u = [full[a] * inverse for a in range(3)]
            for a in range(3):
                speed[a, p - 1, flat(t), :] = u[a]
            part = balance_part(rho, full, u, s, which)
            for i in which:
                value = lin_at[i] + part[i]
                relaxed[i, p - 1, tall(t), :] = value
                if i in TURNED:
                    turned[TURNED.index(i), p - 1, tall(t), :] = rolled(value, VECTORS[i][2])

    each_chunk(collide, unroll=3)

    def streamed(x, rows):
        f = {0: relaxed[0, 1 + x, rows(0), :]}
        for i in range(1, 19):
            cx, cy, cz = VECTORS[i]
            if cz:
                source = turned[TURNED.index(i), 1 + x - cx, rows(-cy), :]
            else:
                source = relaxed[i, 1 + x - cx, rows(-cy), :]
            open_ = masks[cz % 3, 2 + x - cx, rows(-cy), :] > 0
            f[i] = jnp.where(open_, source, relaxed[OPPOSITE[i], 1 + x, rows(0), :])
        return f

    def stream(t):
        lin_sent, chosen_sent = [], []
        for x in range(2):
            s = share[x, flat(t), :]
            f = streamed(x, lambda dy: tall(t, dy))
            total, momentum, linear = linear_part(f, s, (LEFTWARD, RIGHTWARD)[x])
            held = effective[x, flat(t), :]
            eff = jnp.where(s > 0, 1.0 - jnp.exp(-total), held)
            for i in range(19):
                state_out[i, x, flat(t), :] = f[i]
            for a in range(3):
                flow_out[a, x, flat(t), :] = momentum[a]
            density_out[x, flat(t), :] = total
            effective_out[x, flat(t), :] = eff
            next_field[x, tall(t), :] = eff
            next_doubled[x, tall(t), :] = with_sides(eff)
            lin_sent.append(linear)
            chosen_sent.append(jnp.where(s > 0, total, held))
        put_sends(SECOND, send_left, send_right, t, lin_sent, chosen_sent)

    def compare(t):
        for x, near, far in ((0, send_left, send_right), (1, send_right, send_left)):
            f = streamed(x, lambda dy: mid_tall(t, dy))
            s = share[x, mid(t), :]
            misfit = s * (add(*[f[i] for i in range(19)]) - target[x, mid(t), :])
            misfit_out[x, flat(t), :] = misfit
            near[0, flat(t), :] = misfit
            far[1, flat(t), :] = misfit
            far[2, flat(t), :] = s

    if is_first:
        each_chunk(stream)
        each_chunk(functools.partial(send_flow, SECOND, send_left, send_right, flow_out, next_field, next_doubled))
    else:
        each_chunk(compare, 0, MID // 8)


def spread_of(pulled, pulled_doubled, p, rows):
    at = lambda a, dp, dy: pulled[a, p + dp, rows(dy), :]
    two = lambda a, dp, dy: pulled_doubled[a, p + dp, rows(dy), :]
    along_x = two(0, 1, 0) - two(0, -1, 0) + (at(0, 1, 1) + at(0, 1, -1)) - (at(0, -1, 1) + at(0, -1, -1))
    along_y = two(1, 0, 1) - two(1, 0, -1) + (at(1, 1, 1) + at(1, -1, 1)) - (at(1, 1, -1) + at(1, -1, -1))
    star = 2.0 * at(2, 0, 0) + at(2, 1, 0) + at(2, -1, 0) + at(2, 0, 1) + at(2, 0, -1)
    along_z = rolled(star, -1) - rolled(star, 1)
    return (along_x + along_y + along_z) * (-1.0 / 36.0)


def put_pulled(pulled, pulled_doubled, p, rows, psi, q):
    for a in range(3):
        s = (COUPLING / SHEAR) * psi * q[a]
        pulled[a, p, rows(0), :] = s
        if a < 2:
            pulled_doubled[a, p, rows(0), :] = with_sides(s)


def mask_ahead(masks, i, p, rows):
    cx, cy, cz = VECTORS[i]
    return masks[(-cz) % 3, p + cx, rows(cy), :] > 0


def middle(t):
    return lambda dy: mid_tall(t, dy)


def last_reverse_kernel(
    misfit, from_left, from_right, masks, field, speed, pull, early_speed,
    adjoint, turned, wall_out, send_left, send_right, part_left, part_right,
    ahead, far_masks, pulled, pulled_doubled, base,
):
    def place(t):
        rows = middle(t)
        for p in range(6):
            if p < 2:
                d = from_left[1 - p, flat(t), :]
            elif p < 4:
                d = misfit[p - 2, flat(t), :]
            else:
                d = from_right[p - 4, flat(t), :]
            ahead[0, p, rows(0), :] = d
            ahead[1, p, rows(0), :] = rolled(d, 1)
            ahead[2, p, rows(0), :] = rolled(d, -1)
        for k, source in enumerate((from_left, from_right)):
            s = source[2, flat(t), :]
            far_masks[0, k, rows(0), :] = s
            far_masks[1, k, rows(0), :] = rolled(s, 1)
            far_masks[2, k, rows(0), :] = rolled(s, -1)

    each_chunk(place, 0, MID // 8)

    def collide(t):
        rows = middle(t)
        for p in range(1, 5):
            s = masks[0, p, rows(0), :]
            here = ahead[0, p, rows(0), :]
            r = {0: here}
            for i in range(1, 19):
                cx, cy, cz = VECTORS[i]
                there = ahead[(-cz) % 3, p + cx, rows(cy), :]
                if p + cx in (0, 5):
                    open_ = far_masks[(-cz) % 3, (p + cx) // 5, rows(cy), :] > 0
                else:
                    open_ = mask_ahead(masks, i, p, rows)
                r[i] = s * jnp.where(open_, there, here)
            psi = field[p, rows(0), :]
            u = [speed[a, p - 1, mid(t), :] for a in range(3)]
            if p in (2, 3):
                rest, by_density, q = collide_adjoint(r, u)
                along = add(*[q[a] * pull[a, p - 2, mid(t), :] for a in range(3)])
                const = by_density + along * ((PULL / SHEAR) * (1.0 - psi))
                for i in range(19):
                    base[i, p - 2, flat(t), :] = rest[i] + const
            else:
                q = flow_adjoint(*dual(r), u)
            put_pulled(pulled, pulled_doubled, p - 1, rows, psi, q)

    each_chunk(collide, 0, MID // 8)

    def finish(t):
        rows = middle(t)
        for x in range(2):
            s = masks[0, 2 + x, rows(0), :]
            spread = spread_of(pulled, pulled_doubled, 1 + x, rows)
            wall_out[x, flat(t), :] = (1.0 - s) * spread
            more = s * spread * (1.0 - field[2 + x, rows(0), :])
            for i in range(19):
                value = base[i, x, flat(t), :] + more
                adjoint[i, x, rows(0), :] = value
                if i in TURNED:
                    turned[TURNED.index(i), x, rows(0), :] = rolled(value, -VECTORS[i][2])

    each_chunk(finish, 0, MID // 8)

    def part(t):
        rows = middle(t)
        for x, send, kept, sent, skipped in ((0, send_left, part_left, RIGHTWARD, -1), (1, send_right, part_right, LEFTWARD, 1)):
            p = 2 + x
            s = masks[0, p, rows(0), :]
            r = {}
            for i in range(19):
                if VECTORS[i][0] != skipped:
                    r[i] = adjoint_ahead(adjoint, turned, masks, i, x, rows)
            u = [early_speed[a, p - 1, mid(t), :] for a in range(3)]
            q = flow_adjoint(*dual(r), u)
            for a in range(3):
                BACK[sent].put(send, 5 + a, t, s * q[a])
                kept[a, flat(t), :] = s * q[a]
            for k, i in enumerate(sent):
                BACK[sent].put(send, k, t, adjoint[i, x, rows(0), :])

    each_chunk(part, 0, MID // 8)


def adjoint_ahead(adjoint, turned, masks, i, x, rows):
    cx, cy, cz = VECTORS[i]
    if i == 0:
        return adjoint[0, x, rows(0), :]
    if cz:
        there = turned[TURNED.index(i), x + cx, rows(cy), :]
    else:
        there = adjoint[i, x + cx, rows(cy), :]
    return jnp.where(mask_ahead(masks, i, 2 + x, rows), there, adjoint[OPPOSITE[i], x, rows(0), :])


def place_sides(come, from_left, from_right, t):
    for side, source, which in ((0, from_left, LEFTWARD), (1, from_right, RIGHTWARD)):
        for k, i in enumerate(which):
            come[side, k, mid_tall(t), :] = rolled(BACK[which].get(source, k, t), -VECTORS[i][2])


def arrived(come, adjoint, masks, i, x, rows):
    which = LEFTWARD if x == 0 else RIGHTWARD
    there = come[x, which.index(i), rows(VECTORS[i][1]), :]
    return jnp.where(mask_ahead(masks, i, 2 + x, rows), there, adjoint[OPPOSITE[i], x, rows(0), :])


def wall_kernel(
    adjoint, turned, wall, part_left, part_right, from_left, from_right, masks, field, speed, chooser,
    more_out, label_part,
    come, pulled, pulled_doubled, totals,
):
    each_chunk(functools.partial(place_sides, come, from_left, from_right), 0, MID // 8)

    def collide(t):
        rows = middle(t)
        for x, part, which in ((0, part_left, LEFTWARD), (1, part_right, RIGHTWARD)):
            p = 2 + x
            s = masks[0, p, rows(0), :]
            r = {i: arrived(come, adjoint, masks, i, x, rows) for i in which}
            u = [speed[a, p - 1, mid(t), :] for a in range(3)]
            rest = flow_adjoint(*dual(r), u)
            q = [part[a, flat(t), :] + s * rest[a] for a in range(3)]
            put_pulled(pulled, pulled_doubled, p - 1, rows, field[p, rows(0), :], q)
        for x, source, which in ((0, from_left, LEFTWARD), (1, from_right, RIGHTWARD)):
            p = 1 if x == 0 else 4
            s = masks[0, p, rows(0), :]
            r = {}
            for i in [OPPOSITE[j] for j in which]:
                cx, cy, cz = VECTORS[i]
                if cz:
                    there = turned[TURNED.index(i), x, rows(cy), :]
                else:
                    there = adjoint[i, x, rows(cy), :]
                here = BACK[which].get(source, which.index(OPPOSITE[i]), t)
                r[i] = jnp.where(mask_ahead(masks, i, p, rows), there, here)
            u = [speed[a, p - 1, mid(t), :] for a in range(3)]
            rest = flow_adjoint(*dual(r), u)
            q = [BACK[which].get(source, 5 + a, t) + s * rest[a] for a in range(3)]
            put_pulled(pulled, pulled_doubled, p - 1, rows, field[p, rows(0), :], q)

    each_chunk(collide, 0, MID // 8)

    def finish(t):
        total = None
        for x in range(2):
            s = masks[0, 2 + x, tall(t), :]
            spread = spread_of(pulled, pulled_doubled, 1 + x, lambda dy: tall(t, dy))
            step_wall = wall[x, pl.ds(t * 8 - (ROWS - MID) // 2, 8), :]
            total = add(total, (1.0 - s) * spread + step_wall)
            more_out[x, rows_at(t, 0, -HALO), :] = s * spread * (1.0 - field[2 + x, tall(t), :])
        totals[rows_at(t, 0, -HALO), :] = total

    each_chunk(finish, HALO // 8, (HALO + OWN) // 8)

    blocks = (OWN // 2) * (DEPTH // 4)
    column = lax.broadcasted_iota(jnp.int32, (DEPTH, blocks), 1)
    quad = lax.broadcasted_iota(jnp.int32, (DEPTH, blocks), 0) // 4
    gather = (jnp.bitwise_and(column, DEPTH // 4 - 1) == quad).astype(jnp.bfloat16)
    by_block = exact_dot(totals[...], gather)
    pair = lax.broadcasted_iota(jnp.int32, (OWN, blocks), 0) // 2
    wanted = lax.broadcasted_iota(jnp.int32, (OWN, blocks), 1) // (DEPTH // 4)
    by_block = jnp.where(pair == wanted, by_block, 0.0)
    by_label = exact_dot(by_block, chooser[...])
    label_part[...] = jnp.sum(by_label, axis=0, keepdims=True)


def grad_kernel(
    adjoint, turned, more, from_left, from_right, masks, field, speed, pull,
    grad,
    come,
):
    each_chunk(functools.partial(place_sides, come, from_left, from_right), 0, MID // 8)

    def collide(t):
        rows = lambda dy: tall(t, dy)
        for x in range(2):
            p = 2 + x
            s = masks[0, p, tall(t), :]
            r = {}
            for i in range(19):
                if VECTORS[i][0] == 2 * x - 1:
                    r[i] = s * arrived(come, adjoint, masks, i, x, rows)
                else:
                    r[i] = s * adjoint_ahead(adjoint, turned, masks, i, x, rows)
            u = [speed[a, p - 1, flat(t), :] for a in range(3)]
            rest, by_density, q = collide_adjoint(r, u)
            along = add(*[q[a] * pull[a, x, flat(t), :] for a in range(3)])
            const = by_density + along * ((PULL / SHEAR) * (1.0 - field[p, tall(t), :]))
            const = const + more[x, rows_at(t, 0, -HALO), :]
            for i in range(19):
                grad[i, x, rows_at(t, 0, -HALO), :] = rest[i] + const

    each_chunk(collide, HALO // 8, (HALO + OWN) // 8)


def exact_dot(values, zero_one):
    high = values.astype(jnp.bfloat16)
    left = values - high.astype(jnp.float32)
    middle = left.astype(jnp.bfloat16)
    low = (left - middle.astype(jnp.float32)).astype(jnp.bfloat16)
    dot = lambda part: jnp.dot(part, zero_one, preferred_element_type=jnp.float32)
    return dot(high) + (dot(middle) + dot(low))


def call(kernel, args, outs, scratch, anywhere=0, grant=12, filled=0):
    whole = pl.BlockSpec(memory_space=pltpu.VMEM)
    there = pl.BlockSpec(memory_space=pl.ANY)
    size = sum(a.size * a.dtype.itemsize for a in args)
    return pl.pallas_call(
        kernel,
        out_shape=[s if hasattr(s, "dtype") else jax.ShapeDtypeStruct(s, jnp.float32) for s in outs],
        in_specs=[there] * anywhere + [whole] * (len(args) - anywhere),
        out_specs=[whole] * len(outs),
        scratch_shapes=scratch,
        input_output_aliases={len(args) - filled + k: k for k in range(filled)},
        compiler_params=pltpu.CompilerParams(vmem_limit_bytes=grant * 1024 * 1024),
        cost_estimate=pl.CostEstimate(flops=0, bytes_accessed=size, transcendentals=0),
    )(*args)


def ring(axis):
    count = lax.axis_size(axis)
    up = [(i, (i + 1) % count) for i in range(count)]
    return up, [(j, i) for i, j in up]


def both_ways(to_lower, to_upper, axis):
    up, down = ring(axis)
    from_lower = lax.ppermute(to_upper, axis, up)
    from_upper = lax.ppermute(to_lower, axis, down)
    return from_lower, from_upper


def per_device(populations, fluid, label, wall_wetting, target):
    vmem = lambda *shape: pltpu.VMEM(shape, jnp.float32)
    plane = (ROWS, DEPTH)
    two = (2, *plane)
    edge = (22, 2, HALO, DEPTH)
    low, high, small = call(
        edges_kernel,
        (populations, fluid, label, target, wall_wetting.reshape(2, DEPTH)),
        (edge, edge, (4, 2, OWN, DEPTH)),
        (
            pltpu.VMEM((2, 2, OWN, DEPTH), jnp.int32),
            vmem(2, DEPTH),
            pltpu.SemaphoreType.DMA((6,)),
        ),
        anywhere=5,
        grant=56,
    )
    below, above = both_ways(low, high, "gy")
    blocks = (OWN // 2) * (DEPTH // 4)
    started = ((19, *two), (3, *two), two, two, two, two, START[LEFTWARD].shape, START[RIGHTWARD].shape)
    *own, chooser = call(
        own_kernel,
        (populations, small),
        (*started, jax.ShapeDtypeStruct((blocks, LABELS), jnp.bfloat16)),
        (vmem(DEPTH, OWN),),
    )
    beside = (vmem(2, TALL, DEPTH), vmem(2, TALL, DEPTH))
    lin, flow, density, effective, share, target_wide, to_left, to_right = call(
        halo_kernel, (small, below, above, *own), started, beside, filled=len(started)
    )
    from_left, from_right = both_ways(to_left, to_right, "gx")
    wide6 = (6, TALL, DEPTH)
    work = (vmem(19, 4, TALL, DEPTH), vmem(10, 4, TALL, DEPTH))
    begun = call(first_flight_kernel, (effective, share), ((3, *wide6), wide6, wide6), ())
    masks, field0, _, speed0, pull0, state, flow, density, effective, to_left, to_right = call(
        functools.partial(step_kernel, True),
        (lin, flow, density, effective, share, from_left, from_right, *begun),
        (
            (3, *wide6), wide6, wide6, (3, 4, *plane), (3, *two),
            (19, *two), (3, *two), two, two, SECOND[LEFTWARD].shape, SECOND[RIGHTWARD].shape,
        ),
        (*work, *beside),
        filled=3,
    )
    from_left, from_right = both_ways(to_left, to_right, "gx")
    less = (MID, DEPTH)
    field1, doubled, lin = call(
        second_flight_kernel, (state, effective, share), (wide6, wide6, (19, *two)), ()
    )
    field1, _, speed1, pull1, misfit, to_left, to_right = call(
        functools.partial(step_kernel, False),
        (lin, flow, density, share, target_wide, masks, from_left, from_right, field1, doubled),
        (wide6, wide6, (3, 4, *plane), (3, *two), (2, *less), (3, *less), (3, *less)),
        work,
        filled=2,
    )
    from_left, from_right = both_ways(to_left, to_right, "gx")
    pulled = (vmem(3, 4, TALL, DEPTH), vmem(2, 4, TALL, DEPTH))
    adjoint, turned, wall, to_left, to_right, part_left, part_right = call(
        last_reverse_kernel,
        (misfit, from_left, from_right, masks, field1, speed1, pull1, speed0),
        ((19, 2, TALL, DEPTH), (10, 2, TALL, DEPTH), (2, *less), BACK[RIGHTWARD].shape, BACK[LEFTWARD].shape, (3, *less), (3, *less)),
        (vmem(3, *wide6), vmem(3, 2, TALL, DEPTH), *pulled, vmem(19, 2, *less)),
    )
    from_left, from_right = both_ways(to_left, to_right, "gx")
    come = vmem(2, 5, TALL, DEPTH)
    more, label_part = call(
        wall_kernel,
        (adjoint, turned, wall, part_left, part_right, from_left, from_right, masks, field0, speed0, chooser),
        ((2, OWN, DEPTH), (1, LABELS)),
        (come, *pulled, vmem(OWN, DEPTH)),
    )
    count = lax.axis_size("gy")
    wetting_grad = label_part
    for step in range(1, count):
        wetting_grad = wetting_grad + lax.ppermute(
            label_part, "gy", [(i, (i + step) % count) for i in range(count)]
        )
    (grad,) = call(
        grad_kernel,
        (adjoint, turned, more, from_left, from_right, masks, field0, speed0, pull0),
        (populations.shape,),
        (come,),
    )
    return (grad, wetting_grad.reshape(-1))


def solution(mesh):
    return jax.shard_map(
        per_device,
        mesh=mesh,
        in_specs=(
            P(None, "gx", "gy", None),
            P("gx", "gy", None),
            P("gx", "gy", None),
            P("gx"),
            P("gx", "gy", None),
        ),
        out_specs=(P(None, "gx", "gy", None), P("gx")),
        check_vma=False,
    )
```

```python
import functools

import jax
import jax.numpy as jnp
from jax import lax
from jax.experimental import pallas as pl
from jax.experimental.pallas import tpu as pltpu
from jax.sharding import PartitionSpec as P

HALO = 8
PAD = 8
OWN = 32
ROWS = OWN + 2 * HALO
TALL = ROWS + 2 * PAD
MID = OWN + HALO
DEPTH = 128
CHUNKS = ROWS // 8
LABELS = 256

VECTORS = (
    (0, 0, 0), (1, 0, 0), (-1, 0, 0), (0, 1, 0), (0, -1, 0), (0, 0, 1), (0, 0, -1),
    (1, 1, 0), (-1, -1, 0), (1, -1, 0), (-1, 1, 0), (1, 0, 1), (-1, 0, -1), (1, 0, -1), (-1, 0, 1),
    (0, 1, 1), (0, -1, -1), (0, 1, -1), (0, -1, 1),
)
OPPOSITE = (0, 2, 1, 4, 3, 6, 5, 8, 7, 10, 9, 12, 11, 14, 13, 16, 15, 18, 17)
INDEX = {v: i for i, v in enumerate(VECTORS)}
RIGHTWARD = tuple(i for i in range(19) if VECTORS[i][0] == 1)
LEFTWARD = tuple(i for i in range(19) if VECTORS[i][0] == -1)
TURNED = tuple(i for i in range(19) if VECTORS[i][2] != 0)
PLANES = ((0, 1), (1, 2), (0, 2))
COUPLING = 5.0
SHEAR = 1.2
BULK = 1.19
THIRD = 1.5
FOURTH = 1.4
TRACE = (BULK - SHEAR) / 3.0
PULL = COUPLING / 36.0


def axis_index_of(axis, sign):
    v = [0, 0, 0]
    v[axis] = sign
    return INDEX[tuple(v)]


def edge_index_of(a, b, sa, sb):
    v = [0, 0, 0]
    v[a], v[b] = sa, sb
    return INDEX[tuple(v)]


def add(*terms):
    total = None
    for term in terms:
        if term is not None:
            total = term if total is None else total + term
    return total


def sub(a, b):
    if b is None:
        return a
    return -b if a is None else a - b


def scale(c, a):
    return None if a is None else c * a


def mul(a, b):
    return None if a is None or b is None else a * b


def moments(f):
    fourth, mixed, third = {}, {}, {}
    for a, b in PLANES:
        pp, mm = f[edge_index_of(a, b, 1, 1)], f[edge_index_of(a, b, -1, -1)]
        pm, mp = f[edge_index_of(a, b, 1, -1)], f[edge_index_of(a, b, -1, 1)]
        even, odd, cross, skew = pp + mm, pp - mm, pm + mp, pm - mp
        fourth[a, b] = even + cross
        mixed[a, b] = even - cross
        third[a, b] = odd + skew
        third[b, a] = odd - skew
    first, diagonal, total = [], [], f[0]
    for a in range(3):
        b, c = [k for k in range(3) if k != a]
        plus, minus = f[axis_index_of(a, 1)], f[axis_index_of(a, -1)]
        both = plus + minus
        total = total + both
        diagonal.append(both + fourth[tuple(sorted((a, b)))] + fourth[tuple(sorted((a, c)))])
        first.append((plus - minus) + third[a, b] + third[a, c])
    total = total + fourth[0, 1] + fourth[1, 2] + fourth[0, 2]
    return total, first, diagonal, mixed, third, fourth


def from_moments(first, diagonal, mixed, third, fourth, which):
    out = {}
    for a, b in PLANES:
        even, cross = fourth[a, b] + mixed[a, b], fourth[a, b] - mixed[a, b]
        odd, skew = third[a, b] + third[b, a], third[a, b] - third[b, a]
        out[edge_index_of(a, b, 1, 1)] = even + odd
        out[edge_index_of(a, b, -1, -1)] = even - odd
        out[edge_index_of(a, b, 1, -1)] = cross + skew
        out[edge_index_of(a, b, -1, 1)] = cross - skew
    for a in range(3):
        b, c = [k for k in range(3) if k != a]
        even = diagonal[a] - 2.0 * (fourth[tuple(sorted((a, b)))] + fourth[tuple(sorted((a, c)))])
        odd = first[a] - 2.0 * (third[a, b] + third[a, c])
        out[axis_index_of(a, 1)] = even + odd
        out[axis_index_of(a, -1)] = even - odd
    out[0] = 4.0 * (fourth[0, 1] + fourth[1, 2] + fourth[0, 2]) - 2.0 * (diagonal[0] + diagonal[1] + diagonal[2])
    return {i: out[i] for i in which}


def linear_part(f, share, which):
    total, first, diagonal, mixed, third, fourth = moments(f)
    half, quarter = (0.5 * SHEAR) * share, (0.25 * SHEAR) * share
    trace = (0.5 * TRACE) * share * (diagonal[0] + diagonal[1] + diagonal[2])
    by_third, by_fourth = (0.25 * THIRD) * share, (0.25 * FOURTH) * share
    change = from_moments(
        [half * m for m in first],
        [half * m + trace for m in diagonal],
        {k: quarter * m for k, m in mixed.items()},
        {k: by_third * m for k, m in third.items()},
        {k: by_fourth * m for k, m in fourth.items()},
        which,
    )
    return total, first, {i: f[i] - change[i] for i in which}


def balance_part(density, flow, velocity, share, which):
    d = density * share
    m = [flow[a] * share for a in range(3)]
    square = [m[a] * velocity[a] for a in range(3)]
    whole = square[0] + square[1] + square[2]
    level = d * (SHEAR / 6.0 + 0.5 * TRACE) + whole * (0.5 * TRACE)
    diagonal = [(0.5 * SHEAR) * square[a] + level for a in range(3)]
    scaled = [(0.25 * SHEAR) * velocity[a] for a in range(3)]
    mixed = {(a, b): m[a] * scaled[b] for a, b in PLANES}
    part = [(THIRD / 12.0) * m[a] for a in range(3)]
    third = {}
    fourth = {}
    level = d * (FOURTH / 36.0) + whole * (FOURTH / 12.0)
    for a, b in PLANES:
        third[a, b], third[b, a] = part[a], part[b]
        fourth[a, b] = level - (FOURTH / 8.0) * square[3 - a - b]
    return from_moments([(0.5 * SHEAR) * m[a] for a in range(3)], diagonal, mixed, third, fourth, which)


def dual(r):
    rest = r.get(0)
    even_of, odd_of = [], []
    for a in range(3):
        plus, minus = r.get(axis_index_of(a, 1)), r.get(axis_index_of(a, -1))
        even_of.append(add(plus, minus))
        odd_of.append(sub(plus, minus))
    trace = add(scale(0.5 * TRACE, add(*even_of)), scale(-3.0 * TRACE - SHEAR, rest))
    first = [scale(0.5 * SHEAR, odd) for odd in odd_of]
    diagonal = [add(scale(0.5 * SHEAR, even), trace) for even in even_of]
    even_part = [scale(0.5 * FOURTH, even) for even in even_of]
    odd_part = [scale(0.5 * THIRD, odd) for odd in odd_of]
    rest_part = scale(FOURTH, rest)
    mixed, third, fourth = {}, {}, {}
    for a, b in PLANES:
        pp, mm = r.get(edge_index_of(a, b, 1, 1)), r.get(edge_index_of(a, b, -1, -1))
        pm, mp = r.get(edge_index_of(a, b, 1, -1)), r.get(edge_index_of(a, b, -1, 1))
        even, odd, cross, skew = add(pp, mm), sub(pp, mm), add(pm, mp), sub(pm, mp)
        whole = scale(0.25 * FOURTH, add(even, cross))
        fourth[a, b] = add(sub(sub(whole, even_part[a]), even_part[b]), rest_part)
        mixed[a, b] = scale(0.25 * SHEAR, sub(even, cross))
        third[a, b] = sub(scale(0.25 * THIRD, add(odd, skew)), odd_part[a])
        third[b, a] = sub(scale(0.25 * THIRD, sub(odd, skew)), odd_part[b])
    return first, diagonal, mixed, third, fourth


def flow_adjoint(first, diagonal, mixed, third, fourth, u):
    level = scale(2.0 / 3.0, add(*fourth.values()))
    q = []
    for a in range(3):
        b, c = [k for k in range(3) if k != a]
        ab, ac, bc = tuple(sorted((a, b))), tuple(sorted((a, c))), tuple(sorted((b, c)))
        along = sub(add(scale(2.0, diagonal[a]), level), fourth[bc])
        q.append(
            add(
                first[a],
                scale(1.0 / 3.0, add(third[a, b], third[a, c])),
                mul(u[a], along),
                mul(u[b], mixed[ab]),
                mul(u[c], mixed[ac]),
            )
        )
    return q


def collide_adjoint(r, u):
    t = dual(r)
    first, diagonal, mixed, third, fourth = t
    q = flow_adjoint(*t, u)
    square = [u[a] * u[a] for a in range(3)]
    by_density = None
    for a in range(3):
        b, c = [k for k in range(3) if k != a]
        by_density = add(
            by_density,
            u[a] * (first[a] + (1.0 / 3.0) * (third[a, b] + third[a, c]) - q[a]),
            diagonal[a] * (1.0 / 3.0 + square[a]),
        )
    level = 1.0 / 9.0 + (square[0] + square[1] + square[2]) * (1.0 / 3.0)
    by_density = by_density + (fourth[0, 1] + fourth[1, 2] + fourth[0, 2]) * level
    by_density = by_density - 0.5 * add(*[fourth[a, b] * square[3 - a - b] for a, b in PLANES])
    by_density = by_density + add(*[mixed[a, b] * (u[a] * u[b]) for a, b in PLANES])
    drift = [q[a] - first[a] for a in range(3)]
    base = {0: r[0]}
    for a in range(3):
        base[axis_index_of(a, 1)] = r[axis_index_of(a, 1)] + (drift[a] - diagonal[a])
        base[axis_index_of(a, -1)] = r[axis_index_of(a, -1)] - (drift[a] + diagonal[a])
    for a, b in PLANES:
        along = drift[a] - third[a, b]
        across = drift[b] - third[b, a]
        even = diagonal[a] + diagonal[b] + fourth[a, b]
        same, cross = even + mixed[a, b], even - mixed[a, b]
        both, gap = along + across, along - across
        base[edge_index_of(a, b, 1, 1)] = r[edge_index_of(a, b, 1, 1)] + (both - same)
        base[edge_index_of(a, b, -1, -1)] = r[edge_index_of(a, b, -1, -1)] - (both + same)
        base[edge_index_of(a, b, 1, -1)] = r[edge_index_of(a, b, 1, -1)] + (gap - cross)
        base[edge_index_of(a, b, -1, 1)] = r[edge_index_of(a, b, -1, 1)] - (gap + cross)
    return base, by_density, q


def rolled(x, step):
    return x if step == 0 else pltpu.roll(x, step % DEPTH, 1)


def rows_at(t, shift, offset):
    if isinstance(t, int):
        return pl.ds(t * 8 + offset + shift, 8)
    if shift == 0:
        return pl.ds(pl.multiple_of(t * 8 + offset, 8), 8)
    return pl.ds(t * 8 + (offset + shift), 8)


def flat(t):
    return rows_at(t, 0, 0)


def tall(t, shift=0):
    return rows_at(t, shift, PAD)


def mid(t):
    return pl.ds(t * 8 + (ROWS - MID) // 2, 8)


def mid_tall(t, shift=0):
    return pl.ds(t * 8 + ((ROWS - MID) // 2 + PAD + shift), 8)


class Packed:
    def __init__(self, spans, limit):
        self.spans, self.shift, at = spans, [], spans[0][0]
        for low, high in spans:
            self.shift.append(at - low)
            at += high - low
        self.shape = (-(-(max(self.shift) + limit) // 8) * 8, DEPTH)

    def put(self, ref, k, t, value):
        low, high = max(8 * t, self.spans[k][0]), min(8 * t + 8, self.spans[k][1])
        if low < high:
            ref[self.shift[k] + low : self.shift[k] + high, :] = value[low - 8 * t : high - 8 * t, :]

    def get(self, ref, k, t):
        return ref[pl.ds(8 * t + self.shift[k], 8), :]


def step_spans(first, last, which, more):
    return [(first - VECTORS[i][1], last - VECTORS[i][1]) for i in which] + [(first - 1, last + 1)] * 3 + more


def adjoint_spans(which):
    first, last = (MID - OWN) // 2 - 1, (MID + OWN) // 2 + 1
    rows = [(first + min(VECTORS[i][1], 0), last + max(VECTORS[i][1], 0)) for i in which]
    return rows + [(first, last)] * 3


START = {
    which: Packed(step_spans(2, ROWS - 2, which, [(0, ROWS)] * 2), ROWS) for which in (LEFTWARD, RIGHTWARD)
}
SECOND = {
    which: Packed(step_spans(4, ROWS - 4, which, [(2, ROWS - 2)]), ROWS) for which in (LEFTWARD, RIGHTWARD)
}
BACK = {which: Packed(adjoint_spans(which), MID) for which in (LEFTWARD, RIGHTWARD)}


def each_chunk(body, first=0, last=CHUNKS, unroll=0):
    if unroll == 0:
        for t in range(first, last):
            body(t)
        return

    def step(t, carry):
        body(t)
        return carry

    lax.fori_loop(first, last, step, 0, unroll=unroll)


def gradient_of(field, doubled, p, t):
    at = lambda dp, dy: field[p + dp, tall(t, dy), :]
    rp, rm, lp, lm = at(1, 1), at(1, -1), at(-1, 1), at(-1, -1)
    along_x = doubled[p + 1, tall(t), :] - doubled[p - 1, tall(t), :] + (rp + rm) - (lp + lm)
    along_y = doubled[p, tall(t, 1), :] - doubled[p, tall(t, -1), :] + (rp + lp) - (rm + lm)
    star = 2.0 * at(0, 0) + at(1, 0) + at(-1, 0) + at(0, 1) + at(0, -1)
    return [along_x, along_y, rolled(star, -1) - rolled(star, 1)]


def with_sides(x):
    return 2.0 * x + rolled(x, 1) + rolled(x, -1)


def inner_gradient(field, doubled, here, inner, t):
    at = lambda x, dy: field[x, tall(t, dy), :]
    up, down = at(inner, 1), at(inner, -1)
    along_x = doubled[inner, tall(t), :] + (up + down)
    along_y = doubled[here, tall(t, 1), :] - doubled[here, tall(t, -1), :] + (up - down)
    star = 2.0 * at(here, 0) + at(inner, 0) + at(here, 1) + at(here, -1)
    return [along_x if inner > here else -along_x, along_y, rolled(star, -1) - rolled(star, 1)]


def outer_gradient(field, doubled, p, inner, t):
    at = lambda dy: field[inner, tall(t, dy), :]
    up, down, here = at(1), at(-1), at(0)
    along_x = doubled[inner, tall(t), :] + (up + down)
    return [along_x if inner > p else -along_x, up - down, rolled(here, -1) - rolled(here, 1)]


def send_flow(packed, send_left, send_right, flow, field, doubled, t):
    for send, which, here, inner in ((send_left, LEFTWARD, 0, 1), (send_right, RIGHTWARD, 1, 0)):
        push = field[here, tall(t), :] * (PULL / SHEAR)
        pull = inner_gradient(field, doubled, here, inner, t)
        for a in range(3):
            packed[which].put(send, 5 + a, t, flow[a, here, flat(t), :] + push * pull[a])


def edges_kernel(pops, fluid, label, target, table, low, high, small, whole, values, sems):
    copies = []

    def copy(source, goal):
        one = pltpu.make_async_copy(source, goal, sems.at[len(copies)])
        one.start()
        copies.append(one)

    copy(fluid, whole.at[0])
    copy(label, whole.at[1])
    copy(target, small.at[2])
    copy(table, values)
    copy(pops.at[:, :, pl.ds(0, HALO), :], low.at[pl.ds(0, 19)])
    copy(pops.at[:, :, pl.ds(OWN - HALO, HALO), :], high.at[pl.ds(0, 19)])
    for one in copies:
        one.wait()
    small[0] = whole[0].astype(jnp.float32)
    small[1] = whole[1].astype(jnp.float32)
    small[3, 0, 0:2, :] = values[...]
    low[19:22] = small[0:3, :, 0:HALO, :]
    high[19:22] = small[0:3, :, OWN - HALO : OWN, :]


def put_sends(packed, send_left, send_right, t, lin, chosen):
    for x, send, which in ((0, send_left, LEFTWARD), (1, send_right, RIGHTWARD)):
        for k, i in enumerate(which):
            packed[which].put(send, k, t, lin[x][i])
        packed[which].put(send, 8, t, chosen[x])


def start_rows(t, populations, shares, marks, table, outs):
    lin_out, flow_out, density_out, effective_out, share_out, _, send_left, send_right = outs
    half_low = jnp.broadcast_to(table[0:1, :], (8, DEPTH))
    half_high = jnp.broadcast_to(table[1:2, :], (8, DEPTH))
    lin, chosen = [], []
    for x in range(2):
        share = shares[x]
        spot = jnp.bitwise_and(marks[x], DEPTH - 1)
        wall = jnp.where(
            jnp.bitwise_and(marks[x], DEPTH) == 0,
            jnp.take_along_axis(half_low, spot, axis=1),
            jnp.take_along_axis(half_high, spot, axis=1),
        )
        total, momentum, linear = linear_part(populations[x], share, range(19))
        for i in range(19):
            lin_out[i, x, flat(t), :] = linear[i]
        for a in range(3):
            flow_out[a, x, flat(t), :] = momentum[a]
        density_out[x, flat(t), :] = total
        effective_out[x, flat(t), :] = jnp.where(share > 0, 1.0 - jnp.exp(-total), wall)
        share_out[x, flat(t), :] = share
        lin.append(linear)
        chosen.append(jnp.where(share > 0, total, wall))
    put_sends(START, send_left, send_right, t, lin, chosen)
    START[LEFTWARD].put(send_left, 9, t, shares[0])
    START[RIGHTWARD].put(send_right, 9, t, shares[1])


def own_kernel(pops, small, *refs):
    outs, chooser, turned_label = refs[:8], refs[8], refs[9]
    outs[5][:, HALO : HALO + OWN, :] = small[2]

    def body(t):
        rows = rows_at(t, 0, -HALO)
        start_rows(
            t,
            [{i: pops[i, x, rows, :] for i in range(19)} for x in range(2)],
            [small[0, x, rows, :] for x in range(2)],
            [small[1, x, rows, :].astype(jnp.int32) for x in range(2)],
            small[3, 0, 0:2, :],
            outs,
        )

    each_chunk(body, HALO // 8, (HALO + OWN) // 8)

    marks = jnp.bitwise_and(small[1, 0].astype(jnp.int32), LABELS - 1).astype(jnp.float32)
    turned_label[...] = jnp.transpose(marks)
    quads = DEPTH // 4
    by_quad = turned_label[pl.ds(0, quads, stride=4), :]
    names = lax.broadcasted_iota(jnp.int32, (quads, LABELS), 1).astype(jnp.float32)
    for k in range(OWN // 2):
        column = jnp.broadcast_to(by_quad[:, 2 * k : 2 * k + 1], (quads, LABELS))
        chooser[quads * k : quads * (k + 1), :] = (column == names).astype(jnp.bfloat16)


def halo_kernel(small, below, above, *refs):
    outs, field, doubled = refs[8:16], refs[16], refs[17]
    for t, edge in ((0, below), (CHUNKS - 1, above)):
        outs[5][:, 8 * t : 8 * t + 8, :] = edge[21]
        start_rows(
            t,
            [{i: edge[i, x] for i in range(19)} for x in range(2)],
            [edge[19, x] for x in range(2)],
            [edge[20, x].astype(jnp.int32) for x in range(2)],
            small[3, 0, 0:2, :],
            outs,
        )
    flow, effective, send_left, send_right = outs[1], outs[3], outs[6], outs[7]

    def place(t):
        for x in range(2):
            value = effective[x, flat(t), :]
            field[x, tall(t), :] = value
            doubled[x, tall(t), :] = with_sides(value)

    each_chunk(place)
    each_chunk(functools.partial(send_flow, START, send_left, send_right, flow, field, doubled))


def put_field(field, doubled, p, t, value):
    field[p, tall(t), :] = value
    doubled[p, tall(t), :] = with_sides(value)


def put_masks(masks, p, t, share):
    masks[0, p, tall(t), :] = share
    masks[1, p, tall(t), :] = rolled(share, 1)
    masks[2, p, tall(t), :] = rolled(share, -1)


def first_flight_kernel(effective, share, masks, field, doubled):
    def body(t):
        for x in range(2):
            put_field(field, doubled, 2 + x, t, effective[x, flat(t), :])
            put_masks(masks, 2 + x, t, share[x, flat(t), :])

    each_chunk(body)


def second_flight_kernel(state, effective, share, field, doubled, lin):
    def body(t):
        for x in range(2):
            put_field(field, doubled, 2 + x, t, effective[x, flat(t), :])
            f = {i: state[i, x, flat(t), :] for i in range(19)}
            linear = linear_part(f, share[x, flat(t), :], range(19))[2]
            for i in range(19):
                lin[i, x, flat(t), :] = linear[i]

    each_chunk(body)


def step_kernel(is_first, *refs):
    if is_first:
        (lin, flow, density, effective, share, from_left, from_right, _, _, _,
         masks, field, doubled, speed, pull_out, state_out, flow_out, density_out, effective_out,
         send_left, send_right,
         relaxed, turned, next_field, next_doubled) = refs
    else:
        (lin, flow, density, share, target, masks, from_left, from_right, _, _,
         field, doubled, speed, pull_out, misfit_out, send_left, send_right,
         relaxed, turned) = refs

    packed = START if is_first else SECOND

    def place(t):
        for near, come, which in ((1, from_left, RIGHTWARD), (4, from_right, LEFTWARD)):
            s = packed[which].get(come, 9, t) if is_first else masks[0, near, tall(t), :]
            chosen = packed[which].get(come, 8, t)
            put_field(field, doubled, near, t, jnp.where(s > 0, 1.0 - jnp.exp(-chosen), chosen))
            if is_first:
                put_masks(masks, near, t, s)

    each_chunk(place)

    def collide(t):
        for p in range(1, 5):
            psi = field[p, tall(t), :]
            s = masks[0, p, tall(t), :]
            if p in (2, 3):
                pull = gradient_of(field, doubled, p, t)
                rho = density[p - 2, flat(t), :]
                mom = [flow[a, p - 2, flat(t), :] for a in range(3)]
                which = range(19)
                lin_at = {i: lin[i, p - 2, flat(t), :] for i in which}
                for a in range(3):
                    pull_out[a, p - 2, flat(t), :] = pull[a]
            else:
                pull = outer_gradient(field, doubled, p, 2 if p == 1 else 3, t)
                come = from_left if p == 1 else from_right
                which = RIGHTWARD if p == 1 else LEFTWARD
                rho = packed[which].get(come, 8, t)
                mom = [packed[which].get(come, 5 + a, t) for a in range(3)]
                lin_at = {i: packed[which].get(come, k, t) for k, i in enumerate(which)}
            push = psi * (PULL / SHEAR)
            full = [mom[a] + push * pull[a] for a in range(3)]
            inverse = 1.0 / rho
            u = [full[a] * inverse for a in range(3)]
            for a in range(3):
                speed[a, p - 1, flat(t), :] = u[a]
            part = balance_part(rho, full, u, s, which)
            for i in which:
                value = lin_at[i] + part[i]
                relaxed[i, p - 1, tall(t), :] = value
                if i in TURNED:
                    turned[TURNED.index(i), p - 1, tall(t), :] = rolled(value, VECTORS[i][2])

    each_chunk(collide, unroll=3)

    def streamed(x, rows):
        f = {0: relaxed[0, 1 + x, rows(0), :]}
        for i in range(1, 19):
            cx, cy, cz = VECTORS[i]
            if cz:
                source = turned[TURNED.index(i), 1 + x - cx, rows(-cy), :]
            else:
                source = relaxed[i, 1 + x - cx, rows(-cy), :]
            open_ = masks[cz % 3, 2 + x - cx, rows(-cy), :] > 0
            f[i] = jnp.where(open_, source, relaxed[OPPOSITE[i], 1 + x, rows(0), :])
        return f

    def stream(t):
        lin_sent, chosen_sent = [], []
        for x in range(2):
            s = share[x, flat(t), :]
            f = streamed(x, lambda dy: tall(t, dy))
            total, momentum, linear = linear_part(f, s, (LEFTWARD, RIGHTWARD)[x])
            held = effective[x, flat(t), :]
            eff = jnp.where(s > 0, 1.0 - jnp.exp(-total), held)
            for i in range(19):
                state_out[i, x, flat(t), :] = f[i]
            for a in range(3):
                flow_out[a, x, flat(t), :] = momentum[a]
            density_out[x, flat(t), :] = total
            effective_out[x, flat(t), :] = eff
            next_field[x, tall(t), :] = eff
            next_doubled[x, tall(t), :] = with_sides(eff)
            lin_sent.append(linear)
            chosen_sent.append(jnp.where(s > 0, total, held))
        put_sends(SECOND, send_left, send_right, t, lin_sent, chosen_sent)

    def compare(t):
        for x, near, far in ((0, send_left, send_right), (1, send_right, send_left)):
            f = streamed(x, lambda dy: mid_tall(t, dy))
            s = share[x, mid(t), :]
            misfit = s * (add(*[f[i] for i in range(19)]) - target[x, mid(t), :])
            misfit_out[x, flat(t), :] = misfit
            near[0, flat(t), :] = misfit
            far[1, flat(t), :] = misfit
            far[2, flat(t), :] = s

    if is_first:
        each_chunk(stream)
        each_chunk(functools.partial(send_flow, SECOND, send_left, send_right, flow_out, next_field, next_doubled))
    else:
        each_chunk(compare, 0, MID // 8)


def spread_of(pulled, pulled_doubled, p, rows):
    at = lambda a, dp, dy: pulled[a, p + dp, rows(dy), :]
    two = lambda a, dp, dy: pulled_doubled[a, p + dp, rows(dy), :]
    along_x = two(0, 1, 0) - two(0, -1, 0) + (at(0, 1, 1) + at(0, 1, -1)) - (at(0, -1, 1) + at(0, -1, -1))
    along_y = two(1, 0, 1) - two(1, 0, -1) + (at(1, 1, 1) + at(1, -1, 1)) - (at(1, 1, -1) + at(1, -1, -1))
    star = 2.0 * at(2, 0, 0) + at(2, 1, 0) + at(2, -1, 0) + at(2, 0, 1) + at(2, 0, -1)
    along_z = rolled(star, -1) - rolled(star, 1)
    return (along_x + along_y + along_z) * (-1.0 / 36.0)


def put_pulled(pulled, pulled_doubled, p, rows, psi, q):
    for a in range(3):
        s = (COUPLING / SHEAR) * psi * q[a]
        pulled[a, p, rows(0), :] = s
        if a < 2:
            pulled_doubled[a, p, rows(0), :] = with_sides(s)


def mask_ahead(masks, i, p, rows):
    cx, cy, cz = VECTORS[i]
    return masks[(-cz) % 3, p + cx, rows(cy), :] > 0


def middle(t):
    return lambda dy: mid_tall(t, dy)


def last_reverse_kernel(
    misfit, from_left, from_right, masks, field, speed, pull, early_speed,
    adjoint, turned, wall_out, send_left, send_right, part_left, part_right,
    ahead, far_masks, pulled, pulled_doubled, base,
):
    def place(t):
        rows = middle(t)
        for p in range(6):
            if p < 2:
                d = from_left[1 - p, flat(t), :]
            elif p < 4:
                d = misfit[p - 2, flat(t), :]
            else:
                d = from_right[p - 4, flat(t), :]
            ahead[0, p, rows(0), :] = d
            ahead[1, p, rows(0), :] = rolled(d, 1)
            ahead[2, p, rows(0), :] = rolled(d, -1)
        for k, source in enumerate((from_left, from_right)):
            s = source[2, flat(t), :]
            far_masks[0, k, rows(0), :] = s
            far_masks[1, k, rows(0), :] = rolled(s, 1)
            far_masks[2, k, rows(0), :] = rolled(s, -1)

    each_chunk(place, 0, MID // 8)

    def collide(t):
        rows = middle(t)
        for p in range(1, 5):
            s = masks[0, p, rows(0), :]
            here = ahead[0, p, rows(0), :]
            r = {0: here}
            for i in range(1, 19):
                cx, cy, cz = VECTORS[i]
                there = ahead[(-cz) % 3, p + cx, rows(cy), :]
                if p + cx in (0, 5):
                    open_ = far_masks[(-cz) % 3, (p + cx) // 5, rows(cy), :] > 0
                else:
                    open_ = mask_ahead(masks, i, p, rows)
                r[i] = jnp.where(open_, there, here)
            psi = field[p, rows(0), :]
            u = [speed[a, p - 1, mid(t), :] for a in range(3)]
            if p in (2, 3):
                rest, by_density, q = collide_adjoint(r, u)
                along = add(*[q[a] * pull[a, p - 2, mid(t), :] for a in range(3)])
                const = by_density + along * ((PULL / SHEAR) * (1.0 - psi))
                for i in range(19):
                    base[i, p - 2, flat(t), :] = rest[i] + const
            else:
                q = flow_adjoint(*dual(r), u)
            put_pulled(pulled, pulled_doubled, p - 1, rows, s * psi, q)

    each_chunk(collide, 0, MID // 8)

    def finish(t):
        rows = middle(t)
        for x in range(2):
            s = masks[0, 2 + x, rows(0), :]
            spread = spread_of(pulled, pulled_doubled, 1 + x, rows)
            wall_out[x, flat(t), :] = (1.0 - s) * spread
            more = s * spread * (1.0 - field[2 + x, rows(0), :])
            for i in range(19):
                value = base[i, x, flat(t), :] + more
                adjoint[i, x, rows(0), :] = value
                if i in TURNED:
                    turned[TURNED.index(i), x, rows(0), :] = rolled(value, -VECTORS[i][2])

    each_chunk(finish, 0, MID // 8)

    def part(t):
        rows = middle(t)
        for x, send, kept, sent, skipped in ((0, send_left, part_left, RIGHTWARD, -1), (1, send_right, part_right, LEFTWARD, 1)):
            p = 2 + x
            s = masks[0, p, rows(0), :]
            r = {}
            for i in range(19):
                if VECTORS[i][0] != skipped:
                    r[i] = adjoint_ahead(adjoint, turned, masks, i, x, rows)
            u = [early_speed[a, p - 1, mid(t), :] for a in range(3)]
            q = flow_adjoint(*dual(r), u)
            for a in range(3):
                BACK[sent].put(send, 5 + a, t, s * q[a])
                kept[a, flat(t), :] = s * q[a]
            for k, i in enumerate(sent):
                BACK[sent].put(send, k, t, adjoint[i, x, rows(0), :])

    each_chunk(part, 0, MID // 8)


def adjoint_ahead(adjoint, turned, masks, i, x, rows):
    cx, cy, cz = VECTORS[i]
    if i == 0:
        return adjoint[0, x, rows(0), :]
    if cz:
        there = turned[TURNED.index(i), x + cx, rows(cy), :]
    else:
        there = adjoint[i, x + cx, rows(cy), :]
    return jnp.where(mask_ahead(masks, i, 2 + x, rows), there, adjoint[OPPOSITE[i], x, rows(0), :])


def place_sides(come, from_left, from_right, t):
    for side, source, which in ((0, from_left, LEFTWARD), (1, from_right, RIGHTWARD)):
        for k, i in enumerate(which):
            come[side, k, mid_tall(t), :] = rolled(BACK[which].get(source, k, t), -VECTORS[i][2])


def arrived(come, adjoint, masks, i, x, rows):
    which = LEFTWARD if x == 0 else RIGHTWARD
    there = come[x, which.index(i), rows(VECTORS[i][1]), :]
    return jnp.where(mask_ahead(masks, i, 2 + x, rows), there, adjoint[OPPOSITE[i], x, rows(0), :])


def wall_kernel(
    adjoint, turned, wall, part_left, part_right, from_left, from_right, masks, field, speed, chooser,
    more_out, label_part,
    come, pulled, pulled_doubled, totals,
):
    each_chunk(functools.partial(place_sides, come, from_left, from_right), 0, MID // 8)

    def collide(t):
        rows = middle(t)
        for x, part, which in ((0, part_left, LEFTWARD), (1, part_right, RIGHTWARD)):
            p = 2 + x
            s = masks[0, p, rows(0), :]
            r = {i: arrived(come, adjoint, masks, i, x, rows) for i in which}
            u = [speed[a, p - 1, mid(t), :] for a in range(3)]
            rest = flow_adjoint(*dual(r), u)
            q = [part[a, flat(t), :] + s * rest[a] for a in range(3)]
            put_pulled(pulled, pulled_doubled, p - 1, rows, field[p, rows(0), :], q)
        for x, source, which in ((0, from_left, LEFTWARD), (1, from_right, RIGHTWARD)):
            p = 1 if x == 0 else 4
            s = masks[0, p, rows(0), :]
            r = {}
            for i in [OPPOSITE[j] for j in which]:
                cx, cy, cz = VECTORS[i]
                if cz:
                    there = turned[TURNED.index(i), x, rows(cy), :]
                else:
                    there = adjoint[i, x, rows(cy), :]
                here = BACK[which].get(source, which.index(OPPOSITE[i]), t)
                r[i] = jnp.where(mask_ahead(masks, i, p, rows), there, here)
            u = [speed[a, p - 1, mid(t), :] for a in range(3)]
            rest = flow_adjoint(*dual(r), u)
            q = [BACK[which].get(source, 5 + a, t) + s * rest[a] for a in range(3)]
            put_pulled(pulled, pulled_doubled, p - 1, rows, field[p, rows(0), :], q)

    each_chunk(collide, 0, MID // 8)

    def finish(t):
        total = None
        for x in range(2):
            s = masks[0, 2 + x, tall(t), :]
            spread = spread_of(pulled, pulled_doubled, 1 + x, lambda dy: tall(t, dy))
            step_wall = wall[x, pl.ds(t * 8 - (ROWS - MID) // 2, 8), :]
            total = add(total, (1.0 - s) * spread + step_wall)
            more_out[x, rows_at(t, 0, -HALO), :] = s * spread * (1.0 - field[2 + x, tall(t), :])
        totals[rows_at(t, 0, -HALO), :] = total

    each_chunk(finish, HALO // 8, (HALO + OWN) // 8)

    blocks = (OWN // 2) * (DEPTH // 4)
    column = lax.broadcasted_iota(jnp.int32, (DEPTH, blocks), 1)
    quad = lax.broadcasted_iota(jnp.int32, (DEPTH, blocks), 0) // 4
    gather = (jnp.bitwise_and(column, DEPTH // 4 - 1) == quad).astype(jnp.bfloat16)
    by_block = exact_dot(totals[...], gather)
    pair = lax.broadcasted_iota(jnp.int32, (OWN, blocks), 0) // 2
    wanted = lax.broadcasted_iota(jnp.int32, (OWN, blocks), 1) // (DEPTH // 4)
    by_block = jnp.where(pair == wanted, by_block, 0.0)
    by_label = exact_dot(by_block, chooser[...])
    label_part[...] = jnp.sum(by_label, axis=0, keepdims=True)


def grad_kernel(
    adjoint, turned, more, from_left, from_right, masks, field, speed, pull,
    grad,
    come,
):
    each_chunk(functools.partial(place_sides, come, from_left, from_right), 0, MID // 8)

    def collide(t):
        rows = lambda dy: tall(t, dy)
        for x in range(2):
            p = 2 + x
            s = masks[0, p, tall(t), :]
            r = {}
            for i in range(19):
                if VECTORS[i][0] == 2 * x - 1:
                    r[i] = s * arrived(come, adjoint, masks, i, x, rows)
                else:
                    r[i] = s * adjoint_ahead(adjoint, turned, masks, i, x, rows)
            u = [speed[a, p - 1, flat(t), :] for a in range(3)]
            rest, by_density, q = collide_adjoint(r, u)
            along = add(*[q[a] * pull[a, x, flat(t), :] for a in range(3)])
            const = by_density + along * ((PULL / SHEAR) * (1.0 - field[p, tall(t), :]))
            const = const + more[x, rows_at(t, 0, -HALO), :]
            for i in range(19):
                grad[i, x, rows_at(t, 0, -HALO), :] = rest[i] + const

    each_chunk(collide, HALO // 8, (HALO + OWN) // 8)


def exact_dot(values, zero_one):
    rows = values.shape[0]
    high = values.astype(jnp.bfloat16)
    left = values - high.astype(jnp.float32)
    middle = left.astype(jnp.bfloat16)
    low = (left - middle.astype(jnp.float32)).astype(jnp.bfloat16)
    parts = jnp.concatenate([high, middle, low], axis=0)
    sums = jnp.dot(parts, zero_one, preferred_element_type=jnp.float32)
    return sums[:rows] + (sums[rows : 2 * rows] + sums[2 * rows :])


def call(kernel, args, outs, scratch, anywhere=0, grant=12, filled=0):
    whole = pl.BlockSpec(memory_space=pltpu.VMEM)
    there = pl.BlockSpec(memory_space=pl.ANY)
    size = sum(a.size * a.dtype.itemsize for a in args)
    return pl.pallas_call(
        kernel,
        out_shape=[s if hasattr(s, "dtype") else jax.ShapeDtypeStruct(s, jnp.float32) for s in outs],
        in_specs=[there] * anywhere + [whole] * (len(args) - anywhere),
        out_specs=[whole] * len(outs),
        scratch_shapes=scratch,
        input_output_aliases={len(args) - filled + k: k for k in range(filled)},
        compiler_params=pltpu.CompilerParams(vmem_limit_bytes=grant * 1024 * 1024),
        cost_estimate=pl.CostEstimate(flops=0, bytes_accessed=size, transcendentals=0),
    )(*args)


def ring(axis):
    count = lax.axis_size(axis)
    up = [(i, (i + 1) % count) for i in range(count)]
    return up, [(j, i) for i, j in up]


def both_ways(to_lower, to_upper, axis):
    up, down = ring(axis)
    from_lower = lax.ppermute(to_upper, axis, up)
    from_upper = lax.ppermute(to_lower, axis, down)
    return from_lower, from_upper


def per_device(populations, fluid, label, wall_wetting, target):
    vmem = lambda *shape: pltpu.VMEM(shape, jnp.float32)
    plane = (ROWS, DEPTH)
    two = (2, *plane)
    edge = (22, 2, HALO, DEPTH)
    low, high, small = call(
        edges_kernel,
        (populations, fluid, label, target, wall_wetting.reshape(2, DEPTH)),
        (edge, edge, (4, 2, OWN, DEPTH)),
        (
            pltpu.VMEM((2, 2, OWN, DEPTH), jnp.int32),
            vmem(2, DEPTH),
            pltpu.SemaphoreType.DMA((6,)),
        ),
        anywhere=5,
        grant=56,
    )
    below, above = both_ways(low, high, "gy")
    blocks = (OWN // 2) * (DEPTH // 4)
    started = ((19, *two), (3, *two), two, two, two, two, START[LEFTWARD].shape, START[RIGHTWARD].shape)
    *own, chooser = call(
        own_kernel,
        (populations, small),
        (*started, jax.ShapeDtypeStruct((blocks, LABELS), jnp.bfloat16)),
        (vmem(DEPTH, OWN),),
    )
    beside = (vmem(2, TALL, DEPTH), vmem(2, TALL, DEPTH))
    lin, flow, density, effective, share, target_wide, to_left, to_right = call(
        halo_kernel, (small, below, above, *own), started, beside, filled=len(started)
    )
    from_left, from_right = both_ways(to_left, to_right, "gx")
    wide6 = (6, TALL, DEPTH)
    work = (vmem(19, 4, TALL, DEPTH), vmem(10, 4, TALL, DEPTH))
    begun = call(first_flight_kernel, (effective, share), ((3, *wide6), wide6, wide6), ())
    masks, field0, _, speed0, pull0, state, flow, density, effective, to_left, to_right = call(
        functools.partial(step_kernel, True),
        (lin, flow, density, effective, share, from_left, from_right, *begun),
        (
            (3, *wide6), wide6, wide6, (3, 4, *plane), (3, *two),
            (19, *two), (3, *two), two, two, SECOND[LEFTWARD].shape, SECOND[RIGHTWARD].shape,
        ),
        (*work, *beside),
        filled=3,
    )
    from_left, from_right = both_ways(to_left, to_right, "gx")
    less = (MID, DEPTH)
    field1, doubled, lin = call(
        second_flight_kernel, (state, effective, share), (wide6, wide6, (19, *two)), ()
    )
    field1, _, speed1, pull1, misfit, to_left, to_right = call(
        functools.partial(step_kernel, False),
        (lin, flow, density, share, target_wide, masks, from_left, from_right, field1, doubled),
        (wide6, wide6, (3, 4, *plane), (3, *two), (2, *less), (3, *less), (3, *less)),
        work,
        filled=2,
    )
    from_left, from_right = both_ways(to_left, to_right, "gx")
    pulled = (vmem(3, 4, TALL, DEPTH), vmem(2, 4, TALL, DEPTH))
    adjoint, turned, wall, to_left, to_right, part_left, part_right = call(
        last_reverse_kernel,
        (misfit, from_left, from_right, masks, field1, speed1, pull1, speed0),
        ((19, 2, TALL, DEPTH), (10, 2, TALL, DEPTH), (2, *less), BACK[RIGHTWARD].shape, BACK[LEFTWARD].shape, (3, *less), (3, *less)),
        (vmem(3, *wide6), vmem(3, 2, TALL, DEPTH), *pulled, vmem(19, 2, *less)),
    )
    from_left, from_right = both_ways(to_left, to_right, "gx")
    come = vmem(2, 5, TALL, DEPTH)
    more, label_part = call(
        wall_kernel,
        (adjoint, turned, wall, part_left, part_right, from_left, from_right, masks, field0, speed0, chooser),
        ((2, OWN, DEPTH), (1, LABELS)),
        (come, *pulled, vmem(OWN, DEPTH)),
    )
    count = lax.axis_size("gy")
    wetting_grad = label_part
    for step in range(1, count):
        wetting_grad = wetting_grad + lax.ppermute(
            label_part, "gy", [(i, (i + step) % count) for i in range(count)]
        )
    (grad,) = call(
        grad_kernel,
        (adjoint, turned, more, from_left, from_right, masks, field0, speed0, pull0),
        (populations.shape,),
        (come,),
    )
    return (grad, wetting_grad.reshape(-1))


def solution(mesh):
    return jax.shard_map(
        per_device,
        mesh=mesh,
        in_specs=(
            P(None, "gx", "gy", None),
            P("gx", "gy", None),
            P("gx", "gy", None),
            P("gx"),
            P("gx", "gy", None),
        ),
        out_specs=(P(None, "gx", "gy", None), P("gx")),
        check_vma=False,
    )
```

```python
import functools

import jax
import jax.numpy as jnp
from jax import lax
from jax.experimental import pallas as pl
from jax.experimental.pallas import tpu as pltpu
from jax.sharding import PartitionSpec as P

HALO = 8
PAD = 8
OWN = 32
ROWS = OWN + 2 * HALO
TALL = ROWS + 2 * PAD
MID = OWN + HALO
DEPTH = 128
CHUNKS = ROWS // 8
LABELS = 256

VECTORS = (
    (0, 0, 0), (1, 0, 0), (-1, 0, 0), (0, 1, 0), (0, -1, 0), (0, 0, 1), (0, 0, -1),
    (1, 1, 0), (-1, -1, 0), (1, -1, 0), (-1, 1, 0), (1, 0, 1), (-1, 0, -1), (1, 0, -1), (-1, 0, 1),
    (0, 1, 1), (0, -1, -1), (0, 1, -1), (0, -1, 1),
)
OPPOSITE = (0, 2, 1, 4, 3, 6, 5, 8, 7, 10, 9, 12, 11, 14, 13, 16, 15, 18, 17)
INDEX = {v: i for i, v in enumerate(VECTORS)}
RIGHTWARD = tuple(i for i in range(19) if VECTORS[i][0] == 1)
LEFTWARD = tuple(i for i in range(19) if VECTORS[i][0] == -1)
TURNED = tuple(i for i in range(19) if VECTORS[i][2] != 0)
PLANES = ((0, 1), (1, 2), (0, 2))
COUPLING = 5.0
SHEAR = 1.2
BULK = 1.19
THIRD = 1.5
FOURTH = 1.4
TRACE = (BULK - SHEAR) / 3.0
PULL = COUPLING / 36.0


def axis_index_of(axis, sign):
    v = [0, 0, 0]
    v[axis] = sign
    return INDEX[tuple(v)]


def edge_index_of(a, b, sa, sb):
    v = [0, 0, 0]
    v[a], v[b] = sa, sb
    return INDEX[tuple(v)]


def add(*terms):
    total = None
    for term in terms:
        if term is not None:
            total = term if total is None else total + term
    return total


def sub(a, b):
    if b is None:
        return a
    return -b if a is None else a - b


def scale(c, a):
    return None if a is None else c * a


def mul(a, b):
    return None if a is None or b is None else a * b


def moments(f):
    fourth, mixed, third = {}, {}, {}
    for a, b in PLANES:
        pp, mm = f[edge_index_of(a, b, 1, 1)], f[edge_index_of(a, b, -1, -1)]
        pm, mp = f[edge_index_of(a, b, 1, -1)], f[edge_index_of(a, b, -1, 1)]
        even, odd, cross, skew = pp + mm, pp - mm, pm + mp, pm - mp
        fourth[a, b] = even + cross
        mixed[a, b] = even - cross
        third[a, b] = odd + skew
        third[b, a] = odd - skew
    first, diagonal, total = [], [], f[0]
    for a in range(3):
        b, c = [k for k in range(3) if k != a]
        plus, minus = f[axis_index_of(a, 1)], f[axis_index_of(a, -1)]
        both = plus + minus
        total = total + both
        diagonal.append(both + fourth[tuple(sorted((a, b)))] + fourth[tuple(sorted((a, c)))])
        first.append((plus - minus) + third[a, b] + third[a, c])
    total = total + fourth[0, 1] + fourth[1, 2] + fourth[0, 2]
    return total, first, diagonal, mixed, third, fourth


def from_moments(first, diagonal, mixed, third, fourth, which):
    out = {}
    for a, b in PLANES:
        even, cross = fourth[a, b] + mixed[a, b], fourth[a, b] - mixed[a, b]
        odd, skew = third[a, b] + third[b, a], third[a, b] - third[b, a]
        out[edge_index_of(a, b, 1, 1)] = even + odd
        out[edge_index_of(a, b, -1, -1)] = even - odd
        out[edge_index_of(a, b, 1, -1)] = cross + skew
        out[edge_index_of(a, b, -1, 1)] = cross - skew
    for a in range(3):
        b, c = [k for k in range(3) if k != a]
        even = diagonal[a] - 2.0 * (fourth[tuple(sorted((a, b)))] + fourth[tuple(sorted((a, c)))])
        odd = first[a] - 2.0 * (third[a, b] + third[a, c])
        out[axis_index_of(a, 1)] = even + odd
        out[axis_index_of(a, -1)] = even - odd
    out[0] = 4.0 * (fourth[0, 1] + fourth[1, 2] + fourth[0, 2]) - 2.0 * (diagonal[0] + diagonal[1] + diagonal[2])
    return {i: out[i] for i in which}


def linear_part(f, share, which):
    total, first, diagonal, mixed, third, fourth = moments(f)
    half, quarter = (0.5 * SHEAR) * share, (0.25 * SHEAR) * share
    trace = (0.5 * TRACE) * share * (diagonal[0] + diagonal[1] + diagonal[2])
    by_third, by_fourth = (0.25 * THIRD) * share, (0.25 * FOURTH) * share
    change = from_moments(
        [half * m for m in first],
        [half * m + trace for m in diagonal],
        {k: quarter * m for k, m in mixed.items()},
        {k: by_third * m for k, m in third.items()},
        {k: by_fourth * m for k, m in fourth.items()},
        which,
    )
    return total, first, {i: f[i] - change[i] for i in which}


def balance_part(density, flow, velocity, share, which):
    d = density * share
    m = [flow[a] * share for a in range(3)]
    square = [m[a] * velocity[a] for a in range(3)]
    whole = square[0] + square[1] + square[2]
    level = d * (SHEAR / 6.0 + 0.5 * TRACE) + whole * (0.5 * TRACE)
    diagonal = [(0.5 * SHEAR) * square[a] + level for a in range(3)]
    scaled = [(0.25 * SHEAR) * velocity[a] for a in range(3)]
    mixed = {(a, b): m[a] * scaled[b] for a, b in PLANES}
    part = [(THIRD / 12.0) * m[a] for a in range(3)]
    third = {}
    fourth = {}
    level = d * (FOURTH / 36.0) + whole * (FOURTH / 12.0)
    for a, b in PLANES:
        third[a, b], third[b, a] = part[a], part[b]
        fourth[a, b] = level - (FOURTH / 8.0) * square[3 - a - b]
    return from_moments([(0.5 * SHEAR) * m[a] for a in range(3)], diagonal, mixed, third, fourth, which)


def dual(r):
    rest = r.get(0)
    even_of, odd_of = [], []
    for a in range(3):
        plus, minus = r.get(axis_index_of(a, 1)), r.get(axis_index_of(a, -1))
        even_of.append(add(plus, minus))
        odd_of.append(sub(plus, minus))
    trace = add(scale(0.5 * TRACE, add(*even_of)), scale(-3.0 * TRACE - SHEAR, rest))
    first = [scale(0.5 * SHEAR, odd) for odd in odd_of]
    diagonal = [add(scale(0.5 * SHEAR, even), trace) for even in even_of]
    even_part = [scale(0.5 * FOURTH, even) for even in even_of]
    odd_part = [scale(0.5 * THIRD, odd) for odd in odd_of]
    rest_part = scale(FOURTH, rest)
    mixed, third, fourth = {}, {}, {}
    for a, b in PLANES:
        pp, mm = r.get(edge_index_of(a, b, 1, 1)), r.get(edge_index_of(a, b, -1, -1))
        pm, mp = r.get(edge_index_of(a, b, 1, -1)), r.get(edge_index_of(a, b, -1, 1))
        even, odd, cross, skew = add(pp, mm), sub(pp, mm), add(pm, mp), sub(pm, mp)
        whole = scale(0.25 * FOURTH, add(even, cross))
        fourth[a, b] = add(sub(sub(whole, even_part[a]), even_part[b]), rest_part)
        mixed[a, b] = scale(0.25 * SHEAR, sub(even, cross))
        third[a, b] = sub(scale(0.25 * THIRD, add(odd, skew)), odd_part[a])
        third[b, a] = sub(scale(0.25 * THIRD, sub(odd, skew)), odd_part[b])
    return first, diagonal, mixed, third, fourth


def flow_adjoint(first, diagonal, mixed, third, fourth, u):
    level = scale(2.0 / 3.0, add(*fourth.values()))
    q = []
    for a in range(3):
        b, c = [k for k in range(3) if k != a]
        ab, ac, bc = tuple(sorted((a, b))), tuple(sorted((a, c))), tuple(sorted((b, c)))
        along = sub(add(scale(2.0, diagonal[a]), level), fourth[bc])
        q.append(
            add(
                first[a],
                scale(1.0 / 3.0, add(third[a, b], third[a, c])),
                mul(u[a], along),
                mul(u[b], mixed[ab]),
                mul(u[c], mixed[ac]),
            )
        )
    return q


def collide_adjoint(r, u):
    t = dual(r)
    first, diagonal, mixed, third, fourth = t
    q = flow_adjoint(*t, u)
    square = [u[a] * u[a] for a in range(3)]
    by_density = None
    for a in range(3):
        b, c = [k for k in range(3) if k != a]
        by_density = add(
            by_density,
            u[a] * (first[a] + (1.0 / 3.0) * (third[a, b] + third[a, c]) - q[a]),
            diagonal[a] * (1.0 / 3.0 + square[a]),
        )
    level = 1.0 / 9.0 + (square[0] + square[1] + square[2]) * (1.0 / 3.0)
    by_density = by_density + (fourth[0, 1] + fourth[1, 2] + fourth[0, 2]) * level
    by_density = by_density - 0.5 * add(*[fourth[a, b] * square[3 - a - b] for a, b in PLANES])
    by_density = by_density + add(*[mixed[a, b] * (u[a] * u[b]) for a, b in PLANES])
    drift = [q[a] - first[a] for a in range(3)]
    base = {0: r[0]}
    for a in range(3):
        base[axis_index_of(a, 1)] = r[axis_index_of(a, 1)] + (drift[a] - diagonal[a])
        base[axis_index_of(a, -1)] = r[axis_index_of(a, -1)] - (drift[a] + diagonal[a])
    for a, b in PLANES:
        along = drift[a] - third[a, b]
        across = drift[b] - third[b, a]
        even = diagonal[a] + diagonal[b] + fourth[a, b]
        same, cross = even + mixed[a, b], even - mixed[a, b]
        both, gap = along + across, along - across
        base[edge_index_of(a, b, 1, 1)] = r[edge_index_of(a, b, 1, 1)] + (both - same)
        base[edge_index_of(a, b, -1, -1)] = r[edge_index_of(a, b, -1, -1)] - (both + same)
        base[edge_index_of(a, b, 1, -1)] = r[edge_index_of(a, b, 1, -1)] + (gap - cross)
        base[edge_index_of(a, b, -1, 1)] = r[edge_index_of(a, b, -1, 1)] - (gap + cross)
    return base, by_density, q


def rolled(x, step):
    return x if step == 0 else pltpu.roll(x, step % DEPTH, 1)


def rows_at(t, shift, offset):
    if isinstance(t, int):
        return pl.ds(t * 8 + offset + shift, 8)
    if shift == 0:
        return pl.ds(pl.multiple_of(t * 8 + offset, 8), 8)
    return pl.ds(t * 8 + (offset + shift), 8)


def flat(t):
    return rows_at(t, 0, 0)


def tall(t, shift=0):
    return rows_at(t, shift, PAD)


def mid(t):
    return pl.ds(t * 8 + (ROWS - MID) // 2, 8)


def mid_tall(t, shift=0):
    return pl.ds(t * 8 + ((ROWS - MID) // 2 + PAD + shift), 8)


class Packed:
    def __init__(self, spans, limit):
        self.spans, self.shift, at = spans, [], spans[0][0]
        for low, high in spans:
            self.shift.append(at - low)
            at += high - low
        self.shape = (-(-(max(self.shift) + limit) // 8) * 8, DEPTH)

    def put(self, ref, k, t, value):
        low, high = max(8 * t, self.spans[k][0]), min(8 * t + 8, self.spans[k][1])
        if low < high:
            ref[self.shift[k] + low : self.shift[k] + high, :] = value[low - 8 * t : high - 8 * t, :]

    def get(self, ref, k, t):
        return ref[pl.ds(8 * t + self.shift[k], 8), :]


def step_spans(first, last, which, more):
    return [(first - VECTORS[i][1], last - VECTORS[i][1]) for i in which] + [(first - 1, last + 1)] * 3 + more


def adjoint_spans(which):
    first, last = (MID - OWN) // 2 - 1, (MID + OWN) // 2 + 1
    rows = [(first + min(VECTORS[i][1], 0), last + max(VECTORS[i][1], 0)) for i in which]
    return rows + [(first, last)] * 3


START = {
    which: Packed(step_spans(2, ROWS - 2, which, [(0, ROWS)] * 2), ROWS) for which in (LEFTWARD, RIGHTWARD)
}
SECOND = {
    which: Packed(step_spans(4, ROWS - 4, which, [(2, ROWS - 2)]), ROWS) for which in (LEFTWARD, RIGHTWARD)
}
BACK = {which: Packed(adjoint_spans(which), MID) for which in (LEFTWARD, RIGHTWARD)}


def each_chunk(body, first=0, last=CHUNKS, unroll=0):
    if unroll == 0:
        for t in range(first, last):
            body(t)
        return

    def step(t, carry):
        body(t)
        return carry

    lax.fori_loop(first, last, step, 0, unroll=unroll)


def gradient_of(field, doubled, p, t):
    at = lambda dp, dy: field[p + dp, tall(t, dy), :]
    rp, rm, lp, lm = at(1, 1), at(1, -1), at(-1, 1), at(-1, -1)
    along_x = doubled[p + 1, tall(t), :] - doubled[p - 1, tall(t), :] + (rp + rm) - (lp + lm)
    along_y = doubled[p, tall(t, 1), :] - doubled[p, tall(t, -1), :] + (rp + lp) - (rm + lm)
    star = 2.0 * at(0, 0) + at(1, 0) + at(-1, 0) + at(0, 1) + at(0, -1)
    return [along_x, along_y, rolled(star, -1) - rolled(star, 1)]


def with_sides(x):
    return 2.0 * x + rolled(x, 1) + rolled(x, -1)


def inner_gradient(field, doubled, here, inner, t):
    at = lambda x, dy: field[x, tall(t, dy), :]
    up, down = at(inner, 1), at(inner, -1)
    along_x = doubled[inner, tall(t), :] + (up + down)
    along_y = doubled[here, tall(t, 1), :] - doubled[here, tall(t, -1), :] + (up - down)
    star = 2.0 * at(here, 0) + at(inner, 0) + at(here, 1) + at(here, -1)
    return [along_x if inner > here else -along_x, along_y, rolled(star, -1) - rolled(star, 1)]


def outer_gradient(field, doubled, p, inner, t):
    at = lambda dy: field[inner, tall(t, dy), :]
    up, down, here = at(1), at(-1), at(0)
    along_x = doubled[inner, tall(t), :] + (up + down)
    return [along_x if inner > p else -along_x, up - down, rolled(here, -1) - rolled(here, 1)]


def send_flow(packed, send_left, send_right, flow, field, doubled, t):
    for send, which, here, inner in ((send_left, LEFTWARD, 0, 1), (send_right, RIGHTWARD, 1, 0)):
        push = field[here, tall(t), :] * (PULL / SHEAR)
        pull = inner_gradient(field, doubled, here, inner, t)
        for a in range(3):
            packed[which].put(send, 5 + a, t, flow[a, here, flat(t), :] + push * pull[a])


def edges_kernel(pops, fluid, label, target, table, low, high, small, whole, values, sems):
    copies = []

    def copy(source, goal):
        one = pltpu.make_async_copy(source, goal, sems.at[len(copies)])
        one.start()
        copies.append(one)

    copy(fluid, whole.at[0])
    copy(label, whole.at[1])
    copy(target, small.at[2])
    copy(table, values)
    copy(pops.at[:, :, pl.ds(0, HALO), :], low.at[pl.ds(0, 19)])
    copy(pops.at[:, :, pl.ds(OWN - HALO, HALO), :], high.at[pl.ds(0, 19)])
    for one in copies:
        one.wait()
    small[0] = whole[0].astype(jnp.float32)
    small[1] = whole[1].astype(jnp.float32)
    small[3, 0, 0:2, :] = values[...]
    low[19:22] = small[0:3, :, 0:HALO, :]
    high[19:22] = small[0:3, :, OWN - HALO : OWN, :]


def put_sends(packed, send_left, send_right, t, lin, chosen):
    for x, send, which in ((0, send_left, LEFTWARD), (1, send_right, RIGHTWARD)):
        for k, i in enumerate(which):
            packed[which].put(send, k, t, lin[x][i])
        packed[which].put(send, 8, t, chosen[x])


def start_rows(t, populations, shares, marks, table, outs):
    lin_out, flow_out, density_out, effective_out, share_out, _, send_left, send_right = outs
    half_low = jnp.broadcast_to(table[0:1, :], (8, DEPTH))
    half_high = jnp.broadcast_to(table[1:2, :], (8, DEPTH))
    lin, chosen = [], []
    for x in range(2):
        share = shares[x]
        spot = jnp.bitwise_and(marks[x], DEPTH - 1)
        wall = jnp.where(
            jnp.bitwise_and(marks[x], DEPTH) == 0,
            jnp.take_along_axis(half_low, spot, axis=1),
            jnp.take_along_axis(half_high, spot, axis=1),
        )
        total, momentum, linear = linear_part(populations[x], share, range(19))
        for i in range(19):
            lin_out[i, x, flat(t), :] = linear[i]
        for a in range(3):
            flow_out[a, x, flat(t), :] = momentum[a]
        density_out[x, flat(t), :] = total
        effective_out[x, flat(t), :] = jnp.where(share > 0, 1.0 - jnp.exp(-total), wall)
        share_out[x, flat(t), :] = share
        lin.append(linear)
        chosen.append(jnp.where(share > 0, total, wall))
    put_sends(START, send_left, send_right, t, lin, chosen)
    START[LEFTWARD].put(send_left, 9, t, shares[0])
    START[RIGHTWARD].put(send_right, 9, t, shares[1])


def own_kernel(pops, small, *refs):
    outs, chooser, turned_label = refs[:8], refs[8], refs[9]
    outs[5][:, HALO : HALO + OWN, :] = small[2]

    def body(t):
        rows = rows_at(t, 0, -HALO)
        start_rows(
            t,
            [{i: pops[i, x, rows, :] for i in range(19)} for x in range(2)],
            [small[0, x, rows, :] for x in range(2)],
            [small[1, x, rows, :].astype(jnp.int32) for x in range(2)],
            small[3, 0, 0:2, :],
            outs,
        )

    each_chunk(body, HALO // 8, (HALO + OWN) // 8)

    marks = jnp.bitwise_and(small[1, 0].astype(jnp.int32), LABELS - 1).astype(jnp.float32)
    turned_label[...] = jnp.transpose(marks)
    quads = DEPTH // 4
    by_quad = turned_label[pl.ds(0, quads, stride=4), :]
    names = lax.broadcasted_iota(jnp.int32, (quads, LABELS), 1).astype(jnp.float32)
    for k in range(OWN // 2):
        column = jnp.broadcast_to(by_quad[:, 2 * k : 2 * k + 1], (quads, LABELS))
        chooser[quads * k : quads * (k + 1), :] = (column == names).astype(jnp.bfloat16)


def halo_kernel(small, below, above, *refs):
    outs, field, doubled = refs[8:16], refs[16], refs[17]
    for t, edge in ((0, below), (CHUNKS - 1, above)):
        outs[5][:, 8 * t : 8 * t + 8, :] = edge[21]
        start_rows(
            t,
            [{i: edge[i, x] for i in range(19)} for x in range(2)],
            [edge[19, x] for x in range(2)],
            [edge[20, x].astype(jnp.int32) for x in range(2)],
            small[3, 0, 0:2, :],
            outs,
        )
    flow, effective, send_left, send_right = outs[1], outs[3], outs[6], outs[7]

    def place(t):
        for x in range(2):
            value = effective[x, flat(t), :]
            field[x, tall(t), :] = value
            doubled[x, tall(t), :] = with_sides(value)

    each_chunk(place)
    each_chunk(functools.partial(send_flow, START, send_left, send_right, flow, field, doubled))


def put_field(field, doubled, p, t, value):
    field[p, tall(t), :] = value
    doubled[p, tall(t), :] = with_sides(value)


def put_masks(masks, p, t, share):
    masks[0, p, tall(t), :] = share
    masks[1, p, tall(t), :] = rolled(share, 1)
    masks[2, p, tall(t), :] = rolled(share, -1)


def first_flight_kernel(effective, share, masks, field, doubled):
    def body(t):
        for x in range(2):
            put_field(field, doubled, 2 + x, t, effective[x, flat(t), :])
            put_masks(masks, 2 + x, t, share[x, flat(t), :])

    each_chunk(body)


def second_flight_kernel(state, effective, share, field, doubled, lin):
    def body(t):
        for x in range(2):
            put_field(field, doubled, 2 + x, t, effective[x, flat(t), :])
            f = {i: state[i, x, flat(t), :] for i in range(19)}
            linear = linear_part(f, share[x, flat(t), :], range(19))[2]
            for i in range(19):
                lin[i, x, flat(t), :] = linear[i]

    each_chunk(body)


def step_kernel(is_first, *refs):
    if is_first:
        (lin, flow, density, effective, share, from_left, from_right, _, _, _,
         masks, field, doubled, speed, pull_out, state_out, flow_out, density_out, effective_out,
         send_left, send_right,
         relaxed, turned, next_field, next_doubled) = refs
    else:
        (lin, flow, density, share, target, masks, from_left, from_right, _, _,
         field, doubled, speed, pull_out, misfit_out, send_left, send_right,
         relaxed, turned) = refs

    packed = START if is_first else SECOND

    def place(t):
        for near, come, which in ((1, from_left, RIGHTWARD), (4, from_right, LEFTWARD)):
            s = packed[which].get(come, 9, t) if is_first else masks[0, near, tall(t), :]
            chosen = packed[which].get(come, 8, t)
            put_field(field, doubled, near, t, jnp.where(s > 0, 1.0 - jnp.exp(-chosen), chosen))
            if is_first:
                put_masks(masks, near, t, s)

    each_chunk(place)

    def collide(t):
        for p in range(1, 5):
            psi = field[p, tall(t), :]
            s = masks[0, p, tall(t), :]
            if p in (2, 3):
                pull = gradient_of(field, doubled, p, t)
                rho = density[p - 2, flat(t), :]
                mom = [flow[a, p - 2, flat(t), :] for a in range(3)]
                which = range(19)
                lin_at = {i: lin[i, p - 2, flat(t), :] for i in which}
                for a in range(3):
                    pull_out[a, p - 2, flat(t), :] = pull[a]
            else:
                pull = outer_gradient(field, doubled, p, 2 if p == 1 else 3, t)
                come = from_left if p == 1 else from_right
                which = RIGHTWARD if p == 1 else LEFTWARD
                rho = packed[which].get(come, 8, t)
                mom = [packed[which].get(come, 5 + a, t) for a in range(3)]
                lin_at = {i: packed[which].get(come, k, t) for k, i in enumerate(which)}
            push = psi * (PULL / SHEAR)
            full = [mom[a] + push * pull[a] for a in range(3)]
            inverse = 1.0 / rho
            u = [full[a] * inverse for a in range(3)]
            for a in range(3):
                speed[a, p - 1, flat(t), :] = u[a]
            part = balance_part(rho, full, u, s, which)
            for i in which:
                value = lin_at[i] + part[i]
                relaxed[i, p - 1, tall(t), :] = value
                if i in TURNED:
                    turned[TURNED.index(i), p - 1, tall(t), :] = rolled(value, VECTORS[i][2])

    each_chunk(collide, unroll=3)

    def streamed(x, rows):
        f = {0: relaxed[0, 1 + x, rows(0), :]}
        for i in range(1, 19):
            cx, cy, cz = VECTORS[i]
            if cz:
                source = turned[TURNED.index(i), 1 + x - cx, rows(-cy), :]
            else:
                source = relaxed[i, 1 + x - cx, rows(-cy), :]
            open_ = masks[cz % 3, 2 + x - cx, rows(-cy), :] > 0
            f[i] = jnp.where(open_, source, relaxed[OPPOSITE[i], 1 + x, rows(0), :])
        return f

    def stream(t):
        lin_sent, chosen_sent = [], []
        for x in range(2):
            s = share[x, flat(t), :]
            f = streamed(x, lambda dy: tall(t, dy))
            total, momentum, linear = linear_part(f, s, (LEFTWARD, RIGHTWARD)[x])
            held = effective[x, flat(t), :]
            eff = jnp.where(s > 0, 1.0 - jnp.exp(-total), held)
            for i in range(19):
                state_out[i, x, flat(t), :] = f[i]
            for a in range(3):
                flow_out[a, x, flat(t), :] = momentum[a]
            density_out[x, flat(t), :] = total
            effective_out[x, flat(t), :] = eff
            next_field[x, tall(t), :] = eff
            next_doubled[x, tall(t), :] = with_sides(eff)
            lin_sent.append(linear)
            chosen_sent.append(jnp.where(s > 0, total, held))
        put_sends(SECOND, send_left, send_right, t, lin_sent, chosen_sent)

    def compare(t):
        for x, near, far in ((0, send_left, send_right), (1, send_right, send_left)):
            f = streamed(x, lambda dy: mid_tall(t, dy))
            s = share[x, mid(t), :]
            misfit = s * (add(*[f[i] for i in range(19)]) - target[x, mid(t), :])
            misfit_out[x, flat(t), :] = misfit
            near[0, flat(t), :] = misfit
            far[1, flat(t), :] = misfit
            far[2, flat(t), :] = s

    if is_first:
        each_chunk(stream)
        each_chunk(functools.partial(send_flow, SECOND, send_left, send_right, flow_out, next_field, next_doubled))
    else:
        each_chunk(compare, 0, MID // 8)


def spread_of(pulled, pulled_doubled, p, rows):
    at = lambda a, dp, dy: pulled[a, p + dp, rows(dy), :]
    two = lambda a, dp, dy: pulled_doubled[a, p + dp, rows(dy), :]
    along_x = two(0, 1, 0) - two(0, -1, 0) + (at(0, 1, 1) + at(0, 1, -1)) - (at(0, -1, 1) + at(0, -1, -1))
    along_y = two(1, 0, 1) - two(1, 0, -1) + (at(1, 1, 1) + at(1, -1, 1)) - (at(1, 1, -1) + at(1, -1, -1))
    star = 2.0 * at(2, 0, 0) + at(2, 1, 0) + at(2, -1, 0) + at(2, 0, 1) + at(2, 0, -1)
    along_z = rolled(star, -1) - rolled(star, 1)
    return (along_x + along_y + along_z) * (-1.0 / 36.0)


def put_pulled(pulled, pulled_doubled, p, rows, psi, q):
    for a in range(3):
        s = (COUPLING / SHEAR) * psi * q[a]
        pulled[a, p, rows(0), :] = s
        if a < 2:
            pulled_doubled[a, p, rows(0), :] = with_sides(s)


def mask_ahead(masks, i, p, rows):
    cx, cy, cz = VECTORS[i]
    return masks[(-cz) % 3, p + cx, rows(cy), :] > 0


def middle(t):
    return lambda dy: mid_tall(t, dy)


def last_reverse_kernel(
    misfit, from_left, from_right, masks, field, speed, pull, early_speed,
    adjoint, turned, wall_out, send_left, send_right, part_left, part_right,
    ahead, far_masks, pulled, pulled_doubled, base,
):
    def place(t):
        rows = middle(t)
        for p in range(6):
            if p < 2:
                d = from_left[1 - p, flat(t), :]
            elif p < 4:
                d = misfit[p - 2, flat(t), :]
            else:
                d = from_right[p - 4, flat(t), :]
            ahead[0, p, rows(0), :] = d
            ahead[1, p, rows(0), :] = rolled(d, 1)
            ahead[2, p, rows(0), :] = rolled(d, -1)
        for k, source in enumerate((from_left, from_right)):
            s = source[2, flat(t), :]
            far_masks[0, k, rows(0), :] = s
            far_masks[1, k, rows(0), :] = rolled(s, 1)
            far_masks[2, k, rows(0), :] = rolled(s, -1)

    each_chunk(place, 0, MID // 8)

    def collide(t):
        rows = middle(t)
        for p in range(1, 5):
            s = masks[0, p, rows(0), :]
            here = ahead[0, p, rows(0), :]
            r = {0: here}
            for i in range(1, 19):
                cx, cy, cz = VECTORS[i]
                there = ahead[(-cz) % 3, p + cx, rows(cy), :]
                if p + cx in (0, 5):
                    open_ = far_masks[(-cz) % 3, (p + cx) // 5, rows(cy), :] > 0
                else:
                    open_ = mask_ahead(masks, i, p, rows)
                r[i] = jnp.where(open_, there, here)
            psi = field[p, rows(0), :]
            u = [speed[a, p - 1, mid(t), :] for a in range(3)]
            if p in (2, 3):
                rest, by_density, q = collide_adjoint(r, u)
                along = add(*[q[a] * pull[a, p - 2, mid(t), :] for a in range(3)])
                const = by_density + along * ((PULL / SHEAR) * (1.0 - psi))
                for i in range(19):
                    base[i, p - 2, flat(t), :] = rest[i] + const
            else:
                q = flow_adjoint(*dual(r), u)
            put_pulled(pulled, pulled_doubled, p - 1, rows, s * psi, q)

    each_chunk(collide, 0, MID // 8)

    def finish(t):
        rows = middle(t)
        for x in range(2):
            s = masks[0, 2 + x, rows(0), :]
            spread = spread_of(pulled, pulled_doubled, 1 + x, rows)
            wall_out[x, flat(t), :] = (1.0 - s) * spread
            more = s * spread * (1.0 - field[2 + x, rows(0), :])
            for i in range(19):
                value = base[i, x, flat(t), :] + more
                adjoint[i, x, rows(0), :] = value
                if i in TURNED:
                    turned[TURNED.index(i), x, rows(0), :] = rolled(value, -VECTORS[i][2])

    each_chunk(finish, 0, MID // 8)

    def part(t):
        rows = middle(t)
        for x, send, kept, sent, skipped in ((0, send_left, part_left, RIGHTWARD, -1), (1, send_right, part_right, LEFTWARD, 1)):
            p = 2 + x
            s = masks[0, p, rows(0), :]
            r = {}
            for i in range(19):
                if VECTORS[i][0] != skipped:
                    r[i] = adjoint_ahead(adjoint, turned, masks, i, x, rows)
            u = [early_speed[a, p - 1, mid(t), :] for a in range(3)]
            q = flow_adjoint(*dual(r), u)
            for a in range(3):
                BACK[sent].put(send, 5 + a, t, s * q[a])
                kept[a, flat(t), :] = s * q[a]
            for k, i in enumerate(sent):
                BACK[sent].put(send, k, t, adjoint[i, x, rows(0), :])

    each_chunk(part, 0, MID // 8)


def adjoint_ahead(adjoint, turned, masks, i, x, rows):
    cx, cy, cz = VECTORS[i]
    if i == 0:
        return adjoint[0, x, rows(0), :]
    if cz:
        there = turned[TURNED.index(i), x + cx, rows(cy), :]
    else:
        there = adjoint[i, x + cx, rows(cy), :]
    return jnp.where(mask_ahead(masks, i, 2 + x, rows), there, adjoint[OPPOSITE[i], x, rows(0), :])


def place_sides(come, from_left, from_right, t):
    for side, source, which in ((0, from_left, LEFTWARD), (1, from_right, RIGHTWARD)):
        for k, i in enumerate(which):
            come[side, k, mid_tall(t), :] = rolled(BACK[which].get(source, k, t), -VECTORS[i][2])


def arrived(come, adjoint, masks, i, x, rows):
    which = LEFTWARD if x == 0 else RIGHTWARD
    there = come[x, which.index(i), rows(VECTORS[i][1]), :]
    return jnp.where(mask_ahead(masks, i, 2 + x, rows), there, adjoint[OPPOSITE[i], x, rows(0), :])


def wall_kernel(
    adjoint, turned, wall, part_left, part_right, from_left, from_right, masks, field, speed, chooser,
    more_out, label_part,
    come, pulled, pulled_doubled, totals,
):
    each_chunk(functools.partial(place_sides, come, from_left, from_right), 0, MID // 8)

    def collide(t):
        rows = middle(t)
        for x, part, which in ((0, part_left, LEFTWARD), (1, part_right, RIGHTWARD)):
            p = 2 + x
            s = masks[0, p, rows(0), :]
            r = {i: arrived(come, adjoint, masks, i, x, rows) for i in which}
            u = [speed[a, p - 1, mid(t), :] for a in range(3)]
            rest = flow_adjoint(*dual(r), u)
            q = [part[a, flat(t), :] + s * rest[a] for a in range(3)]
            put_pulled(pulled, pulled_doubled, p - 1, rows, field[p, rows(0), :], q)
        for x, source, which in ((0, from_left, LEFTWARD), (1, from_right, RIGHTWARD)):
            p = 1 if x == 0 else 4
            s = masks[0, p, rows(0), :]
            r = {}
            for i in [OPPOSITE[j] for j in which]:
                cx, cy, cz = VECTORS[i]
                if cz:
                    there = turned[TURNED.index(i), x, rows(cy), :]
                else:
                    there = adjoint[i, x, rows(cy), :]
                here = BACK[which].get(source, which.index(OPPOSITE[i]), t)
                r[i] = jnp.where(mask_ahead(masks, i, p, rows), there, here)
            u = [speed[a, p - 1, mid(t), :] for a in range(3)]
            rest = flow_adjoint(*dual(r), u)
            q = [BACK[which].get(source, 5 + a, t) + s * rest[a] for a in range(3)]
            put_pulled(pulled, pulled_doubled, p - 1, rows, field[p, rows(0), :], q)

    each_chunk(collide, 0, MID // 8)

    def finish(t):
        total = None
        for x in range(2):
            s = masks[0, 2 + x, tall(t), :]
            spread = spread_of(pulled, pulled_doubled, 1 + x, lambda dy: tall(t, dy))
            step_wall = wall[x, pl.ds(t * 8 - (ROWS - MID) // 2, 8), :]
            total = add(total, (1.0 - s) * spread + step_wall)
            more_out[x, rows_at(t, 0, -HALO), :] = s * spread * (1.0 - field[2 + x, tall(t), :])
        totals[rows_at(t, 0, -HALO), :] = total

    each_chunk(finish, HALO // 8, (HALO + OWN) // 8)

    blocks = (OWN // 2) * (DEPTH // 4)
    column = lax.broadcasted_iota(jnp.int32, (DEPTH, blocks), 1)
    quad = lax.broadcasted_iota(jnp.int32, (DEPTH, blocks), 0) // 4
    gather = (jnp.bitwise_and(column, DEPTH // 4 - 1) == quad).astype(jnp.bfloat16)
    by_block = exact_dot(totals[...], gather)
    pair = lax.broadcasted_iota(jnp.int32, (OWN, blocks), 0) // 2
    wanted = lax.broadcasted_iota(jnp.int32, (OWN, blocks), 1) // (DEPTH // 4)
    by_block = jnp.where(pair == wanted, by_block, 0.0)
    by_label = exact_dot(by_block, chooser[...])
    label_part[...] = jnp.sum(by_label, axis=0, keepdims=True)


def grad_kernel(
    adjoint, turned, more, from_left, from_right, masks, field, speed, pull,
    grad,
    come,
):
    each_chunk(functools.partial(place_sides, come, from_left, from_right), 0, MID // 8)

    def collide(t):
        rows = lambda dy: tall(t, dy)
        for x in range(2):
            p = 2 + x
            s = masks[0, p, tall(t), :]
            r = {}
            for i in range(19):
                if VECTORS[i][0] == 2 * x - 1:
                    r[i] = s * arrived(come, adjoint, masks, i, x, rows)
                else:
                    r[i] = s * adjoint_ahead(adjoint, turned, masks, i, x, rows)
            u = [speed[a, p - 1, flat(t), :] for a in range(3)]
            rest, by_density, q = collide_adjoint(r, u)
            along = add(*[q[a] * pull[a, x, flat(t), :] for a in range(3)])
            const = by_density + along * ((PULL / SHEAR) * (1.0 - field[p, tall(t), :]))
            const = const + more[x, rows_at(t, 0, -HALO), :]
            for i in range(19):
                grad[i, x, rows_at(t, 0, -HALO), :] = rest[i] + const

    each_chunk(collide, HALO // 8, (HALO + OWN) // 8)


def exact_dot(values, zero_one):
    rows = values.shape[0]
    high = values.astype(jnp.bfloat16)
    left = values - high.astype(jnp.float32)
    middle = left.astype(jnp.bfloat16)
    low = (left - middle.astype(jnp.float32)).astype(jnp.bfloat16)
    parts = jnp.concatenate([high, middle, low], axis=0)
    sums = jnp.dot(parts, zero_one, preferred_element_type=jnp.float32)
    return sums[:rows] + (sums[rows : 2 * rows] + sums[2 * rows :])


def call(kernel, args, outs, scratch, anywhere=0, grant=12, filled=0):
    whole = pl.BlockSpec(memory_space=pltpu.VMEM)
    there = pl.BlockSpec(memory_space=pl.ANY)
    size = sum(a.size * a.dtype.itemsize for a in args)
    return pl.pallas_call(
        kernel,
        out_shape=[s if hasattr(s, "dtype") else jax.ShapeDtypeStruct(s, jnp.float32) for s in outs],
        in_specs=[there] * anywhere + [whole] * (len(args) - anywhere),
        out_specs=[whole] * len(outs),
        scratch_shapes=scratch,
        input_output_aliases={len(args) - filled + k: k for k in range(filled)},
        compiler_params=pltpu.CompilerParams(vmem_limit_bytes=grant * 1024 * 1024),
        cost_estimate=pl.CostEstimate(flops=0, bytes_accessed=size, transcendentals=0),
    )(*[pltpu.with_memory_space_constraint(a, pltpu.HBM) for a in args[:anywhere]], *args[anywhere:])


def ring(axis):
    count = lax.axis_size(axis)
    up = [(i, (i + 1) % count) for i in range(count)]
    return up, [(j, i) for i, j in up]


def both_ways(to_lower, to_upper, axis):
    up, down = ring(axis)
    from_lower = lax.ppermute(to_upper, axis, up)
    from_upper = lax.ppermute(to_lower, axis, down)
    return from_lower, from_upper


def per_device(populations, fluid, label, wall_wetting, target):
    vmem = lambda *shape: pltpu.VMEM(shape, jnp.float32)
    plane = (ROWS, DEPTH)
    two = (2, *plane)
    edge = (22, 2, HALO, DEPTH)
    low, high, small = call(
        edges_kernel,
        (populations, fluid, label, target, wall_wetting.reshape(2, DEPTH)),
        (edge, edge, (4, 2, OWN, DEPTH)),
        (
            pltpu.VMEM((2, 2, OWN, DEPTH), jnp.int32),
            vmem(2, DEPTH),
            pltpu.SemaphoreType.DMA((6,)),
        ),
        anywhere=5,
    )
    below, above = both_ways(low, high, "gy")
    blocks = (OWN // 2) * (DEPTH // 4)
    started = ((19, *two), (3, *two), two, two, two, two, START[LEFTWARD].shape, START[RIGHTWARD].shape)
    *own, chooser = call(
        own_kernel,
        (populations, small),
        (*started, jax.ShapeDtypeStruct((blocks, LABELS), jnp.bfloat16)),
        (vmem(DEPTH, OWN),),
    )
    beside = (vmem(2, TALL, DEPTH), vmem(2, TALL, DEPTH))
    lin, flow, density, effective, share, target_wide, to_left, to_right = call(
        halo_kernel, (small, below, above, *own), started, beside, filled=len(started)
    )
    from_left, from_right = both_ways(to_left, to_right, "gx")
    wide6 = (6, TALL, DEPTH)
    work = (vmem(19, 4, TALL, DEPTH), vmem(10, 4, TALL, DEPTH))
    begun = call(first_flight_kernel, (effective, share), ((3, *wide6), wide6, wide6), ())
    masks, field0, _, speed0, pull0, state, flow, density, effective, to_left, to_right = call(
        functools.partial(step_kernel, True),
        (lin, flow, density, effective, share, from_left, from_right, *begun),
        (
            (3, *wide6), wide6, wide6, (3, 4, *plane), (3, *two),
            (19, *two), (3, *two), two, two, SECOND[LEFTWARD].shape, SECOND[RIGHTWARD].shape,
        ),
        (*work, *beside),
        filled=3,
    )
    from_left, from_right = both_ways(to_left, to_right, "gx")
    less = (MID, DEPTH)
    field1, doubled, lin = call(
        second_flight_kernel, (state, effective, share), (wide6, wide6, (19, *two)), ()
    )
    field1, _, speed1, pull1, misfit, to_left, to_right = call(
        functools.partial(step_kernel, False),
        (lin, flow, density, share, target_wide, masks, from_left, from_right, field1, doubled),
        (wide6, wide6, (3, 4, *plane), (3, *two), (2, *less), (3, *less), (3, *less)),
        work,
        filled=2,
    )
    from_left, from_right = both_ways(to_left, to_right, "gx")
    pulled = (vmem(3, 4, TALL, DEPTH), vmem(2, 4, TALL, DEPTH))
    adjoint, turned, wall, to_left, to_right, part_left, part_right = call(
        last_reverse_kernel,
        (misfit, from_left, from_right, masks, field1, speed1, pull1, speed0),
        ((19, 2, TALL, DEPTH), (10, 2, TALL, DEPTH), (2, *less), BACK[RIGHTWARD].shape, BACK[LEFTWARD].shape, (3, *less), (3, *less)),
        (vmem(3, *wide6), vmem(3, 2, TALL, DEPTH), *pulled, vmem(19, 2, *less)),
    )
    from_left, from_right = both_ways(to_left, to_right, "gx")
    come = vmem(2, 5, TALL, DEPTH)
    more, label_part = call(
        wall_kernel,
        (adjoint, turned, wall, part_left, part_right, from_left, from_right, masks, field0, speed0, chooser),
        ((2, OWN, DEPTH), (1, LABELS)),
        (come, *pulled, vmem(OWN, DEPTH)),
    )
    count = lax.axis_size("gy")
    wetting_grad = label_part
    for step in range(1, count):
        wetting_grad = wetting_grad + lax.ppermute(
            label_part, "gy", [(i, (i + step) % count) for i in range(count)]
        )
    (grad,) = call(
        grad_kernel,
        (adjoint, turned, more, from_left, from_right, masks, field0, speed0, pull0),
        (populations.shape,),
        (come,),
    )
    return (grad, wetting_grad.reshape(-1))


def solution(mesh):
    return jax.shard_map(
        per_device,
        mesh=mesh,
        in_specs=(
            P(None, "gx", "gy", None),
            P("gx", "gy", None),
            P("gx", "gy", None),
            P("gx"),
            P("gx", "gy", None),
        ),
        out_specs=(P(None, "gx", "gy", None), P("gx")),
        check_vma=False,
    )
```

```python
import functools

import jax
import jax.numpy as jnp
from jax import lax
from jax.experimental import pallas as pl
from jax.experimental.pallas import tpu as pltpu
from jax.sharding import PartitionSpec as P

HALO = 8
PAD = 8
OWN = 32
ROWS = OWN + 2 * HALO
TALL = ROWS + 2 * PAD
MID = OWN + HALO
DEPTH = 128
CHUNKS = ROWS // 8
LABELS = 256

VECTORS = (
    (0, 0, 0), (1, 0, 0), (-1, 0, 0), (0, 1, 0), (0, -1, 0), (0, 0, 1), (0, 0, -1),
    (1, 1, 0), (-1, -1, 0), (1, -1, 0), (-1, 1, 0), (1, 0, 1), (-1, 0, -1), (1, 0, -1), (-1, 0, 1),
    (0, 1, 1), (0, -1, -1), (0, 1, -1), (0, -1, 1),
)
OPPOSITE = (0, 2, 1, 4, 3, 6, 5, 8, 7, 10, 9, 12, 11, 14, 13, 16, 15, 18, 17)
INDEX = {v: i for i, v in enumerate(VECTORS)}
RIGHTWARD = tuple(i for i in range(19) if VECTORS[i][0] == 1)
LEFTWARD = tuple(i for i in range(19) if VECTORS[i][0] == -1)
TURNED = tuple(i for i in range(19) if VECTORS[i][2] != 0)
PLANES = ((0, 1), (1, 2), (0, 2))
COUPLING = 5.0
SHEAR = 1.2
BULK = 1.19
THIRD = 1.5
FOURTH = 1.4
TRACE = (BULK - SHEAR) / 3.0
PULL = COUPLING / 36.0


def axis_index_of(axis, sign):
    v = [0, 0, 0]
    v[axis] = sign
    return INDEX[tuple(v)]


def edge_index_of(a, b, sa, sb):
    v = [0, 0, 0]
    v[a], v[b] = sa, sb
    return INDEX[tuple(v)]


def add(*terms):
    total = None
    for term in terms:
        if term is not None:
            total = term if total is None else total + term
    return total


def sub(a, b):
    if b is None:
        return a
    return -b if a is None else a - b


def scale(c, a):
    return None if a is None else c * a


def mul(a, b):
    return None if a is None or b is None else a * b


def moments(f):
    fourth, mixed, third = {}, {}, {}
    for a, b in PLANES:
        pp, mm = f[edge_index_of(a, b, 1, 1)], f[edge_index_of(a, b, -1, -1)]
        pm, mp = f[edge_index_of(a, b, 1, -1)], f[edge_index_of(a, b, -1, 1)]
        even, odd, cross, skew = pp + mm, pp - mm, pm + mp, pm - mp
        fourth[a, b] = even + cross
        mixed[a, b] = even - cross
        third[a, b] = odd + skew
        third[b, a] = odd - skew
    first, diagonal, total = [], [], f[0]
    for a in range(3):
        b, c = [k for k in range(3) if k != a]
        plus, minus = f[axis_index_of(a, 1)], f[axis_index_of(a, -1)]
        both = plus + minus
        total = total + both
        diagonal.append(both + fourth[tuple(sorted((a, b)))] + fourth[tuple(sorted((a, c)))])
        first.append((plus - minus) + third[a, b] + third[a, c])
    total = total + fourth[0, 1] + fourth[1, 2] + fourth[0, 2]
    return total, first, diagonal, mixed, third, fourth


def from_moments(first, diagonal, mixed, third, fourth, which):
    out = {}
    for a, b in PLANES:
        even, cross = fourth[a, b] + mixed[a, b], fourth[a, b] - mixed[a, b]
        odd, skew = third[a, b] + third[b, a], third[a, b] - third[b, a]
        out[edge_index_of(a, b, 1, 1)] = even + odd
        out[edge_index_of(a, b, -1, -1)] = even - odd
        out[edge_index_of(a, b, 1, -1)] = cross + skew
        out[edge_index_of(a, b, -1, 1)] = cross - skew
    for a in range(3):
        b, c = [k for k in range(3) if k != a]
        even = diagonal[a] - 2.0 * (fourth[tuple(sorted((a, b)))] + fourth[tuple(sorted((a, c)))])
        odd = first[a] - 2.0 * (third[a, b] + third[a, c])
        out[axis_index_of(a, 1)] = even + odd
        out[axis_index_of(a, -1)] = even - odd
    out[0] = 4.0 * (fourth[0, 1] + fourth[1, 2] + fourth[0, 2]) - 2.0 * (diagonal[0] + diagonal[1] + diagonal[2])
    return {i: out[i] for i in which}


def linear_part(f, share, which):
    total, first, diagonal, mixed, third, fourth = moments(f)
    half, quarter = (0.5 * SHEAR) * share, (0.25 * SHEAR) * share
    trace = (0.5 * TRACE) * share * (diagonal[0] + diagonal[1] + diagonal[2])
    by_third, by_fourth = (0.25 * THIRD) * share, (0.25 * FOURTH) * share
    change = from_moments(
        [half * m for m in first],
        [half * m + trace for m in diagonal],
        {k: quarter * m for k, m in mixed.items()},
        {k: by_third * m for k, m in third.items()},
        {k: by_fourth * m for k, m in fourth.items()},
        which,
    )
    return total, first, {i: f[i] - change[i] for i in which}


def balance_part(density, flow, velocity, share, which):
    d = density * share
    m = [flow[a] * share for a in range(3)]
    square = [m[a] * velocity[a] for a in range(3)]
    whole = square[0] + square[1] + square[2]
    level = d * (SHEAR / 6.0 + 0.5 * TRACE) + whole * (0.5 * TRACE)
    diagonal = [(0.5 * SHEAR) * square[a] + level for a in range(3)]
    scaled = [(0.25 * SHEAR) * velocity[a] for a in range(3)]
    mixed = {(a, b): m[a] * scaled[b] for a, b in PLANES}
    part = [(THIRD / 12.0) * m[a] for a in range(3)]
    third = {}
    fourth = {}
    level = d * (FOURTH / 36.0) + whole * (FOURTH / 12.0)
    for a, b in PLANES:
        third[a, b], third[b, a] = part[a], part[b]
        fourth[a, b] = level - (FOURTH / 8.0) * square[3 - a - b]
    return from_moments([(0.5 * SHEAR) * m[a] for a in range(3)], diagonal, mixed, third, fourth, which)


def dual(r):
    rest = r.get(0)
    even_of, odd_of = [], []
    for a in range(3):
        plus, minus = r.get(axis_index_of(a, 1)), r.get(axis_index_of(a, -1))
        even_of.append(add(plus, minus))
        odd_of.append(sub(plus, minus))
    trace = add(scale(0.5 * TRACE, add(*even_of)), scale(-3.0 * TRACE - SHEAR, rest))
    first = [scale(0.5 * SHEAR, odd) for odd in odd_of]
    diagonal = [add(scale(0.5 * SHEAR, even), trace) for even in even_of]
    even_part = [scale(0.5 * FOURTH, even) for even in even_of]
    odd_part = [scale(0.5 * THIRD, odd) for odd in odd_of]
    rest_part = scale(FOURTH, rest)
    mixed, third, fourth = {}, {}, {}
    for a, b in PLANES:
        pp, mm = r.get(edge_index_of(a, b, 1, 1)), r.get(edge_index_of(a, b, -1, -1))
        pm, mp = r.get(edge_index_of(a, b, 1, -1)), r.get(edge_index_of(a, b, -1, 1))
        even, odd, cross, skew = add(pp, mm), sub(pp, mm), add(pm, mp), sub(pm, mp)
        whole = scale(0.25 * FOURTH, add(even, cross))
        fourth[a, b] = add(sub(sub(whole, even_part[a]), even_part[b]), rest_part)
        mixed[a, b] = scale(0.25 * SHEAR, sub(even, cross))
        third[a, b] = sub(scale(0.25 * THIRD, add(odd, skew)), odd_part[a])
        third[b, a] = sub(scale(0.25 * THIRD, sub(odd, skew)), odd_part[b])
    return first, diagonal, mixed, third, fourth


def flow_adjoint(first, diagonal, mixed, third, fourth, u):
    level = scale(2.0 / 3.0, add(*fourth.values()))
    q = []
    for a in range(3):
        b, c = [k for k in range(3) if k != a]
        ab, ac, bc = tuple(sorted((a, b))), tuple(sorted((a, c))), tuple(sorted((b, c)))
        along = sub(add(scale(2.0, diagonal[a]), level), fourth[bc])
        q.append(
            add(
                first[a],
                scale(1.0 / 3.0, add(third[a, b], third[a, c])),
                mul(u[a], along),
                mul(u[b], mixed[ab]),
                mul(u[c], mixed[ac]),
            )
        )
    return q


def collide_adjoint(r, u):
    t = dual(r)
    first, diagonal, mixed, third, fourth = t
    q = flow_adjoint(*t, u)
    square = [u[a] * u[a] for a in range(3)]
    by_density = None
    for a in range(3):
        b, c = [k for k in range(3) if k != a]
        by_density = add(
            by_density,
            u[a] * (first[a] + (1.0 / 3.0) * (third[a, b] + third[a, c]) - q[a]),
            diagonal[a] * (1.0 / 3.0 + square[a]),
        )
    level = 1.0 / 9.0 + (square[0] + square[1] + square[2]) * (1.0 / 3.0)
    by_density = by_density + (fourth[0, 1] + fourth[1, 2] + fourth[0, 2]) * level
    by_density = by_density - 0.5 * add(*[fourth[a, b] * square[3 - a - b] for a, b in PLANES])
    by_density = by_density + add(*[mixed[a, b] * (u[a] * u[b]) for a, b in PLANES])
    drift = [q[a] - first[a] for a in range(3)]
    base = {0: r[0]}
    for a in range(3):
        base[axis_index_of(a, 1)] = r[axis_index_of(a, 1)] + (drift[a] - diagonal[a])
        base[axis_index_of(a, -1)] = r[axis_index_of(a, -1)] - (drift[a] + diagonal[a])
    for a, b in PLANES:
        along = drift[a] - third[a, b]
        across = drift[b] - third[b, a]
        even = diagonal[a] + diagonal[b] + fourth[a, b]
        same, cross = even + mixed[a, b], even - mixed[a, b]
        both, gap = along + across, along - across
        base[edge_index_of(a, b, 1, 1)] = r[edge_index_of(a, b, 1, 1)] + (both - same)
        base[edge_index_of(a, b, -1, -1)] = r[edge_index_of(a, b, -1, -1)] - (both + same)
        base[edge_index_of(a, b, 1, -1)] = r[edge_index_of(a, b, 1, -1)] + (gap - cross)
        base[edge_index_of(a, b, -1, 1)] = r[edge_index_of(a, b, -1, 1)] - (gap + cross)
    return base, by_density, q


def rolled(x, step):
    return x if step == 0 else pltpu.roll(x, step % DEPTH, 1)


def rows_at(t, shift, offset):
    if isinstance(t, int):
        return pl.ds(t * 8 + offset + shift, 8)
    if shift == 0:
        return pl.ds(pl.multiple_of(t * 8 + offset, 8), 8)
    return pl.ds(t * 8 + (offset + shift), 8)


def flat(t):
    return rows_at(t, 0, 0)


def tall(t, shift=0):
    return rows_at(t, shift, PAD)


def mid(t):
    return pl.ds(t * 8 + (ROWS - MID) // 2, 8)


def mid_tall(t, shift=0):
    return pl.ds(t * 8 + ((ROWS - MID) // 2 + PAD + shift), 8)


class Packed:
    def __init__(self, spans, limit):
        self.spans, self.shift, at = spans, [], spans[0][0]
        for low, high in spans:
            self.shift.append(at - low)
            at += high - low
        self.shape = (-(-(max(self.shift) + limit) // 8) * 8, DEPTH)

    def put(self, ref, k, t, value):
        low, high = max(8 * t, self.spans[k][0]), min(8 * t + 8, self.spans[k][1])
        if low < high:
            ref[self.shift[k] + low : self.shift[k] + high, :] = value[low - 8 * t : high - 8 * t, :]

    def get(self, ref, k, t):
        return ref[pl.ds(8 * t + self.shift[k], 8), :]


def step_spans(first, last, which, more):
    return [(first - VECTORS[i][1], last - VECTORS[i][1]) for i in which] + [(first - 1, last + 1)] * 3 + more


def adjoint_spans(which):
    first, last = (MID - OWN) // 2 - 1, (MID + OWN) // 2 + 1
    rows = [(first + min(VECTORS[i][1], 0), last + max(VECTORS[i][1], 0)) for i in which]
    return rows + [(first, last)] * 3


START = {
    which: Packed(step_spans(2, ROWS - 2, which, [(0, ROWS)] * 2), ROWS) for which in (LEFTWARD, RIGHTWARD)
}
SECOND = {
    which: Packed(step_spans(4, ROWS - 4, which, [(2, ROWS - 2)]), ROWS) for which in (LEFTWARD, RIGHTWARD)
}
BACK = {which: Packed(adjoint_spans(which), MID) for which in (LEFTWARD, RIGHTWARD)}


def each_chunk(body, first=0, last=CHUNKS, unroll=0):
    if unroll == 0:
        for t in range(first, last):
            body(t)
        return

    def step(t, carry):
        body(t)
        return carry

    lax.fori_loop(first, last, step, 0, unroll=unroll)


def gradient_of(field, doubled, p, t):
    at = lambda dp, dy: field[p + dp, tall(t, dy), :]
    rp, rm, lp, lm = at(1, 1), at(1, -1), at(-1, 1), at(-1, -1)
    along_x = doubled[p + 1, tall(t), :] - doubled[p - 1, tall(t), :] + (rp + rm) - (lp + lm)
    along_y = doubled[p, tall(t, 1), :] - doubled[p, tall(t, -1), :] + (rp + lp) - (rm + lm)
    star = 2.0 * at(0, 0) + at(1, 0) + at(-1, 0) + at(0, 1) + at(0, -1)
    return [along_x, along_y, rolled(star, -1) - rolled(star, 1)]


def with_sides(x):
    return 2.0 * x + rolled(x, 1) + rolled(x, -1)


def inner_gradient(field, doubled, here, inner, t):
    at = lambda x, dy: field[x, tall(t, dy), :]
    up, down = at(inner, 1), at(inner, -1)
    along_x = doubled[inner, tall(t), :] + (up + down)
    along_y = doubled[here, tall(t, 1), :] - doubled[here, tall(t, -1), :] + (up - down)
    star = 2.0 * at(here, 0) + at(inner, 0) + at(here, 1) + at(here, -1)
    return [along_x if inner > here else -along_x, along_y, rolled(star, -1) - rolled(star, 1)]


def outer_gradient(field, doubled, p, inner, t):
    at = lambda dy: field[inner, tall(t, dy), :]
    up, down, here = at(1), at(-1), at(0)
    along_x = doubled[inner, tall(t), :] + (up + down)
    return [along_x if inner > p else -along_x, up - down, rolled(here, -1) - rolled(here, 1)]


def send_flow(packed, send_left, send_right, flow, field, doubled, t):
    for send, which, here, inner in ((send_left, LEFTWARD, 0, 1), (send_right, RIGHTWARD, 1, 0)):
        push = field[here, tall(t), :] * (PULL / SHEAR)
        pull = inner_gradient(field, doubled, here, inner, t)
        for a in range(3):
            packed[which].put(send, 5 + a, t, flow[a, here, flat(t), :] + push * pull[a])


def edges_kernel(pops, fluid, label, target, table, low, high, small, whole, values, sems):
    copies = []

    def copy(source, goal):
        one = pltpu.make_async_copy(source, goal, sems.at[len(copies)])
        one.start()
        copies.append(one)

    copy(fluid, whole.at[0])
    copy(label, whole.at[1])
    copy(table, values)
    copy(target, small.at[2])
    for rows, goal in ((pl.ds(0, HALO), low), (pl.ds(OWN - HALO, HALO), high)):
        copy(target.at[:, rows, :], goal.at[21])
        copy(pops.at[:, :, rows, :], goal.at[pl.ds(0, 19)])
    for one in copies[:3]:
        one.wait()
    small[0] = whole[0].astype(jnp.float32)
    small[1] = whole[1].astype(jnp.float32)
    small[3, 0, 0:2, :] = values[...]
    low[19:21] = small[0:2, :, 0:HALO, :]
    high[19:21] = small[0:2, :, OWN - HALO : OWN, :]
    for one in copies[3:]:
        one.wait()


def put_sends(packed, send_left, send_right, t, lin, chosen):
    for x, send, which in ((0, send_left, LEFTWARD), (1, send_right, RIGHTWARD)):
        for k, i in enumerate(which):
            packed[which].put(send, k, t, lin[x][i])
        packed[which].put(send, 8, t, chosen[x])


def start_rows(t, populations, shares, marks, table, outs):
    lin_out, flow_out, density_out, effective_out, share_out, _, send_left, send_right = outs
    half_low = jnp.broadcast_to(table[0:1, :], (8, DEPTH))
    half_high = jnp.broadcast_to(table[1:2, :], (8, DEPTH))
    lin, chosen = [], []
    for x in range(2):
        share = shares[x]
        spot = jnp.bitwise_and(marks[x], DEPTH - 1)
        wall = jnp.where(
            jnp.bitwise_and(marks[x], DEPTH) == 0,
            jnp.take_along_axis(half_low, spot, axis=1),
            jnp.take_along_axis(half_high, spot, axis=1),
        )
        total, momentum, linear = linear_part(populations[x], share, range(19))
        for i in range(19):
            lin_out[i, x, flat(t), :] = linear[i]
        for a in range(3):
            flow_out[a, x, flat(t), :] = momentum[a]
        density_out[x, flat(t), :] = total
        effective_out[x, flat(t), :] = jnp.where(share > 0, 1.0 - jnp.exp(-total), wall)
        share_out[x, flat(t), :] = share
        lin.append(linear)
        chosen.append(jnp.where(share > 0, total, wall))
    put_sends(START, send_left, send_right, t, lin, chosen)
    START[LEFTWARD].put(send_left, 9, t, shares[0])
    START[RIGHTWARD].put(send_right, 9, t, shares[1])


def own_kernel(pops, small, *refs):
    outs, chooser, turned_label = refs[:8], refs[8], refs[9]
    outs[5][:, HALO : HALO + OWN, :] = small[2]

    def body(t):
        rows = rows_at(t, 0, -HALO)
        start_rows(
            t,
            [{i: pops[i, x, rows, :] for i in range(19)} for x in range(2)],
            [small[0, x, rows, :] for x in range(2)],
            [small[1, x, rows, :].astype(jnp.int32) for x in range(2)],
            small[3, 0, 0:2, :],
            outs,
        )

    each_chunk(body, HALO // 8, (HALO + OWN) // 8)

    marks = jnp.bitwise_and(small[1, 0].astype(jnp.int32), LABELS - 1).astype(jnp.float32)
    turned_label[...] = jnp.transpose(marks)
    quads = DEPTH // 4
    by_quad = turned_label[pl.ds(0, quads, stride=4), :]
    names = lax.broadcasted_iota(jnp.int32, (quads, LABELS), 1).astype(jnp.float32)
    for k in range(OWN // 2):
        column = jnp.broadcast_to(by_quad[:, 2 * k : 2 * k + 1], (quads, LABELS))
        chooser[quads * k : quads * (k + 1), :] = (column == names).astype(jnp.bfloat16)


def halo_kernel(small, below, above, *refs):
    outs, field, doubled = refs[8:16], refs[16], refs[17]
    for t, edge in ((0, below), (CHUNKS - 1, above)):
        outs[5][:, 8 * t : 8 * t + 8, :] = edge[21]
        start_rows(
            t,
            [{i: edge[i, x] for i in range(19)} for x in range(2)],
            [edge[19, x] for x in range(2)],
            [edge[20, x].astype(jnp.int32) for x in range(2)],
            small[3, 0, 0:2, :],
            outs,
        )
    flow, effective, send_left, send_right = outs[1], outs[3], outs[6], outs[7]

    def place(t):
        for x in range(2):
            value = effective[x, flat(t), :]
            field[x, tall(t), :] = value
            doubled[x, tall(t), :] = with_sides(value)

    each_chunk(place)
    each_chunk(functools.partial(send_flow, START, send_left, send_right, flow, field, doubled))


def put_field(field, doubled, p, t, value):
    field[p, tall(t), :] = value
    doubled[p, tall(t), :] = with_sides(value)


def put_masks(masks, p, t, share):
    masks[0, p, tall(t), :] = share
    masks[1, p, tall(t), :] = rolled(share, 1)
    masks[2, p, tall(t), :] = rolled(share, -1)


def first_flight_kernel(effective, share, masks, field, doubled):
    def body(t):
        for x in range(2):
            put_field(field, doubled, 2 + x, t, effective[x, flat(t), :])
            put_masks(masks, 2 + x, t, share[x, flat(t), :])

    each_chunk(body)


def second_flight_kernel(state, effective, share, field, doubled, lin):
    def body(t):
        for x in range(2):
            put_field(field, doubled, 2 + x, t, effective[x, flat(t), :])
            f = {i: state[i, x, flat(t), :] for i in range(19)}
            linear = linear_part(f, share[x, flat(t), :], range(19))[2]
            for i in range(19):
                lin[i, x, flat(t), :] = linear[i]

    each_chunk(body)


def step_kernel(is_first, *refs):
    if is_first:
        (lin, flow, density, effective, share, from_left, from_right, _, _, _,
         masks, field, doubled, speed, pull_out, state_out, flow_out, density_out, effective_out,
         send_left, send_right,
         relaxed, turned, next_field, next_doubled) = refs
    else:
        (lin, flow, density, share, target, masks, from_left, from_right, _, _,
         field, doubled, speed, pull_out, misfit_out, send_left, send_right,
         relaxed, turned) = refs

    packed = START if is_first else SECOND

    def place(t):
        for near, come, which in ((1, from_left, RIGHTWARD), (4, from_right, LEFTWARD)):
            s = packed[which].get(come, 9, t) if is_first else masks[0, near, tall(t), :]
            chosen = packed[which].get(come, 8, t)
            put_field(field, doubled, near, t, jnp.where(s > 0, 1.0 - jnp.exp(-chosen), chosen))
            if is_first:
                put_masks(masks, near, t, s)

    each_chunk(place)

    def collide(t):
        for p in range(1, 5):
            psi = field[p, tall(t), :]
            s = masks[0, p, tall(t), :]
            if p in (2, 3):
                pull = gradient_of(field, doubled, p, t)
                rho = density[p - 2, flat(t), :]
                mom = [flow[a, p - 2, flat(t), :] for a in range(3)]
                which = range(19)
                lin_at = {i: lin[i, p - 2, flat(t), :] for i in which}
                for a in range(3):
                    pull_out[a, p - 2, flat(t), :] = pull[a]
            else:
                pull = outer_gradient(field, doubled, p, 2 if p == 1 else 3, t)
                come = from_left if p == 1 else from_right
                which = RIGHTWARD if p == 1 else LEFTWARD
                rho = packed[which].get(come, 8, t)
                mom = [packed[which].get(come, 5 + a, t) for a in range(3)]
                lin_at = {i: packed[which].get(come, k, t) for k, i in enumerate(which)}
            push = psi * (PULL / SHEAR)
            full = [mom[a] + push * pull[a] for a in range(3)]
            inverse = 1.0 / rho
            u = [full[a] * inverse for a in range(3)]
            for a in range(3):
                speed[a, p - 1, flat(t), :] = u[a]
            part = balance_part(rho, full, u, s, which)
            for i in which:
                value = lin_at[i] + part[i]
                relaxed[i, p - 1, tall(t), :] = value
                if i in TURNED:
                    turned[TURNED.index(i), p - 1, tall(t), :] = rolled(value, VECTORS[i][2])

    each_chunk(collide, unroll=3)

    def streamed(x, rows):
        f = {0: relaxed[0, 1 + x, rows(0), :]}
        for i in range(1, 19):
            cx, cy, cz = VECTORS[i]
            if cz:
                source = turned[TURNED.index(i), 1 + x - cx, rows(-cy), :]
            else:
                source = relaxed[i, 1 + x - cx, rows(-cy), :]
            open_ = masks[cz % 3, 2 + x - cx, rows(-cy), :] > 0
            f[i] = jnp.where(open_, source, relaxed[OPPOSITE[i], 1 + x, rows(0), :])
        return f

    def stream(t):
        lin_sent, chosen_sent = [], []
        for x in range(2):
            s = share[x, flat(t), :]
            f = streamed(x, lambda dy: tall(t, dy))
            total, momentum, linear = linear_part(f, s, (LEFTWARD, RIGHTWARD)[x])
            held = effective[x, flat(t), :]
            eff = jnp.where(s > 0, 1.0 - jnp.exp(-total), held)
            for i in range(19):
                state_out[i, x, flat(t), :] = f[i]
            for a in range(3):
                flow_out[a, x, flat(t), :] = momentum[a]
            density_out[x, flat(t), :] = total
            effective_out[x, flat(t), :] = eff
            next_field[x, tall(t), :] = eff
            next_doubled[x, tall(t), :] = with_sides(eff)
            lin_sent.append(linear)
            chosen_sent.append(jnp.where(s > 0, total, held))
        put_sends(SECOND, send_left, send_right, t, lin_sent, chosen_sent)

    def compare(t):
        for x, near, far in ((0, send_left, send_right), (1, send_right, send_left)):
            f = streamed(x, lambda dy: mid_tall(t, dy))
            s = share[x, mid(t), :]
            misfit = s * (add(*[f[i] for i in range(19)]) - target[x, mid(t), :])
            misfit_out[x, flat(t), :] = misfit
            near[0, flat(t), :] = misfit
            far[1, flat(t), :] = misfit
            far[2, flat(t), :] = s

    if is_first:
        each_chunk(stream)
        each_chunk(functools.partial(send_flow, SECOND, send_left, send_right, flow_out, next_field, next_doubled))
    else:
        each_chunk(compare, 0, MID // 8)


def spread_of(pulled, pulled_doubled, p, rows):
    at = lambda a, dp, dy: pulled[a, p + dp, rows(dy), :]
    two = lambda a, dp, dy: pulled_doubled[a, p + dp, rows(dy), :]
    along_x = two(0, 1, 0) - two(0, -1, 0) + (at(0, 1, 1) + at(0, 1, -1)) - (at(0, -1, 1) + at(0, -1, -1))
    along_y = two(1, 0, 1) - two(1, 0, -1) + (at(1, 1, 1) + at(1, -1, 1)) - (at(1, 1, -1) + at(1, -1, -1))
    star = 2.0 * at(2, 0, 0) + at(2, 1, 0) + at(2, -1, 0) + at(2, 0, 1) + at(2, 0, -1)
    along_z = rolled(star, -1) - rolled(star, 1)
    return (along_x + along_y + along_z) * (-1.0 / 36.0)


def put_pulled(pulled, pulled_doubled, p, rows, psi, q):
    for a in range(3):
        s = (COUPLING / SHEAR) * psi * q[a]
        pulled[a, p, rows(0), :] = s
        if a < 2:
            pulled_doubled[a, p, rows(0), :] = with_sides(s)


def mask_ahead(masks, i, p, rows):
    cx, cy, cz = VECTORS[i]
    return masks[(-cz) % 3, p + cx, rows(cy), :] > 0


def middle(t):
    return lambda dy: mid_tall(t, dy)


def put_ahead(ahead, p, rows, value):
    ahead[0, p, rows(0), :] = value
    ahead[1, p, rows(0), :] = rolled(value, 1)
    ahead[2, p, rows(0), :] = rolled(value, -1)


def third_flight_kernel(misfit, ahead):
    def body(t):
        for x in range(2):
            put_ahead(ahead, 2 + x, middle(t), misfit[x, flat(t), :])

    each_chunk(body, 0, MID // 8)


def last_reverse_kernel(
    from_left, from_right, masks, field, speed, pull, early_speed, _,
    ahead, adjoint, turned, wall_out, send_left, send_right, part_left, part_right,
    far_masks, pulled, pulled_doubled, base,
):
    def place(t):
        rows = middle(t)
        for p in (0, 1, 4, 5):
            put_ahead(ahead, p, rows, from_left[1 - p, flat(t), :] if p < 2 else from_right[p - 4, flat(t), :])
        for k, source in enumerate((from_left, from_right)):
            s = source[2, flat(t), :]
            far_masks[0, k, rows(0), :] = s
            far_masks[1, k, rows(0), :] = rolled(s, 1)
            far_masks[2, k, rows(0), :] = rolled(s, -1)

    each_chunk(place, 0, MID // 8)

    def collide(t):
        rows = middle(t)
        for p in range(1, 5):
            s = masks[0, p, rows(0), :]
            here = ahead[0, p, rows(0), :]
            r = {0: here}
            for i in range(1, 19):
                cx, cy, cz = VECTORS[i]
                there = ahead[(-cz) % 3, p + cx, rows(cy), :]
                if p + cx in (0, 5):
                    open_ = far_masks[(-cz) % 3, (p + cx) // 5, rows(cy), :] > 0
                else:
                    open_ = mask_ahead(masks, i, p, rows)
                r[i] = jnp.where(open_, there, here)
            psi = field[p, rows(0), :]
            u = [speed[a, p - 1, mid(t), :] for a in range(3)]
            if p in (2, 3):
                rest, by_density, q = collide_adjoint(r, u)
                along = add(*[q[a] * pull[a, p - 2, mid(t), :] for a in range(3)])
                const = by_density + along * ((PULL / SHEAR) * (1.0 - psi))
                for i in range(19):
                    base[i, p - 2, flat(t), :] = rest[i] + const
            else:
                q = flow_adjoint(*dual(r), u)
            put_pulled(pulled, pulled_doubled, p - 1, rows, s * psi, q)

    each_chunk(collide, 0, MID // 8)

    def finish(t):
        rows = middle(t)
        for x in range(2):
            s = masks[0, 2 + x, rows(0), :]
            spread = spread_of(pulled, pulled_doubled, 1 + x, rows)
            wall_out[x, flat(t), :] = (1.0 - s) * spread
            more = s * spread * (1.0 - field[2 + x, rows(0), :])
            for i in range(19):
                value = base[i, x, flat(t), :] + more
                adjoint[i, x, rows(0), :] = value
                if i in TURNED:
                    turned[TURNED.index(i), x, rows(0), :] = rolled(value, -VECTORS[i][2])

    each_chunk(finish, 0, MID // 8)

    def part(t):
        rows = middle(t)
        for x, send, kept, sent, skipped in ((0, send_left, part_left, RIGHTWARD, -1), (1, send_right, part_right, LEFTWARD, 1)):
            p = 2 + x
            s = masks[0, p, rows(0), :]
            r = {}
            for i in range(19):
                if VECTORS[i][0] != skipped:
                    r[i] = adjoint_ahead(adjoint, turned, masks, i, x, rows)
            u = [early_speed[a, p - 1, mid(t), :] for a in range(3)]
            q = flow_adjoint(*dual(r), u)
            for a in range(3):
                BACK[sent].put(send, 5 + a, t, s * q[a])
                kept[a, flat(t), :] = s * q[a]
            for k, i in enumerate(sent):
                BACK[sent].put(send, k, t, adjoint[i, x, rows(0), :])

    each_chunk(part, 0, MID // 8)


def adjoint_ahead(adjoint, turned, masks, i, x, rows):
    cx, cy, cz = VECTORS[i]
    if i == 0:
        return adjoint[0, x, rows(0), :]
    if cz:
        there = turned[TURNED.index(i), x + cx, rows(cy), :]
    else:
        there = adjoint[i, x + cx, rows(cy), :]
    return jnp.where(mask_ahead(masks, i, 2 + x, rows), there, adjoint[OPPOSITE[i], x, rows(0), :])


def place_sides(come, from_left, from_right, t):
    for side, source, which in ((0, from_left, LEFTWARD), (1, from_right, RIGHTWARD)):
        for k, i in enumerate(which):
            come[side, k, mid_tall(t), :] = rolled(BACK[which].get(source, k, t), -VECTORS[i][2])


def arrived(come, adjoint, masks, i, x, rows):
    which = LEFTWARD if x == 0 else RIGHTWARD
    there = come[x, which.index(i), rows(VECTORS[i][1]), :]
    return jnp.where(mask_ahead(masks, i, 2 + x, rows), there, adjoint[OPPOSITE[i], x, rows(0), :])


def wall_kernel(
    adjoint, turned, wall, part_left, part_right, from_left, from_right, masks, field, speed, chooser,
    more_out, label_part,
    come, pulled, pulled_doubled, totals,
):
    each_chunk(functools.partial(place_sides, come, from_left, from_right), 0, MID // 8)

    def collide(t):
        rows = middle(t)
        for x, part, which in ((0, part_left, LEFTWARD), (1, part_right, RIGHTWARD)):
            p = 2 + x
            s = masks[0, p, rows(0), :]
            r = {i: arrived(come, adjoint, masks, i, x, rows) for i in which}
            u = [speed[a, p - 1, mid(t), :] for a in range(3)]
            rest = flow_adjoint(*dual(r), u)
            q = [part[a, flat(t), :] + s * rest[a] for a in range(3)]
            put_pulled(pulled, pulled_doubled, p - 1, rows, field[p, rows(0), :], q)
        for x, source, which in ((0, from_left, LEFTWARD), (1, from_right, RIGHTWARD)):
            p = 1 if x == 0 else 4
            s = masks[0, p, rows(0), :]
            r = {}
            for i in [OPPOSITE[j] for j in which]:
                cx, cy, cz = VECTORS[i]
                if cz:
                    there = turned[TURNED.index(i), x, rows(cy), :]
                else:
                    there = adjoint[i, x, rows(cy), :]
                here = BACK[which].get(source, which.index(OPPOSITE[i]), t)
                r[i] = jnp.where(mask_ahead(masks, i, p, rows), there, here)
            u = [speed[a, p - 1, mid(t), :] for a in range(3)]
            rest = flow_adjoint(*dual(r), u)
            q = [BACK[which].get(source, 5 + a, t) + s * rest[a] for a in range(3)]
            put_pulled(pulled, pulled_doubled, p - 1, rows, field[p, rows(0), :], q)

    each_chunk(collide, 0, MID // 8)

    def finish(t):
        total = None
        for x in range(2):
            s = masks[0, 2 + x, tall(t), :]
            spread = spread_of(pulled, pulled_doubled, 1 + x, lambda dy: tall(t, dy))
            step_wall = wall[x, pl.ds(t * 8 - (ROWS - MID) // 2, 8), :]
            total = add(total, (1.0 - s) * spread + step_wall)
            more_out[x, rows_at(t, 0, -HALO), :] = s * spread * (1.0 - field[2 + x, tall(t), :])
        totals[rows_at(t, 0, -HALO), :] = total

    each_chunk(finish, HALO // 8, (HALO + OWN) // 8)

    blocks = (OWN // 2) * (DEPTH // 4)
    column = lax.broadcasted_iota(jnp.int32, (DEPTH, blocks), 1)
    quad = lax.broadcasted_iota(jnp.int32, (DEPTH, blocks), 0) // 4
    gather = (jnp.bitwise_and(column, DEPTH // 4 - 1) == quad).astype(jnp.bfloat16)
    by_block = exact_dot(totals[...], gather)
    pair = lax.broadcasted_iota(jnp.int32, (OWN, blocks), 0) // 2
    wanted = lax.broadcasted_iota(jnp.int32, (OWN, blocks), 1) // (DEPTH // 4)
    by_block = jnp.where(pair == wanted, by_block, 0.0)
    by_label = exact_dot(by_block, chooser[...])
    label_part[...] = jnp.sum(by_label, axis=0, keepdims=True)


def grad_kernel(
    adjoint, turned, more, from_left, from_right, masks, field, speed, pull,
    grad,
    come,
):
    each_chunk(functools.partial(place_sides, come, from_left, from_right), 0, MID // 8)

    def collide(t):
        rows = lambda dy: tall(t, dy)
        for x in range(2):
            p = 2 + x
            s = masks[0, p, tall(t), :]
            r = {}
            for i in range(19):
                if VECTORS[i][0] == 2 * x - 1:
                    r[i] = s * arrived(come, adjoint, masks, i, x, rows)
                else:
                    r[i] = s * adjoint_ahead(adjoint, turned, masks, i, x, rows)
            u = [speed[a, p - 1, flat(t), :] for a in range(3)]
            rest, by_density, q = collide_adjoint(r, u)
            along = add(*[q[a] * pull[a, x, flat(t), :] for a in range(3)])
            const = by_density + along * ((PULL / SHEAR) * (1.0 - field[p, tall(t), :]))
            const = const + more[x, rows_at(t, 0, -HALO), :]
            for i in range(19):
                grad[i, x, rows_at(t, 0, -HALO), :] = rest[i] + const

    each_chunk(collide, HALO // 8, (HALO + OWN) // 8)


def exact_dot(values, zero_one):
    rows = values.shape[0]
    high = values.astype(jnp.bfloat16)
    left = values - high.astype(jnp.float32)
    middle = left.astype(jnp.bfloat16)
    low = (left - middle.astype(jnp.float32)).astype(jnp.bfloat16)
    parts = jnp.concatenate([high, middle, low], axis=0)
    sums = jnp.dot(parts, zero_one, preferred_element_type=jnp.float32)
    return sums[:rows] + (sums[rows : 2 * rows] + sums[2 * rows :])


def call(kernel, args, outs, scratch, anywhere=0, grant=12, filled=0):
    whole = pl.BlockSpec(memory_space=pltpu.VMEM)
    there = pl.BlockSpec(memory_space=pl.ANY)
    size = sum(a.size * a.dtype.itemsize for a in args)
    return pl.pallas_call(
        kernel,
        out_shape=[s if hasattr(s, "dtype") else jax.ShapeDtypeStruct(s, jnp.float32) for s in outs],
        in_specs=[there] * anywhere + [whole] * (len(args) - anywhere),
        out_specs=[whole] * len(outs),
        scratch_shapes=scratch,
        input_output_aliases={len(args) - filled + k: k for k in range(filled)},
        compiler_params=pltpu.CompilerParams(vmem_limit_bytes=grant * 1024 * 1024),
        cost_estimate=pl.CostEstimate(flops=0, bytes_accessed=size, transcendentals=0),
    )(*[pltpu.with_memory_space_constraint(a, pltpu.HBM) for a in args[:anywhere]], *args[anywhere:])


def ring(axis):
    count = lax.axis_size(axis)
    up = [(i, (i + 1) % count) for i in range(count)]
    return up, [(j, i) for i, j in up]


def both_ways(to_lower, to_upper, axis):
    up, down = ring(axis)
    from_lower = lax.ppermute(to_upper, axis, up)
    from_upper = lax.ppermute(to_lower, axis, down)
    return from_lower, from_upper


def per_device(populations, fluid, label, wall_wetting, target):
    vmem = lambda *shape: pltpu.VMEM(shape, jnp.float32)
    plane = (ROWS, DEPTH)
    two = (2, *plane)
    edge = (22, 2, HALO, DEPTH)
    low, high, small = call(
        edges_kernel,
        (populations, fluid, label, target, wall_wetting.reshape(2, DEPTH)),
        (edge, edge, (4, 2, OWN, DEPTH)),
        (
            pltpu.VMEM((2, 2, OWN, DEPTH), jnp.int32),
            vmem(2, DEPTH),
            pltpu.SemaphoreType.DMA((8,)),
        ),
        anywhere=5,
    )
    below, above = both_ways(low, high, "gy")
    blocks = (OWN // 2) * (DEPTH // 4)
    started = ((19, *two), (3, *two), two, two, two, two, START[LEFTWARD].shape, START[RIGHTWARD].shape)
    *own, chooser = call(
        own_kernel,
        (populations, small),
        (*started, jax.ShapeDtypeStruct((blocks, LABELS), jnp.bfloat16)),
        (vmem(DEPTH, OWN),),
    )
    beside = (vmem(2, TALL, DEPTH), vmem(2, TALL, DEPTH))
    lin, flow, density, effective, share, target_wide, to_left, to_right = call(
        halo_kernel, (small, below, above, *own), started, beside, filled=len(started)
    )
    from_left, from_right = both_ways(to_left, to_right, "gx")
    wide6 = (6, TALL, DEPTH)
    work = (vmem(19, 4, TALL, DEPTH), vmem(10, 4, TALL, DEPTH))
    begun = call(first_flight_kernel, (effective, share), ((3, *wide6), wide6, wide6), ())
    masks, field0, _, speed0, pull0, state, flow, density, effective, to_left, to_right = call(
        functools.partial(step_kernel, True),
        (lin, flow, density, effective, share, from_left, from_right, *begun),
        (
            (3, *wide6), wide6, wide6, (3, 4, *plane), (3, *two),
            (19, *two), (3, *two), two, two, SECOND[LEFTWARD].shape, SECOND[RIGHTWARD].shape,
        ),
        (*work, *beside),
        filled=3,
    )
    from_left, from_right = both_ways(to_left, to_right, "gx")
    less = (MID, DEPTH)
    field1, doubled, lin = call(
        second_flight_kernel, (state, effective, share), (wide6, wide6, (19, *two)), ()
    )
    field1, _, speed1, pull1, misfit, to_left, to_right = call(
        functools.partial(step_kernel, False),
        (lin, flow, density, share, target_wide, masks, from_left, from_right, field1, doubled),
        (wide6, wide6, (3, 4, *plane), (3, *two), (2, *less), (3, *less), (3, *less)),
        work,
        filled=2,
    )
    from_left, from_right = both_ways(to_left, to_right, "gx")
    pulled = (vmem(3, 4, TALL, DEPTH), vmem(2, 4, TALL, DEPTH))
    (ahead,) = call(third_flight_kernel, (misfit,), ((3, *wide6),), ())
    _, adjoint, turned, wall, to_left, to_right, part_left, part_right = call(
        last_reverse_kernel,
        (from_left, from_right, masks, field1, speed1, pull1, speed0, ahead),
        ((3, *wide6), (19, 2, TALL, DEPTH), (10, 2, TALL, DEPTH), (2, *less), BACK[RIGHTWARD].shape, BACK[LEFTWARD].shape, (3, *less), (3, *less)),
        (vmem(3, 2, TALL, DEPTH), *pulled, vmem(19, 2, *less)),
        filled=1,
    )
    from_left, from_right = both_ways(to_left, to_right, "gx")
    come = vmem(2, 5, TALL, DEPTH)
    more, label_part = call(
        wall_kernel,
        (adjoint, turned, wall, part_left, part_right, from_left, from_right, masks, field0, speed0, chooser),
        ((2, OWN, DEPTH), (1, LABELS)),
        (come, *pulled, vmem(OWN, DEPTH)),
    )
    count = lax.axis_size("gy")
    wetting_grad = label_part
    for step in range(1, count):
        wetting_grad = wetting_grad + lax.ppermute(
            label_part, "gy", [(i, (i + step) % count) for i in range(count)]
        )
    (grad,) = call(
        grad_kernel,
        (adjoint, turned, more, from_left, from_right, masks, field0, speed0, pull0),
        (populations.shape,),
        (come,),
    )
    return (grad, wetting_grad.reshape(-1))


def solution(mesh):
    return jax.shard_map(
        per_device,
        mesh=mesh,
        in_specs=(
            P(None, "gx", "gy", None),
            P("gx", "gy", None),
            P("gx", "gy", None),
            P("gx"),
            P("gx", "gy", None),
        ),
        out_specs=(P(None, "gx", "gy", None), P("gx")),
        check_vma=False,
    )
```

```python
import functools

import jax
import jax.numpy as jnp
from jax import lax
from jax.experimental import pallas as pl
from jax.experimental.pallas import tpu as pltpu
from jax.sharding import PartitionSpec as P

HALO = 8
PAD = 8
OWN = 32
ROWS = OWN + 2 * HALO
TALL = ROWS + 2 * PAD
MID = OWN + HALO
DEPTH = 128
CHUNKS = ROWS // 8
LABELS = 256

VECTORS = (
    (0, 0, 0), (1, 0, 0), (-1, 0, 0), (0, 1, 0), (0, -1, 0), (0, 0, 1), (0, 0, -1),
    (1, 1, 0), (-1, -1, 0), (1, -1, 0), (-1, 1, 0), (1, 0, 1), (-1, 0, -1), (1, 0, -1), (-1, 0, 1),
    (0, 1, 1), (0, -1, -1), (0, 1, -1), (0, -1, 1),
)
OPPOSITE = (0, 2, 1, 4, 3, 6, 5, 8, 7, 10, 9, 12, 11, 14, 13, 16, 15, 18, 17)
INDEX = {v: i for i, v in enumerate(VECTORS)}
RIGHTWARD = tuple(i for i in range(19) if VECTORS[i][0] == 1)
LEFTWARD = tuple(i for i in range(19) if VECTORS[i][0] == -1)
TURNED = tuple(i for i in range(19) if VECTORS[i][2] != 0)
PLANES = ((0, 1), (1, 2), (0, 2))
COUPLING = 5.0
SHEAR = 1.2
BULK = 1.19
THIRD = 1.5
FOURTH = 1.4
TRACE = (BULK - SHEAR) / 3.0
PULL = COUPLING / 36.0


def axis_index_of(axis, sign):
    v = [0, 0, 0]
    v[axis] = sign
    return INDEX[tuple(v)]


def edge_index_of(a, b, sa, sb):
    v = [0, 0, 0]
    v[a], v[b] = sa, sb
    return INDEX[tuple(v)]


def add(*terms):
    total = None
    for term in terms:
        if term is not None:
            total = term if total is None else total + term
    return total


def sub(a, b):
    if b is None:
        return a
    return -b if a is None else a - b


def scale(c, a):
    return None if a is None else c * a


def mul(a, b):
    return None if a is None or b is None else a * b


def moments(f):
    fourth, mixed, third = {}, {}, {}
    for a, b in PLANES:
        pp, mm = f[edge_index_of(a, b, 1, 1)], f[edge_index_of(a, b, -1, -1)]
        pm, mp = f[edge_index_of(a, b, 1, -1)], f[edge_index_of(a, b, -1, 1)]
        even, odd, cross, skew = pp + mm, pp - mm, pm + mp, pm - mp
        fourth[a, b] = even + cross
        mixed[a, b] = even - cross
        third[a, b] = odd + skew
        third[b, a] = odd - skew
    first, diagonal, total = [], [], f[0]
    for a in range(3):
        b, c = [k for k in range(3) if k != a]
        plus, minus = f[axis_index_of(a, 1)], f[axis_index_of(a, -1)]
        both = plus + minus
        total = total + both
        diagonal.append(both + fourth[tuple(sorted((a, b)))] + fourth[tuple(sorted((a, c)))])
        first.append((plus - minus) + third[a, b] + third[a, c])
    total = total + fourth[0, 1] + fourth[1, 2] + fourth[0, 2]
    return total, first, diagonal, mixed, third, fourth


def from_moments(first, diagonal, mixed, third, fourth, which):
    out = {}
    for a, b in PLANES:
        even, cross = fourth[a, b] + mixed[a, b], fourth[a, b] - mixed[a, b]
        odd, skew = third[a, b] + third[b, a], third[a, b] - third[b, a]
        out[edge_index_of(a, b, 1, 1)] = even + odd
        out[edge_index_of(a, b, -1, -1)] = even - odd
        out[edge_index_of(a, b, 1, -1)] = cross + skew
        out[edge_index_of(a, b, -1, 1)] = cross - skew
    for a in range(3):
        b, c = [k for k in range(3) if k != a]
        even = diagonal[a] - 2.0 * (fourth[tuple(sorted((a, b)))] + fourth[tuple(sorted((a, c)))])
        odd = first[a] - 2.0 * (third[a, b] + third[a, c])
        out[axis_index_of(a, 1)] = even + odd
        out[axis_index_of(a, -1)] = even - odd
    out[0] = 4.0 * (fourth[0, 1] + fourth[1, 2] + fourth[0, 2]) - 2.0 * (diagonal[0] + diagonal[1] + diagonal[2])
    return {i: out[i] for i in which}


def linear_part(f, share, which):
    total, first, diagonal, mixed, third, fourth = moments(f)
    half, quarter = (0.5 * SHEAR) * share, (0.25 * SHEAR) * share
    trace = (0.5 * TRACE) * share * (diagonal[0] + diagonal[1] + diagonal[2])
    by_third, by_fourth = (0.25 * THIRD) * share, (0.25 * FOURTH) * share
    change = from_moments(
        [half * m for m in first],
        [half * m + trace for m in diagonal],
        {k: quarter * m for k, m in mixed.items()},
        {k: by_third * m for k, m in third.items()},
        {k: by_fourth * m for k, m in fourth.items()},
        which,
    )
    return total, first, {i: f[i] - change[i] for i in which}


def balance_part(density, flow, velocity, share, which):
    d = density * share
    m = [flow[a] * share for a in range(3)]
    square = [m[a] * velocity[a] for a in range(3)]
    whole = square[0] + square[1] + square[2]
    level = d * (SHEAR / 6.0 + 0.5 * TRACE) + whole * (0.5 * TRACE)
    diagonal = [(0.5 * SHEAR) * square[a] + level for a in range(3)]
    scaled = [(0.25 * SHEAR) * velocity[a] for a in range(3)]
    mixed = {(a, b): m[a] * scaled[b] for a, b in PLANES}
    part = [(THIRD / 12.0) * m[a] for a in range(3)]
    third = {}
    fourth = {}
    level = d * (FOURTH / 36.0) + whole * (FOURTH / 12.0)
    for a, b in PLANES:
        third[a, b], third[b, a] = part[a], part[b]
        fourth[a, b] = level - (FOURTH / 8.0) * square[3 - a - b]
    return from_moments([(0.5 * SHEAR) * m[a] for a in range(3)], diagonal, mixed, third, fourth, which)


def dual(r):
    rest = r.get(0)
    even_of, odd_of = [], []
    for a in range(3):
        plus, minus = r.get(axis_index_of(a, 1)), r.get(axis_index_of(a, -1))
        even_of.append(add(plus, minus))
        odd_of.append(sub(plus, minus))
    trace = add(scale(0.5 * TRACE, add(*even_of)), scale(-3.0 * TRACE - SHEAR, rest))
    first = [scale(0.5 * SHEAR, odd) for odd in odd_of]
    diagonal = [add(scale(0.5 * SHEAR, even), trace) for even in even_of]
    even_part = [scale(0.5 * FOURTH, even) for even in even_of]
    odd_part = [scale(0.5 * THIRD, odd) for odd in odd_of]
    rest_part = scale(FOURTH, rest)
    mixed, third, fourth = {}, {}, {}
    for a, b in PLANES:
        pp, mm = r.get(edge_index_of(a, b, 1, 1)), r.get(edge_index_of(a, b, -1, -1))
        pm, mp = r.get(edge_index_of(a, b, 1, -1)), r.get(edge_index_of(a, b, -1, 1))
        even, odd, cross, skew = add(pp, mm), sub(pp, mm), add(pm, mp), sub(pm, mp)
        whole = scale(0.25 * FOURTH, add(even, cross))
        fourth[a, b] = add(sub(sub(whole, even_part[a]), even_part[b]), rest_part)
        mixed[a, b] = scale(0.25 * SHEAR, sub(even, cross))
        third[a, b] = sub(scale(0.25 * THIRD, add(odd, skew)), odd_part[a])
        third[b, a] = sub(scale(0.25 * THIRD, sub(odd, skew)), odd_part[b])
    return first, diagonal, mixed, third, fourth


def flow_adjoint(first, diagonal, mixed, third, fourth, u):
    level = scale(2.0 / 3.0, add(*fourth.values()))
    q = []
    for a in range(3):
        b, c = [k for k in range(3) if k != a]
        ab, ac, bc = tuple(sorted((a, b))), tuple(sorted((a, c))), tuple(sorted((b, c)))
        along = sub(add(scale(2.0, diagonal[a]), level), fourth[bc])
        q.append(
            add(
                first[a],
                scale(1.0 / 3.0, add(third[a, b], third[a, c])),
                mul(u[a], along),
                mul(u[b], mixed[ab]),
                mul(u[c], mixed[ac]),
            )
        )
    return q


def collide_adjoint(r, u):
    t = dual(r)
    first, diagonal, mixed, third, fourth = t
    q = flow_adjoint(*t, u)
    square = [u[a] * u[a] for a in range(3)]
    by_density = None
    for a in range(3):
        b, c = [k for k in range(3) if k != a]
        by_density = add(
            by_density,
            u[a] * (first[a] + (1.0 / 3.0) * (third[a, b] + third[a, c]) - q[a]),
            diagonal[a] * (1.0 / 3.0 + square[a]),
        )
    level = 1.0 / 9.0 + (square[0] + square[1] + square[2]) * (1.0 / 3.0)
    by_density = by_density + (fourth[0, 1] + fourth[1, 2] + fourth[0, 2]) * level
    by_density = by_density - 0.5 * add(*[fourth[a, b] * square[3 - a - b] for a, b in PLANES])
    by_density = by_density + add(*[mixed[a, b] * (u[a] * u[b]) for a, b in PLANES])
    drift = [q[a] - first[a] for a in range(3)]
    base = {0: r[0]}
    for a in range(3):
        base[axis_index_of(a, 1)] = r[axis_index_of(a, 1)] + (drift[a] - diagonal[a])
        base[axis_index_of(a, -1)] = r[axis_index_of(a, -1)] - (drift[a] + diagonal[a])
    for a, b in PLANES:
        along = drift[a] - third[a, b]
        across = drift[b] - third[b, a]
        even = diagonal[a] + diagonal[b] + fourth[a, b]
        same, cross = even + mixed[a, b], even - mixed[a, b]
        both, gap = along + across, along - across
        base[edge_index_of(a, b, 1, 1)] = r[edge_index_of(a, b, 1, 1)] + (both - same)
        base[edge_index_of(a, b, -1, -1)] = r[edge_index_of(a, b, -1, -1)] - (both + same)
        base[edge_index_of(a, b, 1, -1)] = r[edge_index_of(a, b, 1, -1)] + (gap - cross)
        base[edge_index_of(a, b, -1, 1)] = r[edge_index_of(a, b, -1, 1)] - (gap + cross)
    return base, by_density, q


def rolled(x, step):
    return x if step == 0 else pltpu.roll(x, step % DEPTH, 1)


def rows_at(t, shift, offset):
    if isinstance(t, int):
        return pl.ds(t * 8 + offset + shift, 8)
    if shift == 0:
        return pl.ds(pl.multiple_of(t * 8 + offset, 8), 8)
    return pl.ds(t * 8 + (offset + shift), 8)


def flat(t):
    return rows_at(t, 0, 0)


def tall(t, shift=0):
    return rows_at(t, shift, PAD)


def mid(t):
    return pl.ds(t * 8 + (ROWS - MID) // 2, 8)


def mid_tall(t, shift=0):
    return pl.ds(t * 8 + ((ROWS - MID) // 2 + PAD + shift), 8)


class Packed:
    def __init__(self, spans, limit):
        self.spans, self.shift, at = spans, [], spans[0][0]
        for low, high in spans:
            self.shift.append(at - low)
            at += high - low
        self.shape = (-(-(max(self.shift) + limit) // 8) * 8, DEPTH)

    def put(self, ref, k, t, value):
        low, high = max(8 * t, self.spans[k][0]), min(8 * t + 8, self.spans[k][1])
        if low < high:
            ref[self.shift[k] + low : self.shift[k] + high, :] = value[low - 8 * t : high - 8 * t, :]

    def get(self, ref, k, t):
        return ref[pl.ds(8 * t + self.shift[k], 8), :]


def step_spans(first, last, which, more):
    return [(first - VECTORS[i][1], last - VECTORS[i][1]) for i in which] + [(first - 1, last + 1)] * 3 + more


def adjoint_spans(which):
    first, last = (MID - OWN) // 2 - 1, (MID + OWN) // 2 + 1
    rows = [(first + min(VECTORS[i][1], 0), last + max(VECTORS[i][1], 0)) for i in which]
    return rows + [(first, last)] * 3


START = {
    which: Packed(step_spans(2, ROWS - 2, which, [(0, ROWS)] * 2), ROWS) for which in (LEFTWARD, RIGHTWARD)
}
SECOND = {
    which: Packed(step_spans(4, ROWS - 4, which, [(2, ROWS - 2)]), ROWS) for which in (LEFTWARD, RIGHTWARD)
}
BACK = {which: Packed(adjoint_spans(which), MID) for which in (LEFTWARD, RIGHTWARD)}


def each_chunk(body, first=0, last=CHUNKS, unroll=0):
    if unroll == 0:
        for t in range(first, last):
            body(t)
        return

    def step(t, carry):
        body(t)
        return carry

    lax.fori_loop(first, last, step, 0, unroll=unroll)


def gradient_of(field, doubled, p, t):
    at = lambda dp, dy: field[p + dp, tall(t, dy), :]
    rp, rm, lp, lm = at(1, 1), at(1, -1), at(-1, 1), at(-1, -1)
    along_x = doubled[p + 1, tall(t), :] - doubled[p - 1, tall(t), :] + (rp + rm) - (lp + lm)
    along_y = doubled[p, tall(t, 1), :] - doubled[p, tall(t, -1), :] + (rp + lp) - (rm + lm)
    star = 2.0 * at(0, 0) + at(1, 0) + at(-1, 0) + at(0, 1) + at(0, -1)
    return [along_x, along_y, rolled(star, -1) - rolled(star, 1)]


def with_sides(x):
    return 2.0 * x + rolled(x, 1) + rolled(x, -1)


def inner_gradient(field, doubled, here, inner, t):
    at = lambda x, dy: field[x, tall(t, dy), :]
    up, down = at(inner, 1), at(inner, -1)
    along_x = doubled[inner, tall(t), :] + (up + down)
    along_y = doubled[here, tall(t, 1), :] - doubled[here, tall(t, -1), :] + (up - down)
    star = 2.0 * at(here, 0) + at(inner, 0) + at(here, 1) + at(here, -1)
    return [along_x if inner > here else -along_x, along_y, rolled(star, -1) - rolled(star, 1)]


def outer_gradient(field, doubled, p, inner, t):
    at = lambda dy: field[inner, tall(t, dy), :]
    up, down, here = at(1), at(-1), at(0)
    along_x = doubled[inner, tall(t), :] + (up + down)
    return [along_x if inner > p else -along_x, up - down, rolled(here, -1) - rolled(here, 1)]


def send_flow(packed, send_left, send_right, flow, field, doubled, t):
    for send, which, here, inner in ((send_left, LEFTWARD, 0, 1), (send_right, RIGHTWARD, 1, 0)):
        push = field[here, tall(t), :] * (PULL / SHEAR)
        pull = inner_gradient(field, doubled, here, inner, t)
        for a in range(3):
            packed[which].put(send, 5 + a, t, flow[a, here, flat(t), :] + push * pull[a])


def edges_kernel(pops, fluid, label, target, table, low, high, small, whole, values, sems):
    copies = []

    def copy(source, goal):
        one = pltpu.make_async_copy(source, goal, sems.at[len(copies)])
        one.start()
        copies.append(one)

    copy(fluid, whole.at[0])
    copy(label, whole.at[1])
    copy(table, values)
    copy(target, small.at[2])
    for rows, goal in ((pl.ds(0, HALO), low), (pl.ds(OWN - HALO, HALO), high)):
        copy(target.at[:, rows, :], goal.at[21])
        copy(pops.at[:, :, rows, :], goal.at[pl.ds(0, 19)])
    for one in copies[:3]:
        one.wait()
    small[0] = whole[0].astype(jnp.float32)
    small[1] = whole[1].astype(jnp.float32)
    small[3, 0, 0:2, :] = values[...]
    low[19:21] = small[0:2, :, 0:HALO, :]
    high[19:21] = small[0:2, :, OWN - HALO : OWN, :]
    for one in copies[3:]:
        one.wait()


def put_sends(packed, send_left, send_right, t, lin, chosen):
    for x, send, which in ((0, send_left, LEFTWARD), (1, send_right, RIGHTWARD)):
        for k, i in enumerate(which):
            packed[which].put(send, k, t, lin[x][i])
        packed[which].put(send, 8, t, chosen[x])


def start_rows(t, populations, shares, marks, table, outs):
    lin_out, flow_out, density_out, effective_out, share_out, _, send_left, send_right = outs[:8]
    half_low = jnp.broadcast_to(table[0:1, :], (8, DEPTH))
    half_high = jnp.broadcast_to(table[1:2, :], (8, DEPTH))
    lin, chosen = [], []
    for x in range(2):
        share = shares[x]
        spot = jnp.bitwise_and(marks[x], DEPTH - 1)
        wall = jnp.where(
            jnp.bitwise_and(marks[x], DEPTH) == 0,
            jnp.take_along_axis(half_low, spot, axis=1),
            jnp.take_along_axis(half_high, spot, axis=1),
        )
        total, momentum, linear = linear_part(populations[x], share, range(19))
        for i in range(19):
            lin_out[i, x, flat(t), :] = linear[i]
        for a in range(3):
            flow_out[a, x, flat(t), :] = momentum[a]
        density_out[x, flat(t), :] = total
        effective_out[x, flat(t), :] = jnp.where(share > 0, 1.0 - jnp.exp(-total), wall)
        share_out[x, flat(t), :] = share
        lin.append(linear)
        chosen.append(jnp.where(share > 0, total, wall))
    put_sends(START, send_left, send_right, t, lin, chosen)
    START[LEFTWARD].put(send_left, 9, t, shares[0])
    START[RIGHTWARD].put(send_right, 9, t, shares[1])


def place_own(outs, t):
    for x in range(2):
        value = outs[3][x, flat(t), :]
        outs[8][x, tall(t), :] = value
        outs[9][x, tall(t), :] = with_sides(value)


def send_own(outs, t):
    send_flow(START, outs[6], outs[7], outs[1], outs[8], outs[9], t)


def own_kernel(pops, small, *refs):
    outs, chooser, turned_label = refs[:10], refs[10], refs[11]
    outs[5][:, HALO : HALO + OWN, :] = small[2]

    def body(t):
        rows = rows_at(t, 0, -HALO)
        start_rows(
            t,
            [{i: pops[i, x, rows, :] for i in range(19)} for x in range(2)],
            [small[0, x, rows, :] for x in range(2)],
            [small[1, x, rows, :].astype(jnp.int32) for x in range(2)],
            small[3, 0, 0:2, :],
            outs,
        )

    each_chunk(body, HALO // 8, (HALO + OWN) // 8)

    each_chunk(functools.partial(place_own, outs), HALO // 8, (HALO + OWN) // 8)
    each_chunk(functools.partial(send_own, outs), HALO // 8 + 1, (HALO + OWN) // 8 - 1)

    marks = jnp.bitwise_and(small[1, 0].astype(jnp.int32), LABELS - 1).astype(jnp.float32)
    turned_label[...] = jnp.transpose(marks)
    quads = DEPTH // 4
    by_quad = turned_label[pl.ds(0, quads, stride=4), :]
    names = lax.broadcasted_iota(jnp.int32, (quads, LABELS), 1).astype(jnp.float32)
    for k in range(OWN // 2):
        column = jnp.broadcast_to(by_quad[:, 2 * k : 2 * k + 1], (quads, LABELS))
        chooser[quads * k : quads * (k + 1), :] = (column == names).astype(jnp.bfloat16)


def halo_kernel(small, below, above, *refs):
    outs = refs[10:]
    for t, edge in ((0, below), (CHUNKS - 1, above)):
        outs[5][:, 8 * t : 8 * t + 8, :] = edge[21]
        start_rows(
            t,
            [{i: edge[i, x] for i in range(19)} for x in range(2)],
            [edge[19, x] for x in range(2)],
            [edge[20, x].astype(jnp.int32) for x in range(2)],
            small[3, 0, 0:2, :],
            outs,
        )
        place_own(outs, t)
    for t in (0, 1, CHUNKS - 2, CHUNKS - 1):
        send_own(outs, t)


def put_field(field, doubled, p, t, value):
    field[p, tall(t), :] = value
    doubled[p, tall(t), :] = with_sides(value)


def put_masks(masks, p, t, share):
    masks[0, p, tall(t), :] = share
    masks[1, p, tall(t), :] = rolled(share, 1)
    masks[2, p, tall(t), :] = rolled(share, -1)


def first_flight_kernel(effective, share, masks, field, doubled):
    def body(t):
        for x in range(2):
            put_field(field, doubled, 2 + x, t, effective[x, flat(t), :])
            put_masks(masks, 2 + x, t, share[x, flat(t), :])

    each_chunk(body)


def second_flight_kernel(state, effective, share, field, doubled, lin):
    def body(t):
        for x in range(2):
            put_field(field, doubled, 2 + x, t, effective[x, flat(t), :])
            f = {i: state[i, x, flat(t), :] for i in range(19)}
            linear = linear_part(f, share[x, flat(t), :], range(19))[2]
            for i in range(19):
                lin[i, x, flat(t), :] = linear[i]

    each_chunk(body)


def step_kernel(is_first, *refs):
    if is_first:
        (lin, flow, density, effective, share, from_left, from_right, _, _, _,
         masks, field, doubled, speed, pull_out, state_out, flow_out, density_out, effective_out,
         send_left, send_right,
         relaxed, turned, next_field, next_doubled) = refs
    else:
        (lin, flow, density, share, target, masks, from_left, from_right, _, _,
         field, doubled, speed, pull_out, misfit_out, send_left, send_right,
         relaxed, turned) = refs

    packed = START if is_first else SECOND

    def place(t):
        for near, come, which in ((1, from_left, RIGHTWARD), (4, from_right, LEFTWARD)):
            s = packed[which].get(come, 9, t) if is_first else masks[0, near, tall(t), :]
            chosen = packed[which].get(come, 8, t)
            put_field(field, doubled, near, t, jnp.where(s > 0, 1.0 - jnp.exp(-chosen), chosen))
            if is_first:
                put_masks(masks, near, t, s)

    each_chunk(place)

    def collide(t):
        for p in range(1, 5):
            psi = field[p, tall(t), :]
            s = masks[0, p, tall(t), :]
            if p in (2, 3):
                pull = gradient_of(field, doubled, p, t)
                rho = density[p - 2, flat(t), :]
                mom = [flow[a, p - 2, flat(t), :] for a in range(3)]
                which = range(19)
                lin_at = {i: lin[i, p - 2, flat(t), :] for i in which}
                for a in range(3):
                    pull_out[a, p - 2, flat(t), :] = pull[a]
            else:
                pull = outer_gradient(field, doubled, p, 2 if p == 1 else 3, t)
                come = from_left if p == 1 else from_right
                which = RIGHTWARD if p == 1 else LEFTWARD
                rho = packed[which].get(come, 8, t)
                mom = [packed[which].get(come, 5 + a, t) for a in range(3)]
                lin_at = {i: packed[which].get(come, k, t) for k, i in enumerate(which)}
            push = psi * (PULL / SHEAR)
            full = [mom[a] + push * pull[a] for a in range(3)]
            inverse = 1.0 / rho
            u = [full[a] * inverse for a in range(3)]
            for a in range(3):
                speed[a, p - 1, flat(t), :] = u[a]
            part = balance_part(rho, full, u, s, which)
            for i in which:
                value = lin_at[i] + part[i]
                relaxed[i, p - 1, tall(t), :] = value
                if i in TURNED:
                    turned[TURNED.index(i), p - 1, tall(t), :] = rolled(value, VECTORS[i][2])

    each_chunk(collide, unroll=3)

    def streamed(x, rows):
        f = {0: relaxed[0, 1 + x, rows(0), :]}
        for i in range(1, 19):
            cx, cy, cz = VECTORS[i]
            if cz:
                source = turned[TURNED.index(i), 1 + x - cx, rows(-cy), :]
            else:
                source = relaxed[i, 1 + x - cx, rows(-cy), :]
            open_ = masks[cz % 3, 2 + x - cx, rows(-cy), :] > 0
            f[i] = jnp.where(open_, source, relaxed[OPPOSITE[i], 1 + x, rows(0), :])
        return f

    def stream(t):
        lin_sent, chosen_sent = [], []
        for x in range(2):
            s = share[x, flat(t), :]
            f = streamed(x, lambda dy: tall(t, dy))
            total, momentum, linear = linear_part(f, s, (LEFTWARD, RIGHTWARD)[x])
            held = effective[x, flat(t), :]
            eff = jnp.where(s > 0, 1.0 - jnp.exp(-total), held)
            for i in range(19):
                state_out[i, x, flat(t), :] = f[i]
            for a in range(3):
                flow_out[a, x, flat(t), :] = momentum[a]
            density_out[x, flat(t), :] = total
            effective_out[x, flat(t), :] = eff
            next_field[x, tall(t), :] = eff
            next_doubled[x, tall(t), :] = with_sides(eff)
            lin_sent.append(linear)
            chosen_sent.append(jnp.where(s > 0, total, held))
        put_sends(SECOND, send_left, send_right, t, lin_sent, chosen_sent)

    def compare(t):
        for x, near, far in ((0, send_left, send_right), (1, send_right, send_left)):
            f = streamed(x, lambda dy: mid_tall(t, dy))
            s = share[x, mid(t), :]
            misfit = s * (add(*[f[i] for i in range(19)]) - target[x, mid(t), :])
            misfit_out[x, flat(t), :] = misfit
            near[0, flat(t), :] = misfit
            far[1, flat(t), :] = misfit
            far[2, flat(t), :] = s

    if is_first:
        each_chunk(stream)
        each_chunk(functools.partial(send_flow, SECOND, send_left, send_right, flow_out, next_field, next_doubled))
    else:
        each_chunk(compare, 0, MID // 8)


def spread_of(pulled, pulled_doubled, p, rows):
    at = lambda a, dp, dy: pulled[a, p + dp, rows(dy), :]
    two = lambda a, dp, dy: pulled_doubled[a, p + dp, rows(dy), :]
    along_x = two(0, 1, 0) - two(0, -1, 0) + (at(0, 1, 1) + at(0, 1, -1)) - (at(0, -1, 1) + at(0, -1, -1))
    along_y = two(1, 0, 1) - two(1, 0, -1) + (at(1, 1, 1) + at(1, -1, 1)) - (at(1, 1, -1) + at(1, -1, -1))
    star = 2.0 * at(2, 0, 0) + at(2, 1, 0) + at(2, -1, 0) + at(2, 0, 1) + at(2, 0, -1)
    along_z = rolled(star, -1) - rolled(star, 1)
    return (along_x + along_y + along_z) * (-1.0 / 36.0)


def put_pulled(pulled, pulled_doubled, p, rows, psi, q):
    for a in range(3):
        s = (COUPLING / SHEAR) * psi * q[a]
        pulled[a, p, rows(0), :] = s
        if a < 2:
            pulled_doubled[a, p, rows(0), :] = with_sides(s)


def mask_ahead(masks, i, p, rows):
    cx, cy, cz = VECTORS[i]
    return masks[(-cz) % 3, p + cx, rows(cy), :] > 0


def middle(t):
    return lambda dy: mid_tall(t, dy)


def put_ahead(ahead, p, rows, value):
    ahead[0, p, rows(0), :] = value
    ahead[1, p, rows(0), :] = rolled(value, 1)
    ahead[2, p, rows(0), :] = rolled(value, -1)


def third_flight_kernel(misfit, ahead):
    def body(t):
        for x in range(2):
            put_ahead(ahead, 2 + x, middle(t), misfit[x, flat(t), :])

    each_chunk(body, 0, MID // 8)


def last_reverse_kernel(
    from_left, from_right, masks, field, speed, pull, early_speed, _,
    ahead, adjoint, turned, wall_out, send_left, send_right, part_left, part_right,
    far_masks, pulled, pulled_doubled, base,
):
    def place(t):
        rows = middle(t)
        for p in (0, 1, 4, 5):
            put_ahead(ahead, p, rows, from_left[1 - p, flat(t), :] if p < 2 else from_right[p - 4, flat(t), :])
        for k, source in enumerate((from_left, from_right)):
            s = source[2, flat(t), :]
            far_masks[0, k, rows(0), :] = s
            far_masks[1, k, rows(0), :] = rolled(s, 1)
            far_masks[2, k, rows(0), :] = rolled(s, -1)

    each_chunk(place, 0, MID // 8)

    def collide(t):
        rows = middle(t)
        for p in range(1, 5):
            s = masks[0, p, rows(0), :]
            here = ahead[0, p, rows(0), :]
            r = {0: here}
            for i in range(1, 19):
                cx, cy, cz = VECTORS[i]
                there = ahead[(-cz) % 3, p + cx, rows(cy), :]
                if p + cx in (0, 5):
                    open_ = far_masks[(-cz) % 3, (p + cx) // 5, rows(cy), :] > 0
                else:
                    open_ = mask_ahead(masks, i, p, rows)
                r[i] = jnp.where(open_, there, here)
            psi = field[p, rows(0), :]
            u = [speed[a, p - 1, mid(t), :] for a in range(3)]
            if p in (2, 3):
                rest, by_density, q = collide_adjoint(r, u)
                along = add(*[q[a] * pull[a, p - 2, mid(t), :] for a in range(3)])
                const = by_density + along * ((PULL / SHEAR) * (1.0 - psi))
                for i in range(19):
                    base[i, p - 2, flat(t), :] = rest[i] + const
            else:
                q = flow_adjoint(*dual(r), u)
            put_pulled(pulled, pulled_doubled, p - 1, rows, s * psi, q)

    each_chunk(collide, 0, MID // 8)

    def finish(t):
        rows = middle(t)
        for x in range(2):
            s = masks[0, 2 + x, rows(0), :]
            spread = spread_of(pulled, pulled_doubled, 1 + x, rows)
            wall_out[x, flat(t), :] = (1.0 - s) * spread
            more = s * spread * (1.0 - field[2 + x, rows(0), :])
            for i in range(19):
                value = base[i, x, flat(t), :] + more
                adjoint[i, x, rows(0), :] = value
                if i in TURNED:
                    turned[TURNED.index(i), x, rows(0), :] = rolled(value, -VECTORS[i][2])

    each_chunk(finish, 0, MID // 8)

    def part(t):
        rows = middle(t)
        for x, send, kept, sent, skipped in ((0, send_left, part_left, RIGHTWARD, -1), (1, send_right, part_right, LEFTWARD, 1)):
            p = 2 + x
            s = masks[0, p, rows(0), :]
            r = {}
            for i in range(19):
                if VECTORS[i][0] != skipped:
                    r[i] = adjoint_ahead(adjoint, turned, masks, i, x, rows)
            u = [early_speed[a, p - 1, mid(t), :] for a in range(3)]
            q = flow_adjoint(*dual(r), u)
            for a in range(3):
                BACK[sent].put(send, 5 + a, t, s * q[a])
                kept[a, flat(t), :] = s * q[a]
            for k, i in enumerate(sent):
                BACK[sent].put(send, k, t, adjoint[i, x, rows(0), :])

    each_chunk(part, 0, MID // 8)


def adjoint_ahead(adjoint, turned, masks, i, x, rows):
    cx, cy, cz = VECTORS[i]
    if i == 0:
        return adjoint[0, x, rows(0), :]
    if cz:
        there = turned[TURNED.index(i), x + cx, rows(cy), :]
    else:
        there = adjoint[i, x + cx, rows(cy), :]
    return jnp.where(mask_ahead(masks, i, 2 + x, rows), there, adjoint[OPPOSITE[i], x, rows(0), :])


def place_sides(come, from_left, from_right, t):
    for side, source, which in ((0, from_left, LEFTWARD), (1, from_right, RIGHTWARD)):
        for k, i in enumerate(which):
            come[side, k, mid_tall(t), :] = rolled(BACK[which].get(source, k, t), -VECTORS[i][2])


def arrived(come, adjoint, masks, i, x, rows):
    which = LEFTWARD if x == 0 else RIGHTWARD
    there = come[x, which.index(i), rows(VECTORS[i][1]), :]
    return jnp.where(mask_ahead(masks, i, 2 + x, rows), there, adjoint[OPPOSITE[i], x, rows(0), :])


def wall_kernel(
    adjoint, turned, wall, part_left, part_right, from_left, from_right, masks, field, speed, chooser,
    more_out, label_part,
    come, pulled, pulled_doubled, totals,
):
    each_chunk(functools.partial(place_sides, come, from_left, from_right), 0, MID // 8)

    def collide(t):
        rows = middle(t)
        for x, part, which in ((0, part_left, LEFTWARD), (1, part_right, RIGHTWARD)):
            p = 2 + x
            s = masks[0, p, rows(0), :]
            r = {i: arrived(come, adjoint, masks, i, x, rows) for i in which}
            u = [speed[a, p - 1, mid(t), :] for a in range(3)]
            rest = flow_adjoint(*dual(r), u)
            q = [part[a, flat(t), :] + s * rest[a] for a in range(3)]
            put_pulled(pulled, pulled_doubled, p - 1, rows, field[p, rows(0), :], q)
        for x, source, which in ((0, from_left, LEFTWARD), (1, from_right, RIGHTWARD)):
            p = 1 if x == 0 else 4
            s = masks[0, p, rows(0), :]
            r = {}
            for i in [OPPOSITE[j] for j in which]:
                cx, cy, cz = VECTORS[i]
                if cz:
                    there = turned[TURNED.index(i), x, rows(cy), :]
                else:
                    there = adjoint[i, x, rows(cy), :]
                here = BACK[which].get(source, which.index(OPPOSITE[i]), t)
                r[i] = jnp.where(mask_ahead(masks, i, p, rows), there, here)
            u = [speed[a, p - 1, mid(t), :] for a in range(3)]
            rest = flow_adjoint(*dual(r), u)
            q = [BACK[which].get(source, 5 + a, t) + s * rest[a] for a in range(3)]
            put_pulled(pulled, pulled_doubled, p - 1, rows, field[p, rows(0), :], q)

    each_chunk(collide, 0, MID // 8)

    def finish(t):
        total = None
        for x in range(2):
            s = masks[0, 2 + x, tall(t), :]
            spread = spread_of(pulled, pulled_doubled, 1 + x, lambda dy: tall(t, dy))
            step_wall = wall[x, pl.ds(t * 8 - (ROWS - MID) // 2, 8), :]
            total = add(total, (1.0 - s) * spread + step_wall)
            more_out[x, rows_at(t, 0, -HALO), :] = s * spread * (1.0 - field[2 + x, tall(t), :])
        totals[rows_at(t, 0, -HALO), :] = total

    each_chunk(finish, HALO // 8, (HALO + OWN) // 8)

    blocks = (OWN // 2) * (DEPTH // 4)
    column = lax.broadcasted_iota(jnp.int32, (DEPTH, blocks), 1)
    quad = lax.broadcasted_iota(jnp.int32, (DEPTH, blocks), 0) // 4
    gather = (jnp.bitwise_and(column, DEPTH // 4 - 1) == quad).astype(jnp.bfloat16)
    by_block = exact_dot(totals[...], gather)
    pair = lax.broadcasted_iota(jnp.int32, (OWN, blocks), 0) // 2
    wanted = lax.broadcasted_iota(jnp.int32, (OWN, blocks), 1) // (DEPTH // 4)
    by_block = jnp.where(pair == wanted, by_block, 0.0)
    by_label = exact_dot(by_block, chooser[...])
    label_part[...] = jnp.sum(by_label, axis=0, keepdims=True)


def grad_kernel(
    adjoint, turned, more, from_left, from_right, masks, field, speed, pull,
    grad,
    come,
):
    each_chunk(functools.partial(place_sides, come, from_left, from_right), 0, MID // 8)

    def collide(t):
        rows = lambda dy: tall(t, dy)
        for x in range(2):
            p = 2 + x
            s = masks[0, p, tall(t), :]
            r = {}
            for i in range(19):
                if VECTORS[i][0] == 2 * x - 1:
                    r[i] = s * arrived(come, adjoint, masks, i, x, rows)
                else:
                    r[i] = s * adjoint_ahead(adjoint, turned, masks, i, x, rows)
            u = [speed[a, p - 1, flat(t), :] for a in range(3)]
            rest, by_density, q = collide_adjoint(r, u)
            along = add(*[q[a] * pull[a, x, flat(t), :] for a in range(3)])
            const = by_density + along * ((PULL / SHEAR) * (1.0 - field[p, tall(t), :]))
            const = const + more[x, rows_at(t, 0, -HALO), :]
            for i in range(19):
                grad[i, x, rows_at(t, 0, -HALO), :] = rest[i] + const

    each_chunk(collide, HALO // 8, (HALO + OWN) // 8)


def exact_dot(values, zero_one):
    rows = values.shape[0]
    high = values.astype(jnp.bfloat16)
    left = values - high.astype(jnp.float32)
    middle = left.astype(jnp.bfloat16)
    low = (left - middle.astype(jnp.float32)).astype(jnp.bfloat16)
    parts = jnp.concatenate([high, middle, low], axis=0)
    sums = jnp.dot(parts, zero_one, preferred_element_type=jnp.float32)
    return sums[:rows] + (sums[rows : 2 * rows] + sums[2 * rows :])


def call(kernel, args, outs, scratch, anywhere=0, grant=12, filled=0):
    whole = pl.BlockSpec(memory_space=pltpu.VMEM)
    there = pl.BlockSpec(memory_space=pl.ANY)
    size = sum(a.size * a.dtype.itemsize for a in args)
    return pl.pallas_call(
        kernel,
        out_shape=[s if hasattr(s, "dtype") else jax.ShapeDtypeStruct(s, jnp.float32) for s in outs],
        in_specs=[there] * anywhere + [whole] * (len(args) - anywhere),
        out_specs=[whole] * len(outs),
        scratch_shapes=scratch,
        input_output_aliases={len(args) - filled + k: k for k in range(filled)},
        compiler_params=pltpu.CompilerParams(vmem_limit_bytes=grant * 1024 * 1024),
        cost_estimate=pl.CostEstimate(flops=0, bytes_accessed=size, transcendentals=0),
    )(*[pltpu.with_memory_space_constraint(a, pltpu.HBM) for a in args[:anywhere]], *args[anywhere:])


def ring(axis):
    count = lax.axis_size(axis)
    up = [(i, (i + 1) % count) for i in range(count)]
    return up, [(j, i) for i, j in up]


def both_ways(to_lower, to_upper, axis):
    up, down = ring(axis)
    from_lower = lax.ppermute(to_upper, axis, up)
    from_upper = lax.ppermute(to_lower, axis, down)
    return from_lower, from_upper


def per_device(populations, fluid, label, wall_wetting, target):
    vmem = lambda *shape: pltpu.VMEM(shape, jnp.float32)
    plane = (ROWS, DEPTH)
    two = (2, *plane)
    edge = (22, 2, HALO, DEPTH)
    low, high, small = call(
        edges_kernel,
        (populations, fluid, label, target, wall_wetting.reshape(2, DEPTH)),
        (edge, edge, (4, 2, OWN, DEPTH)),
        (
            pltpu.VMEM((2, 2, OWN, DEPTH), jnp.int32),
            vmem(2, DEPTH),
            pltpu.SemaphoreType.DMA((8,)),
        ),
        anywhere=5,
    )
    below, above = both_ways(low, high, "gy")
    blocks = (OWN // 2) * (DEPTH // 4)
    started = ((19, *two), (3, *two), two, two, two, two, START[LEFTWARD].shape, START[RIGHTWARD].shape)
    started += ((2, TALL, DEPTH),) * 2
    *own, chooser = call(
        own_kernel,
        (populations, small),
        (*started, jax.ShapeDtypeStruct((blocks, LABELS), jnp.bfloat16)),
        (vmem(DEPTH, OWN),),
    )
    beside = (vmem(2, TALL, DEPTH), vmem(2, TALL, DEPTH))
    lin, flow, density, effective, share, target_wide, to_left, to_right, _, _ = call(
        halo_kernel, (small, below, above, *own), started, (), filled=len(started)
    )
    from_left, from_right = both_ways(to_left, to_right, "gx")
    wide6 = (6, TALL, DEPTH)
    work = (vmem(19, 4, TALL, DEPTH), vmem(10, 4, TALL, DEPTH))
    begun = call(first_flight_kernel, (effective, share), ((3, *wide6), wide6, wide6), ())
    masks, field0, _, speed0, pull0, state, flow, density, effective, to_left, to_right = call(
        functools.partial(step_kernel, True),
        (lin, flow, density, effective, share, from_left, from_right, *begun),
        (
            (3, *wide6), wide6, wide6, (3, 4, *plane), (3, *two),
            (19, *two), (3, *two), two, two, SECOND[LEFTWARD].shape, SECOND[RIGHTWARD].shape,
        ),
        (*work, *beside),
        filled=3,
    )
    from_left, from_right = both_ways(to_left, to_right, "gx")
    less = (MID, DEPTH)
    field1, doubled, lin = call(
        second_flight_kernel, (state, effective, share), (wide6, wide6, (19, *two)), ()
    )
    field1, _, speed1, pull1, misfit, to_left, to_right = call(
        functools.partial(step_kernel, False),
        (lin, flow, density, share, target_wide, masks, from_left, from_right, field1, doubled),
        (wide6, wide6, (3, 4, *plane), (3, *two), (2, *less), (3, *less), (3, *less)),
        work,
        filled=2,
    )
    from_left, from_right = both_ways(to_left, to_right, "gx")
    pulled = (vmem(3, 4, TALL, DEPTH), vmem(2, 4, TALL, DEPTH))
    (ahead,) = call(third_flight_kernel, (misfit,), ((3, *wide6),), ())
    _, adjoint, turned, wall, to_left, to_right, part_left, part_right = call(
        last_reverse_kernel,
        (from_left, from_right, masks, field1, speed1, pull1, speed0, ahead),
        ((3, *wide6), (19, 2, TALL, DEPTH), (10, 2, TALL, DEPTH), (2, *less), BACK[RIGHTWARD].shape, BACK[LEFTWARD].shape, (3, *less), (3, *less)),
        (vmem(3, 2, TALL, DEPTH), *pulled, vmem(19, 2, *less)),
        filled=1,
    )
    from_left, from_right = both_ways(to_left, to_right, "gx")
    come = vmem(2, 5, TALL, DEPTH)
    more, label_part = call(
        wall_kernel,
        (adjoint, turned, wall, part_left, part_right, from_left, from_right, masks, field0, speed0, chooser),
        ((2, OWN, DEPTH), (1, LABELS)),
        (come, *pulled, vmem(OWN, DEPTH)),
    )
    count = lax.axis_size("gy")
    wetting_grad = label_part
    for step in range(1, count):
        wetting_grad = wetting_grad + lax.ppermute(
            label_part, "gy", [(i, (i + step) % count) for i in range(count)]
        )
    (grad,) = call(
        grad_kernel,
        (adjoint, turned, more, from_left, from_right, masks, field0, speed0, pull0),
        (populations.shape,),
        (come,),
    )
    return (grad, wetting_grad.reshape(-1))


def solution(mesh):
    return jax.shard_map(
        per_device,
        mesh=mesh,
        in_specs=(
            P(None, "gx", "gy", None),
            P("gx", "gy", None),
            P("gx", "gy", None),
            P("gx"),
            P("gx", "gy", None),
        ),
        out_specs=(P(None, "gx", "gy", None), P("gx")),
        check_vma=False,
    )
```
